32 devices in a mesh: lat: 4 (over z), lon: 8 (over y, x, core).
Axes of the slice: x: 2, y: 2, z: 4, core: 2. Of those that a mesh axis runs over, the one named last changes fastest.
Arguments:
- sensitivity: bfloat16 [4, 8, 60, 256, 128], P('lat', 'lon'), may hold values from 0 to 0.07470703
- block_ids: int32 [4, 8, 60], P('lat', 'lon'), may hold values from 0 to 32767, as said below
- block_offsets: int32 [4, 8, 4], P('lat', 'lon'), may hold values from 0 to 60, as said below
- ray_counts: int32 [4, 8], P('lat', 'lon'), may hold values from 1 to 768, as said below
- ray_vector: float32 [4, 4, 8, 768], P(None, 'lat', 'lon'), may hold values from -6 to 6
- damping_vector: float32 [4, 128, 256, 128], P(None, 'lat', 'lon'), may hold values from -6 to 6
- model_vector: float32 [4, 128, 256, 128], P(None, 'lat', 'lon'), may hold values from -6 to 6
- solution: float32 [4, 128, 256, 128], P(None, 'lat', 'lon'), may hold values from -6 to 6
- search: float32 [4, 128, 256, 128], P(None, 'lat', 'lon'), may hold values from -6 to 6
- recurrence: float32 [3, 4], replicated, may hold values from 0.5 to 1.5
Outputs:
- ray_out: float32 [4, 4, 8, 768], P(None, 'lat', 'lon')
- damp_out: float32 [4, 128, 256, 128], P(None, 'lat', 'lon')
- model_out: float32 [4, 128, 256, 128], P(None, 'lat', 'lon')
- solution_out: float32 [4, 128, 256, 128], P(None, 'lat', 'lon')
- search_out: float32 [4, 128, 256, 128], P(None, 'lat', 'lon')
- recurrence_out: float32 [3, 4], replicated
The draws below stay inside these ranges and needn't reach their ends.
Inputs may be any that keep to these rules, and one draw needn't show every extreme that they name: `block_ids`: of the 60 entries of one device at most 4 name blocks of one owner device; some owner is named exactly 4 times by every device. Entries of tiles that belong to no ray block name blocks too. The entries of all devices that name one owner's blocks lie in one patch of 4 x 4 neighbouring columns of that owner. `block_offsets`: each device's offsets start at 0 and never fall; a ray block holding some live ray has 10 to 20 tiles, the others none; some device uses all 60 tiles. A device's live rays are its first ray_counts rays; some device has all 768 live.
All inputs are finite; a program needn't handle non-finite values.
Results may differ from the reference program's by a relative error of at most 0.0003.
Values may be sent and summed in bfloat16 or wider, within the bound.
No kernel may reach another device: no remote copies, remote signals or barrier semaphores. Data moves between devices by JAX's collectives and lax.ppermute only.
A program may use at most 64 MiB of HBM per device.

```python
import jax
import jax.numpy as jnp
from jax import lax

DEPTH = 128
RAYS_BLK = 256
R = 4
KPB = 20
CLAT = 32
CLON = 32
RBMAX = 3
TILES = 60
RAYS = 768
BLK = 1024
CAP = 4
NLAT = 128
NLON = 256
CELLS = 4194304
ROWS_ALL = 4218880
N_LAT = 4
N_LON = 8


def layout(key):
    devices = N_LAT * N_LON
    span = RBMAX * RAYS_BLK
    slots = devices * CAP
    keys = jax.random.split(jax.random.fold_in(key, 7321), 10)
    place = jnp.arange(devices, dtype=jnp.int32)
    raw = jax.random.randint(keys[0], (devices,), 0, span, dtype=jnp.int32)
    counts = 1 + raw * raw // span
    fullest = jax.random.randint(keys[1], (), 0, devices, dtype=jnp.int32)
    counts = jnp.where(place == fullest, span, counts).astype(jnp.int32)
    live_blocks = (counts + RAYS_BLK - 1) // RAYS_BLK
    per_block = jax.random.randint(keys[2], (devices, RBMAX), KPB // 2, KPB + 1, dtype=jnp.int32)
    per_block = jnp.where(place[:, None] == fullest, KPB, per_block)
    per_block = jnp.where(jnp.arange(RBMAX, dtype=jnp.int32)[None, :] < live_blocks[:, None], per_block, 0)
    offsets = jnp.concatenate([jnp.zeros((devices, 1), jnp.int32), jnp.cumsum(per_block, axis=1).astype(jnp.int32)], axis=1)
    hottest = jax.random.randint(keys[3], (), 0, devices, dtype=jnp.int32)
    orders = jax.vmap(lambda sub: jax.random.permutation(sub, slots))(jax.random.split(keys[4], devices)).astype(jnp.int32)
    priority = jnp.where(orders // CAP == hottest, 0, slots) + jnp.arange(slots, dtype=jnp.int32)[None, :]
    ranking = jnp.argsort(priority, axis=1)
    chosen = jnp.take_along_axis(orders, ranking[:, :TILES], axis=1)
    shuffle = jax.vmap(lambda sub: jax.random.permutation(sub, TILES))(jax.random.split(keys[5], devices))
    chosen = jnp.take_along_axis(chosen, shuffle, axis=1)
    owner = (chosen // CAP).astype(jnp.int32)
    corner_lat = jax.random.randint(keys[7], (devices,), 0, CLAT - 3, dtype=jnp.int32)
    corner_lon = jax.random.randint(keys[8], (devices,), 0, CLON - 3, dtype=jnp.int32)
    step_lat = jax.random.randint(keys[6], (devices, TILES), 0, 4, dtype=jnp.int32)
    step_lon = jax.random.randint(keys[9], (devices, TILES), 0, 4, dtype=jnp.int32)
    column = (corner_lat[owner] + step_lat) * CLON + corner_lon[owner] + step_lon
    block_list = (owner * BLK + column).astype(jnp.int32)
    return (counts, offsets, block_list)


def draw_block_ids(key, part):
    return layout(key)[2].reshape(N_LAT, N_LON, TILES)


def draw_block_offsets(key, part):
    return layout(key)[1].reshape(N_LAT, N_LON, RBMAX + 1)


def draw_ray_counts(key, part):
    return layout(key)[0].reshape(N_LAT, N_LON)


def draw_model_vector(key, part):
    level_key, noise_key = jax.random.split(jax.random.fold_in(key, 4409))
    level = jax.random.uniform(level_key, (R, NLAT, NLON, 1), jnp.float32, 0.5, 1.5)
    noise = jnp.clip(jax.random.normal(noise_key, (R, NLAT, NLON, DEPTH), jnp.float32), -4.0, 4.0)
    return (level + noise).astype(jnp.float32)


def block_levels(own_key, shape, shards, least, high):
    gain, own = 1.0, jax.random.fold_in(own_key, 6)
    for axis_at, parts in shards:
        steps = jnp.exp(jax.random.uniform(jax.random.fold_in(own, axis_at), (parts,), jnp.float32, least / len(shards), high / len(shards)))
        gain = gain * jnp.repeat(steps, shape[axis_at] // parts).reshape([-1 if axis == axis_at else 1 for axis in range(len(shape))])
    return gain


def bell_draw(key, extent, scale, limit, cuts=(), kind=jnp.bfloat16):
    factor_of = block_levels(key, extent, cuts, -0.22, 0.18) if cuts else 1.0
    result = jax.random.normal(key, extent, jnp.float32) * scale * factor_of
    return jnp.minimum(jnp.maximum(result, -limit), limit).astype(kind)


def setup_inputs(seed: int = 0) -> dict:
    arg_keys = jax.random.split(jax.random.key(seed), 11)
    sensitivity = jnp.clip(0.07470703 * jax.random.uniform(arg_keys[0], (N_LAT, N_LON, TILES, RAYS_BLK, DEPTH), jnp.float32) ** block_levels(arg_keys[0], (N_LAT, N_LON, TILES, RAYS_BLK, DEPTH), ((0, 4), (1, 8)), -0.2, 0.2), 0.0, 0.07470703).astype(jnp.bfloat16)
    block_ids = draw_block_ids(jax.random.fold_in(arg_keys[10], 71), 0)
    block_offsets = draw_block_offsets(jax.random.fold_in(arg_keys[10], 71), 0)
    ray_counts = draw_ray_counts(jax.random.fold_in(arg_keys[10], 71), 0)
    ray_vector = bell_draw(arg_keys[4], (R, N_LAT, N_LON, RAYS), 1.0, 6.0, ((1, 4), (2, 8)), jnp.float32)
    damping_vector = bell_draw(arg_keys[5], (R, NLAT, NLON, DEPTH), 1.0, 6.0, ((1, 4), (2, 8)), jnp.float32)
    model_vector = draw_model_vector(jax.random.fold_in(arg_keys[10], 71), 0)
    solution = bell_draw(arg_keys[7], (R, NLAT, NLON, DEPTH), 1.0, 6.0, ((1, 4), (2, 8)), jnp.float32)
    search = bell_draw(arg_keys[8], (R, NLAT, NLON, DEPTH), 1.0, 6.0, ((1, 4), (2, 8)), jnp.float32)
    recurrence = jnp.clip(jax.random.uniform(arg_keys[9], (3, R), jnp.float32, 0.5, 1.5), 0.5, 1.5)
    return dict(sensitivity=sensitivity, block_ids=block_ids, block_offsets=block_offsets, ray_counts=ray_counts, ray_vector=ray_vector, damping_vector=damping_vector, model_vector=model_vector, solution=solution, search=search, recurrence=recurrence)


DAMP_WEIGHT = 0.15
EPSILON = 1e-05
HIGHEST_PRECISION = lax.Precision.HIGHEST

def laplace(field):
    padded = jnp.pad(field, ((0, 0), (1, 1), (1, 1), (1, 1)))
    beside_all = padded[:, 2:, 1:-1, 1:-1] + padded[:, :-2, 1:-1, 1:-1]
    beside_all = beside_all + padded[:, 1:-1, 2:, 1:-1] + padded[:, 1:-1, :-2, 1:-1]
    beside_all = beside_all + padded[:, 1:-1, 1:-1, 2:] + padded[:, 1:-1, 1:-1, :-2]
    return 6.0 * field - beside_all

def to_table(field):
    shaped = field.reshape(R, N_LAT, CLAT, N_LON, CLON, DEPTH)
    return shaped.transpose(1, 3, 2, 4, 0, 5).reshape(N_LAT * N_LON * CLAT * CLON, R, DEPTH)

def from_table(table):
    shaped = table.reshape(N_LAT, N_LON, CLAT, CLON, R, DEPTH)
    return shaped.transpose(4, 0, 2, 1, 3, 5).reshape(R, N_LAT * CLAT, N_LON * CLON, DEPTH)

def membership(limits):
    position = jnp.arange(TILES, dtype=jnp.int32)[:, None]
    inside = (position >= limits[None, :-1]) & (position < limits[None, 1:])
    return inside.astype(jnp.float32)

def reference(sensitivity, block_ids, block_offsets, ray_counts, ray_vector, damping_vector, model_vector, solution, search, recurrence):
    devices = N_LAT * N_LON
    alpha_old = recurrence[0]
    rho_bar = recurrence[1]
    phi_bar = recurrence[2]
    kernels = sensitivity.reshape(devices, TILES, RAYS_BLK, DEPTH)
    block_list = block_ids.reshape(devices, TILES)
    bounds = block_offsets.reshape(devices, RBMAX + 1)
    counts = ray_counts.reshape(devices)
    ray_old = ray_vector.reshape(R, devices, RBMAX, RAYS_BLK)
    model_low = to_table(model_vector).astype(jnp.bfloat16)

    def forward(operands):
        kernel, listed, limits = operands
        picked = model_low[listed].astype(jnp.float32)
        products = jnp.einsum('tid,trd->tri', kernel.astype(jnp.float32), picked, precision=HIGHEST_PRECISION)
        return jnp.einsum('tb,tri->rbi', membership(limits), products, precision=HIGHEST_PRECISION)
    traced = lax.map(forward, (kernels, block_list, bounds)).transpose(1, 0, 2, 3)
    ray_index = jnp.arange(RBMAX * RAYS_BLK, dtype=jnp.int32).reshape(RBMAX, RAYS_BLK)
    live_rows = ray_index[None, :, :] < counts[:, None, None]
    alpha_wide = alpha_old[:, None, None, None]
    ray_bar = jnp.where(live_rows[None], traced - alpha_wide * ray_old, 0.0)
    damp_bar = DAMP_WEIGHT * laplace(model_vector) - alpha_wide * damping_vector
    residual_sq = lax.optimization_barrier(jnp.sum(ray_bar * ray_bar, axis=(1, 2, 3))) + lax.optimization_barrier(jnp.sum(damp_bar * damp_bar, axis=(1, 2, 3)))
    beta_new = jnp.sqrt(residual_sq / ROWS_ALL + EPSILON)
    ray_low = ray_bar.astype(jnp.bfloat16)

    def adjoint(operands):
        kernel, limits, ray_rows = operands
        spread = jnp.einsum('tb,rbi->tri', membership(limits), ray_rows.astype(jnp.float32), precision=HIGHEST_PRECISION)
        return jnp.einsum('tid,tri->trd', kernel.astype(jnp.float32), spread, precision=HIGHEST_PRECISION)
    pieces = lax.map(adjoint, (kernels, bounds, ray_low.transpose(1, 0, 2, 3)))
    summed = jax.ops.segment_sum(pieces.reshape(devices * TILES, R, DEPTH), block_list.reshape(devices * TILES), num_segments=devices * CLAT * CLON)
    adjoint_image = from_table(summed) + DAMP_WEIGHT * laplace(damp_bar)
    beta_wide = beta_new[:, None, None, None]
    update = adjoint_image / beta_wide - beta_wide * model_vector
    alpha_new = jnp.sqrt(lax.optimization_barrier(jnp.sum(update * update, axis=(1, 2, 3))) / CELLS + EPSILON)
    model_out = update / alpha_new[:, None, None, None]
    rho_new = jnp.sqrt(rho_bar * rho_bar + beta_new * beta_new)
    cosine = rho_bar / rho_new
    sine_new = beta_new / rho_new
    solution_out = solution + (cosine * phi_bar / rho_new)[:, None, None, None] * search
    search_out = model_out - (sine_new * alpha_new / rho_new)[:, None, None, None] * search
    ray_out = (ray_bar / beta_wide).reshape(R, N_LAT, N_LON, RBMAX * RAYS_BLK)
    damp_out = damp_bar / beta_wide
    recurrence_out = jnp.stack([alpha_new, -cosine * alpha_new, sine_new * phi_bar])
    return (ray_out, damp_out, model_out, solution_out, search_out, recurrence_out)
```

```python
import jax
import jax.numpy as jnp
from jax import lax
from jax.sharding import PartitionSpec as P

DAMP_WEIGHT = 0.15
EPSILON = 1e-05
HIGHEST_PRECISION = lax.Precision.HIGHEST


def with_halo(cells, sides, width):
    for axis, dim in sides:
        count = lax.axis_size(axis)
        ends = count - 1
        head = lax.slice_in_dim(cells, 0, width, axis=dim)
        tail = lax.slice_in_dim(cells, cells.shape[dim] - width, cells.shape[dim], axis=dim)
        cells = jnp.concatenate(
            [
                lax.ppermute(tail, axis, [(i, (i + 1) % count) for i in range(ends)]),
                cells,
                lax.ppermute(head, axis, [((i + 1) % count, i) for i in range(ends)]),
            ],
            axis=dim,
        )
    return cells


def laplace(field):
    padded = with_halo(field, (("lat", 1), ("lon", 2)), 1)
    depth_pad = jnp.pad(field, ((0, 0), (0, 0), (0, 0), (1, 1)))
    beside_all = (
        padded[:, 2:, 1:-1] + padded[:, :-2, 1:-1] + padded[:, 1:-1, 2:] + padded[:, 1:-1, :-2]
    )
    beside_all = beside_all + depth_pad[..., 2:] + depth_pad[..., :-2]
    return 6.0 * field - beside_all


def membership(limits, tiles):
    position = jnp.arange(tiles, dtype=jnp.int32)[:, None]
    inside = (position >= limits[None, :-1]) & (position < limits[None, 1:])
    return inside.astype(jnp.float32)


def per_device(
    sensitivity,
    block_ids,
    block_offsets,
    ray_counts,
    ray_vector,
    damping_vector,
    model_vector,
    solution,
    search,
    recurrence,
):
    lat_size = lax.axis_size("lat")
    lon_size = lax.axis_size("lon")
    devices = lat_size * lon_size
    kernel = sensitivity[0, 0]
    tiles, ray_width, depth = kernel.shape
    block_list = block_ids[0, 0]
    bounds = block_offsets[0, 0]
    count_here = ray_counts[0, 0]
    blocks_dev = bounds.shape[0] - 1
    systems, clat_dev, clon_dev = (
        model_vector.shape[0],
        model_vector.shape[1],
        model_vector.shape[2],
    )
    columns_dev = clat_dev * clon_dev
    capacity = 2 * ((tiles + devices - 1) // devices)
    cells_all = devices * columns_dev * depth
    rows_all = devices * blocks_dev * ray_width + cells_all
    alpha_old = recurrence[0]
    rho_bar = recurrence[1]
    phi_bar = recurrence[2]
    owner_dev = block_list // columns_dev
    column = block_list - owner_dev * columns_dev
    owner_hits = (owner_dev[:, None] == jnp.arange(devices, dtype=jnp.int32)[None, :]).astype(
        jnp.int32
    )
    slot_rank = jnp.sum(owner_hits * (jnp.cumsum(owner_hits, axis=0) - 1), axis=1)
    slot_index = owner_dev * capacity + slot_rank
    every_list = lax.all_gather(block_list, ("lat", "lon"), axis=0)
    me = lax.axis_index(("lat", "lon"))
    mine = every_list // columns_dev == me
    mine_rank = jnp.cumsum(mine.astype(jnp.int32), axis=1) - 1
    mine_slot = jnp.where(mine, mine_rank, capacity)
    wanted = jnp.sum(
        jnp.where(
            mine_slot[:, :, None] == jnp.arange(capacity, dtype=jnp.int32),
            (every_list - me * columns_dev + 1)[:, :, None],
            0,
        ),
        axis=1,
    ).reshape(devices * capacity)
    table = (
        model_vector.transpose(1, 2, 0, 3).reshape(columns_dev, systems, depth).astype(jnp.bfloat16)
    )
    served = jnp.where(
        (wanted > 0)[:, None, None],
        jnp.take(table, jnp.maximum(wanted - 1, 0), axis=0),
        jnp.zeros((), jnp.bfloat16),
    )
    fetched = lax.all_to_all(served, ("lat", "lon"), split_axis=0, concat_axis=0, tiled=True)
    tile_model = jnp.take(fetched, slot_index, axis=0)
    member = membership(bounds, tiles)
    products = jnp.einsum("tid,trd->tri", kernel, tile_model, preferred_element_type=jnp.float32)
    traced = jnp.einsum("tb,tri->rbi", member, products, precision=HIGHEST_PRECISION)
    ray_old = ray_vector.reshape(systems, blocks_dev, ray_width)
    ray_index = jnp.arange(blocks_dev * ray_width, dtype=jnp.int32).reshape(blocks_dev, ray_width)
    live_rows = ray_index < count_here
    ray_bar = jnp.where(live_rows[None], traced - alpha_old[:, None, None] * ray_old, 0.0)
    damp_bar = DAMP_WEIGHT * laplace(model_vector) - alpha_old[:, None, None, None] * damping_vector
    residual_sq = jnp.sum(ray_bar * ray_bar, axis=(1, 2)) + jnp.sum(
        damp_bar * damp_bar, axis=(1, 2, 3)
    )
    ray_low = ray_bar.astype(jnp.bfloat16)
    spread = jnp.einsum(
        "tb,rbi->tri", member.astype(jnp.bfloat16), ray_low, preferred_element_type=jnp.float32
    ).astype(jnp.bfloat16)
    sent_terms = jnp.einsum("tid,tri->trd", kernel, spread, preferred_element_type=jnp.float32)
    outgoing = (
        jnp.zeros((devices * capacity, systems, depth), jnp.float32).at[slot_index].set(sent_terms)
    )
    incoming = lax.all_to_all(outgoing, ("lat", "lon"), split_axis=0, concat_axis=0, tiled=True)
    collected = jnp.zeros((columns_dev + 1, systems, depth), jnp.float32).at[wanted].add(incoming)
    remote_part = collected[1:].reshape(clat_dev, clon_dev, systems, depth).transpose(2, 0, 1, 3)
    adjoint_image = remote_part + DAMP_WEIGHT * laplace(damp_bar)
    image_sq = jnp.sum(adjoint_image * adjoint_image, axis=(1, 2, 3))
    cross_sum = jnp.sum(adjoint_image * model_vector, axis=(1, 2, 3))
    model_sq = jnp.sum(model_vector * model_vector, axis=(1, 2, 3))
    partial = jnp.stack([residual_sq, image_sq, cross_sum, model_sq])
    every_partial = lax.all_gather(partial, ("lat", "lon"), axis=0)
    residual_sq, image_sq, cross_sum, model_sq = jnp.sum(every_partial, axis=0)
    beta_new = jnp.sqrt(residual_sq / rows_all + EPSILON)
    beta_wide = beta_new[:, None, None, None]
    update = adjoint_image / beta_wide - beta_wide * model_vector
    update_sq = image_sq / (beta_new * beta_new) - 2.0 * cross_sum + beta_new * beta_new * model_sq
    alpha_new = jnp.sqrt(update_sq / cells_all + EPSILON)
    model_out = update / alpha_new[:, None, None, None]
    rho_new = jnp.sqrt(rho_bar * rho_bar + beta_new * beta_new)
    cosine = rho_bar / rho_new
    sine_new = beta_new / rho_new
    solution_out = solution + (cosine * phi_bar / rho_new)[:, None, None, None] * search
    search_out = model_out - (sine_new * alpha_new / rho_new)[:, None, None, None] * search
    ray_out = (ray_bar / beta_new[:, None, None]).reshape(systems, 1, 1, blocks_dev * ray_width)
    damp_out = damp_bar / beta_wide
    recurrence_out = jnp.stack([alpha_new, -cosine * alpha_new, sine_new * phi_bar])
    return (ray_out, damp_out, model_out, solution_out, search_out, recurrence_out)


def solution(mesh):
    return jax.shard_map(
        per_device,
        mesh=mesh,
        in_specs=(
            P("lat", "lon", None, None, None),
            P("lat", "lon", None),
            P("lat", "lon", None),
            P("lat", "lon"),
            P(None, "lat", "lon", None),
            P(None, "lat", "lon", None),
            P(None, "lat", "lon", None),
            P(None, "lat", "lon", None),
            P(None, "lat", "lon", None),
            P(),
        ),
        out_specs=(
            P(None, "lat", "lon", None),
            P(None, "lat", "lon", None),
            P(None, "lat", "lon", None),
            P(None, "lat", "lon", None),
            P(None, "lat", "lon", None),
            P(),
        ),
        check_vma=False,
    )
```

```python
import functools

import jax
import jax.numpy as jnp
from jax import lax
from jax.experimental import pallas as pl
from jax.experimental.pallas import tpu as pltpu
from jax.sharding import PartitionSpec as P

DAMP_WEIGHT = 0.15
EPSILON = 1e-05
AXES = ("lat", "lon")
PATCH = 4
F32, BF16, I32 = jnp.float32, jnp.bfloat16, jnp.int32


def iota(shape, dim):
    return lax.broadcasted_iota(I32, shape, dim)


def vmem():
    return pl.BlockSpec(memory_space=pltpu.VMEM)


def smem():
    return pl.BlockSpec(memory_space=pltpu.SMEM)


def call(body, name, out_shape, in_specs, out_specs, scratch=(), grid=(), mib=16, flops=0, moved=0):
    return pl.pallas_call(
        body,
        name=name,
        grid=grid,
        out_shape=out_shape,
        in_specs=in_specs,
        out_specs=out_specs,
        scratch_shapes=list(scratch),
        compiler_params=pltpu.CompilerParams(vmem_limit_bytes=mib * 2**20),
        cost_estimate=pl.CostEstimate(flops=flops, bytes_accessed=moved, transcendentals=0),
    )


def request_body(shift, cap, blocks, ids_ref, off_ref, req_ref, meta_ref):
    tiles = ids_ref.shape[-1]
    devices = req_ref.shape[0]
    lanes = 128
    ids = jnp.concatenate(
        [ids_ref[0], jnp.full((1, lanes - tiles), -1, I32)], axis=1
    )
    owner = lax.shift_right_arithmetic(ids, shift)
    column = ids - lax.shift_left(owner, shift)
    square = (lanes, lanes)
    down, across = iota(square, 0), iota(square, 1)
    owner_f = jnp.broadcast_to(owner.astype(F32), square)
    owner_col = jnp.sum(jnp.where(down == across, owner_f, 0.0), axis=1, keepdims=True)
    same = jnp.where((owner_f == owner_col) & (down < across), 1.0, 0.0)
    rank = jnp.sum(same, axis=0, keepdims=True).astype(I32)
    lane = iota((1, lanes), 1)
    block = jnp.zeros((1, lanes), I32)
    for b in range(1, blocks + 1):
        block = block + (lane >= off_ref[0, 0, b]).astype(I32)
    meta_ref[...] = jnp.concatenate([owner, rank, block] + [owner] * 5, axis=0)
    wide = (devices, lanes)
    hit = jnp.broadcast_to(owner, wide) == iota(wide, 0)
    value = jnp.broadcast_to((column + 1).astype(F32), wide)
    rank_wide = jnp.broadcast_to(rank, wide)
    at = iota(wide, 1)
    req = jnp.zeros(wide, F32)
    for c in range(cap):
        picked = jnp.sum(jnp.where(hit & (rank_wide == c), value, 0.0), axis=1, keepdims=True)
        req = jnp.where(at == c, picked, req)
    req_ref[...] = req.astype(I32)


def wanted_column(wanted, cap):
    devices, lanes = wanted.shape
    rows = devices * cap
    spread = jnp.broadcast_to(wanted.astype(F32)[:, None, :], (devices, cap, lanes))
    spread = spread.reshape(rows, lanes)
    pick = iota((rows, lanes), 1) == (iota((rows, lanes), 0) & (cap - 1))
    return jnp.sum(jnp.where(pick, spread, 0.0), axis=1, keepdims=True).astype(I32)


def serve_body(clat, cap, wanted_ref, model_ref, served_ref, corner_ref, patch, mixed, sem):
    systems, _, clon, depth = patch.shape
    wanted = wanted_ref[...]
    shift = clon.bit_length() - 1
    first = jnp.min(jnp.where(wanted > 0, wanted - 1, clat * clon))
    corner = jnp.minimum(lax.shift_right_logical(first, shift), clat - PATCH)
    corner_ref[0] = corner
    copy = pltpu.make_async_copy(model_ref.at[:, pl.ds(corner, PATCH)], patch, sem)
    copy.start()
    col = wanted_column(wanted, cap)
    rows = col.shape[0]
    target = jnp.where(col > 0, col - 1 - corner * clon, -1)
    width = PATCH * clon
    chosen = (jnp.broadcast_to(target, (rows, width)) == iota((rows, width), 1)).astype(F32).astype(BF16)
    copy.wait()
    for r in range(systems):
        table = patch[r].reshape(width, depth).astype(BF16)
        mixed[pl.ds(r, rows, stride=systems), :] = jnp.dot(
            chosen, table, preferred_element_type=F32
        )
    served_ref[...] = mixed[...].astype(BF16)


def rays_body(
    cap, blocks, meta_ref, count_ref, rec_ref, tiles_ref, fetched_ref, old_ref, bar_ref, term_ref, masks, lows
):
    tiles, width, depth = tiles_ref.shape[2:]
    systems = old_ref.shape[0]
    group = cap * systems
    for c in range(cap + 1):
        here = lax.shift_right_logical(iota((group, depth), 0), systems.bit_length() - 1) == c
        masks[c] = here.astype(F32).astype(BF16)
    term_ref[...] = jnp.zeros(term_ref.shape, F32)
    lows[...] = jnp.zeros(lows.shape, BF16)
    total = jnp.zeros((blocks * group, width), F32)
    for t in range(tiles):
        owner, rank, block = meta_ref[0, t], meta_ref[1, t], meta_ref[2, t]
        rows = fetched_ref[pl.ds(pl.multiple_of(owner * group, group), group), :]
        left = jnp.concatenate(
            [rows * masks[jnp.where(block == b, rank, cap)] for b in range(blocks)], axis=0
        )
        total = total + lax.dot_general(
            left, tiles_ref[0, 0, t], (((1,), (1,)), ((), ())), preferred_element_type=F32
        )
    for b in range(blocks):
        traced = jnp.zeros((systems, width), F32)
        for c in range(cap):
            at = b * group + c * systems
            traced = traced + total[at : at + systems]
        old = jnp.concatenate(
            [old_ref[r, 0, :, b * width : (b + 1) * width] * rec_ref[0, r] for r in range(systems)], axis=0
        )
        live = iota((systems, width), 1) + b * width < count_ref[0, 0]
        bar = jnp.where(live, traced - old, 0.0)
        for r in range(systems):
            bar_ref[r, 0, :, b * width : (b + 1) * width] = bar[r : r + 1]
        lows[b] = jnp.concatenate([bar, jnp.zeros((16 - systems, width), F32)], axis=0).astype(BF16)
    for t in range(tiles):
        slot = meta_ref[0, t] * cap + meta_ref[1, t]
        term = jnp.dot(lows[meta_ref[2, t]], tiles_ref[0, 0, t], preferred_element_type=F32)
        term_ref[slot] = term[:systems]


def six(x, north, south, west, east):
    sub, lane = iota(x.shape, 0), iota(x.shape, 1)
    rows, depth = x.shape
    left = jnp.where(sub == 0, jnp.broadcast_to(west, x.shape), pltpu.roll(x, 1, 0))
    right = jnp.where(sub == rows - 1, jnp.broadcast_to(east, x.shape), pltpu.roll(x, rows - 1, 0))
    above = jnp.where(lane == 0, 0.0, pltpu.roll(x, 1, 1))
    below = jnp.where(lane == depth - 1, 0.0, pltpu.roll(x, depth - 1, 1))
    beside = north + south + left + right + above + below
    return DAMP_WEIGHT * (6.0 * x - beside)


def dense_body(
    cap,
    flag_ref,
    rec_ref,
    corner_ref,
    wanted_ref,
    bar_ref,
    model_ref,
    damp_ref,
    north_ref,
    south_ref,
    west_ref,
    east_ref,
    westmost_ref,
    eastmost_ref,
    bar_out,
    image_out,
    sums_out,
    patch_out,
    model_patch_out,
    chosen_out,
    rows_s,
    west_s,
    east_s,
):
    r = pl.program_id(0)
    _, clat, clon, depth = model_ref.shape
    alpha = rec_ref[0, r]

    @pl.when(r == 0)
    def _():
        sums_out[...] = jnp.zeros(sums_out.shape, F32)
        col = wanted_column(wanted_ref[...], cap)
        slots = col.shape[0]
        target = jnp.where(col > 0, col - 1 - corner_ref[0] * clon, -1).astype(F32)
        square = (slots, slots)
        flat = jnp.sum(
            jnp.where(iota(square, 0) == iota(square, 1), jnp.broadcast_to(target, square), 0.0),
            axis=0,
            keepdims=True,
        ).astype(I32)
        wide = (PATCH * clon, slots)
        chosen_out[...] = (jnp.broadcast_to(flat, wide) == iota(wide, 0)).astype(F32).astype(BF16)

    def side(ref, near, own, flag):
        x, beyond, old = ref[0, 0:clat], ref[0, clat : 2 * clat], ref[0, 2 * clat : 3 * clat]
        upper, lower = ref[0, 3 * clat : 3 * clat + 1], ref[0, 3 * clat + 1 : 3 * clat + 2]
        return (six(x, beyond, own, upper, lower) - alpha * old) * flag

    west_s[...] = side(west_ref, 0, westmost_ref[0, 0:clat], flag_ref[2])
    east_s[...] = side(east_ref, 0, eastmost_ref[0, 0:clat], flag_ref[3])
    corner_n, corner_s = 3 * clat, 3 * clat + 1
    rows_s[0] = flag_ref[0] * (
        six(
            north_ref[0, 1],
            north_ref[0, 0],
            model_ref[0, 0],
            west_ref[0, corner_n : corner_n + 1],
            east_ref[0, corner_n : corner_n + 1],
        )
        - alpha * north_ref[0, 2]
    )
    rows_s[clat + 1] = flag_ref[1] * (
        six(
            south_ref[0, 0],
            model_ref[0, clat - 1],
            south_ref[0, 1],
            west_ref[0, corner_s : corner_s + 1],
            east_ref[0, corner_s : corner_s + 1],
        )
        - alpha * south_ref[0, 2]
    )

    def fold(x):
        parts = [x[i * 8 : (i + 1) * 8] for i in range(x.shape[0] // 8)]
        return functools.reduce(lambda a, b: a + b, parts)

    def first(i, north, south, acc):
        x = model_ref[0, i]
        bar = six(x, north, south, west_ref[0, pl.ds(i, 1)], east_ref[0, pl.ds(i, 1)])
        bar = bar - alpha * damp_ref[0, i]
        rows_s[i + 1] = bar
        bar_out[0, i] = bar
        return acc[0] + fold(bar * bar), acc[1] + fold(x * x)

    zero = jnp.zeros((8, depth), F32)
    acc = first(0, north_ref[0, 1], model_ref[0, 1], (zero, zero))
    acc = lax.fori_loop(
        1, clat - 1, lambda i, acc: first(i, model_ref[0, i - 1], model_ref[0, i + 1], acc), acc, unroll=2
    )
    bar_sq, model_sq = first(clat - 1, model_ref[0, clat - 2], south_ref[0, 0], acc)

    def second(i, acc):
        image = six(rows_s[i + 1], rows_s[i], rows_s[i + 2], west_s[pl.ds(i, 1)], east_s[pl.ds(i, 1)])
        image_out[0, i] = image
        return acc[0] + fold(image * image), acc[1] + fold(image * model_ref[0, i])

    image_sq, cross = lax.fori_loop(0, clat, second, (zero, zero), unroll=2)
    for a in range(PATCH):
        patch_out[0, pl.ds(a * clon, clon), :] = image_out[0, corner_ref[0] + a]
        model_patch_out[0, pl.ds(a * clon, clon), :] = model_ref[0, corner_ref[0] + a]
    ray = bar_ref[0, 0]
    res = jnp.sum(bar_sq, keepdims=True) + jnp.sum(ray * ray, keepdims=True)
    lane = iota((1, depth), 1)
    row = sums_out[...]
    systems = pl.num_programs(0)
    values = (
        res,
        jnp.sum(image_sq, keepdims=True),
        jnp.sum(cross, keepdims=True),
        jnp.sum(model_sq, keepdims=True),
    )
    for q, value in enumerate(values):
        row = row + jnp.where(lane == q * systems + r, jnp.broadcast_to(value, (1, depth)), 0.0)
    sums_out[...] = row


def combine_body(terms_ref, chosen_ref, patch_ref, model_patch_ref, sums_ref, added_ref, parts_ref):
    systems, width, depth = patch_ref.shape
    slots = chosen_ref.shape[1]
    chosen = chosen_ref[...]
    row = sums_ref[...]
    lane = iota(row.shape, 1)
    for r in range(systems):
        x = terms_ref[pl.ds(r, slots, stride=systems), :]
        high = x.astype(BF16)
        rest = x - high.astype(F32)
        middle = rest.astype(BF16)
        low = (rest - middle.astype(F32)).astype(BF16)
        added = (
            jnp.dot(chosen, low, preferred_element_type=F32)
            + jnp.dot(chosen, middle, preferred_element_type=F32)
            + jnp.dot(chosen, high, preferred_element_type=F32)
        )
        added_ref[r] = added
        square = jnp.sum(added * (2.0 * patch_ref[r] + added), keepdims=True)
        cross = jnp.sum(added * model_patch_ref[r], keepdims=True)
        row = row + jnp.where(lane == systems + r, jnp.broadcast_to(square, row.shape), 0.0)
        row = row + jnp.where(lane == 2 * systems + r, jnp.broadcast_to(cross, row.shape), 0.0)
    parts_ref[...] = jnp.broadcast_to(row, parts_ref.shape)


def finish_body(
    rows_all,
    cells_all,
    corner_ref,
    parts_ref,
    rec_ref,
    bar_ref,
    added_ref,
    image_ref,
    model_ref,
    damp_ref,
    solution_ref,
    search_ref,
    ray_out,
    damp_out,
    model_out,
    solution_out,
    search_out,
    rec_out,
    coef,
):
    r, piece = pl.program_id(0), pl.program_id(1)
    systems = rec_ref.shape[1]
    _, rows, clon, depth = image_ref.shape

    @pl.when((r == 0) & (piece == 0))
    def _():
        total = jnp.sum(parts_ref[...], axis=0, keepdims=True)
        residual_sq, image_sq, cross, model_sq = (
            total[:, q * systems : (q + 1) * systems] for q in range(4)
        )
        alpha_old, rho_bar, phi_bar = rec_ref[0:1], rec_ref[1:2], rec_ref[2:3]
        beta = jnp.sqrt(residual_sq / rows_all + EPSILON)
        update_sq = image_sq / (beta * beta) - 2.0 * cross + beta * beta * model_sq
        alpha = jnp.sqrt(jnp.maximum(update_sq, 0.0) / cells_all + EPSILON)
        rho = jnp.sqrt(rho_bar * rho_bar + beta * beta)
        cosine = rho_bar / rho
        sine = beta / rho
        rec_out[...] = jnp.concatenate([alpha, -cosine * alpha, sine * phi_bar], axis=0)
        scales = (
            1.0 / beta,
            1.0 / (beta * alpha),
            beta / alpha,
            cosine * phi_bar / rho,
            sine * alpha / rho,
        )
        for q, scale in enumerate(scales):
            for s in range(systems):
                coef[q, s] = scale[0, s]
        for s in range(systems):
            ray_out[s] = bar_ref[s] * coef[0, s]

    damp_out[...] = damp_ref[...] * coef[0, r]
    image_scale, model_scale, search_scale = coef[1, r], coef[2, r], coef[4, r]
    search = search_ref[...]
    new = image_ref[...] * image_scale - model_ref[...] * model_scale
    model_out[...] = new
    search_out[...] = new - search * search_scale
    solution_out[...] = solution_ref[...] + search * coef[3, r]
    for a in range(PATCH):
        at = corner_ref[0] + a - piece * rows

        @pl.when((at >= 0) & (at < rows))
        def _():
            more = added_ref[0, pl.ds(a * clon, clon), :] * image_scale
            model_out[0, at] = model_out[0, at] + more
            search_out[0, at] = search_out[0, at] + more


def shifted(x, axis, step):
    count = lax.axis_size(axis)
    if step > 0:
        pairs = [(i, i + 1) for i in range(count - 1)]
    else:
        pairs = [(i + 1, i) for i in range(count - 1)]
    return lax.ppermute(x, axis, pairs)


def exchange(x):
    return lax.all_to_all(x, AXES, split_axis=0, concat_axis=0, tiled=True)


def per_device(
    sensitivity,
    block_ids,
    block_offsets,
    ray_counts,
    ray_vector,
    damping_vector,
    model_vector,
    solution,
    search,
    recurrence,
):
    lat_size, lon_size = lax.axis_size("lat"), lax.axis_size("lon")
    devices = lat_size * lon_size
    tiles, width, depth = sensitivity.shape[2:]
    blocks = block_offsets.shape[-1] - 1
    systems, clat, clon, _ = model_vector.shape
    columns = clat * clon
    cap = max(2 * ((tiles + devices - 1) // devices), 16 // systems)
    slots = devices * cap
    group = cap * systems
    cells_all = devices * columns * depth
    rows_all = devices * blocks * width + cells_all
    lanes = 128
    field = jax.ShapeDtypeStruct(model_vector.shape, F32)

    req, meta = call(
        functools.partial(request_body, columns.bit_length() - 1, cap, blocks),
        "request",
        (jax.ShapeDtypeStruct((devices, lanes), I32), jax.ShapeDtypeStruct((8, lanes), I32)),
        [vmem(), smem()],
        (vmem(), vmem()),
    )(block_ids, block_offsets)
    wanted = exchange(req.reshape(devices, 1, lanes)).reshape(devices, lanes)

    last, before = clat - 1, clat - 2
    south_msg = jnp.concatenate([model_vector[:, before:], damping_vector[:, last:]], axis=1)
    north_msg = jnp.concatenate([model_vector[:, :2], damping_vector[:, :1]], axis=1)
    north = shifted(south_msg, "lat", 1)
    south = shifted(north_msg, "lat", -1)

    def column_msg(near, beyond):
        return jnp.concatenate(
            [
                model_vector[:, :, near],
                model_vector[:, :, beyond],
                damping_vector[:, :, near],
                north[:, 1:2, near],
                south[:, 0:1, near],
                jnp.zeros((systems, 6, depth), F32),
            ],
            axis=1,
        )

    served, corner = call(
        functools.partial(serve_body, clat, cap),
        "serve",
        (jax.ShapeDtypeStruct((slots * systems, depth), BF16), jax.ShapeDtypeStruct((1,), I32)),
        [vmem(), pl.BlockSpec(memory_space=pl.ANY)],
        (vmem(), smem()),
        scratch=[
            pltpu.VMEM((systems, PATCH, clon, depth), F32),
            pltpu.VMEM((slots * systems, depth), F32),
            pltpu.SemaphoreType.DMA,
        ],
    )(wanted, model_vector)
    fetched = exchange(served.reshape(devices, group, depth)).reshape(slots * systems, depth)

    east_msg = column_msg(clon - 1, clon - 2)
    west_msg = column_msg(0, 1)
    west = shifted(east_msg, "lon", 1)
    east = shifted(west_msg, "lon", -1)

    ray_bar, terms = call(
        functools.partial(rays_body, cap, blocks),
        "rays",
        (jax.ShapeDtypeStruct(ray_vector.shape, F32), jax.ShapeDtypeStruct((slots, systems, depth), F32)),
        [smem(), smem(), smem(), vmem(), vmem(), vmem()],
        (vmem(), vmem()),
        scratch=[
            pltpu.VMEM((cap + 1, group, depth), BF16),
            pltpu.VMEM((blocks + 1, 16, width), BF16),
        ],
        flops=4 * tiles * width * depth * 16,
        moved=2 * tiles * width * depth,
    )(meta, ray_counts, recurrence, sensitivity, fetched, ray_vector)
    arrived = exchange(terms.reshape(devices, cap * systems, depth)).reshape(slots * systems, depth)

    lat_at, lon_at = lax.axis_index("lat"), lax.axis_index("lon")
    flags = jnp.stack(
        [lat_at > 0, lat_at < lat_size - 1, lon_at > 0, lon_at < lon_size - 1]
    ).astype(F32)
    slab = lambda shape: pl.BlockSpec((1,) + shape[1:], lambda r: (r,) + (0,) * (len(shape) - 1))
    patch_shape = (systems, PATCH * clon, depth)
    damp_bar, image, sums, patch, model_patch, chosen = call(
        functools.partial(dense_body, cap),
        "dense",
        (
            field,
            field,
            jax.ShapeDtypeStruct((1, lanes), F32),
            jax.ShapeDtypeStruct(patch_shape, F32),
            jax.ShapeDtypeStruct(patch_shape, F32),
            jax.ShapeDtypeStruct((PATCH * clon, slots), BF16),
        ),
        [
            smem(),
            smem(),
            smem(),
            pl.BlockSpec((devices, lanes), lambda r: (0, 0)),
            slab(ray_vector.shape),
            slab(field.shape),
            slab(field.shape),
            slab(north.shape),
            slab(south.shape),
            slab(west.shape),
            slab(east.shape),
            slab(west_msg.shape),
            slab(east_msg.shape),
        ],
        (
            slab(field.shape),
            slab(field.shape),
            pl.BlockSpec((1, lanes), lambda r: (0, 0)),
            slab(patch_shape),
            slab(patch_shape),
            pl.BlockSpec((PATCH * clon, slots), lambda r: (0, 0)),
        ),
        scratch=[
            pltpu.VMEM((clat + 2, clon, depth), F32),
            pltpu.VMEM((clat, depth), F32),
            pltpu.VMEM((clat, depth), F32),
        ],
        grid=(systems,),
        flops=40 * systems * columns * depth,
        moved=16 * systems * columns * depth,
    )(
        flags,
        recurrence,
        corner,
        wanted,
        ray_bar,
        model_vector,
        damping_vector,
        north,
        south,
        west,
        east,
        west_msg,
        east_msg,
    )

    added, parts = call(
        combine_body,
        "combine",
        (jax.ShapeDtypeStruct(patch_shape, F32), jax.ShapeDtypeStruct((devices, lanes), F32)),
        [vmem()] * 5,
        (vmem(), vmem()),
    )(arrived, chosen, patch, model_patch, sums)
    every = exchange(parts.reshape(devices, 1, lanes)).reshape(devices, lanes)

    pieces = 2
    rows = clat // pieces
    whole = lambda shape: pl.BlockSpec(shape, lambda r, p: (0,) * len(shape))
    part = pl.BlockSpec((1, rows, clon, depth), lambda r, p: (r, p, 0, 0))
    outs = call(
        functools.partial(finish_body, float(rows_all), float(cells_all)),
        "finish",
        (
            jax.ShapeDtypeStruct(ray_vector.shape, F32),
            field,
            field,
            field,
            field,
            jax.ShapeDtypeStruct(recurrence.shape, F32),
        ),
        [
            smem(),
            whole((devices, lanes)),
            whole(recurrence.shape),
            whole(ray_vector.shape),
            pl.BlockSpec((1,) + patch_shape[1:], lambda r, p: (r, 0, 0)),
        ]
        + [part] * 5,
        (whole(ray_vector.shape), part, part, part, part, whole(recurrence.shape)),
        scratch=[pltpu.SMEM((8, systems), F32)],
        grid=(systems, pieces),
        flops=10 * systems * columns * depth,
        moved=36 * systems * columns * depth,
    )(corner, every, recurrence, ray_bar, added, image, model_vector, damp_bar, solution, search)
    return outs


def solution(mesh):
    fields = P(None, "lat", "lon", None)
    return jax.shard_map(
        per_device,
        mesh=mesh,
        in_specs=(
            P("lat", "lon", None, None, None),
            P("lat", "lon", None),
            P("lat", "lon", None),
            P("lat", "lon"),
            fields,
            fields,
            fields,
            fields,
            fields,
            P(),
        ),
        out_specs=(fields, fields, fields, fields, fields, P()),
        check_vma=False,
    )
```

```python
import functools

import jax
import jax.numpy as jnp
from jax import lax
from jax.experimental import pallas as pl
from jax.experimental.pallas import tpu as pltpu
from jax.sharding import PartitionSpec as P

DAMP_WEIGHT = 0.15
EPSILON = 1e-05
AXES = ("lat", "lon")
PATCH = 4
F32, BF16, I32 = jnp.float32, jnp.bfloat16, jnp.int32


def iota(shape, dim):
    return lax.broadcasted_iota(I32, shape, dim)


def vmem():
    return pl.BlockSpec(memory_space=pltpu.VMEM)


def hbm():
    return pl.BlockSpec(memory_space=pltpu.HBM)


def far(x):
    return pltpu.with_memory_space_constraint(x, pltpu.HBM)


def smem():
    return pl.BlockSpec(memory_space=pltpu.SMEM)


def call(body, name, out_shape, in_specs, out_specs, scratch=(), grid=(), mib=16, flops=0, moved=0):
    return pl.pallas_call(
        body,
        name=name,
        grid=grid,
        out_shape=out_shape,
        in_specs=in_specs,
        out_specs=out_specs,
        scratch_shapes=list(scratch),
        compiler_params=pltpu.CompilerParams(vmem_limit_bytes=mib * 2**20),
        cost_estimate=pl.CostEstimate(flops=flops, bytes_accessed=moved, transcendentals=0),
    )


def load_body(
    shift, blocks, ids_ref, off_ref, count_ref, model_in, damp_in, model_out, damp_out, north_ref, south_ref, meta_ref, sems
):
    last = model_in.shape[1] - 1
    pairs = (
        (model_in.at[:, pl.ds(last - 1, 2)], south_ref.at[:, pl.ds(0, 2)]),
        (damp_in.at[:, pl.ds(last, 1)], south_ref.at[:, pl.ds(2, 1)]),
        (model_in.at[:, pl.ds(0, 2)], north_ref.at[:, pl.ds(0, 2)]),
        (damp_in.at[:, pl.ds(0, 1)], north_ref.at[:, pl.ds(2, 1)]),
        (model_in, model_out),
        (damp_in, damp_out),
    )
    copies = [pltpu.make_async_copy(a, b, sems.at[i]) for i, (a, b) in enumerate(pairs)]
    for copy in copies:
        copy.start()
    tiles = ids_ref.shape[-1]
    lanes = 128
    ids = jnp.concatenate([ids_ref[0], jnp.full((1, lanes - tiles), -1, I32)], axis=1)
    owner = lax.shift_right_arithmetic(ids, shift)
    square = (lanes, lanes)
    down, across = iota(square, 0), iota(square, 1)
    owner_f = jnp.broadcast_to(owner.astype(F32), square)
    owner_col = jnp.sum(jnp.where(down == across, owner_f, 0.0), axis=1, keepdims=True)
    same = jnp.where((owner_f == owner_col) & (down < across), 1.0, 0.0)
    rank = jnp.sum(same, axis=0, keepdims=True).astype(I32)
    lane = iota((1, lanes), 1)
    block = jnp.zeros((1, lanes), I32)
    for b in range(1, blocks + 1):
        block = block + (lane >= off_ref[0, 0, b]).astype(I32)
    count = jnp.full((1, lanes), count_ref[0, 0], I32)
    meta_ref[...] = jnp.concatenate([owner, rank, block, count] + [owner] * 4, axis=0)
    for copy in copies:
        copy.wait()


def wanted_column(wanted, cap):
    devices, lanes = wanted.shape
    rows = devices * cap
    spread = jnp.broadcast_to(wanted[:, None, :], (devices, cap, lanes)).reshape(rows, lanes)
    pick = iota((rows, lanes), 1) == (iota((rows, lanes), 0) & (cap - 1))
    return jnp.sum(jnp.where(pick, spread, 0.0), axis=1, keepdims=True)


def serve_body(cap, lists_ref, model_ref, served_ref, wanted_ref, corner_ref, mixed):
    systems, clat, clon, depth = model_ref.shape
    devices, tiles = lists_ref.shape
    lanes = 128
    shift = (clat * clon).bit_length() - 1
    me = lax.axis_index("lat") * lax.axis_size("lon") + lax.axis_index("lon")
    ids = jnp.concatenate([lists_ref[...], jnp.full((devices, lanes - tiles), -1, I32)], axis=1)
    column = ids - lax.shift_left(me, shift)
    mine = (column >= 0) & (column < clat * clon) & (ids >= 0)
    first = jnp.min(jnp.where(mine, column, clat * clon))
    corner = jnp.minimum(lax.shift_right_logical(first, clon.bit_length() - 1), clat - PATCH)
    corner_ref[0] = corner
    ahead = (iota((lanes, lanes), 0) < iota((lanes, lanes), 1)).astype(F32).astype(BF16)
    rank = jnp.dot(mine.astype(F32).astype(BF16), ahead, preferred_element_type=F32)
    value = (column - corner * clon + 1).astype(F32)
    at = iota((devices, lanes), 1)
    wanted = jnp.zeros((devices, lanes), F32)
    for c in range(cap):
        picked = jnp.sum(jnp.where(mine & (rank == c), value, 0.0), axis=1, keepdims=True)
        wanted = jnp.where(at == c, picked, wanted)
    wanted_ref[...] = wanted
    target = wanted_column(wanted, cap).astype(I32) - 1
    rows = target.shape[0]
    width = PATCH * clon
    chosen = (jnp.broadcast_to(target, (rows, width)) == iota((rows, width), 1)).astype(F32).astype(BF16)
    for r in range(systems):
        table = model_ref[r, pl.ds(corner, PATCH)].reshape(width, depth).astype(BF16)
        mixed[pl.ds(r, rows, stride=systems), :] = jnp.dot(chosen, table, preferred_element_type=F32)
    served_ref[...] = mixed[...].astype(BF16)


def columns_body(clat, clon, model_ref, damp_ref, north_ref, south_ref, east_ref, west_ref):
    systems, _, depth = model_ref.shape
    for r in range(systems):
        for out, near, beyond in ((east_ref, clon - 1, clon - 2), (west_ref, 0, 1)):
            out[r, 0:clat] = model_ref[r, pl.ds(near, clat, stride=clon), :]
            out[r, clat : 2 * clat] = model_ref[r, pl.ds(beyond, clat, stride=clon), :]
            out[r, 2 * clat : 3 * clat] = damp_ref[r, pl.ds(near, clat, stride=clon), :]
            out[r, 3 * clat :] = jnp.concatenate(
                [
                    north_ref[r, 1, near : near + 1],
                    south_ref[r, 0, near : near + 1],
                    jnp.zeros((6, depth), F32),
                ],
                axis=0,
            )


def six(x, north, south, west, east):
    sub, lane = iota(x.shape, 0), iota(x.shape, 1)
    rows, depth = x.shape
    left = jnp.where(sub == 0, jnp.broadcast_to(west, x.shape), pltpu.roll(x, 1, 0))
    right = jnp.where(sub == rows - 1, jnp.broadcast_to(east, x.shape), pltpu.roll(x, rows - 1, 0))
    above = jnp.where(lane == 0, 0.0, pltpu.roll(x, 1, 1))
    below = jnp.where(lane == depth - 1, 0.0, pltpu.roll(x, depth - 1, 1))
    beside = north + south + left + right + above + below
    return DAMP_WEIGHT * (6.0 * x - beside)


def fold(x):
    parts = [x[i * 8 : (i + 1) * 8] for i in range(x.shape[0] // 8)]
    return functools.reduce(lambda a, b: a + b, parts)


def place(row, lane, value):
    return row + jnp.where(iota(row.shape, 1) == lane, jnp.broadcast_to(value, row.shape), 0.0)


STEP = 8


def damp_body(
    rec_ref,
    model_ref,
    damp_ref,
    north_ref,
    south_ref,
    west_ref,
    east_ref,
    westmost_ref,
    eastmost_ref,
    bar_out,
    north_out,
    south_out,
    west_out,
    east_out,
    sums_out,
):
    systems, clat, clon, depth = model_ref.shape
    lat_at, lon_at = lax.axis_index("lat"), lax.axis_index("lon")
    has_north = (lat_at > 0).astype(F32)
    has_south = (lat_at < lax.axis_size("lat") - 1).astype(F32)
    has_west = (lon_at > 0).astype(F32)
    has_east = (lon_at < lax.axis_size("lon") - 1).astype(F32)
    corner_n, corner_s = 3 * clat, 3 * clat + 1

    def system(r, row):
        alpha = rec_ref[0, r]

        def side(ref, own, flag):
            x, beyond, old = ref[r, 0:clat], ref[r, clat : 2 * clat], ref[r, 2 * clat : 3 * clat]
            upper, lower = ref[r, corner_n : corner_n + 1], ref[r, corner_s : corner_s + 1]
            return (six(x, beyond, own, upper, lower) - alpha * old) * flag

        west_out[r] = side(west_ref, westmost_ref[r, 0:clat], has_west)
        east_out[r] = side(east_ref, eastmost_ref[r, 0:clat], has_east)
        north_out[r] = has_north * (
            six(
                north_ref[r, 1],
                north_ref[r, 0],
                model_ref[r, 0],
                west_ref[r, corner_n : corner_n + 1],
                east_ref[r, corner_n : corner_n + 1],
            )
            - alpha * north_ref[r, 2]
        )
        south_out[r] = has_south * (
            six(
                south_ref[r, 0],
                model_ref[r, clat - 1],
                south_ref[r, 1],
                west_ref[r, corner_s : corner_s + 1],
                east_ref[r, corner_s : corner_s + 1],
            )
            - alpha * south_ref[r, 2]
        )

        def chunk(k, acc):
            bar_sq, model_sq = acc
            base = k * STEP
            for j in range(STEP):
                i = base + j
                x = model_ref[r, i]
                if j == 0:
                    north = jnp.where(k > 0, model_ref[r, jnp.maximum(i - 1, 0)], north_ref[r, 1])
                else:
                    north = model_ref[r, i - 1]
                if j == STEP - 1:
                    more = jnp.minimum(i + 1, clat - 1)
                    south = jnp.where(i + 1 < clat, model_ref[r, more], south_ref[r, 0])
                else:
                    south = model_ref[r, i + 1]
                bar = six(x, north, south, west_ref[r, pl.ds(i, 1)], east_ref[r, pl.ds(i, 1)])
                bar = bar - alpha * damp_ref[r, i]
                bar_out[r, i] = bar
                bar_sq, model_sq = bar_sq + fold(bar * bar), model_sq + fold(x * x)
            return bar_sq, model_sq

        zero = jnp.zeros((8, depth), F32)
        bar_sq, model_sq = lax.fori_loop(0, clat // STEP, chunk, (zero, zero))
        row = place(row, r, jnp.sum(bar_sq, keepdims=True))
        return place(row, 3 * systems + r, jnp.sum(model_sq, keepdims=True))

    sums_out[...] = lax.fori_loop(0, systems, system, jnp.zeros((1, depth), F32))


def stage_body(after_ref, tiles_in, tiles_out, sem):
    copy = pltpu.make_async_copy(tiles_in, tiles_out, sem)
    copy.start()
    copy.wait()


def rays_body(cap, blocks, meta_ref, rec_ref, tiles_ref, fetched_ref, old_ref, sums_ref, bar_ref, term_ref, masks, lows):
    tiles, width, depth = tiles_ref.shape[2:]
    systems = old_ref.shape[0]
    group = cap * systems
    chunk = group + 1
    devices = term_ref.shape[0] // chunk
    for c in range(cap + 1):
        here = lax.shift_right_logical(iota((group, depth), 0), systems.bit_length() - 1) == c
        masks[c] = here.astype(F32).astype(BF16)
    term_ref[...] = jnp.zeros(term_ref.shape, F32)
    lows[...] = jnp.zeros(lows.shape, BF16)
    total = jnp.zeros((blocks * group, width), F32)
    for t in range(tiles):
        owner, rank, block = meta_ref[0, t], meta_ref[1, t], meta_ref[2, t]
        rows = fetched_ref[pl.ds(pl.multiple_of(owner * group, group), group), :]
        left = jnp.concatenate(
            [rows * masks[jnp.where(block == b, rank, cap)] for b in range(blocks)], axis=0
        )
        total = total + lax.dot_general(
            left, tiles_ref[0, 0, t], (((1,), (1,)), ((), ())), preferred_element_type=F32
        )
    square = jnp.zeros((systems, width), F32)
    for b in range(blocks):
        traced = jnp.zeros((systems, width), F32)
        for c in range(cap):
            at = b * group + c * systems
            traced = traced + total[at : at + systems]
        old = jnp.concatenate(
            [old_ref[r, 0, :, b * width : (b + 1) * width] * rec_ref[0, r] for r in range(systems)], axis=0
        )
        live = iota((systems, width), 1) + b * width < meta_ref[3, 0]
        bar = jnp.where(live, traced - old, 0.0)
        square = square + bar * bar
        for r in range(systems):
            bar_ref[r, 0, :, b * width : (b + 1) * width] = bar[r : r + 1]
        lows[b] = jnp.concatenate([bar, jnp.zeros((16 - systems, width), F32)], axis=0).astype(BF16)
    ray_sq = jnp.sum(square, axis=1, keepdims=True)
    part = sums_ref[...]
    for r in range(systems):
        part = place(part, r, ray_sq[r : r + 1])
    for e in range(devices):
        term_ref[e * chunk + group] = part
    for t in range(tiles):
        row = meta_ref[0, t] * chunk + meta_ref[1, t] * systems
        term = jnp.dot(lows[meta_ref[2, t]], tiles_ref[0, 0, t], preferred_element_type=F32)
        for r in range(systems):
            term_ref[row + r] = term[r : r + 1]


def image_body(
    chunk,
    cap,
    corner_ref,
    wanted_ref,
    bar_ref,
    north_ref,
    south_ref,
    west_ref,
    east_ref,
    model_ref,
    sums_ref,
    image_out,
    sums_out,
    patch_out,
    model_patch_out,
    chosen_out,
):
    systems, clat, clon, depth = model_ref.shape
    corner = corner_ref[0]
    wanted = wanted_ref[...]
    devices = wanted.shape[0]
    height, slots = chosen_out.shape
    at = iota((1, slots), 1)
    source = jnp.floor((at.astype(F32) + 0.5) * (1.0 / chunk)).astype(I32)
    inner = at - source * chunk
    from_e = (jnp.broadcast_to(source, (devices, slots)) == iota((devices, slots), 0)).astype(F32).astype(BF16)
    turned = jnp.transpose(wanted)[0:8].astype(BF16)
    listed = jnp.dot(turned, from_e, preferred_element_type=F32)
    slot_of = lax.shift_right_logical(inner, systems.bit_length() - 1)
    mine = jnp.broadcast_to(slot_of, listed.shape) == iota(listed.shape, 0)
    flat = jnp.sum(jnp.where(mine, listed, 0.0), axis=0, keepdims=True).astype(I32)
    used = (flat > 0) & (inner < chunk - 1)
    target = jnp.where(used, (inner & (systems - 1)) * (PATCH * clon) + flat - 1, -1)
    for k in range(height // 64):
        shape = (64, slots)
        hit = jnp.broadcast_to(target, shape) == iota(shape, 0) + k * 64
        chosen_out[k * 64 : (k + 1) * 64] = hit.astype(F32).astype(BF16)

    def system(r, row):
        def rows(k, acc):
            image_sq, cross = acc
            base = k * STEP
            for j in range(STEP):
                i = base + j
                x = bar_ref[r, i]
                if j == 0:
                    north = jnp.where(k > 0, bar_ref[r, jnp.maximum(i - 1, 0)], north_ref[r])
                else:
                    north = bar_ref[r, i - 1]
                if j == STEP - 1:
                    more = jnp.minimum(i + 1, clat - 1)
                    south = jnp.where(i + 1 < clat, bar_ref[r, more], south_ref[r])
                else:
                    south = bar_ref[r, i + 1]
                image = six(x, north, south, west_ref[r, pl.ds(i, 1)], east_ref[r, pl.ds(i, 1)])
                image_out[r, i] = image
                image_sq, cross = image_sq + fold(image * image), cross + fold(image * model_ref[r, i])
            return image_sq, cross

        zero = jnp.zeros((8, depth), F32)
        image_sq, cross = lax.fori_loop(0, clat // STEP, rows, (zero, zero))
        for a in range(PATCH):
            patch_out[pl.ds(pl.multiple_of((r * PATCH + a) * clon, clon), clon), :] = image_out[r, corner + a]
            model_patch_out[pl.ds(pl.multiple_of((r * PATCH + a) * clon, clon), clon), :] = model_ref[r, corner + a]
        row = place(row, systems + r, jnp.sum(image_sq, keepdims=True))
        return place(row, 2 * systems + r, jnp.sum(cross, keepdims=True))

    sums_out[...] = lax.fori_loop(0, systems, system, sums_ref[...])


def combine_body(chunk, systems, terms_ref, chosen_ref, patch_ref, model_patch_ref, sums_ref, added_ref, residual_ref, parts_ref, split):
    arrived, depth = terms_ref.shape
    devices = parts_ref.shape[0]
    width = patch_ref.shape[0]
    x = terms_ref[...]
    high = x.astype(BF16)
    rest = x - high.astype(F32)
    middle = rest.astype(BF16)
    low = (rest - middle.astype(F32)).astype(BF16)
    padded = split.shape[0]
    if padded > arrived:
        split[arrived:] = jnp.zeros((padded - arrived, split.shape[1]), BF16)
    split[0:arrived, 0:depth] = high
    split[0:arrived, depth : 2 * depth] = middle
    split[0:arrived, 2 * depth :] = low
    three = jnp.dot(chosen_ref[...], split[...], preferred_element_type=F32)
    added = three[:, 0:depth] + (three[:, depth : 2 * depth] + three[:, 2 * depth :])
    added_ref[...] = added
    every = terms_ref[pl.ds(chunk - 1, devices, stride=chunk), :]
    residual_ref[...] = jnp.sum(every, axis=0, keepdims=True)
    square = added * (2.0 * patch_ref[...] + added)
    cross = added * model_patch_ref[...]
    row = sums_ref[...]
    each = width // systems
    for r in range(systems):
        row = place(row, systems + r, jnp.sum(square[r * each : (r + 1) * each], keepdims=True))
        row = place(row, 2 * systems + r, jnp.sum(cross[r * each : (r + 1) * each], keepdims=True))
    parts_ref[...] = jnp.broadcast_to(row, parts_ref.shape)


def first_norm(residual_ref, systems, rows_all):
    return jnp.sqrt(residual_ref[0:1, 0:systems] / rows_all + EPSILON)


def early_body(
    rows_all, residual_ref, rec_ref, bar_ref, damp_ref, solution_ref, search_ref, ray_out, damp_out, solution_out, coef
):
    r, piece = pl.program_id(0), pl.program_id(1)
    systems = rec_ref.shape[1]

    @pl.when((r == 0) & (piece == 0))
    def _():
        rho_bar, phi_bar = rec_ref[1:2], rec_ref[2:3]
        beta = first_norm(residual_ref, systems, rows_all)
        rho = jnp.sqrt(rho_bar * rho_bar + beta * beta)
        scales = (1.0 / beta, (rho_bar / rho) * phi_bar / rho)
        for q, scale in enumerate(scales):
            for s in range(systems):
                coef[q, s] = scale[0, s]
        for s in range(systems):
            ray_out[s] = bar_ref[s] * coef[0, s]

    damp_out[...] = damp_ref[...] * coef[0, r]
    solution_out[...] = solution_ref[...] + search_ref[...] * coef[1, r]


def finish_body(
    rows_all,
    cells_all,
    corner_ref,
    residual_ref,
    parts_ref,
    rec_ref,
    added_ref,
    image_ref,
    model_ref,
    search_ref,
    model_out,
    search_out,
    rec_out,
    coef,
):
    r, piece = pl.program_id(0), pl.program_id(1)
    systems = rec_ref.shape[1]
    _, rows, clon, depth = image_ref.shape

    @pl.when((r == 0) & (piece == 0))
    def _():
        total = jnp.sum(parts_ref[...], axis=0, keepdims=True)
        image_sq, cross, model_sq = (total[:, q * systems : (q + 1) * systems] for q in range(1, 4))
        rho_bar, phi_bar = rec_ref[1:2], rec_ref[2:3]
        beta = first_norm(residual_ref, systems, rows_all)
        update_sq = image_sq / (beta * beta) - 2.0 * cross + beta * beta * model_sq
        alpha = jnp.sqrt(jnp.maximum(update_sq, 0.0) / cells_all + EPSILON)
        rho = jnp.sqrt(rho_bar * rho_bar + beta * beta)
        cosine = rho_bar / rho
        sine = beta / rho
        rec_out[...] = jnp.concatenate([alpha, -cosine * alpha, sine * phi_bar], axis=0)
        scales = (1.0 / (beta * alpha), beta / alpha, sine * alpha / rho)
        for q, scale in enumerate(scales):
            for s in range(systems):
                coef[q, s] = scale[0, s]

    image_scale, model_scale, search_scale = coef[0, r], coef[1, r], coef[2, r]
    new = image_ref[...] * image_scale - model_ref[...] * model_scale
    model_out[...] = new
    search_out[...] = new - search_ref[...] * search_scale
    for a in range(PATCH):
        at = corner_ref[0] + a - piece * rows

        @pl.when((at >= 0) & (at < rows))
        def _():
            more = added_ref[0, pl.ds(a * clon, clon), :] * image_scale
            model_out[0, at] = model_out[0, at] + more
            search_out[0, at] = search_out[0, at] + more


def shifted(x, axis, step):
    count = lax.axis_size(axis)
    if step > 0:
        pairs = [(i, i + 1) for i in range(count - 1)]
    else:
        pairs = [(i + 1, i) for i in range(count - 1)]
    return lax.ppermute(x, axis, pairs)


def exchange(x):
    return lax.all_to_all(x, AXES, split_axis=0, concat_axis=0, tiled=True)


def per_device(
    sensitivity,
    block_ids,
    block_offsets,
    ray_counts,
    ray_vector,
    damping_vector,
    model_vector,
    solution,
    search,
    recurrence,
):
    lat_size, lon_size = lax.axis_size("lat"), lax.axis_size("lon")
    devices = lat_size * lon_size
    tiles, width, depth = sensitivity.shape[2:]
    blocks = block_offsets.shape[-1] - 1
    systems, clat, clon, _ = model_vector.shape
    columns = clat * clon
    cap = max(2 * ((tiles + devices - 1) // devices), 16 // systems)
    slots = devices * cap
    group = cap * systems
    chunk = group + 1
    cells_all = devices * columns * depth
    rows_all = devices * blocks * width + cells_all
    lanes = 128
    shape = jax.ShapeDtypeStruct
    field = shape(model_vector.shape, F32)
    flat_shape = (systems, columns, depth)

    lists = exchange(jnp.broadcast_to(block_ids[0], (devices, 1, tiles))).reshape(devices, tiles)

    band = shape((systems, 3, clon, depth), F32)
    model, damping, north_msg, south_msg, meta = call(
        functools.partial(load_body, columns.bit_length() - 1, blocks),
        "load",
        (field, field, band, band, shape((8, lanes), I32)),
        [vmem(), smem(), smem(), hbm(), hbm()],
        (vmem(),) * 5,
        scratch=[pltpu.SemaphoreType.DMA((6,))],
        moved=8 * systems * columns * depth,
    )(block_ids, block_offsets, ray_counts, far(model_vector), far(damping_vector))
    north = shifted(south_msg, "lat", 1)
    south = shifted(north_msg, "lat", -1)

    served, wanted, corner = call(
        functools.partial(serve_body, cap),
        "serve",
        (shape((slots * systems, depth), BF16), shape((devices, lanes), F32), shape((1,), I32)),
        [vmem(), vmem()],
        (vmem(), vmem(), smem()),
        scratch=[pltpu.VMEM((slots * systems, depth), F32)],
    )(lists, model)
    fetched = exchange(served.reshape(devices, group, depth)).reshape(slots * systems, depth)

    side = shape((systems, 3 * clat + 8, depth), F32)
    east_msg, west_msg = call(
        functools.partial(columns_body, clat, clon),
        "columns",
        (side, side),
        [vmem()] * 4,
        (vmem(), vmem()),
    )(model.reshape(flat_shape), damping.reshape(flat_shape), north, south)
    west = shifted(east_msg, "lon", 1)
    east = shifted(west_msg, "lon", -1)

    held = call(
        stage_body,
        "stage",
        shape(sensitivity.shape, BF16),
        [smem(), hbm()],
        vmem(),
        scratch=[pltpu.SemaphoreType.DMA],
        moved=2 * tiles * width * depth,
    )(corner, far(sensitivity))

    edge = shape((systems, clon, depth), F32)
    flank = shape((systems, clat, depth), F32)
    damp_bar, *border, sums = call(
        damp_body,
        "damp",
        (field, edge, edge, flank, flank, shape((1, lanes), F32)),
        [smem()] + [vmem()] * 8,
        (vmem(),) * 6,
        flops=20 * systems * columns * depth,
        moved=12 * systems * columns * depth,
    )(recurrence, model, damping, north, south, west, east, west_msg, east_msg)

    ray_bar, terms = call(
        functools.partial(rays_body, cap, blocks),
        "rays",
        (shape(ray_vector.shape, F32), shape((devices * chunk, 1, depth), F32)),
        [smem(), smem()] + [vmem()] * 4,
        (vmem(), vmem()),
        scratch=[
            pltpu.VMEM((cap + 1, group, depth), BF16),
            pltpu.VMEM((blocks + 1, 16, width), BF16),
        ],
        flops=4 * tiles * width * depth * 16,
        moved=2 * tiles * width * depth,
    )(meta, recurrence, held, fetched, ray_vector, sums)
    arrived = exchange(terms.reshape(devices, 1, chunk * depth)).reshape(devices * chunk, depth)

    padded = -(-devices * chunk // lanes) * lanes
    height = systems * PATCH * clon
    patch_shape = shape((height, depth), F32)
    image, sums, patch, model_patch, chosen = call(
        functools.partial(image_body, chunk, cap),
        "image",
        (field, shape((1, lanes), F32), patch_shape, patch_shape, shape((height, padded), BF16)),
        [smem()] + [vmem()] * 8,
        (vmem(),) * 5,
        flops=20 * systems * columns * depth,
        moved=12 * systems * columns * depth,
    )(corner, wanted, damp_bar, *border, model, sums)

    added, residual, parts = call(
        functools.partial(combine_body, chunk, systems),
        "combine",
        (patch_shape, shape((1, lanes), F32), shape((devices, lanes), F32)),
        [vmem()] * 5,
        (vmem(),) * 3,
        scratch=[pltpu.VMEM((padded, 3 * depth), BF16)],
    )(arrived, chosen, patch, model_patch, sums)
    every = exchange(parts.reshape(devices, 1, lanes)).reshape(devices, lanes)

    pieces = 2
    rows = clat // pieces
    whole = lambda dims: pl.BlockSpec(dims, lambda r, p: (0,) * len(dims))
    part = pl.BlockSpec((1, rows, clon, depth), lambda r, p: (r, p, 0, 0))
    search = far(search)
    ray_out, damp_out, solution_out = call(
        functools.partial(early_body, float(rows_all)),
        "early",
        (shape(ray_vector.shape, F32), field, field),
        [whole((1, lanes)), whole(recurrence.shape), whole(ray_vector.shape)] + [part] * 3,
        (whole(ray_vector.shape), part, part),
        scratch=[pltpu.SMEM((2, systems), F32)],
        grid=(systems, pieces),
        flops=4 * systems * columns * depth,
        moved=20 * systems * columns * depth,
    )(residual, recurrence, ray_bar, damp_bar, far(solution), search)
    model_out, search_out, rec_out = call(
        functools.partial(finish_body, float(rows_all), float(cells_all)),
        "finish",
        (field, field, shape(recurrence.shape, F32)),
        [
            smem(),
            whole((1, lanes)),
            whole((devices, lanes)),
            whole(recurrence.shape),
            pl.BlockSpec((1, PATCH * clon, depth), lambda r, p: (r, 0, 0)),
        ]
        + [part] * 3,
        (part, part, whole(recurrence.shape)),
        scratch=[pltpu.SMEM((3, systems), F32)],
        grid=(systems, pieces),
        flops=6 * systems * columns * depth,
        moved=20 * systems * columns * depth,
    )(
        corner,
        residual,
        every,
        recurrence,
        added.reshape(systems, PATCH * clon, depth),
        image,
        model,
        search,
    )
    return ray_out, damp_out, model_out, solution_out, search_out, rec_out


def solution(mesh):
    fields = P(None, "lat", "lon", None)
    return jax.shard_map(
        per_device,
        mesh=mesh,
        in_specs=(
            P("lat", "lon", None, None, None),
            P("lat", "lon", None),
            P("lat", "lon", None),
            P("lat", "lon"),
            fields,
            fields,
            fields,
            fields,
            fields,
            P(),
        ),
        out_specs=(fields, fields, fields, fields, fields, P()),
        check_vma=False,
    )
```

```python
import functools

import jax
import jax.numpy as jnp
from jax import lax
from jax.experimental import pallas as pl
from jax.experimental.pallas import tpu as pltpu
from jax.sharding import PartitionSpec as P

DAMP_WEIGHT = 0.15
EPSILON = 1e-05
AXES = ("lat", "lon")
PATCH = 4
F32, BF16, I32 = jnp.float32, jnp.bfloat16, jnp.int32


def iota(shape, dim):
    return lax.broadcasted_iota(I32, shape, dim)


def vmem():
    return pl.BlockSpec(memory_space=pltpu.VMEM)


def hbm():
    return pl.BlockSpec(memory_space=pltpu.HBM)


def near(x):
    return pltpu.with_memory_space_constraint(x, pltpu.VMEM)


def far(x):
    return pltpu.with_memory_space_constraint(x, pltpu.HBM)


def smem():
    return pl.BlockSpec(memory_space=pltpu.SMEM)


def call(body, name, out_shape, in_specs, out_specs, scratch=(), grid=(), mib=16, flops=0, moved=0):
    return pl.pallas_call(
        body,
        name=name,
        grid=grid,
        out_shape=out_shape,
        in_specs=in_specs,
        out_specs=out_specs,
        scratch_shapes=list(scratch),
        compiler_params=pltpu.CompilerParams(vmem_limit_bytes=mib * 2**20),
        cost_estimate=pl.CostEstimate(flops=flops, bytes_accessed=moved, transcendentals=0),
    )


def wanted_column(wanted, cap):
    devices, lanes = wanted.shape
    rows = devices * cap
    spread = jnp.broadcast_to(wanted[:, None, :], (devices, cap, lanes)).reshape(rows, lanes)
    pick = iota((rows, lanes), 1) == (iota((rows, lanes), 0) & (cap - 1))
    return jnp.sum(jnp.where(pick, spread, 0.0), axis=1, keepdims=True)


def serve_body(cap, clat, clon, lists_ref, model_in, served_ref, wanted_ref, corner_ref, model_ref, mixed, sems):
    systems, _, depth = model_ref.shape
    copies = [pltpu.make_async_copy(model_in.at[r], model_ref.at[r], sems.at[r]) for r in range(systems)]
    for copy in copies:
        copy.start()
    devices, tiles = lists_ref.shape
    lanes = 128
    shift = (clat * clon).bit_length() - 1
    me = lax.axis_index("lat") * lax.axis_size("lon") + lax.axis_index("lon")
    ids = jnp.concatenate([lists_ref[...], jnp.full((devices, lanes - tiles), -1, I32)], axis=1)
    column = ids - lax.shift_left(me, shift)
    mine = (column >= 0) & (column < clat * clon) & (ids >= 0)
    first = jnp.min(jnp.where(mine, column, clat * clon))
    corner = jnp.minimum(lax.shift_right_logical(first, clon.bit_length() - 1), clat - PATCH)
    corner_ref[0] = corner
    ahead = (iota((lanes, lanes), 0) < iota((lanes, lanes), 1)).astype(F32).astype(BF16)
    rank = jnp.dot(mine.astype(F32).astype(BF16), ahead, preferred_element_type=F32)
    value = (column - corner * clon + 1).astype(F32)
    at = iota((devices, lanes), 1)
    wanted = jnp.zeros((devices, lanes), F32)
    for c in range(cap):
        picked = jnp.sum(jnp.where(mine & (rank == c), value, 0.0), axis=1, keepdims=True)
        wanted = jnp.where(at == c, picked, wanted)
    wanted_ref[...] = wanted
    target = wanted_column(wanted, cap).astype(I32) - 1
    rows = target.shape[0]
    width = PATCH * clon
    chosen = (jnp.broadcast_to(target, (rows, width)) == iota((rows, width), 1)).astype(F32).astype(BF16)
    for r in range(systems):
        copies[r].wait()
        table = model_ref[r, pl.ds(pl.multiple_of(corner * clon, clon), width), :].astype(BF16)
        mixed[pl.ds(r, rows, stride=systems), :] = jnp.dot(chosen, table, preferred_element_type=F32)
    served_ref[...] = mixed[...].astype(BF16)


def pack_body(
    shift,
    clon,
    blocks,
    ids_ref,
    off_ref,
    count_ref,
    model_ref,
    damp_in,
    tiles_in,
    damp_out,
    tiles_out,
    north_ref,
    south_ref,
    meta_ref,
    sems,
):
    systems, columns, _ = model_ref.shape
    half = tiles_in.shape[2] // 2
    copies = [pltpu.make_async_copy(damp_in.at[r], damp_out.at[r], sems.at[r]) for r in range(systems)]
    for k, part in enumerate((pl.ds(0, half), pl.ds(half, tiles_in.shape[2] - half))):
        at = (0, 0, part)
        copies.append(pltpu.make_async_copy(tiles_in.at[at], tiles_out.at[at], sems.at[systems + k]))
    for copy in copies:
        copy.start()
    tiles = ids_ref.shape[-1]
    lanes = 128
    ids = jnp.concatenate([ids_ref[0], jnp.full((1, lanes - tiles), -1, I32)], axis=1)
    owner = lax.shift_right_arithmetic(ids, shift)
    square = (lanes, lanes)
    down, across = iota(square, 0), iota(square, 1)
    owner_f = jnp.broadcast_to(owner.astype(F32), square)
    owner_col = jnp.sum(jnp.where(down == across, owner_f, 0.0), axis=1, keepdims=True)
    same = jnp.where((owner_f == owner_col) & (down < across), 1.0, 0.0)
    rank = jnp.sum(same, axis=0, keepdims=True).astype(I32)
    lane = iota((1, lanes), 1)
    block = jnp.zeros((1, lanes), I32)
    starts = off_ref[0]
    for b in range(1, blocks + 1):
        block = block + (lane >= jnp.broadcast_to(starts[:, b : b + 1], (1, lanes))).astype(I32)
    count = jnp.broadcast_to(count_ref[...], (1, lanes))
    meta_ref[...] = jnp.concatenate([owner, rank, block, count] + [owner] * 4, axis=0)
    end = columns - clon
    for r in range(systems):
        copies[r].wait()
        south_ref[r, 0] = model_ref[r, end - clon : end]
        south_ref[r, 1] = model_ref[r, end:]
        south_ref[r, 2] = damp_out[r, end:]
        north_ref[r, 0] = model_ref[r, 0:clon]
        north_ref[r, 1] = model_ref[r, clon : 2 * clon]
        north_ref[r, 2] = damp_out[r, 0:clon]
    for copy in copies[systems:]:
        copy.wait()


def columns_body(clat, clon, model_ref, damp_ref, north_ref, south_ref, east_ref, west_ref):
    systems, _, depth = model_ref.shape
    for r in range(systems):
        for out, near, beyond in ((east_ref, clon - 1, clon - 2), (west_ref, 0, 1)):
            out[r, 0:clat] = model_ref[r, pl.ds(near, clat, stride=clon), :]
            out[r, clat : 2 * clat] = model_ref[r, pl.ds(beyond, clat, stride=clon), :]
            out[r, 2 * clat : 3 * clat] = damp_ref[r, pl.ds(near, clat, stride=clon), :]
            out[r, 3 * clat :] = jnp.concatenate(
                [
                    north_ref[r, 1, near : near + 1],
                    south_ref[r, 0, near : near + 1],
                    jnp.zeros((6, depth), F32),
                ],
                axis=0,
            )


def six(x, north, south, west, east):
    sub, lane = iota(x.shape, 0), iota(x.shape, 1)
    rows, depth = x.shape
    left = jnp.where(sub == 0, jnp.broadcast_to(west, x.shape), pltpu.roll(x, 1, 0))
    right = jnp.where(sub == rows - 1, jnp.broadcast_to(east, x.shape), pltpu.roll(x, rows - 1, 0))
    above = jnp.where(lane == 0, 0.0, pltpu.roll(x, 1, 1))
    below = jnp.where(lane == depth - 1, 0.0, pltpu.roll(x, depth - 1, 1))
    beside = north + south + left + right + above + below
    return DAMP_WEIGHT * (6.0 * x - beside)


def fold(x):
    parts = [x[i * 8 : (i + 1) * 8] for i in range(x.shape[0] // 8)]
    return functools.reduce(lambda a, b: a + b, parts)


def place(row, lane, value):
    return row + jnp.where(iota(row.shape, 1) == lane, jnp.broadcast_to(value, row.shape), 0.0)


STEP = 8


def dense_body(
    cap,
    clat,
    clon,
    rec_ref,
    corner_ref,
    wanted_ref,
    ray_ref,
    model_ref,
    damp_ref,
    north_ref,
    south_ref,
    west_ref,
    east_ref,
    solution_in,
    search_in,
    bar_out,
    image_out,
    solution_out,
    search_out,
    sums_out,
    chosen_out,
    north_s,
    south_s,
    west_s,
    east_s,
    alphas,
    sems,
):
    systems, _, depth = model_ref.shape
    copies = []
    for r in range(systems):
        for k, (a, b) in enumerate(((solution_in, solution_out), (search_in, search_out))):
            copies.append(pltpu.make_async_copy(a.at[r], b.at[r], sems.at[2 * r + k]))
    for copy in copies:
        copy.start()
    for r in range(systems):
        alphas[r] = jnp.sum(rec_ref[0:1, r : r + 1])
    lat_at, lon_at = lax.axis_index("lat"), lax.axis_index("lon")
    has_north = (lat_at > 0).astype(F32)
    has_south = (lat_at < lax.axis_size("lat") - 1).astype(F32)
    has_west = (lon_at > 0).astype(F32)
    has_east = (lon_at < lax.axis_size("lon") - 1).astype(F32)
    corner_n, corner_s = 3 * clat, 3 * clat + 1

    target = wanted_column(wanted_ref[...], cap) - 1.0
    slots = target.shape[0]
    square = (slots, slots)
    flat = jnp.sum(
        jnp.where(iota(square, 0) == iota(square, 1), jnp.broadcast_to(target, square), 0.0),
        axis=0,
        keepdims=True,
    ).astype(I32)
    wide = (PATCH * clon, slots)
    chosen_out[...] = (jnp.broadcast_to(flat, wide) == iota(wide, 0)).astype(F32).astype(BF16)

    def line(ref, r, i):
        return ref[r, pl.ds(pl.multiple_of(i * clon, clon), clon), :]

    def stencils(ref, r, k, first, last, west, east):
        base = k * STEP
        for j in range(STEP):
            i = base + j
            x = line(ref, r, i)
            if j == 0:
                above = jnp.where(k > 0, line(ref, r, jnp.maximum(i - 1, 0)), first)
            else:
                above = line(ref, r, i - 1)
            if j == STEP - 1:
                below = jnp.where(i + 1 < clat, line(ref, r, jnp.minimum(i + 1, clat - 1)), last)
            else:
                below = line(ref, r, i + 1)
            yield i, x, six(x, above, below, west[pl.ds(i, 1)], east[pl.ds(i, 1)])

    def system(r, row):
        alpha = alphas[r]

        def side(ref, own, flag):
            x, beyond, old = ref[r, 0:clat], ref[r, clat : 2 * clat], ref[r, 2 * clat : 3 * clat]
            upper, lower = ref[r, corner_n : corner_n + 1], ref[r, corner_s : corner_s + 1]
            return (six(x, beyond, own, upper, lower) - alpha * old) * flag

        west_s[...] = side(west_ref, model_ref[r, pl.ds(0, clat, stride=clon), :], has_west)
        east_s[...] = side(east_ref, model_ref[r, pl.ds(clon - 1, clat, stride=clon), :], has_east)
        north_s[...] = has_north * (
            six(
                north_ref[r, 1],
                north_ref[r, 0],
                line(model_ref, r, 0),
                west_ref[r, corner_n : corner_n + 1],
                east_ref[r, corner_n : corner_n + 1],
            )
            - alpha * north_ref[r, 2]
        )
        south_s[...] = has_south * (
            six(
                south_ref[r, 0],
                line(model_ref, r, clat - 1),
                south_ref[r, 1],
                west_ref[r, corner_s : corner_s + 1],
                east_ref[r, corner_s : corner_s + 1],
            )
            - alpha * south_ref[r, 2]
        )

        def damped(k, acc):
            bar_sq, model_sq = acc
            ends = (north_ref[r, 1], south_ref[r, 0], west_ref.at[r], east_ref.at[r])
            for i, x, got in stencils(model_ref, r, k, *ends):
                bar = got - alpha * line(damp_ref, r, i)
                bar_out[r, pl.ds(pl.multiple_of(i * clon, clon), clon), :] = bar
                bar_sq, model_sq = bar_sq + fold(bar * bar), model_sq + fold(x * x)
            return bar_sq, model_sq

        def imaged(k, acc):
            image_sq, cross = acc
            for i, x, image in stencils(bar_out, r, k, north_s[...], south_s[...], west_s, east_s):
                image_out[r, pl.ds(pl.multiple_of(i * clon, clon), clon), :] = image
                image_sq, cross = image_sq + fold(image * image), cross + fold(image * line(model_ref, r, i))
            return image_sq, cross

        zero = jnp.zeros((8, depth), F32)
        bar_sq, model_sq = lax.fori_loop(0, clat // STEP, damped, (zero, zero))
        image_sq, cross = lax.fori_loop(0, clat // STEP, imaged, (zero, zero))
        ray = ray_ref[r, 0]
        residual = jnp.sum(bar_sq, keepdims=True) + jnp.sum(ray * ray, keepdims=True)
        row = place(row, r, residual)
        row = place(row, systems + r, jnp.sum(image_sq, keepdims=True))
        row = place(row, 2 * systems + r, jnp.sum(cross, keepdims=True))
        return place(row, 3 * systems + r, jnp.sum(model_sq, keepdims=True))

    sums_out[...] = lax.fori_loop(0, systems, system, jnp.zeros((1, depth), F32))
    for copy in copies:
        copy.wait()


def combine_body(clon, corner_ref, terms_ref, chosen_ref, image_ref, model_ref, sums_ref, added_ref, parts_ref):
    systems, width, depth = added_ref.shape
    slots = chosen_ref.shape[1]
    chosen = chosen_ref[...]
    row = sums_ref[...]
    here = pl.ds(pl.multiple_of(corner_ref[0] * clon, clon), width)
    for r in range(systems):
        x = terms_ref[pl.ds(r, slots, stride=systems), :]
        high = x.astype(BF16)
        rest = x - high.astype(F32)
        middle = rest.astype(BF16)
        low = (rest - middle.astype(F32)).astype(BF16)
        three = jnp.dot(chosen, jnp.concatenate([high, middle, low], axis=1), preferred_element_type=F32)
        added = three[:, 0:depth] + (three[:, depth : 2 * depth] + three[:, 2 * depth :])
        added_ref[r] = added
        square = jnp.sum(added * (2.0 * image_ref[r, here, :] + added), keepdims=True)
        cross = jnp.sum(added * model_ref[r, here, :], keepdims=True)
        row = place(row, systems + r, square)
        row = place(row, 2 * systems + r, cross)
    parts_ref[...] = jnp.broadcast_to(row, parts_ref.shape)


def finish_body(
    rows_all,
    cells_all,
    clon,
    corner_ref,
    parts_ref,
    rec_ref,
    ray_ref,
    added_ref,
    image_ref,
    model_ref,
    bar_ref,
    solution_ref,
    search_ref,
    ray_out,
    damp_out,
    model_out,
    solution_out,
    search_out,
    rec_out,
    damp_s,
    model_s,
    solution_s,
    search_s,
    coef,
    sems,
):
    systems, columns, depth = image_ref.shape
    total = jnp.sum(parts_ref[...], axis=0, keepdims=True)
    residual_sq, image_sq, cross, model_sq = (total[:, q * systems : (q + 1) * systems] for q in range(4))
    rho_bar, phi_bar = rec_ref[1:2], rec_ref[2:3]
    beta = jnp.sqrt(residual_sq / rows_all + EPSILON)
    update_sq = image_sq / (beta * beta) - 2.0 * cross + beta * beta * model_sq
    alpha = jnp.sqrt(jnp.maximum(update_sq, 0.0) / cells_all + EPSILON)
    rho = jnp.sqrt(rho_bar * rho_bar + beta * beta)
    cosine = rho_bar / rho
    sine = beta / rho
    rec_out[...] = jnp.concatenate([alpha, -cosine * alpha, sine * phi_bar], axis=0)
    scales = (
        1.0 / beta,
        1.0 / (beta * alpha),
        beta / alpha,
        cosine * phi_bar / rho,
        sine * alpha / rho,
    )
    for q, scale in enumerate(scales):
        for s in range(systems):
            coef[q, s] = scale[0, s]
    rows = columns // PIECES

    def outgoing(r, p):
        at = pl.ds(pl.multiple_of(p * rows, rows), rows)
        pairs = (
            (damp_s, damp_out),
            (model_s, model_out),
            (solution_s, solution_out),
            (search_s, search_out),
        )
        return [
            pltpu.make_async_copy(a.at[r, at], b.at[r, at], sems.at[r, p, k]) for k, (a, b) in enumerate(pairs)
        ]

    def piece(n, _):
        r, p = n // PIECES, n % PIECES
        at = pl.ds(pl.multiple_of(p * rows, rows), rows)
        search = search_ref[r, at, :]
        damp_s[r, at, :] = bar_ref[r, at, :] * coef[0, r]
        new = image_ref[r, at, :] * coef[1, r] - model_ref[r, at, :] * coef[2, r]
        model_s[r, at, :] = new
        solution_s[r, at, :] = solution_ref[r, at, :] + search * coef[3, r]
        search_s[r, at, :] = new - search * coef[4, r]
        for k in range(PATCH):
            begin = (corner_ref[0] + k) * clon

            @pl.when((begin >= p * rows) & (begin < (p + 1) * rows))
            def _():
                line = pl.ds(pl.multiple_of(begin, clon), clon)
                more = added_ref[r, k * clon : (k + 1) * clon, :] * coef[1, r]
                model_s[r, line, :] = model_s[r, line, :] + more
                search_s[r, line, :] = search_s[r, line, :] + more

        for copy in outgoing(r, p):
            copy.start()
        return 0

    lax.fori_loop(0, systems * PIECES, piece, 0)
    for r in range(systems):
        ray_out[r] = ray_ref[r] * coef[0, r]

    def settle(n, _):
        for copy in outgoing(n // PIECES, n % PIECES):
            copy.wait()
        return 0

    lax.fori_loop(0, systems * PIECES, settle, 0)


PIECES = 4


def rays_body(cap, blocks, meta_ref, rec_ref, tiles_ref, fetched_ref, old_ref, bar_ref, term_ref, masks, lows):
    tiles, width, depth = tiles_ref.shape[2:]
    systems = old_ref.shape[0]
    group = cap * systems
    for c in range(cap + 1):
        here = lax.shift_right_logical(iota((group, depth), 0), systems.bit_length() - 1) == c
        masks[c] = here.astype(F32).astype(BF16)
    term_ref[...] = jnp.zeros(term_ref.shape, F32)
    lows[...] = jnp.zeros(lows.shape, BF16)
    total = jnp.zeros((blocks * group, width), F32)
    for t in range(tiles):
        owner, rank, block = meta_ref[0, t], meta_ref[1, t], meta_ref[2, t]
        rows = fetched_ref[pl.ds(pl.multiple_of(owner * group, group), group), :]
        left = jnp.concatenate(
            [rows * masks[jnp.where(block == b, rank, cap)] for b in range(blocks)], axis=0
        )
        total = total + lax.dot_general(
            left, tiles_ref[0, 0, t], (((1,), (1,)), ((), ())), preferred_element_type=F32
        )
    for b in range(blocks):
        traced = jnp.zeros((systems, width), F32)
        for c in range(cap):
            at = b * group + c * systems
            traced = traced + total[at : at + systems]
        old = jnp.concatenate(
            [old_ref[r, 0, :, b * width : (b + 1) * width] * rec_ref[0:1, r : r + 1] for r in range(systems)], axis=0
        )
        live = iota((systems, width), 1) + b * width < meta_ref[3, 0]
        bar = jnp.where(live, traced - old, 0.0)
        for r in range(systems):
            bar_ref[r, 0, :, b * width : (b + 1) * width] = bar[r : r + 1]
        lows[b] = jnp.concatenate([bar, jnp.zeros((16 - systems, width), F32)], axis=0).astype(BF16)
    for t in range(tiles):
        slot = meta_ref[0, t] * cap + meta_ref[1, t]
        term = jnp.dot(lows[meta_ref[2, t]], tiles_ref[0, 0, t], preferred_element_type=F32)
        term_ref[slot] = term[:systems]


def shifted(x, axis, step):
    count = lax.axis_size(axis)
    if step > 0:
        pairs = [(i, i + 1) for i in range(count - 1)]
    else:
        pairs = [(i + 1, i) for i in range(count - 1)]
    return lax.ppermute(x, axis, pairs)


def exchange(x):
    return lax.all_to_all(x, AXES, split_axis=0, concat_axis=0, tiled=True)


def per_device(
    sensitivity,
    block_ids,
    block_offsets,
    ray_counts,
    ray_vector,
    damping_vector,
    model_vector,
    solution,
    search,
    recurrence,
):
    lat_size, lon_size = lax.axis_size("lat"), lax.axis_size("lon")
    devices = lat_size * lon_size
    tiles, width, depth = sensitivity.shape[2:]
    blocks = block_offsets.shape[-1] - 1
    systems, clat, clon, _ = model_vector.shape
    columns = clat * clon
    cap = max(2 * ((tiles + devices - 1) // devices), 16 // systems)
    slots = devices * cap
    group = cap * systems
    cells_all = devices * columns * depth
    rows_all = devices * blocks * width + cells_all
    lanes = 128
    full, flat = model_vector.shape, (systems, columns, depth)
    here, there = pltpu.VMEM, pltpu.HBM

    lists = exchange(jnp.broadcast_to(block_ids[0], (devices, 1, tiles))).reshape(devices, tiles)

    served, wanted, corner, model = call(
        functools.partial(serve_body, cap, clat, clon),
        "serve",
        (
            there((slots * systems, depth), BF16),
            here((devices, lanes), F32),
            jax.ShapeDtypeStruct((1,), I32),
            here(flat, F32),
        ),
        [vmem(), hbm()],
        (vmem(), vmem(), smem(), vmem()),
        scratch=[pltpu.VMEM((slots * systems, depth), F32), pltpu.SemaphoreType.DMA((systems,))],
    )(lists, far(model_vector.reshape(flat)))
    fetched = exchange(served.reshape(devices, group, depth)).reshape(slots * systems, depth)

    band = (systems, 3, clon, depth)
    damping, held, north_msg, south_msg, meta = call(
        functools.partial(pack_body, columns.bit_length() - 1, clon, blocks),
        "pack",
        (here(flat, F32), here(sensitivity.shape, BF16), there(band, F32), there(band, F32), jax.ShapeDtypeStruct((8, lanes), I32)),
        [vmem()] * 4 + [hbm(), hbm()],
        (vmem(),) * 5,
        scratch=[pltpu.SemaphoreType.DMA((systems + 2,))],
        moved=4 * systems * columns * depth + 2 * tiles * width * depth,
    )(
        far(block_ids),
        block_offsets,
        ray_counts,
        near(model),
        far(damping_vector.reshape(flat)),
        far(sensitivity),
    )
    north = shifted(south_msg, "lat", 1)
    south = shifted(north_msg, "lat", -1)

    side = (systems, 3 * clat + 8, depth)
    east_msg, west_msg = call(
        functools.partial(columns_body, clat, clon),
        "columns",
        (there(side, F32), there(side, F32)),
        [vmem()] * 4,
        (vmem(), vmem()),
    )(near(model), near(damping), far(north), far(south))
    west = shifted(east_msg, "lon", 1)
    east = shifted(west_msg, "lon", -1)

    ray_bar, terms = call(
        functools.partial(rays_body, cap, blocks),
        "rays",
        (here(ray_vector.shape, F32), there((slots, systems, depth), F32)),
        [smem()] + [vmem()] * 4,
        (vmem(), vmem()),
        scratch=[
            pltpu.VMEM((cap + 1, group, depth), BF16),
            pltpu.VMEM((blocks + 1, 16, width), BF16),
        ],
        flops=4 * tiles * width * depth * 16,
        moved=2 * tiles * width * depth,
    )(meta, far(recurrence), near(held), fetched, far(ray_vector))
    arrived = exchange(terms.reshape(devices, group, depth)).reshape(slots * systems, depth)

    bar, image, solution, search, sums, chosen = call(
        functools.partial(dense_body, cap, clat, clon),
        "dense",
        (here(flat, F32),) * 4 + (here((1, lanes), F32), here((PATCH * clon, slots), BF16)),
        [vmem(), smem()] + [vmem()] * 8 + [hbm()] * 2,
        (vmem(),) * 6,
        scratch=[
            pltpu.VMEM((clon, depth), F32),
            pltpu.VMEM((clon, depth), F32),
            pltpu.VMEM((clat, depth), F32),
            pltpu.VMEM((clat, depth), F32),
            pltpu.SMEM((systems,), F32),
            pltpu.SemaphoreType.DMA((2 * systems,)),
        ],
        flops=40 * systems * columns * depth,
        moved=24 * systems * columns * depth,
    )(
        far(recurrence),
        corner,
        near(wanted),
        near(ray_bar),
        near(model),
        near(damping),
        far(north),
        far(south),
        far(west),
        far(east),
        far(solution.reshape(flat)),
        far(search.reshape(flat)),
    )

    added, parts = call(
        functools.partial(combine_body, clon),
        "combine",
        (here((systems, PATCH * clon, depth), F32), there((devices, lanes), F32)),
        [smem()] + [vmem()] * 5,
        (vmem(),) * 2,
    )(corner, arrived, near(chosen), near(image), near(model), near(sums))
    every = exchange(parts.reshape(devices, 1, lanes)).reshape(devices, lanes)

    outs = call(
        functools.partial(finish_body, float(rows_all), float(cells_all), clon),
        "finish",
        (there(ray_vector.shape, F32),) + (there(flat, F32),) * 4 + (there(recurrence.shape, F32),),
        [smem()] + [vmem()] * 9,
        (vmem(),) + (hbm(),) * 4 + (vmem(),),
        scratch=[
            pltpu.VMEM(flat, F32),
            pltpu.VMEM(flat, F32),
            pltpu.VMEM(flat, F32),
            pltpu.VMEM(flat, F32),
            pltpu.SMEM((5, systems), F32),
            pltpu.SemaphoreType.DMA((systems, PIECES, 4)),
        ],
        flops=10 * systems * columns * depth,
        moved=16 * systems * columns * depth,
    )(
        corner,
        every,
        far(recurrence),
        near(ray_bar),
        near(added),
        near(image),
        near(model),
        near(bar),
        near(solution),
        near(search),
    )
    ray_out, damp_out, model_out, solution_out, search_out, rec_out = outs
    fields = (x.reshape(full) for x in (damp_out, model_out, solution_out, search_out))
    return (ray_out, *fields, rec_out)


def solution(mesh):
    fields = P(None, "lat", "lon", None)
    return jax.shard_map(
        per_device,
        mesh=mesh,
        in_specs=(
            P("lat", "lon", None, None, None),
            P("lat", "lon", None),
            P("lat", "lon", None),
            P("lat", "lon"),
            fields,
            fields,
            fields,
            fields,
            fields,
            P(),
        ),
        out_specs=(fields, fields, fields, fields, fields, P()),
        check_vma=False,
    )
```

```python
import functools

import jax
import jax.numpy as jnp
from jax import lax
from jax.experimental import pallas as pl
from jax.experimental.pallas import tpu as pltpu
from jax.sharding import PartitionSpec as P

DAMP_WEIGHT = 0.15
EPSILON = 1e-05
AXES = ("lat", "lon")
PATCH = 4
F32, BF16, I32 = jnp.float32, jnp.bfloat16, jnp.int32


def iota(shape, dim):
    return lax.broadcasted_iota(I32, shape, dim)


def vmem():
    return pl.BlockSpec(memory_space=pltpu.VMEM)


def hbm():
    return pl.BlockSpec(memory_space=pltpu.HBM)


def near(x):
    return pltpu.with_memory_space_constraint(x, pltpu.VMEM)


def far(x):
    return pltpu.with_memory_space_constraint(x, pltpu.HBM)


def smem():
    return pl.BlockSpec(memory_space=pltpu.SMEM)


def call(body, name, out_shape, in_specs, out_specs, scratch=(), grid=(), mib=16, flops=0, moved=0):
    return pl.pallas_call(
        body,
        name=name,
        grid=grid,
        out_shape=out_shape,
        in_specs=in_specs,
        out_specs=out_specs,
        scratch_shapes=list(scratch),
        compiler_params=pltpu.CompilerParams(vmem_limit_bytes=mib * 2**20),
        cost_estimate=pl.CostEstimate(flops=flops, bytes_accessed=moved, transcendentals=0),
    )


STEP = 8


def wanted_column(wanted, cap):
    devices, lanes = wanted.shape
    rows = devices * cap
    spread = jnp.broadcast_to(wanted[:, None, :], (devices, cap, lanes)).reshape(rows, lanes)
    pick = iota((rows, lanes), 1) == (iota((rows, lanes), 0) & (cap - 1))
    return jnp.sum(jnp.where(pick, spread, 0.0), axis=1, keepdims=True)


def serve_body(cap, clat, clon, lists_ref, model_in, served_ref, wanted_ref, corner_ref, patch, mixed, sems):
    systems, width, depth = patch.shape
    devices, tiles = lists_ref.shape
    lanes = 128
    shift = (clat * clon).bit_length() - 1
    me = lax.axis_index("lat") * lax.axis_size("lon") + lax.axis_index("lon")
    ids = jnp.concatenate([lists_ref[...], jnp.full((devices, lanes - tiles), -1, I32)], axis=1)
    column = ids - lax.shift_left(me, shift)
    mine = (column >= 0) & (column < clat * clon) & (ids >= 0)
    first = jnp.min(jnp.where(mine, column, clat * clon))
    corner = jnp.minimum(lax.shift_right_logical(first, clon.bit_length() - 1), clat - PATCH)
    corner_ref[0] = corner
    at = pl.ds(pl.multiple_of(corner * clon, clon), width)
    copies = [pltpu.make_async_copy(model_in.at[r, at], patch.at[r], sems.at[r]) for r in range(systems)]
    for copy in copies:
        copy.start()
    ahead = (iota((lanes, lanes), 0) < iota((lanes, lanes), 1)).astype(F32).astype(BF16)
    rank = jnp.dot(mine.astype(F32).astype(BF16), ahead, preferred_element_type=F32)
    value = (column - corner * clon + 1).astype(F32)
    at = iota((devices, lanes), 1)
    wanted = jnp.zeros((devices, lanes), F32)
    for c in range(cap):
        picked = jnp.sum(jnp.where(mine & (rank == c), value, 0.0), axis=1, keepdims=True)
        wanted = jnp.where(at == c, picked, wanted)
    wanted_ref[...] = wanted
    target = wanted_column(wanted, cap).astype(I32) - 1
    rows = target.shape[0]
    chosen = (jnp.broadcast_to(target, (rows, width)) == iota((rows, width), 1)).astype(F32).astype(BF16)
    for r in range(systems):
        copies[r].wait()
        table = patch[r].astype(BF16)
        mixed[pl.ds(r, rows, stride=systems), :] = jnp.dot(chosen, table, preferred_element_type=F32)
    served_ref[...] = mixed[...].astype(BF16)


def pack_body(after_ref, model_in, damp_in, north_ref, south_ref, sems):
    last = model_in.shape[1] - 1
    pairs = (
        (model_in.at[:, pl.ds(last - 1, 2)], south_ref.at[:, pl.ds(0, 2)]),
        (damp_in.at[:, pl.ds(last, 1)], south_ref.at[:, pl.ds(2, 1)]),
        (model_in.at[:, pl.ds(0, 2)], north_ref.at[:, pl.ds(0, 2)]),
        (damp_in.at[:, pl.ds(0, 1)], north_ref.at[:, pl.ds(2, 1)]),
    )
    copies = [pltpu.make_async_copy(a, b, sems.at[i]) for i, (a, b) in enumerate(pairs)]
    for copy in copies:
        copy.start()
    for copy in copies:
        copy.wait()


def flanks_body(
    shift, blocks, after_ref, ids_ref, off_ref, count_ref, model_in, damp_in, east_ref, west_ref, meta_ref, slabs, sems
):
    systems, clat, clon, depth = model_in.shape
    copies = []
    for k, (ref, at) in enumerate(((model_in, 0), (model_in, clon - 8), (damp_in, 0), (damp_in, clon - 8))):
        copies.append(pltpu.make_async_copy(ref.at[:, :, pl.ds(at, 8)], slabs.at[k], sems.at[k]))
    for copy in copies:
        copy.start()
    tiles = ids_ref.shape[-1]
    lanes = 128
    ids = jnp.concatenate([ids_ref[0], jnp.full((1, lanes - tiles), -1, I32)], axis=1)
    owner = lax.shift_right_arithmetic(ids, shift)
    square = (lanes, lanes)
    down, across = iota(square, 0), iota(square, 1)
    owner_f = jnp.broadcast_to(owner.astype(F32), square)
    owner_col = jnp.sum(jnp.where(down == across, owner_f, 0.0), axis=1, keepdims=True)
    same = jnp.where((owner_f == owner_col) & (down < across), 1.0, 0.0)
    rank = jnp.sum(same, axis=0, keepdims=True).astype(I32)
    lane = iota((1, lanes), 1)
    block = jnp.zeros((1, lanes), I32)
    starts = off_ref[0]
    for b in range(1, blocks + 1):
        block = block + (lane >= jnp.broadcast_to(starts[:, b : b + 1], (1, lanes))).astype(I32)
    count = jnp.broadcast_to(count_ref[...], (1, lanes))
    meta_ref[...] = jnp.concatenate([owner, rank, block, count] + [owner] * 4, axis=0)
    for copy in copies:
        copy.wait()
    rows = slabs.reshape(4, systems, clat * 8, depth)
    for r in range(systems):
        for out, slab, near_at, beyond in ((east_ref, 1, 7, 6), (west_ref, 0, 0, 1)):
            out[r, 0:clat] = rows[slab, r, pl.ds(near_at, clat, stride=8), :]
            out[r, clat : 2 * clat] = rows[slab, r, pl.ds(beyond, clat, stride=8), :]
            out[r, 2 * clat : 3 * clat] = rows[slab + 2, r, pl.ds(near_at, clat, stride=8), :]
            out[r, 3 * clat :] = jnp.zeros((8, depth), F32)


def corners_body(east_in, west_in, north_ref, south_ref, east_ref, west_ref):
    systems, long, depth = east_ref.shape
    at = long - 8
    clon = north_ref.shape[2]
    for r in range(systems):
        for ref, out, near_at in ((east_in, east_ref, clon - 1), (west_in, west_ref, 0)):
            out[r, 0:at] = ref[r, 0:at]
            out[r, at:] = jnp.concatenate(
                [
                    north_ref[r, 1, near_at : near_at + 1],
                    south_ref[r, 0, near_at : near_at + 1],
                    jnp.zeros((6, depth), F32),
                ],
                axis=0,
            )


def six(x, north, south, west, east):
    lane = iota(x.shape, 1)
    rows, depth = x.shape
    left, right = pltpu.roll(x, 1, 0), pltpu.roll(x, rows - 1, 0)
    ends = (8, depth)
    row = iota(ends, 0)
    left = jnp.concatenate([jnp.where(row == 0, jnp.broadcast_to(west, ends), left[:8]), left[8:]], axis=0)
    right = jnp.concatenate([right[:-8], jnp.where(row == 7, jnp.broadcast_to(east, ends), right[-8:])], axis=0)
    above = jnp.where(lane == 0, 0.0, pltpu.roll(x, 1, 1))
    below = jnp.where(lane == depth - 1, 0.0, pltpu.roll(x, depth - 1, 1))
    beside = north + south + left + right + above + below
    return DAMP_WEIGHT * (6.0 * x - beside)


def fold(x):
    parts = [x[i * 8 : (i + 1) * 8] for i in range(x.shape[0] // 8)]
    return functools.reduce(lambda a, b: a + b, parts)


def place(row, lane, value):
    return row + jnp.where(iota(row.shape, 1) == lane, jnp.broadcast_to(value, row.shape), 0.0)


def dense_body(
    cap,
    clat,
    clon,
    rec_ref,
    corner_ref,
    wanted_ref,
    ray_ref,
    model_in,
    damp_in,
    north_ref,
    south_ref,
    west_ref,
    east_ref,
    bar_sent,
    image_sent,
    sums_out,
    patch_out,
    model_patch_out,
    chosen_out,
    model_ref,
    damp_ref,
    bar_out,
    image_out,
    north_s,
    south_s,
    west_s,
    east_s,
    alphas,
    sems,
):
    systems, _, depth = model_ref.shape

    def incoming(r):
        return (
            pltpu.make_async_copy(model_in.at[r], model_ref.at[r], sems.at[r, 0]),
            pltpu.make_async_copy(damp_in.at[r], damp_ref.at[r], sems.at[r, 1]),
        )

    def outgoing(r):
        return (
            pltpu.make_async_copy(bar_out.at[r], bar_sent.at[r], sems.at[r, 2]),
            pltpu.make_async_copy(image_out.at[r], image_sent.at[r], sems.at[r, 3]),
        )

    for r in range(systems):
        for copy in incoming(r):
            copy.start()
    for r in range(systems):
        alphas[r] = jnp.sum(rec_ref[0:1, r : r + 1])
    lat_at, lon_at = lax.axis_index("lat"), lax.axis_index("lon")
    has_north = (lat_at > 0).astype(F32)
    has_south = (lat_at < lax.axis_size("lat") - 1).astype(F32)
    has_west = (lon_at > 0).astype(F32)
    has_east = (lon_at < lax.axis_size("lon") - 1).astype(F32)
    corner_n, corner_s = 3 * clat, 3 * clat + 1

    target = wanted_column(wanted_ref[...], cap) - 1.0
    slots = target.shape[0]
    square = (slots, slots)
    flat = jnp.sum(
        jnp.where(iota(square, 0) == iota(square, 1), jnp.broadcast_to(target, square), 0.0),
        axis=0,
        keepdims=True,
    ).astype(I32)
    wide = (PATCH * clon, slots)
    chosen_out[...] = (jnp.broadcast_to(flat, wide) == iota(wide, 0)).astype(F32).astype(BF16)

    def line(ref, r, i):
        return ref[r, pl.ds(pl.multiple_of(i * clon, clon), clon), :]

    def stencils(ref, r, k, first, last, west, east):
        base = k * STEP
        for j in range(STEP):
            i = base + j
            x = line(ref, r, i)
            if j == 0:
                above = jnp.where(k > 0, line(ref, r, jnp.maximum(i - 1, 0)), first)
            else:
                above = line(ref, r, i - 1)
            if j == STEP - 1:
                below = jnp.where(i + 1 < clat, line(ref, r, jnp.minimum(i + 1, clat - 1)), last)
            else:
                below = line(ref, r, i + 1)
            yield i, x, six(x, above, below, west[pl.ds(i, 1)], east[pl.ds(i, 1)])

    def system(r, row):
        alpha = alphas[r]
        for copy in incoming(r):
            copy.wait()

        def side(ref, own, flag):
            x, beyond, old = ref[r, 0:clat], ref[r, clat : 2 * clat], ref[r, 2 * clat : 3 * clat]
            upper, lower = ref[r, corner_n : corner_n + 1], ref[r, corner_s : corner_s + 1]
            return (six(x, beyond, own, upper, lower) - alpha * old) * flag

        west_s[...] = side(west_ref, model_ref[r, pl.ds(0, clat, stride=clon), :], has_west)
        east_s[...] = side(east_ref, model_ref[r, pl.ds(clon - 1, clat, stride=clon), :], has_east)
        north_s[...] = has_north * (
            six(
                north_ref[r, 1],
                north_ref[r, 0],
                line(model_ref, r, 0),
                west_ref[r, corner_n : corner_n + 1],
                east_ref[r, corner_n : corner_n + 1],
            )
            - alpha * north_ref[r, 2]
        )
        south_s[...] = has_south * (
            six(
                south_ref[r, 0],
                line(model_ref, r, clat - 1),
                south_ref[r, 1],
                west_ref[r, corner_s : corner_s + 1],
                east_ref[r, corner_s : corner_s + 1],
            )
            - alpha * south_ref[r, 2]
        )

        def damped(k, acc):
            bar_sq, model_sq = acc
            ends = (north_ref[r, 1], south_ref[r, 0], west_ref.at[r], east_ref.at[r])
            for i, x, got in stencils(model_ref, r, k, *ends):
                bar = got - alpha * line(damp_ref, r, i)
                bar_out[r, pl.ds(pl.multiple_of(i * clon, clon), clon), :] = bar
                bar_sq, model_sq = bar_sq + fold(bar * bar), model_sq + fold(x * x)
            return bar_sq, model_sq

        def imaged(k, acc):
            image_sq, cross = acc
            for i, x, image in stencils(bar_out, r, k, north_s[...], south_s[...], west_s, east_s):
                image_out[r, pl.ds(pl.multiple_of(i * clon, clon), clon), :] = image
                image_sq, cross = image_sq + fold(image * image), cross + fold(image * line(model_ref, r, i))
            return image_sq, cross

        zero = jnp.zeros((8, depth), F32)
        bar_sq, model_sq = lax.fori_loop(0, clat // STEP, damped, (zero, zero))
        image_sq, cross = lax.fori_loop(0, clat // STEP, imaged, (zero, zero))
        for copy in outgoing(r):
            copy.start()
        here = pl.ds(pl.multiple_of(corner_ref[0] * clon, clon), PATCH * clon)
        patch_out[r] = image_out[r, here, :]
        model_patch_out[r] = model_ref[r, here, :]
        ray = ray_ref[r, 0]
        residual = jnp.sum(bar_sq, keepdims=True) + jnp.sum(ray * ray, keepdims=True)
        row = place(row, r, residual)
        row = place(row, systems + r, jnp.sum(image_sq, keepdims=True))
        row = place(row, 2 * systems + r, jnp.sum(cross, keepdims=True))
        return place(row, 3 * systems + r, jnp.sum(model_sq, keepdims=True))

    sums_out[...] = lax.fori_loop(0, systems, system, jnp.zeros((1, depth), F32))
    for r in range(systems):
        for copy in outgoing(r):
            copy.wait()


def combine_body(terms_ref, chosen_ref, patch_ref, model_patch_ref, sums_ref, added_ref, parts_ref):
    systems, _, depth = added_ref.shape
    slots = chosen_ref.shape[1]
    chosen = chosen_ref[...]
    row = sums_ref[...]
    for r in range(systems):
        x = terms_ref[pl.ds(r, slots, stride=systems), :]
        high = x.astype(BF16)
        rest = x - high.astype(F32)
        middle = rest.astype(BF16)
        low = (rest - middle.astype(F32)).astype(BF16)
        three = jnp.dot(chosen, jnp.concatenate([high, middle, low], axis=1), preferred_element_type=F32)
        added = three[:, 0:depth] + (three[:, depth : 2 * depth] + three[:, 2 * depth :])
        added_ref[r] = added
        square = jnp.sum(added * (2.0 * patch_ref[r] + added), keepdims=True)
        cross = jnp.sum(added * model_patch_ref[r], keepdims=True)
        row = place(row, systems + r, square)
        row = place(row, 2 * systems + r, cross)
    parts_ref[...] = jnp.broadcast_to(row, parts_ref.shape)


def finish_body(
    rows_all,
    cells_all,
    clon,
    corner_ref,
    parts_ref,
    rec_ref,
    ray_ref,
    added_ref,
    image_in,
    model_in,
    bar_in,
    solution_in,
    search_in,
    ray_out,
    damp_out,
    model_out,
    solution_out,
    search_out,
    rec_out,
    image_ref,
    model_ref,
    bar_ref,
    solution_ref,
    search_ref,
    damp_s,
    model_s,
    solution_s,
    search_s,
    coef,
    sems,
    in_sems,
):
    systems, columns, depth = image_ref.shape
    rows = columns // PIECES

    def incoming(r, p):
        at = pl.ds(pl.multiple_of(p * rows, rows), rows)
        pairs = (
            (search_in, search_ref),
            (bar_in, bar_ref),
            (image_in, image_ref),
            (model_in, model_ref),
            (solution_in, solution_ref),
        )
        return [
            pltpu.make_async_copy(a.at[r, at], b.at[r, at], in_sems.at[r, p, k]) for k, (a, b) in enumerate(pairs)
        ]

    def begin_piece(n, _):
        for copy in incoming(n // PIECES, n % PIECES):
            copy.start()
        return 0

    lax.fori_loop(0, systems * PIECES, begin_piece, 0)
    total = jnp.sum(parts_ref[...], axis=0, keepdims=True)
    residual_sq, image_sq, cross, model_sq = (total[:, q * systems : (q + 1) * systems] for q in range(4))
    rho_bar, phi_bar = rec_ref[1:2], rec_ref[2:3]
    beta = jnp.sqrt(residual_sq / rows_all + EPSILON)
    update_sq = image_sq / (beta * beta) - 2.0 * cross + beta * beta * model_sq
    alpha = jnp.sqrt(jnp.maximum(update_sq, 0.0) / cells_all + EPSILON)
    rho = jnp.sqrt(rho_bar * rho_bar + beta * beta)
    cosine = rho_bar / rho
    sine = beta / rho
    rec_out[...] = jnp.concatenate([alpha, -cosine * alpha, sine * phi_bar], axis=0)
    scales = (
        1.0 / beta,
        1.0 / (beta * alpha),
        beta / alpha,
        cosine * phi_bar / rho,
        sine * alpha / rho,
    )
    for q, scale in enumerate(scales):
        for s in range(systems):
            coef[q, s] = scale[0, s]
    def outgoing(r, p):
        at = pl.ds(pl.multiple_of(p * rows, rows), rows)
        pairs = (
            (damp_s, damp_out),
            (model_s, model_out),
            (solution_s, solution_out),
            (search_s, search_out),
        )
        return [
            pltpu.make_async_copy(a.at[r, at], b.at[r, at], sems.at[r, p, k]) for k, (a, b) in enumerate(pairs)
        ]

    def piece(n, _):
        r, p = n // PIECES, n % PIECES
        at = pl.ds(pl.multiple_of(p * rows, rows), rows)
        for copy in incoming(r, p):
            copy.wait()
        search = search_ref[r, at, :]
        damp_s[r, at, :] = bar_ref[r, at, :] * coef[0, r]
        new = image_ref[r, at, :] * coef[1, r] - model_ref[r, at, :] * coef[2, r]
        model_s[r, at, :] = new
        solution_s[r, at, :] = solution_ref[r, at, :] + search * coef[3, r]
        search_s[r, at, :] = new - search * coef[4, r]
        for k in range(PATCH):
            begin = (corner_ref[0] + k) * clon

            @pl.when((begin >= p * rows) & (begin < (p + 1) * rows))
            def _():
                line = pl.ds(pl.multiple_of(begin, clon), clon)
                more = added_ref[r, k * clon : (k + 1) * clon, :] * coef[1, r]
                model_s[r, line, :] = model_s[r, line, :] + more
                search_s[r, line, :] = search_s[r, line, :] + more

        for copy in outgoing(r, p):
            copy.start()
        return 0

    lax.fori_loop(0, systems * PIECES, piece, 0)
    for r in range(systems):
        ray_out[r] = ray_ref[r] * coef[0, r]

    def settle(n, _):
        for copy in outgoing(n // PIECES, n % PIECES):
            copy.wait()
        return 0

    lax.fori_loop(0, systems * PIECES, settle, 0)


PIECES = 2


def rays_body(
    cap, blocks, meta_ref, rec_ref, tiles_in, fetched_ref, old_ref, after_ref, bar_ref, term_ref, tiles_ref, masks, lows, sems
):
    tiles, width, depth = tiles_in.shape[2:]
    part = -(-tiles // PARTS)
    copies = []
    for k in range(PARTS):
        at = (0, 0, pl.ds(k * part, min(part, tiles - k * part)))
        copies.append(pltpu.make_async_copy(tiles_in.at[at], tiles_ref.at[at], sems.at[k]))
    for copy in copies:
        copy.start()
    systems = old_ref.shape[0]
    group = cap * systems
    for c in range(cap + 1):
        here = lax.shift_right_logical(iota((group, depth), 0), systems.bit_length() - 1) == c
        masks[c] = here.astype(F32).astype(BF16)
    term_ref[...] = jnp.zeros(term_ref.shape, F32)
    lows[...] = jnp.zeros(lows.shape, BF16)
    total = jnp.zeros((blocks * group, width), F32)
    for t in range(tiles):
        if t % part == 0:
            copies[t // part].wait()
        owner, rank, block = meta_ref[0, t], meta_ref[1, t], meta_ref[2, t]
        rows = fetched_ref[pl.ds(pl.multiple_of(owner * group, group), group), :]
        left = jnp.concatenate(
            [rows * masks[jnp.where(block == b, rank, cap)] for b in range(blocks)], axis=0
        )
        total = total + lax.dot_general(
            left, tiles_ref[0, 0, t], (((1,), (1,)), ((), ())), preferred_element_type=F32
        )
    for b in range(blocks):
        traced = jnp.zeros((systems, width), F32)
        for c in range(cap):
            at = b * group + c * systems
            traced = traced + total[at : at + systems]
        old = jnp.concatenate(
            [old_ref[r, 0, :, b * width : (b + 1) * width] * rec_ref[0:1, r : r + 1] for r in range(systems)], axis=0
        )
        live = iota((systems, width), 1) + b * width < meta_ref[3, 0]
        bar = jnp.where(live, traced - old, 0.0)
        for r in range(systems):
            bar_ref[r, 0, :, b * width : (b + 1) * width] = bar[r : r + 1]
        lows[b] = jnp.concatenate([bar, jnp.zeros((16 - systems, width), F32)], axis=0).astype(BF16)
    for t in range(tiles):
        slot = meta_ref[0, t] * cap + meta_ref[1, t]
        term = jnp.dot(lows[meta_ref[2, t]], tiles_ref[0, 0, t], preferred_element_type=F32)
        term_ref[slot] = term[:systems]


PARTS = 6


def shifted(x, axis, step):
    count = lax.axis_size(axis)
    if step > 0:
        pairs = [(i, i + 1) for i in range(count - 1)]
    else:
        pairs = [(i + 1, i) for i in range(count - 1)]
    return lax.ppermute(x, axis, pairs)


def exchange(x):
    return lax.all_to_all(x, AXES, split_axis=0, concat_axis=0, tiled=True)


def per_device(
    sensitivity,
    block_ids,
    block_offsets,
    ray_counts,
    ray_vector,
    damping_vector,
    model_vector,
    solution,
    search,
    recurrence,
):
    lat_size, lon_size = lax.axis_size("lat"), lax.axis_size("lon")
    devices = lat_size * lon_size
    tiles, width, depth = sensitivity.shape[2:]
    blocks = block_offsets.shape[-1] - 1
    systems, clat, clon, _ = model_vector.shape
    columns = clat * clon
    cap = max(2 * ((tiles + devices - 1) // devices), 16 // systems)
    slots = devices * cap
    group = cap * systems
    cells_all = devices * columns * depth
    rows_all = devices * blocks * width + cells_all
    lanes = 128
    full, flat = model_vector.shape, (systems, columns, depth)
    patch = (systems, PATCH * clon, depth)
    here, there, plain = pltpu.VMEM, pltpu.HBM, jax.ShapeDtypeStruct
    dma = pltpu.SemaphoreType.DMA
    model, damping = far(model_vector), far(damping_vector)
    model_flat, damping_flat = far(model_vector.reshape(flat)), far(damping_vector.reshape(flat))

    lists = exchange(jnp.broadcast_to(block_ids[0], (devices, 1, tiles))).reshape(devices, tiles)

    served, wanted, corner = call(
        functools.partial(serve_body, cap, clat, clon),
        "serve",
        (there((slots * systems, depth), BF16), plain((devices, lanes), F32), plain((1,), I32)),
        [vmem(), hbm()],
        (vmem(), vmem(), smem()),
        scratch=[pltpu.VMEM(patch, F32), pltpu.VMEM((slots * systems, depth), F32), dma((systems,))],
    )(lists, model_flat)
    fetched = exchange(served.reshape(devices, group, depth)).reshape(slots * systems, depth)

    band = there((systems, 3, clon, depth), F32)
    north_msg, south_msg = call(
        pack_body,
        "pack",
        (band, band),
        [smem(), hbm(), hbm()],
        (hbm(), hbm()),
        scratch=[dma((4,))],
        moved=24 * systems * clon * depth,
    )(corner, model, damping)
    north = shifted(south_msg, "lat", 1)
    south = shifted(north_msg, "lat", -1)

    side = (systems, 3 * clat + 8, depth)
    east_part, west_part, meta = call(
        functools.partial(flanks_body, columns.bit_length() - 1, blocks),
        "flanks",
        (plain(side, F32), plain(side, F32), plain((8, lanes), I32)),
        [smem()] + [vmem()] * 3 + [hbm(), hbm()],
        (vmem(),) * 3,
        scratch=[pltpu.VMEM((4, systems, clat, 8, depth), F32), dma((4,))],
        moved=128 * systems * clat * depth,
    )(corner, far(block_ids), block_offsets, ray_counts, model, damping)
    east_msg, west_msg = call(
        corners_body,
        "corners",
        (there(side, F32), there(side, F32)),
        [vmem()] * 4,
        (vmem(), vmem()),
    )(east_part, west_part, far(north), far(south))
    west = shifted(east_msg, "lon", 1)
    east = shifted(west_msg, "lon", -1)

    ray_bar, terms = call(
        functools.partial(rays_body, cap, blocks),
        "rays",
        (plain(ray_vector.shape, F32), there((slots, systems, depth), F32)),
        [smem(), vmem(), hbm(), vmem(), vmem(), hbm()],
        (vmem(), vmem()),
        scratch=[
            pltpu.VMEM(sensitivity.shape, BF16),
            pltpu.VMEM((cap + 1, group, depth), BF16),
            pltpu.VMEM((blocks + 1, 16, width), BF16),
            dma((PARTS,)),
        ],
        flops=4 * tiles * width * depth * 16,
        moved=2 * tiles * width * depth,
    )(meta, far(recurrence), far(sensitivity), fetched, far(ray_vector), far(east_msg))
    arrived = exchange(terms.reshape(devices, group, depth)).reshape(slots * systems, depth)

    bar, image, sums, patched, model_patch, chosen = call(
        functools.partial(dense_body, cap, clat, clon),
        "dense",
        (there(flat, F32),) * 2
        + (plain((1, lanes), F32), plain(patch, F32), plain(patch, F32), plain((PATCH * clon, slots), BF16)),
        [vmem(), smem()] + [vmem()] * 2 + [hbm()] * 2 + [vmem()] * 4,
        (hbm(),) * 2 + (vmem(),) * 4,
        scratch=[pltpu.VMEM(flat, F32)] * 4
        + [
            pltpu.VMEM((clon, depth), F32),
            pltpu.VMEM((clon, depth), F32),
            pltpu.VMEM((clat, depth), F32),
            pltpu.VMEM((clat, depth), F32),
            pltpu.SMEM((systems,), F32),
            dma((systems, 4)),
        ],
        flops=40 * systems * columns * depth,
        moved=16 * systems * columns * depth,
    )(
        far(recurrence),
        corner,
        wanted,
        ray_bar,
        model_flat,
        damping_flat,
        far(north),
        far(south),
        far(west),
        far(east),
    )

    added, parts = call(
        combine_body,
        "combine",
        (plain(patch, F32), there((devices, lanes), F32)),
        [vmem()] * 5,
        (vmem(),) * 2,
    )(arrived, chosen, patched, model_patch, sums)
    every = exchange(parts.reshape(devices, 1, lanes)).reshape(devices, lanes)

    outs = call(
        functools.partial(finish_body, float(rows_all), float(cells_all), clon),
        "finish",
        (there(ray_vector.shape, F32),) + (there(flat, F32),) * 4 + (there(recurrence.shape, F32),),
        [smem()] + [vmem()] * 4 + [hbm()] * 5,
        (vmem(),) + (hbm(),) * 4 + (vmem(),),
        scratch=[pltpu.VMEM(flat, F32)] * 9
        + [
            pltpu.SMEM((5, systems), F32),
            dma((systems, PIECES, 4)),
            dma((systems, PIECES, 5)),
        ],
        mib=32,
        flops=10 * systems * columns * depth,
        moved=36 * systems * columns * depth,
    )(
        corner,
        every,
        far(recurrence),
        ray_bar,
        added,
        far(image),
        model_flat,
        far(bar),
        far(solution.reshape(flat)),
        far(search.reshape(flat)),
    )
    ray_out, damp_out, model_out, solution_out, search_out, rec_out = outs
    fields = (x.reshape(full) for x in (damp_out, model_out, solution_out, search_out))
    return (ray_out, *fields, rec_out)


def solution(mesh):
    fields = P(None, "lat", "lon", None)
    return jax.shard_map(
        per_device,
        mesh=mesh,
        in_specs=(
            P("lat", "lon", None, None, None),
            P("lat", "lon", None),
            P("lat", "lon", None),
            P("lat", "lon"),
            fields,
            fields,
            fields,
            fields,
            fields,
            P(),
        ),
        out_specs=(fields, fields, fields, fields, fields, P()),
        check_vma=False,
    )
```

```python
import functools

import jax
import jax.numpy as jnp
from jax import lax
from jax.experimental import pallas as pl
from jax.experimental.pallas import tpu as pltpu
from jax.sharding import PartitionSpec as P

DAMP_WEIGHT = 0.15
EPSILON = 1e-05
AXES = ("lat", "lon")
PATCH = 4
F32, BF16, I32 = jnp.float32, jnp.bfloat16, jnp.int32


def iota(shape, dim):
    return lax.broadcasted_iota(I32, shape, dim)


def vmem():
    return pl.BlockSpec(memory_space=pltpu.VMEM)


def hbm():
    return pl.BlockSpec(memory_space=pltpu.HBM)


def near(x):
    return pltpu.with_memory_space_constraint(x, pltpu.VMEM)


def far(x):
    return pltpu.with_memory_space_constraint(x, pltpu.HBM)


def smem():
    return pl.BlockSpec(memory_space=pltpu.SMEM)


def call(body, name, out_shape, in_specs, out_specs, scratch=(), grid=(), mib=16, flops=0, moved=0):
    return pl.pallas_call(
        body,
        name=name,
        grid=grid,
        out_shape=out_shape,
        in_specs=in_specs,
        out_specs=out_specs,
        scratch_shapes=list(scratch),
        compiler_params=pltpu.CompilerParams(vmem_limit_bytes=mib * 2**20),
        cost_estimate=pl.CostEstimate(flops=flops, bytes_accessed=moved, transcendentals=0),
    )


STEP = 8


def ask_body(ids_ref, model_in, out_ref, slabs, sems):
    systems, clat, clon, depth = model_in.shape
    copies = []
    for k in range(4):
        at = (slice(None), pl.ds((k // 2) * (clat - 1), 1), pl.ds((k % 2) * (clon - 8), 8))
        copies.append(pltpu.make_async_copy(model_in.at[at], slabs.at[k], sems.at[k]))
    for copy in copies:
        copy.start()
    tiles = ids_ref.shape[-1]
    ids = jnp.concatenate([ids_ref[0].astype(F32), jnp.full((1, depth - tiles), -1.0, F32)], axis=1)
    for copy in copies:
        copy.wait()
    corners = [
        [slabs[k, r, 0, (k % 2) * 7 : (k % 2) * 7 + 1] for r in range(systems)] for k in range(4)
    ]
    lat_at, lon_at = lax.axis_index("lat"), lax.axis_index("lon")
    width = lax.axis_size("lon")
    for e in range(out_ref.shape[0]):
        out_ref[e, :, 0:depth] = ids
        south, east = e // width > lat_at, e % width > lon_at
        for r in range(systems):
            upper = jnp.where(east, corners[1][r], corners[0][r])
            lower = jnp.where(east, corners[3][r], corners[2][r])
            out_ref[e, :, (r + 1) * depth : (r + 2) * depth] = jnp.where(south, lower, upper)


def wanted_column(wanted, cap):
    devices, lanes = wanted.shape
    rows = devices * cap
    spread = jnp.broadcast_to(wanted[:, None, :], (devices, cap, lanes)).reshape(rows, lanes)
    pick = iota((rows, lanes), 1) == (iota((rows, lanes), 0) & (cap - 1))
    return jnp.sum(jnp.where(pick, spread, 0.0), axis=1, keepdims=True)


def serve_body(cap, clat, clon, lists_ref, model_in, served_ref, wanted_ref, corner_ref, diagonal_ref, patch, mixed, sems):
    systems, width, depth = patch.shape
    devices = lists_ref.shape[0]
    lanes = 128
    shift = (clat * clon).bit_length() - 1
    me = lax.axis_index("lat") * lax.axis_size("lon") + lax.axis_index("lon")
    ids = lists_ref[:, 0, 0:lanes].astype(I32)
    column = ids - lax.shift_left(me, shift)
    mine = (column >= 0) & (column < clat * clon) & (ids >= 0)
    first = jnp.min(jnp.where(mine, column, clat * clon))
    corner = jnp.minimum(lax.shift_right_logical(first, clon.bit_length() - 1), clat - PATCH)
    corner_ref[0] = corner
    at = pl.ds(pl.multiple_of(corner * clon, clon), width)
    copies = [pltpu.make_async_copy(model_in.at[r, at], patch.at[r], sems.at[r]) for r in range(systems)]
    for copy in copies:
        copy.start()
    ahead = (iota((lanes, lanes), 0) < iota((lanes, lanes), 1)).astype(F32).astype(BF16)
    rank = jnp.dot(mine.astype(F32).astype(BF16), ahead, preferred_element_type=F32)
    value = (column - corner * clon + 1).astype(F32)
    at = iota((devices, lanes), 1)
    wanted = jnp.zeros((devices, lanes), F32)
    for c in range(cap):
        picked = jnp.sum(jnp.where(mine & (rank == c), value, 0.0), axis=1, keepdims=True)
        wanted = jnp.where(at == c, picked, wanted)
    wanted_ref[...] = wanted
    target = wanted_column(wanted, cap).astype(I32) - 1
    rows = target.shape[0]
    chosen = (jnp.broadcast_to(target, (rows, width)) == iota((rows, width), 1)).astype(F32).astype(BF16)
    for r in range(systems):
        copies[r].wait()
        table = patch[r].astype(BF16)
        mixed[pl.ds(r, rows, stride=systems), :] = jnp.dot(chosen, table, preferred_element_type=F32)
    served_ref[...] = mixed[...].astype(BF16)
    lat_at, lon_at = lax.axis_index("lat"), lax.axis_index("lon")
    lat_size, lon_size = lax.axis_size("lat"), lax.axis_size("lon")
    for k in range(4):
        lat_to, lon_to = lat_at + 2 * (k // 2) - 1, lon_at + 2 * (k % 2) - 1
        inside = (lat_to >= 0) & (lat_to < lat_size) & (lon_to >= 0) & (lon_to < lon_size)
        source = jnp.where(inside, lat_to * lon_size + lon_to, 0)
        flag = inside.astype(F32)
        for r in range(systems):
            got = lists_ref[source, :, (r + 1) * depth : (r + 2) * depth]
            diagonal_ref[k * systems + r : k * systems + r + 1, :] = got * flag


def flanks_body(
    shift,
    blocks,
    after_ref,
    ids_ref,
    off_ref,
    count_ref,
    model_in,
    damp_in,
    north_ref,
    south_ref,
    east_ref,
    west_ref,
    meta_ref,
    slabs,
    sems,
):
    systems, clat, clon, depth = model_in.shape
    copies = []
    for k, (ref, at) in enumerate(((model_in, 0), (model_in, clon - 8), (damp_in, 0), (damp_in, clon - 8))):
        copies.append(pltpu.make_async_copy(ref.at[:, :, pl.ds(at, 8)], slabs.at[k], sems.at[k]))
    last = clat - 1
    pairs = (
        (model_in.at[:, pl.ds(last - 1, 2)], south_ref.at[:, pl.ds(0, 2)]),
        (damp_in.at[:, pl.ds(last, 1)], south_ref.at[:, pl.ds(2, 1)]),
        (model_in.at[:, pl.ds(0, 2)], north_ref.at[:, pl.ds(0, 2)]),
        (damp_in.at[:, pl.ds(0, 1)], north_ref.at[:, pl.ds(2, 1)]),
    )
    copies += [pltpu.make_async_copy(a, b, sems.at[i + 4]) for i, (a, b) in enumerate(pairs)]
    for copy in copies:
        copy.start()
    tiles = ids_ref.shape[-1]
    lanes = 128
    ids = jnp.concatenate([ids_ref[0], jnp.full((1, lanes - tiles), -1, I32)], axis=1)
    owner = lax.shift_right_arithmetic(ids, shift)
    square = (lanes, lanes)
    down, across = iota(square, 0), iota(square, 1)
    owner_f = jnp.broadcast_to(owner.astype(F32), square)
    owner_col = jnp.sum(jnp.where(down == across, owner_f, 0.0), axis=1, keepdims=True)
    same = jnp.where((owner_f == owner_col) & (down < across), 1.0, 0.0)
    rank = jnp.sum(same, axis=0, keepdims=True).astype(I32)
    lane = iota((1, lanes), 1)
    block = jnp.zeros((1, lanes), I32)
    starts = off_ref[0]
    for b in range(1, blocks + 1):
        block = block + (lane >= jnp.broadcast_to(starts[:, b : b + 1], (1, lanes))).astype(I32)
    count = jnp.broadcast_to(count_ref[...], (1, lanes))
    meta_ref[...] = jnp.concatenate([owner, rank, block, count] + [owner] * 4, axis=0)
    for copy in copies:
        copy.wait()
    rows = slabs.reshape(4, systems, clat * 8, depth)
    for r in range(systems):
        for out, slab, near_at, beyond in ((east_ref, 1, 7, 6), (west_ref, 0, 0, 1)):
            out[r, 0:clat] = rows[slab, r, pl.ds(near_at, clat, stride=8), :]
            out[r, clat : 2 * clat] = rows[slab, r, pl.ds(beyond, clat, stride=8), :]
            out[r, 2 * clat : 3 * clat] = rows[slab + 2, r, pl.ds(near_at, clat, stride=8), :]


def six(x, north, south, west, east):
    lane = iota(x.shape, 1)
    rows, depth = x.shape
    left, right = pltpu.roll(x, 1, 0), pltpu.roll(x, rows - 1, 0)
    ends = (8, depth)
    row = iota(ends, 0)
    left = jnp.concatenate([jnp.where(row == 0, jnp.broadcast_to(west, ends), left[:8]), left[8:]], axis=0)
    right = jnp.concatenate([right[:-8], jnp.where(row == 7, jnp.broadcast_to(east, ends), right[-8:])], axis=0)
    above = jnp.where(lane == 0, 0.0, pltpu.roll(x, 1, 1))
    below = jnp.where(lane == depth - 1, 0.0, pltpu.roll(x, depth - 1, 1))
    beside = north + south + left + right + above + below
    return DAMP_WEIGHT * (6.0 * x - beside)


def fold(x):
    parts = [x[i * 8 : (i + 1) * 8] for i in range(x.shape[0] // 8)]
    return functools.reduce(lambda a, b: a + b, parts)


def place(row, lane, value):
    return row + jnp.where(iota(row.shape, 1) == lane, jnp.broadcast_to(value, row.shape), 0.0)


def dense_body(
    cap,
    clat,
    clon,
    rec_ref,
    corner_ref,
    wanted_ref,
    diagonal_ref,
    ray_ref,
    model_in,
    damp_in,
    north_ref,
    south_ref,
    west_ref,
    east_ref,
    bar_sent,
    image_sent,
    sums_out,
    patch_out,
    model_patch_out,
    chosen_out,
    model_ref,
    damp_ref,
    bar_out,
    image_out,
    north_s,
    south_s,
    west_s,
    east_s,
    alphas,
    sems,
):
    systems, _, depth = model_ref.shape

    def incoming(r):
        return (
            pltpu.make_async_copy(model_in.at[r], model_ref.at[r], sems.at[r, 0]),
            pltpu.make_async_copy(damp_in.at[r], damp_ref.at[r], sems.at[r, 1]),
        )

    def outgoing(r):
        return (
            pltpu.make_async_copy(bar_out.at[r], bar_sent.at[r], sems.at[r, 2]),
            pltpu.make_async_copy(image_out.at[r], image_sent.at[r], sems.at[r, 3]),
        )

    for r in range(systems):
        for copy in incoming(r):
            copy.start()
    for r in range(systems):
        alphas[r] = jnp.sum(rec_ref[0:1, r : r + 1])
    lat_at, lon_at = lax.axis_index("lat"), lax.axis_index("lon")
    has_north = (lat_at > 0).astype(F32)
    has_south = (lat_at < lax.axis_size("lat") - 1).astype(F32)
    has_west = (lon_at > 0).astype(F32)
    has_east = (lon_at < lax.axis_size("lon") - 1).astype(F32)

    def diagonal(k, r):
        return diagonal_ref[pl.ds(k * alphas.shape[0] + r, 1), :]

    target = wanted_column(wanted_ref[...], cap) - 1.0
    slots = target.shape[0]
    square = (slots, slots)
    flat = jnp.sum(
        jnp.where(iota(square, 0) == iota(square, 1), jnp.broadcast_to(target, square), 0.0),
        axis=0,
        keepdims=True,
    ).astype(I32)
    wide = (PATCH * clon, slots)
    chosen_out[...] = (jnp.broadcast_to(flat, wide) == iota(wide, 0)).astype(F32).astype(BF16)

    def line(ref, r, i):
        return ref[r, pl.ds(pl.multiple_of(i * clon, clon), clon), :]

    def stencils(ref, r, k, first, last, west, east):
        base = k * STEP
        for j in range(STEP):
            i = base + j
            x = line(ref, r, i)
            if j == 0:
                above = jnp.where(k > 0, line(ref, r, jnp.maximum(i - 1, 0)), first)
            else:
                above = line(ref, r, i - 1)
            if j == STEP - 1:
                below = jnp.where(i + 1 < clat, line(ref, r, jnp.minimum(i + 1, clat - 1)), last)
            else:
                below = line(ref, r, i + 1)
            yield i, x, six(x, above, below, west[pl.ds(i, 1)], east[pl.ds(i, 1)])

    def system(r, row):
        alpha = alphas[r]
        for copy in incoming(r):
            copy.wait()

        def side(ref, own, flag, east):
            x, beyond, old = ref[r, 0:clat], ref[r, clat : 2 * clat], ref[r, 2 * clat : 3 * clat]
            upper, lower = diagonal(east, r), diagonal(2 + east, r)
            return (six(x, beyond, own, upper, lower) - alpha * old) * flag

        west_s[...] = side(west_ref, model_ref[r, pl.ds(0, clat, stride=clon), :], has_west, 0)
        east_s[...] = side(east_ref, model_ref[r, pl.ds(clon - 1, clat, stride=clon), :], has_east, 1)
        north_s[...] = has_north * (
            six(
                north_ref[r, 1],
                north_ref[r, 0],
                line(model_ref, r, 0),
                diagonal(0, r),
                diagonal(1, r),
            )
            - alpha * north_ref[r, 2]
        )
        south_s[...] = has_south * (
            six(
                south_ref[r, 0],
                line(model_ref, r, clat - 1),
                south_ref[r, 1],
                diagonal(2, r),
                diagonal(3, r),
            )
            - alpha * south_ref[r, 2]
        )

        def damped(k, acc):
            bar_sq, model_sq = acc
            ends = (north_ref[r, 1], south_ref[r, 0], west_ref.at[r], east_ref.at[r])
            for i, x, got in stencils(model_ref, r, k, *ends):
                bar = got - alpha * line(damp_ref, r, i)
                bar_out[r, pl.ds(pl.multiple_of(i * clon, clon), clon), :] = bar
                bar_sq, model_sq = bar_sq + fold(bar * bar), model_sq + fold(x * x)
            return bar_sq, model_sq

        def imaged(k, acc):
            image_sq, cross = acc
            for i, x, image in stencils(bar_out, r, k, north_s[...], south_s[...], west_s, east_s):
                image_out[r, pl.ds(pl.multiple_of(i * clon, clon), clon), :] = image
                image_sq, cross = image_sq + fold(image * image), cross + fold(image * line(model_ref, r, i))
            return image_sq, cross

        zero = jnp.zeros((8, depth), F32)
        bar_sq, model_sq = lax.fori_loop(0, clat // STEP, damped, (zero, zero))
        image_sq, cross = lax.fori_loop(0, clat // STEP, imaged, (zero, zero))
        for copy in outgoing(r):
            copy.start()
        here = pl.ds(pl.multiple_of(corner_ref[0] * clon, clon), PATCH * clon)
        patch_out[r] = image_out[r, here, :]
        model_patch_out[r] = model_ref[r, here, :]
        ray = ray_ref[r, 0]
        residual = jnp.sum(bar_sq, keepdims=True) + jnp.sum(ray * ray, keepdims=True)
        row = place(row, r, residual)
        row = place(row, systems + r, jnp.sum(image_sq, keepdims=True))
        row = place(row, 2 * systems + r, jnp.sum(cross, keepdims=True))
        return place(row, 3 * systems + r, jnp.sum(model_sq, keepdims=True))

    sums_out[...] = lax.fori_loop(0, systems, system, jnp.zeros((1, depth), F32))
    for r in range(systems):
        for copy in outgoing(r):
            copy.wait()


def combine_body(terms_ref, chosen_ref, patch_ref, model_patch_ref, sums_ref, added_ref, parts_ref):
    systems, _, depth = added_ref.shape
    slots = chosen_ref.shape[1]
    chosen = chosen_ref[...]
    row = sums_ref[...]
    for r in range(systems):
        x = terms_ref[pl.ds(r, slots, stride=systems), :]
        high = x.astype(BF16)
        rest = x - high.astype(F32)
        middle = rest.astype(BF16)
        low = (rest - middle.astype(F32)).astype(BF16)
        three = jnp.dot(chosen, jnp.concatenate([high, middle, low], axis=1), preferred_element_type=F32)
        added = three[:, 0:depth] + (three[:, depth : 2 * depth] + three[:, 2 * depth :])
        added_ref[r] = added
        square = jnp.sum(added * (2.0 * patch_ref[r] + added), keepdims=True)
        cross = jnp.sum(added * model_patch_ref[r], keepdims=True)
        row = place(row, systems + r, square)
        row = place(row, 2 * systems + r, cross)
    parts_ref[...] = jnp.broadcast_to(row, parts_ref.shape)


def finish_body(
    rows_all,
    cells_all,
    clon,
    corner_ref,
    parts_ref,
    rec_ref,
    ray_ref,
    added_ref,
    image_in,
    model_in,
    bar_in,
    solution_in,
    search_in,
    ray_out,
    damp_out,
    model_out,
    solution_out,
    search_out,
    rec_out,
    image_ref,
    model_ref,
    bar_ref,
    solution_ref,
    search_ref,
    damp_s,
    model_s,
    solution_s,
    search_s,
    coef,
    sems,
    in_sems,
):
    systems, columns, depth = image_ref.shape
    rows = columns // PIECES

    def incoming(r, p):
        at = pl.ds(pl.multiple_of(p * rows, rows), rows)
        pairs = (
            (search_in, search_ref),
            (bar_in, bar_ref),
            (image_in, image_ref),
            (model_in, model_ref),
            (solution_in, solution_ref),
        )
        return [
            pltpu.make_async_copy(a.at[r, at], b.at[r, at], in_sems.at[r, p, k]) for k, (a, b) in enumerate(pairs)
        ]

    def begin_piece(n, _):
        for copy in incoming(n // PIECES, n % PIECES):
            copy.start()
        return 0

    lax.fori_loop(0, systems * PIECES, begin_piece, 0)
    total = jnp.sum(parts_ref[...], axis=0, keepdims=True)
    residual_sq, image_sq, cross, model_sq = (total[:, q * systems : (q + 1) * systems] for q in range(4))
    rho_bar, phi_bar = rec_ref[1:2], rec_ref[2:3]
    beta = jnp.sqrt(residual_sq / rows_all + EPSILON)
    update_sq = image_sq / (beta * beta) - 2.0 * cross + beta * beta * model_sq
    alpha = jnp.sqrt(jnp.maximum(update_sq, 0.0) / cells_all + EPSILON)
    rho = jnp.sqrt(rho_bar * rho_bar + beta * beta)
    cosine = rho_bar / rho
    sine = beta / rho
    rec_out[...] = jnp.concatenate([alpha, -cosine * alpha, sine * phi_bar], axis=0)
    scales = (
        1.0 / beta,
        1.0 / (beta * alpha),
        beta / alpha,
        cosine * phi_bar / rho,
        sine * alpha / rho,
    )
    for q, scale in enumerate(scales):
        for s in range(systems):
            coef[q, s] = scale[0, s]
    def outgoing(r, p):
        at = pl.ds(pl.multiple_of(p * rows, rows), rows)
        pairs = (
            (damp_s, damp_out),
            (model_s, model_out),
            (solution_s, solution_out),
            (search_s, search_out),
        )
        return [
            pltpu.make_async_copy(a.at[r, at], b.at[r, at], sems.at[r, p, k]) for k, (a, b) in enumerate(pairs)
        ]

    def piece(n, _):
        r, p = n // PIECES, n % PIECES
        at = pl.ds(pl.multiple_of(p * rows, rows), rows)
        for copy in incoming(r, p):
            copy.wait()
        search = search_ref[r, at, :]
        damp_s[r, at, :] = bar_ref[r, at, :] * coef[0, r]
        new = image_ref[r, at, :] * coef[1, r] - model_ref[r, at, :] * coef[2, r]
        model_s[r, at, :] = new
        solution_s[r, at, :] = solution_ref[r, at, :] + search * coef[3, r]
        search_s[r, at, :] = new - search * coef[4, r]
        for k in range(PATCH):
            begin = (corner_ref[0] + k) * clon

            @pl.when((begin >= p * rows) & (begin < (p + 1) * rows))
            def _():
                line = pl.ds(pl.multiple_of(begin, clon), clon)
                more = added_ref[r, k * clon : (k + 1) * clon, :] * coef[1, r]
                model_s[r, line, :] = model_s[r, line, :] + more
                search_s[r, line, :] = search_s[r, line, :] + more

        for copy in outgoing(r, p):
            copy.start()
        return 0

    lax.fori_loop(0, systems * PIECES, piece, 0)
    for r in range(systems):
        ray_out[r] = ray_ref[r] * coef[0, r]

    def settle(n, _):
        for copy in outgoing(n // PIECES, n % PIECES):
            copy.wait()
        return 0

    lax.fori_loop(0, systems * PIECES, settle, 0)


PIECES = 2


def rays_body(
    cap, blocks, meta_ref, rec_ref, tiles_in, fetched_ref, old_ref, north, south, west, east, bar_ref, term_ref, tiles_ref, masks, lows, sems
):
    tiles, width, depth = tiles_in.shape[2:]
    part = -(-tiles // PARTS)
    copies = []
    for k in range(PARTS):
        at = (0, 0, pl.ds(k * part, min(part, tiles - k * part)))
        copies.append(pltpu.make_async_copy(tiles_in.at[at], tiles_ref.at[at], sems.at[k]))
    for copy in copies:
        copy.start()
    systems = old_ref.shape[0]
    group = cap * systems
    for c in range(cap + 1):
        here = lax.shift_right_logical(iota((group, depth), 0), systems.bit_length() - 1) == c
        masks[c] = here.astype(F32).astype(BF16)
    term_ref[...] = jnp.zeros(term_ref.shape, F32)
    lows[...] = jnp.zeros(lows.shape, BF16)
    total = jnp.zeros((blocks * group, width), F32)
    for t in range(tiles):
        if t % part == 0:
            copies[t // part].wait()
        owner, rank, block = meta_ref[0, t], meta_ref[1, t], meta_ref[2, t]
        rows = fetched_ref[pl.ds(pl.multiple_of(owner * group, group), group), :]
        left = jnp.concatenate(
            [rows * masks[jnp.where(block == b, rank, cap)] for b in range(blocks)], axis=0
        )
        total = total + lax.dot_general(
            left, tiles_ref[0, 0, t], (((1,), (1,)), ((), ())), preferred_element_type=F32
        )
    for b in range(blocks):
        traced = jnp.zeros((systems, width), F32)
        for c in range(cap):
            at = b * group + c * systems
            traced = traced + total[at : at + systems]
        old = jnp.concatenate(
            [old_ref[r, 0, :, b * width : (b + 1) * width] * rec_ref[0:1, r : r + 1] for r in range(systems)], axis=0
        )
        live = iota((systems, width), 1) + b * width < meta_ref[3, 0]
        bar = jnp.where(live, traced - old, 0.0)
        for r in range(systems):
            bar_ref[r, 0, :, b * width : (b + 1) * width] = bar[r : r + 1]
        lows[b] = jnp.concatenate([bar, jnp.zeros((16 - systems, width), F32)], axis=0).astype(BF16)
    for t in range(tiles):
        slot = meta_ref[0, t] * cap + meta_ref[1, t]
        term = jnp.dot(lows[meta_ref[2, t]], tiles_ref[0, 0, t], preferred_element_type=F32)
        term_ref[slot] = term[:systems]


PARTS = 6


def shifted(x, axis, step):
    count = lax.axis_size(axis)
    if step > 0:
        pairs = [(i, i + 1) for i in range(count - 1)]
    else:
        pairs = [(i + 1, i) for i in range(count - 1)]
    return lax.ppermute(x, axis, pairs)


def exchange(x):
    return lax.all_to_all(x, AXES, split_axis=0, concat_axis=0, tiled=True)


def per_device(
    sensitivity,
    block_ids,
    block_offsets,
    ray_counts,
    ray_vector,
    damping_vector,
    model_vector,
    solution,
    search,
    recurrence,
):
    lat_size, lon_size = lax.axis_size("lat"), lax.axis_size("lon")
    devices = lat_size * lon_size
    tiles, width, depth = sensitivity.shape[2:]
    blocks = block_offsets.shape[-1] - 1
    systems, clat, clon, _ = model_vector.shape
    columns = clat * clon
    cap = max(2 * ((tiles + devices - 1) // devices), 16 // systems)
    slots = devices * cap
    group = cap * systems
    cells_all = devices * columns * depth
    rows_all = devices * blocks * width + cells_all
    lanes = 128
    full, flat = model_vector.shape, (systems, columns, depth)
    patch = (systems, PATCH * clon, depth)
    here, there, plain = pltpu.VMEM, pltpu.HBM, jax.ShapeDtypeStruct
    dma = pltpu.SemaphoreType.DMA
    model, damping = far(model_vector), far(damping_vector)
    model_flat, damping_flat = far(model_vector.reshape(flat)), far(damping_vector.reshape(flat))

    asked = (devices, 1, (1 + systems) * depth)
    asking = call(
        ask_body,
        "ask",
        there(asked, F32),
        [vmem(), hbm()],
        vmem(),
        scratch=[pltpu.VMEM((4, systems, 1, 8, depth), F32), dma((4,))],
    )(far(block_ids), model)
    lists = exchange(asking)

    served, wanted, corner, diagonal = call(
        functools.partial(serve_body, cap, clat, clon),
        "serve",
        (
            there((slots * systems, depth), BF16),
            plain((devices, lanes), F32),
            plain((1,), I32),
            plain((4 * systems, depth), F32),
        ),
        [vmem(), hbm()],
        (vmem(), vmem(), smem(), vmem()),
        scratch=[pltpu.VMEM(patch, F32), pltpu.VMEM((slots * systems, depth), F32), dma((systems,))],
    )(lists, model_flat)
    fetched = exchange(served.reshape(devices, group, depth)).reshape(slots * systems, depth)

    side = there((systems, 3 * clat, depth), F32)
    band = there((systems, 3, clon, depth), F32)
    north_msg, south_msg, east_msg, west_msg, meta = call(
        functools.partial(flanks_body, columns.bit_length() - 1, blocks),
        "flanks",
        (band, band, side, side, plain((8, lanes), I32)),
        [smem()] + [vmem()] * 3 + [hbm(), hbm()],
        (vmem(),) * 5,
        scratch=[pltpu.VMEM((4, systems, clat, 8, depth), F32), dma((8,))],
        flops=1,
        moved=128 * systems * clat * depth,
    )(corner, far(block_ids), block_offsets, ray_counts, model, damping)

    north = shifted(south_msg, "lat", 1)
    south = shifted(north_msg, "lat", -1)
    west = shifted(east_msg, "lon", 1)
    east = shifted(west_msg, "lon", -1)

    ray_bar, terms = call(
        functools.partial(rays_body, cap, blocks),
        "rays",
        (plain(ray_vector.shape, F32), there((slots, systems, depth), F32)),
        [smem(), vmem(), hbm(), vmem(), vmem()] + [pl.BlockSpec(memory_space=pl.ANY)] * 4,
        (vmem(), vmem()),
        scratch=[
            pltpu.VMEM(sensitivity.shape, BF16),
            pltpu.VMEM((cap + 1, group, depth), BF16),
            pltpu.VMEM((blocks + 1, 16, width), BF16),
            dma((PARTS,)),
        ],
        flops=4 * tiles * width * depth * 16,
        moved=2 * tiles * width * depth,
    )(meta, far(recurrence), far(sensitivity), fetched, far(ray_vector), north, south, west, east)
    arrived = exchange(terms.reshape(devices, group, depth)).reshape(slots * systems, depth)

    bar, image, sums, patched, model_patch, chosen = call(
        functools.partial(dense_body, cap, clat, clon),
        "dense",
        (there(flat, F32),) * 2
        + (plain((1, lanes), F32), plain(patch, F32), plain(patch, F32), plain((PATCH * clon, slots), BF16)),
        [vmem(), smem()] + [vmem()] * 3 + [hbm()] * 2 + [vmem()] * 4,
        (hbm(),) * 2 + (vmem(),) * 4,
        scratch=[pltpu.VMEM(flat, F32)] * 4
        + [
            pltpu.VMEM((clon, depth), F32),
            pltpu.VMEM((clon, depth), F32),
            pltpu.VMEM((clat, depth), F32),
            pltpu.VMEM((clat, depth), F32),
            pltpu.SMEM((systems,), F32),
            dma((systems, 4)),
        ],
        flops=40 * systems * columns * depth,
        moved=16 * systems * columns * depth,
    )(
        far(recurrence),
        corner,
        wanted,
        diagonal,
        ray_bar,
        model_flat,
        damping_flat,
        north,
        south,
        west,
        east,
    )

    added, parts = call(
        combine_body,
        "combine",
        (plain(patch, F32), there((devices, lanes), F32)),
        [vmem()] * 5,
        (vmem(),) * 2,
    )(arrived, chosen, patched, model_patch, sums)
    every = exchange(parts.reshape(devices, 1, lanes)).reshape(devices, lanes)

    outs = call(
        functools.partial(finish_body, float(rows_all), float(cells_all), clon),
        "finish",
        (there(ray_vector.shape, F32),) + (there(flat, F32),) * 4 + (there(recurrence.shape, F32),),
        [smem()] + [vmem()] * 4 + [hbm()] * 5,
        (vmem(),) + (hbm(),) * 4 + (vmem(),),
        scratch=[pltpu.VMEM(flat, F32)] * 9
        + [
            pltpu.SMEM((5, systems), F32),
            dma((systems, PIECES, 4)),
            dma((systems, PIECES, 5)),
        ],
        mib=32,
        flops=10 * systems * columns * depth,
        moved=36 * systems * columns * depth,
    )(
        corner,
        every,
        far(recurrence),
        ray_bar,
        added,
        far(image),
        model_flat,
        far(bar),
        far(solution.reshape(flat)),
        far(search.reshape(flat)),
    )
    ray_out, damp_out, model_out, solution_out, search_out, rec_out = outs
    fields = (x.reshape(full) for x in (damp_out, model_out, solution_out, search_out))
    return (ray_out, *fields, rec_out)


def solution(mesh):
    fields = P(None, "lat", "lon", None)
    return jax.shard_map(
        per_device,
        mesh=mesh,
        in_specs=(
            P("lat", "lon", None, None, None),
            P("lat", "lon", None),
            P("lat", "lon", None),
            P("lat", "lon"),
            fields,
            fields,
            fields,
            fields,
            fields,
            P(),
        ),
        out_specs=(fields, fields, fields, fields, fields, P()),
        check_vma=False,
    )
```

```python
import functools

import jax
import jax.numpy as jnp
from jax import lax
from jax.experimental import pallas as pl
from jax.experimental.pallas import tpu as pltpu
from jax.sharding import PartitionSpec as P

DAMP_WEIGHT = 0.15
EPSILON = 1e-05
AXES = ("lat", "lon")
PATCH = 4
F32, BF16, I32 = jnp.float32, jnp.bfloat16, jnp.int32


def iota(shape, dim):
    return lax.broadcasted_iota(I32, shape, dim)


def vmem():
    return pl.BlockSpec(memory_space=pltpu.VMEM)


def hbm():
    return pl.BlockSpec(memory_space=pltpu.HBM)


def near(x):
    return pltpu.with_memory_space_constraint(x, pltpu.VMEM)


def far(x):
    return pltpu.with_memory_space_constraint(x, pltpu.HBM)


def smem():
    return pl.BlockSpec(memory_space=pltpu.SMEM)


def call(body, name, out_shape, in_specs, out_specs, scratch=(), grid=(), mib=16, flops=0, moved=0):
    return pl.pallas_call(
        body,
        name=name,
        grid=grid,
        out_shape=out_shape,
        in_specs=in_specs,
        out_specs=out_specs,
        scratch_shapes=list(scratch),
        compiler_params=pltpu.CompilerParams(vmem_limit_bytes=mib * 2**20),
        cost_estimate=pl.CostEstimate(flops=flops, bytes_accessed=moved, transcendentals=0),
    )


STEP = 8


def ask_body(ids_ref, model_in, out_ref, slabs, sems):
    systems, clat, clon, depth = model_in.shape
    copies = []
    for k in range(4):
        at = (slice(None), pl.ds((k // 2) * (clat - 1), 1), pl.ds((k % 2) * (clon - 8), 8))
        copies.append(pltpu.make_async_copy(model_in.at[at], slabs.at[k], sems.at[k]))
    for copy in copies:
        copy.start()
    tiles = ids_ref.shape[-1]
    ids = jnp.concatenate([ids_ref[0].astype(F32), jnp.full((1, depth - tiles), -1.0, F32)], axis=1)
    for copy in copies:
        copy.wait()
    corners = [
        [slabs[k, r, 0, (k % 2) * 7 : (k % 2) * 7 + 1] for r in range(systems)] for k in range(4)
    ]
    lat_at, lon_at = lax.axis_index("lat"), lax.axis_index("lon")
    width = lax.axis_size("lon")
    for e in range(out_ref.shape[0]):
        out_ref[e, :, 0:depth] = ids
        south, east = e // width > lat_at, e % width > lon_at
        for r in range(systems):
            upper = jnp.where(east, corners[1][r], corners[0][r])
            lower = jnp.where(east, corners[3][r], corners[2][r])
            out_ref[e, :, (r + 1) * depth : (r + 2) * depth] = jnp.where(south, lower, upper)


def wanted_column(wanted, cap):
    devices, lanes = wanted.shape
    rows = devices * cap
    spread = jnp.broadcast_to(wanted[:, None, :], (devices, cap, lanes)).reshape(rows, lanes)
    pick = iota((rows, lanes), 1) == (iota((rows, lanes), 0) & (cap - 1))
    return jnp.sum(jnp.where(pick, spread, 0.0), axis=1, keepdims=True)


def serve_body(cap, clat, clon, lists_ref, model_in, served_ref, wanted_ref, corner_ref, diagonal_ref, patch, mixed, sems):
    systems, width, depth = patch.shape
    devices = lists_ref.shape[0]
    lanes = 128
    shift = (clat * clon).bit_length() - 1
    me = lax.axis_index("lat") * lax.axis_size("lon") + lax.axis_index("lon")
    ids = lists_ref[:, 0, 0:lanes].astype(I32)
    column = ids - lax.shift_left(me, shift)
    mine = (column >= 0) & (column < clat * clon) & (ids >= 0)
    first = jnp.min(jnp.where(mine, column, clat * clon))
    corner = jnp.minimum(lax.shift_right_logical(first, clon.bit_length() - 1), clat - PATCH)
    corner_ref[0] = corner
    at = pl.ds(pl.multiple_of(corner * clon, clon), width)
    copies = [pltpu.make_async_copy(model_in.at[r, at], patch.at[r], sems.at[r]) for r in range(systems)]
    for copy in copies:
        copy.start()
    ahead = (iota((lanes, lanes), 0) < iota((lanes, lanes), 1)).astype(F32).astype(BF16)
    rank = jnp.dot(mine.astype(F32).astype(BF16), ahead, preferred_element_type=F32)
    value = (column - corner * clon + 1).astype(F32)
    at = iota((devices, lanes), 1)
    wanted = jnp.zeros((devices, lanes), F32)
    for c in range(cap):
        picked = jnp.sum(jnp.where(mine & (rank == c), value, 0.0), axis=1, keepdims=True)
        wanted = jnp.where(at == c, picked, wanted)
    wanted_ref[...] = wanted
    target = wanted_column(wanted, cap).astype(I32) - 1
    rows = target.shape[0]
    chosen = (jnp.broadcast_to(target, (rows, width)) == iota((rows, width), 1)).astype(F32).astype(BF16)
    for r in range(systems):
        copies[r].wait()
        table = patch[r].astype(BF16)
        mixed[pl.ds(r, rows, stride=systems), :] = jnp.dot(chosen, table, preferred_element_type=F32)
    served_ref[...] = mixed[...].astype(BF16)
    lat_at, lon_at = lax.axis_index("lat"), lax.axis_index("lon")
    lat_size, lon_size = lax.axis_size("lat"), lax.axis_size("lon")
    for k in range(4):
        lat_to, lon_to = lat_at + 2 * (k // 2) - 1, lon_at + 2 * (k % 2) - 1
        inside = (lat_to >= 0) & (lat_to < lat_size) & (lon_to >= 0) & (lon_to < lon_size)
        source = jnp.where(inside, lat_to * lon_size + lon_to, 0)
        flag = inside.astype(F32)
        for r in range(systems):
            got = lists_ref[source, :, (r + 1) * depth : (r + 2) * depth]
            diagonal_ref[k * systems + r : k * systems + r + 1, :] = got * flag


def flanks_body(
    shift,
    blocks,
    after_ref,
    ids_ref,
    off_ref,
    count_ref,
    model_in,
    damp_in,
    north_ref,
    south_ref,
    east_ref,
    west_ref,
    meta_ref,
    slabs,
    sems,
):
    systems, clat, clon, depth = model_in.shape
    copies = []
    for k, (ref, at) in enumerate(((model_in, 0), (model_in, clon - 8), (damp_in, 0), (damp_in, clon - 8))):
        copies.append(pltpu.make_async_copy(ref.at[:, :, pl.ds(at, 8)], slabs.at[k], sems.at[k]))
    last = clat - 1
    pairs = (
        (model_in.at[:, pl.ds(last - 1, 2)], south_ref.at[:, pl.ds(0, 2)]),
        (damp_in.at[:, pl.ds(last, 1)], south_ref.at[:, pl.ds(2, 1)]),
        (model_in.at[:, pl.ds(0, 2)], north_ref.at[:, pl.ds(0, 2)]),
        (damp_in.at[:, pl.ds(0, 1)], north_ref.at[:, pl.ds(2, 1)]),
    )
    copies += [pltpu.make_async_copy(a, b, sems.at[i + 4]) for i, (a, b) in enumerate(pairs)]
    for copy in copies:
        copy.start()
    tiles = ids_ref.shape[-1]
    lanes = 128
    ids = jnp.concatenate([ids_ref[0], jnp.full((1, lanes - tiles), -1, I32)], axis=1)
    owner = lax.shift_right_arithmetic(ids, shift)
    square = (lanes, lanes)
    down, across = iota(square, 0), iota(square, 1)
    owner_f = jnp.broadcast_to(owner.astype(F32), square)
    owner_col = jnp.sum(jnp.where(down == across, owner_f, 0.0), axis=1, keepdims=True)
    same = jnp.where((owner_f == owner_col) & (down < across), 1.0, 0.0)
    rank = jnp.sum(same, axis=0, keepdims=True).astype(I32)
    lane = iota((1, lanes), 1)
    block = jnp.zeros((1, lanes), I32)
    starts = off_ref[0]
    for b in range(1, blocks + 1):
        block = block + (lane >= jnp.broadcast_to(starts[:, b : b + 1], (1, lanes))).astype(I32)
    count = jnp.broadcast_to(count_ref[...], (1, lanes))
    meta_ref[...] = jnp.concatenate([owner, rank, block, count] + [owner] * 4, axis=0)
    for copy in copies:
        copy.wait()
    rows = slabs.reshape(4, systems, clat * 8, depth)
    for r in range(systems):
        for out, slab, near_at, beyond in ((east_ref, 1, 7, 6), (west_ref, 0, 0, 1)):
            out[r, 0:clat] = rows[slab, r, pl.ds(near_at, clat, stride=8), :]
            out[r, clat : 2 * clat] = rows[slab, r, pl.ds(beyond, clat, stride=8), :]
            out[r, 2 * clat : 3 * clat] = rows[slab + 2, r, pl.ds(near_at, clat, stride=8), :]


def six(x, north, south, west, east):
    lane = iota(x.shape, 1)
    rows, depth = x.shape
    left, right = pltpu.roll(x, 1, 0), pltpu.roll(x, rows - 1, 0)
    ends = (8, depth)
    row = iota(ends, 0)
    left = jnp.concatenate([jnp.where(row == 0, jnp.broadcast_to(west, ends), left[:8]), left[8:]], axis=0)
    right = jnp.concatenate([right[:-8], jnp.where(row == 7, jnp.broadcast_to(east, ends), right[-8:])], axis=0)
    above = jnp.where(lane == 0, 0.0, pltpu.roll(x, 1, 1))
    below = jnp.where(lane == depth - 1, 0.0, pltpu.roll(x, depth - 1, 1))
    beside = north + south + left + right + above + below
    return DAMP_WEIGHT * (6.0 * x - beside)


def fold(x):
    parts = [x[i * 8 : (i + 1) * 8] for i in range(x.shape[0] // 8)]
    return functools.reduce(lambda a, b: a + b, parts)


def place(row, lane, value):
    return row + jnp.where(iota(row.shape, 1) == lane, jnp.broadcast_to(value, row.shape), 0.0)


def line(ref, r, i, clon):
    return ref[r, pl.ds(pl.multiple_of(i * clon, clon), clon), :]


def stencils(ref, r, k, clat, clon, first, last, west, east):
    base = k * STEP
    for j in range(STEP):
        i = base + j
        x = line(ref, r, i, clon)
        if j == 0:
            above = jnp.where(k > 0, line(ref, r, jnp.maximum(i - 1, 0), clon), first)
        else:
            above = line(ref, r, i - 1, clon)
        if j == STEP - 1:
            below = jnp.where(i + 1 < clat, line(ref, r, jnp.minimum(i + 1, clat - 1), clon), last)
        else:
            below = line(ref, r, i + 1, clon)
        yield i, x, six(x, above, below, west[pl.ds(i, 1)], east[pl.ds(i, 1)])


def damp_body(
    clat,
    clon,
    rec_ref,
    diagonal_ref,
    model_in,
    damp_in,
    north_ref,
    south_ref,
    west_ref,
    east_ref,
    bar_sent,
    north_out,
    south_out,
    west_out,
    east_out,
    sums_out,
    model_ref,
    damp_ref,
    bar_out,
    alphas,
    sems,
):
    systems, _, depth = model_ref.shape

    def incoming(r):
        return (
            pltpu.make_async_copy(model_in.at[r], model_ref.at[r], sems.at[r, 0]),
            pltpu.make_async_copy(damp_in.at[r], damp_ref.at[r], sems.at[r, 1]),
        )

    def outgoing(r):
        return pltpu.make_async_copy(bar_out.at[r], bar_sent.at[r], sems.at[r, 2])

    for r in range(systems):
        for copy in incoming(r):
            copy.start()
    for r in range(systems):
        alphas[r] = jnp.sum(rec_ref[0:1, r : r + 1])
    lat_at, lon_at = lax.axis_index("lat"), lax.axis_index("lon")
    has_north = (lat_at > 0).astype(F32)
    has_south = (lat_at < lax.axis_size("lat") - 1).astype(F32)
    has_west = (lon_at > 0).astype(F32)
    has_east = (lon_at < lax.axis_size("lon") - 1).astype(F32)

    def diagonal(k, r):
        return diagonal_ref[pl.ds(k * systems + r, 1), :]

    def system(r, row):
        alpha = alphas[r]
        for copy in incoming(r):
            copy.wait()

        def side(ref, own, flag, east):
            x, beyond, old = ref[r, 0:clat], ref[r, clat : 2 * clat], ref[r, 2 * clat : 3 * clat]
            upper, lower = diagonal(east, r), diagonal(2 + east, r)
            return (six(x, beyond, own, upper, lower) - alpha * old) * flag

        west_out[r] = side(west_ref, model_ref[r, pl.ds(0, clat, stride=clon), :], has_west, 0)
        east_out[r] = side(east_ref, model_ref[r, pl.ds(clon - 1, clat, stride=clon), :], has_east, 1)
        top, bottom = line(model_ref, r, 0, clon), line(model_ref, r, clat - 1, clon)
        edge = six(north_ref[r, 1], north_ref[r, 0], top, diagonal(0, r), diagonal(1, r))
        north_out[r] = has_north * (edge - alpha * north_ref[r, 2])
        edge = six(south_ref[r, 0], bottom, south_ref[r, 1], diagonal(2, r), diagonal(3, r))
        south_out[r] = has_south * (edge - alpha * south_ref[r, 2])

        def damped(k, acc):
            bar_sq, model_sq = acc
            ends = (north_ref[r, 1], south_ref[r, 0], west_ref.at[r], east_ref.at[r])
            for i, x, got in stencils(model_ref, r, k, clat, clon, *ends):
                bar = got - alpha * line(damp_ref, r, i, clon)
                bar_out[r, pl.ds(pl.multiple_of(i * clon, clon), clon), :] = bar
                bar_sq, model_sq = bar_sq + fold(bar * bar), model_sq + fold(x * x)
            return bar_sq, model_sq

        zero = jnp.zeros((8, depth), F32)
        bar_sq, model_sq = lax.fori_loop(0, clat // STEP, damped, (zero, zero))
        outgoing(r).start()
        row = place(row, r, jnp.sum(bar_sq, keepdims=True))
        return place(row, 3 * systems + r, jnp.sum(model_sq, keepdims=True))

    sums_out[...] = lax.fori_loop(0, systems, system, jnp.zeros((1, depth), F32))
    for r in range(systems):
        outgoing(r).wait()


def image_body(
    chunk,
    clat,
    clon,
    corner_ref,
    wanted_ref,
    bar_in,
    north_ref,
    south_ref,
    west_ref,
    east_ref,
    model_in,
    sums_ref,
    image_sent,
    sums_out,
    patch_out,
    model_patch_out,
    chosen_out,
    bar_ref,
    model_ref,
    image_out,
    sems,
):
    systems, _, depth = model_ref.shape

    def incoming(r):
        return (
            pltpu.make_async_copy(bar_in.at[r], bar_ref.at[r], sems.at[r, 0]),
            pltpu.make_async_copy(model_in.at[r], model_ref.at[r], sems.at[r, 1]),
        )

    def outgoing(r):
        return pltpu.make_async_copy(image_out.at[r], image_sent.at[r], sems.at[r, 2])

    for r in range(systems):
        for copy in incoming(r):
            copy.start()
    corner = corner_ref[0]
    wanted = wanted_ref[...]
    devices = wanted.shape[0]
    height, slots = chosen_out.shape
    width = PATCH * clon
    at = iota((1, slots), 1)
    source = jnp.floor((at.astype(F32) + 0.5) * (1.0 / chunk)).astype(I32)
    inner = at - source * chunk
    from_e = (jnp.broadcast_to(source, (devices, slots)) == iota((devices, slots), 0)).astype(F32).astype(BF16)
    turned = jnp.transpose(wanted)[0:8].astype(BF16)
    listed = jnp.dot(turned, from_e, preferred_element_type=F32)
    slot_of = lax.shift_right_logical(inner, systems.bit_length() - 1)
    mine = jnp.broadcast_to(slot_of, listed.shape) == iota(listed.shape, 0)
    flat = jnp.sum(jnp.where(mine, listed, 0.0), axis=0, keepdims=True).astype(I32)
    used = (flat > 0) & (inner < chunk - 1)
    target = jnp.where(used, (inner & (systems - 1)) * width + flat - 1, -1)
    for k in range(height // 64):
        shape = (64, slots)
        hit = jnp.broadcast_to(target, shape) == iota(shape, 0) + k * 64
        chosen_out[k * 64 : (k + 1) * 64] = hit.astype(F32).astype(BF16)

    def system(r, row):
        for copy in incoming(r):
            copy.wait()

        def imaged(k, acc):
            image_sq, cross = acc
            ends = (north_ref[r], south_ref[r], west_ref.at[r], east_ref.at[r])
            for i, x, image in stencils(bar_ref, r, k, clat, clon, *ends):
                image_out[r, pl.ds(pl.multiple_of(i * clon, clon), clon), :] = image
                image_sq = image_sq + fold(image * image)
                cross = cross + fold(image * line(model_ref, r, i, clon))
            return image_sq, cross

        zero = jnp.zeros((8, depth), F32)
        image_sq, cross = lax.fori_loop(0, clat // STEP, imaged, (zero, zero))
        outgoing(r).start()
        here = pl.ds(pl.multiple_of(corner * clon, clon), width)
        there = pl.ds(pl.multiple_of(r * width, width), width)
        patch_out[there, :] = image_out[r, here, :]
        model_patch_out[there, :] = model_ref[r, here, :]
        row = place(row, systems + r, jnp.sum(image_sq, keepdims=True))
        return place(row, 2 * systems + r, jnp.sum(cross, keepdims=True))

    sums_out[...] = lax.fori_loop(0, systems, system, sums_ref[...])
    for r in range(systems):
        outgoing(r).wait()


def rays_body(
    cap, blocks, meta_ref, rec_ref, tiles_in, fetched_ref, old_ref, sums_ref, bar_ref, term_ref, tiles_ref, masks, lows, sems
):
    tiles, width, depth = tiles_in.shape[2:]
    part = -(-tiles // PARTS)
    copies = []
    for k in range(PARTS):
        at = (0, 0, pl.ds(k * part, min(part, tiles - k * part)))
        copies.append(pltpu.make_async_copy(tiles_in.at[at], tiles_ref.at[at], sems.at[k]))
    for copy in copies:
        copy.start()
    systems = old_ref.shape[0]
    group = cap * systems
    chunk = group + 1
    devices = term_ref.shape[0] // chunk
    for c in range(cap + 1):
        here = lax.shift_right_logical(iota((group, depth), 0), systems.bit_length() - 1) == c
        masks[c] = here.astype(F32).astype(BF16)
    term_ref[...] = jnp.zeros(term_ref.shape, F32)
    lows[...] = jnp.zeros(lows.shape, BF16)
    total = jnp.zeros((blocks * group, width), F32)
    for t in range(tiles):
        if t % part == 0:
            copies[t // part].wait()
        owner, rank, block = meta_ref[0, t], meta_ref[1, t], meta_ref[2, t]
        rows = fetched_ref[pl.ds(pl.multiple_of(owner * group, group), group), :]
        left = jnp.concatenate(
            [rows * masks[jnp.where(block == b, rank, cap)] for b in range(blocks)], axis=0
        )
        total = total + lax.dot_general(
            left, tiles_ref[0, 0, t], (((1,), (1,)), ((), ())), preferred_element_type=F32
        )
    square = jnp.zeros((systems, width), F32)
    for b in range(blocks):
        traced = jnp.zeros((systems, width), F32)
        for c in range(cap):
            at = b * group + c * systems
            traced = traced + total[at : at + systems]
        old = jnp.concatenate(
            [old_ref[r, 0, :, b * width : (b + 1) * width] * rec_ref[0:1, r : r + 1] for r in range(systems)], axis=0
        )
        live = iota((systems, width), 1) + b * width < meta_ref[3, 0]
        bar = jnp.where(live, traced - old, 0.0)
        square = square + bar * bar
        for r in range(systems):
            bar_ref[r, 0, :, b * width : (b + 1) * width] = bar[r : r + 1]
        lows[b] = jnp.concatenate([bar, jnp.zeros((16 - systems, width), F32)], axis=0).astype(BF16)
    ray_sq = jnp.sum(square, axis=1, keepdims=True)
    part = sums_ref[...]
    for r in range(systems):
        part = place(part, r, ray_sq[r : r + 1])
    for e in range(devices):
        term_ref[e * chunk + group] = part
    for t in range(tiles):
        row = meta_ref[0, t] * chunk + meta_ref[1, t] * systems
        term = jnp.dot(lows[meta_ref[2, t]], tiles_ref[0, 0, t], preferred_element_type=F32)
        for r in range(systems):
            term_ref[row + r] = term[r : r + 1]


def combine_body(chunk, systems, terms_ref, chosen_ref, patch_ref, model_patch_ref, sums_ref, added_ref, residual_ref, parts_ref, split):
    arrived, depth = terms_ref.shape
    devices = parts_ref.shape[0]
    width = patch_ref.shape[0]
    x = terms_ref[...]
    high = x.astype(BF16)
    rest = x - high.astype(F32)
    middle = rest.astype(BF16)
    low = (rest - middle.astype(F32)).astype(BF16)
    padded = split.shape[0]
    if padded > arrived:
        split[arrived:] = jnp.zeros((padded - arrived, split.shape[1]), BF16)
    split[0:arrived, 0:depth] = high
    split[0:arrived, depth : 2 * depth] = middle
    split[0:arrived, 2 * depth :] = low
    three = jnp.dot(chosen_ref[...], split[...], preferred_element_type=F32)
    added = three[:, 0:depth] + (three[:, depth : 2 * depth] + three[:, 2 * depth :])
    added_ref[...] = added
    every = terms_ref[pl.ds(chunk - 1, devices, stride=chunk), :]
    residual_ref[...] = jnp.sum(every, axis=0, keepdims=True)
    square = added * (2.0 * patch_ref[...] + added)
    cross = added * model_patch_ref[...]
    row = sums_ref[...]
    each = width // systems
    for r in range(systems):
        row = place(row, systems + r, jnp.sum(square[r * each : (r + 1) * each], keepdims=True))
        row = place(row, 2 * systems + r, jnp.sum(cross[r * each : (r + 1) * each], keepdims=True))
    parts_ref[...] = jnp.broadcast_to(row, parts_ref.shape)


def first_norm(residual_ref, systems, rows_all):
    return jnp.sqrt(residual_ref[0:1, 0:systems] / rows_all + EPSILON)


def early_body(
    rows_all,
    residual_ref,
    rec_ref,
    ray_ref,
    bar_in,
    solution_in,
    search_in,
    ray_out,
    damp_out,
    solution_out,
    bar_ref,
    solution_ref,
    search_ref,
    damp_s,
    solution_s,
    coef,
    in_sems,
    sems,
):
    systems, columns, _ = bar_ref.shape
    rows = columns // PIECES
    ins = ((bar_in, bar_ref), (solution_in, solution_ref), (search_in, search_ref))
    outs = ((damp_s, damp_out), (solution_s, solution_out))
    start_all(ins, in_sems, systems, rows)
    rho_bar, phi_bar = rec_ref[1:2], rec_ref[2:3]
    beta = first_norm(residual_ref, systems, rows_all)
    rho = jnp.sqrt(rho_bar * rho_bar + beta * beta)
    scales = (1.0 / beta, (rho_bar / rho) * phi_bar / rho)
    for q, scale in enumerate(scales):
        for s in range(systems):
            coef[q, s] = scale[0, s]
    for s in range(systems):
        ray_out[s] = ray_ref[s] * coef[0, s]

    def piece(n, _):
        r, p = n // PIECES, n % PIECES
        at = pl.ds(pl.multiple_of(p * rows, rows), rows)
        for copy in pieces(ins, in_sems, r, p, rows):
            copy.wait()
        damp_s[r, at, :] = bar_ref[r, at, :] * coef[0, r]
        solution_s[r, at, :] = solution_ref[r, at, :] + search_ref[r, at, :] * coef[1, r]
        for copy in pieces(outs, sems, r, p, rows):
            copy.start()
        return 0

    lax.fori_loop(0, systems * PIECES, piece, 0)
    wait_all(outs, sems, systems, rows)


def finish_body(
    rows_all,
    cells_all,
    clon,
    corner_ref,
    residual_ref,
    parts_ref,
    rec_ref,
    added_ref,
    image_in,
    model_in,
    search_in,
    model_out,
    search_out,
    rec_out,
    image_ref,
    model_ref,
    search_ref,
    model_s,
    search_s,
    coef,
    in_sems,
    sems,
):
    systems, columns, _ = image_ref.shape
    rows = columns // PIECES
    ins = ((image_in, image_ref), (model_in, model_ref), (search_in, search_ref))
    outs = ((model_s, model_out), (search_s, search_out))
    start_all(ins, in_sems, systems, rows)
    total = jnp.sum(parts_ref[...], axis=0, keepdims=True)
    image_sq, cross, model_sq = (total[:, q * systems : (q + 1) * systems] for q in range(1, 4))
    rho_bar, phi_bar = rec_ref[1:2], rec_ref[2:3]
    beta = first_norm(residual_ref, systems, rows_all)
    update_sq = image_sq / (beta * beta) - 2.0 * cross + beta * beta * model_sq
    alpha = jnp.sqrt(jnp.maximum(update_sq, 0.0) / cells_all + EPSILON)
    rho = jnp.sqrt(rho_bar * rho_bar + beta * beta)
    cosine = rho_bar / rho
    sine = beta / rho
    rec_out[...] = jnp.concatenate([alpha, -cosine * alpha, sine * phi_bar], axis=0)
    scales = (1.0 / (beta * alpha), beta / alpha, sine * alpha / rho)
    for q, scale in enumerate(scales):
        for s in range(systems):
            coef[q, s] = scale[0, s]
    width = PATCH * clon

    def piece(n, _):
        r, p = n // PIECES, n % PIECES
        at = pl.ds(pl.multiple_of(p * rows, rows), rows)
        for copy in pieces(ins, in_sems, r, p, rows):
            copy.wait()
        new = image_ref[r, at, :] * coef[0, r] - model_ref[r, at, :] * coef[1, r]
        model_s[r, at, :] = new
        search_s[r, at, :] = new - search_ref[r, at, :] * coef[2, r]
        for k in range(PATCH):
            begin = (corner_ref[0] + k) * clon

            @pl.when((begin >= p * rows) & (begin < (p + 1) * rows))
            def _():
                cells = pl.ds(pl.multiple_of(begin, clon), clon)
                source = pl.ds(pl.multiple_of(r * width + k * clon, clon), clon)
                more = added_ref[source, :] * coef[0, r]
                model_s[r, cells, :] = model_s[r, cells, :] + more
                search_s[r, cells, :] = search_s[r, cells, :] + more

        for copy in pieces(outs, sems, r, p, rows):
            copy.start()
        return 0

    lax.fori_loop(0, systems * PIECES, piece, 0)
    wait_all(outs, sems, systems, rows)


PIECES = 2


def pieces(pairs, sems, r, p, rows):
    at = pl.ds(pl.multiple_of(p * rows, rows), rows)
    return [pltpu.make_async_copy(a.at[r, at], b.at[r, at], sems.at[r, p, k]) for k, (a, b) in enumerate(pairs)]


def start_all(pairs, sems, systems, rows):
    def one(n, _):
        for copy in pieces(pairs, sems, n // PIECES, n % PIECES, rows):
            copy.start()
        return 0

    lax.fori_loop(0, systems * PIECES, one, 0)


def wait_all(pairs, sems, systems, rows):
    def one(n, _):
        for copy in pieces(pairs, sems, n // PIECES, n % PIECES, rows):
            copy.wait()
        return 0

    lax.fori_loop(0, systems * PIECES, one, 0)


PARTS = 6


def shifted(x, axis, step):
    count = lax.axis_size(axis)
    if step > 0:
        pairs = [(i, i + 1) for i in range(count - 1)]
    else:
        pairs = [(i + 1, i) for i in range(count - 1)]
    return lax.ppermute(x, axis, pairs)


def exchange(x):
    return lax.all_to_all(x, AXES, split_axis=0, concat_axis=0, tiled=True)


def per_device(
    sensitivity,
    block_ids,
    block_offsets,
    ray_counts,
    ray_vector,
    damping_vector,
    model_vector,
    solution,
    search,
    recurrence,
):
    lat_size, lon_size = lax.axis_size("lat"), lax.axis_size("lon")
    devices = lat_size * lon_size
    tiles, width, depth = sensitivity.shape[2:]
    blocks = block_offsets.shape[-1] - 1
    systems, clat, clon, _ = model_vector.shape
    columns = clat * clon
    cap = max(2 * ((tiles + devices - 1) // devices), 16 // systems)
    slots = devices * cap
    group = cap * systems
    chunk = group + 1
    cells_all = devices * columns * depth
    rows_all = devices * blocks * width + cells_all
    lanes = 128
    full, flat = model_vector.shape, (systems, columns, depth)
    lines = (systems, PATCH * clon, depth)
    here, there, plain = pltpu.VMEM, pltpu.HBM, jax.ShapeDtypeStruct
    dma = pltpu.SemaphoreType.DMA
    model, damping = far(model_vector), far(damping_vector)
    model_flat, damping_flat = far(model_vector.reshape(flat)), far(damping_vector.reshape(flat))

    asked = (devices, 1, (1 + systems) * depth)
    asking = call(
        ask_body,
        "ask",
        there(asked, F32),
        [vmem(), hbm()],
        vmem(),
        scratch=[pltpu.VMEM((4, systems, 1, 8, depth), F32), dma((4,))],
    )(far(block_ids), model)
    lists = exchange(asking)

    side = there((systems, 3 * clat, depth), F32)
    band = there((systems, 3, clon, depth), F32)
    north_msg, south_msg, east_msg, west_msg, meta = call(
        functools.partial(flanks_body, columns.bit_length() - 1, blocks),
        "flanks",
        (band, band, side, side, there((8, lanes), I32)),
        [hbm()] + [vmem()] * 3 + [hbm(), hbm()],
        (vmem(),) * 5,
        scratch=[pltpu.VMEM((4, systems, clat, 8, depth), F32), dma((8,))],
        flops=1,
        moved=128 * systems * clat * depth,
    )(far(asking), far(block_ids), block_offsets, ray_counts, model, damping)

    served, wanted, corner, diagonal = call(
        functools.partial(serve_body, cap, clat, clon),
        "serve",
        (
            there((slots * systems, depth), BF16),
            plain((devices, lanes), F32),
            plain((1,), I32),
            plain((4 * systems, depth), F32),
        ),
        [vmem(), hbm()],
        (vmem(), vmem(), smem(), vmem()),
        scratch=[pltpu.VMEM(lines, F32), pltpu.VMEM((slots * systems, depth), F32), dma((systems,))],
    )(lists, model_flat)
    fetched = exchange(served.reshape(devices, group, depth)).reshape(slots * systems, depth)

    north = shifted(south_msg, "lat", 1)
    south = shifted(north_msg, "lat", -1)
    west = shifted(east_msg, "lon", 1)
    east = shifted(west_msg, "lon", -1)

    edge, flank = there((systems, clon, depth), F32), there((systems, clat, depth), F32)
    bar, *border, sums = call(
        functools.partial(damp_body, clat, clon),
        "damp",
        (there(flat, F32), edge, edge, flank, flank, there((1, lanes), F32)),
        [vmem()] * 2 + [hbm()] * 2 + [vmem()] * 4,
        (hbm(),) + (vmem(),) * 5,
        scratch=[pltpu.VMEM(flat, F32)] * 3 + [pltpu.SMEM((systems,), F32), dma((systems, 3))],
        flops=20 * systems * columns * depth,
        moved=12 * systems * columns * depth,
    )(far(recurrence), diagonal, model_flat, damping_flat, north, south, west, east)

    ray_bar, terms = call(
        functools.partial(rays_body, cap, blocks),
        "rays",
        (there(ray_vector.shape, F32), there((devices * chunk, 1, depth), F32)),
        [smem(), vmem(), hbm()] + [vmem()] * 3,
        (vmem(), vmem()),
        scratch=[
            pltpu.VMEM(sensitivity.shape, BF16),
            pltpu.VMEM((cap + 1, group, depth), BF16),
            pltpu.VMEM((blocks + 1, 16, width), BF16),
            dma((PARTS,)),
        ],
        flops=4 * tiles * width * depth * 16,
        moved=2 * tiles * width * depth,
    )(meta, far(recurrence), far(sensitivity), fetched, far(ray_vector), far(sums))
    arrived = exchange(terms.reshape(devices, 1, chunk * depth)).reshape(devices * chunk, depth)

    padded = -(-devices * chunk // lanes) * lanes
    height = systems * PATCH * clon
    patch = (height, depth)
    image, sums, patched, model_patch, chosen = call(
        functools.partial(image_body, chunk, clat, clon),
        "image",
        (
            there(flat, F32),
            plain((1, lanes), F32),
            plain(patch, F32),
            plain(patch, F32),
            plain((height, padded), BF16),
        ),
        [smem(), vmem(), hbm()] + [vmem()] * 4 + [hbm(), vmem()],
        (hbm(),) + (vmem(),) * 4,
        scratch=[pltpu.VMEM(flat, F32)] * 3 + [dma((systems, 3))],
        flops=20 * systems * columns * depth,
        moved=12 * systems * columns * depth,
    )(corner, wanted, far(bar), *(far(x) for x in border), model_flat, far(sums))

    added, residual, parts = call(
        functools.partial(combine_body, chunk, systems),
        "combine",
        (plain(patch, F32), plain((1, lanes), F32), there((devices, lanes), F32)),
        [vmem()] * 5,
        (vmem(),) * 3,
        scratch=[pltpu.VMEM((padded, 3 * depth), BF16)],
    )(arrived, chosen, patched, model_patch, sums)
    every = exchange(parts.reshape(devices, 1, lanes)).reshape(devices, lanes)

    search_flat = far(search.reshape(flat))
    ray_out, damp_out, solution_out = call(
        functools.partial(early_body, float(rows_all)),
        "early",
        (there(ray_vector.shape, F32), there(flat, F32), there(flat, F32)),
        [vmem()] * 3 + [hbm()] * 3,
        (vmem(), hbm(), hbm()),
        scratch=[pltpu.VMEM(flat, F32)] * 5
        + [pltpu.SMEM((2, systems), F32), dma((systems, PIECES, 3)), dma((systems, PIECES, 2))],
        mib=32,
        flops=4 * systems * columns * depth,
        moved=20 * systems * columns * depth,
    )(residual, far(recurrence), far(ray_bar), far(bar), far(solution.reshape(flat)), search_flat)
    model_out, search_out, rec_out = call(
        functools.partial(finish_body, float(rows_all), float(cells_all), clon),
        "finish",
        (there(flat, F32), there(flat, F32), there(recurrence.shape, F32)),
        [smem()] + [vmem()] * 4 + [hbm()] * 3,
        (hbm(), hbm(), vmem()),
        scratch=[pltpu.VMEM(flat, F32)] * 5
        + [pltpu.SMEM((3, systems), F32), dma((systems, PIECES, 3)), dma((systems, PIECES, 2))],
        mib=32,
        flops=6 * systems * columns * depth,
        moved=20 * systems * columns * depth,
    )(corner, residual, every, far(recurrence), added, far(image), model_flat, search_flat)
    fields = (x.reshape(full) for x in (damp_out, model_out, solution_out, search_out))
    return (ray_out, *fields, rec_out)


def solution(mesh):
    fields = P(None, "lat", "lon", None)
    return jax.shard_map(
        per_device,
        mesh=mesh,
        in_specs=(
            P("lat", "lon", None, None, None),
            P("lat", "lon", None),
            P("lat", "lon", None),
            P("lat", "lon"),
            fields,
            fields,
            fields,
            fields,
            fields,
            P(),
        ),
        out_specs=(fields, fields, fields, fields, fields, P()),
        check_vma=False,
    )
```

```python
import functools

import jax
import jax.numpy as jnp
from jax import lax
from jax.experimental import pallas as pl
from jax.experimental.pallas import tpu as pltpu
from jax.sharding import PartitionSpec as P

DAMP_WEIGHT = 0.15
EPSILON = 1e-05
AXES = ("lat", "lon")
PATCH = 4
F32, BF16, I32 = jnp.float32, jnp.bfloat16, jnp.int32


def iota(shape, dim):
    return lax.broadcasted_iota(I32, shape, dim)


def vmem():
    return pl.BlockSpec(memory_space=pltpu.VMEM)


def hbm():
    return pl.BlockSpec(memory_space=pltpu.HBM)


def near(x):
    return pltpu.with_memory_space_constraint(x, pltpu.VMEM)


def far(x):
    return pltpu.with_memory_space_constraint(x, pltpu.HBM)


def smem():
    return pl.BlockSpec(memory_space=pltpu.SMEM)


def call(body, name, out_shape, in_specs, out_specs, scratch=(), grid=(), mib=16, flops=0, moved=0):
    return pl.pallas_call(
        body,
        name=name,
        grid=grid,
        out_shape=out_shape,
        in_specs=in_specs,
        out_specs=out_specs,
        scratch_shapes=list(scratch),
        compiler_params=pltpu.CompilerParams(vmem_limit_bytes=mib * 2**20),
        cost_estimate=pl.CostEstimate(flops=flops, bytes_accessed=moved, transcendentals=0),
    )


STEP = 8


def ask_body(ids_ref, model_in, out_ref, slabs, sems):
    systems, clat, clon, depth = model_in.shape
    copies = []
    for k in range(4):
        at = (slice(None), pl.ds((k // 2) * (clat - 1), 1), pl.ds((k % 2) * (clon - 8), 8))
        copies.append(pltpu.make_async_copy(model_in.at[at], slabs.at[k], sems.at[k]))
    for copy in copies:
        copy.start()
    tiles = ids_ref.shape[-1]
    ids = jnp.concatenate([ids_ref[0].astype(F32), jnp.full((1, depth - tiles), -1.0, F32)], axis=1)
    for copy in copies:
        copy.wait()
    corners = [
        [slabs[k, r, 0, (k % 2) * 7 : (k % 2) * 7 + 1] for r in range(systems)] for k in range(4)
    ]
    lat_at, lon_at = lax.axis_index("lat"), lax.axis_index("lon")
    width = lax.axis_size("lon")
    for e in range(out_ref.shape[0]):
        out_ref[e, :, 0:depth] = ids
        south, east = e // width > lat_at, e % width > lon_at
        for r in range(systems):
            upper = jnp.where(east, corners[1][r], corners[0][r])
            lower = jnp.where(east, corners[3][r], corners[2][r])
            out_ref[e, :, (r + 1) * depth : (r + 2) * depth] = jnp.where(south, lower, upper)


def wanted_column(wanted, cap):
    devices, lanes = wanted.shape
    rows = devices * cap
    spread = jnp.broadcast_to(wanted[:, None, :], (devices, cap, lanes)).reshape(rows, lanes)
    pick = iota((rows, lanes), 1) == (iota((rows, lanes), 0) & (cap - 1))
    return jnp.sum(jnp.where(pick, spread, 0.0), axis=1, keepdims=True)


def serve_body(cap, clat, clon, lists_ref, model_in, north, south, west, east, served_ref, wanted_ref, corner_ref, diagonal_ref, patch, mixed, sems):
    systems, width, depth = patch.shape
    devices = lists_ref.shape[0]
    lanes = 128
    shift = (clat * clon).bit_length() - 1
    me = lax.axis_index("lat") * lax.axis_size("lon") + lax.axis_index("lon")
    ids = lists_ref[:, 0, 0:lanes].astype(I32)
    column = ids - lax.shift_left(me, shift)
    mine = (column >= 0) & (column < clat * clon) & (ids >= 0)
    first = jnp.min(jnp.where(mine, column, clat * clon))
    corner = jnp.minimum(lax.shift_right_logical(first, clon.bit_length() - 1), clat - PATCH)
    corner_ref[0] = corner
    at = pl.ds(pl.multiple_of(corner * clon, clon), width)
    copies = [pltpu.make_async_copy(model_in.at[r, at], patch.at[r], sems.at[r]) for r in range(systems)]
    for copy in copies:
        copy.start()
    ahead = (iota((lanes, lanes), 0) < iota((lanes, lanes), 1)).astype(F32).astype(BF16)
    rank = jnp.dot(mine.astype(F32).astype(BF16), ahead, preferred_element_type=F32)
    value = (column - corner * clon + 1).astype(F32)
    at = iota((devices, lanes), 1)
    wanted = jnp.zeros((devices, lanes), F32)
    for c in range(cap):
        picked = jnp.sum(jnp.where(mine & (rank == c), value, 0.0), axis=1, keepdims=True)
        wanted = jnp.where(at == c, picked, wanted)
    wanted_ref[...] = wanted
    target = wanted_column(wanted, cap).astype(I32) - 1
    rows = target.shape[0]
    chosen = (jnp.broadcast_to(target, (rows, width)) == iota((rows, width), 1)).astype(F32).astype(BF16)
    for r in range(systems):
        copies[r].wait()
        table = patch[r].astype(BF16)
        mixed[pl.ds(r, rows, stride=systems), :] = jnp.dot(chosen, table, preferred_element_type=F32)
    served_ref[...] = mixed[...].astype(BF16)
    lat_at, lon_at = lax.axis_index("lat"), lax.axis_index("lon")
    lat_size, lon_size = lax.axis_size("lat"), lax.axis_size("lon")
    for k in range(4):
        lat_to, lon_to = lat_at + 2 * (k // 2) - 1, lon_at + 2 * (k % 2) - 1
        inside = (lat_to >= 0) & (lat_to < lat_size) & (lon_to >= 0) & (lon_to < lon_size)
        source = jnp.where(inside, lat_to * lon_size + lon_to, 0)
        flag = inside.astype(F32)
        for r in range(systems):
            got = lists_ref[source, :, (r + 1) * depth : (r + 2) * depth]
            diagonal_ref[k * systems + r : k * systems + r + 1, :] = got * flag


def flanks_body(
    shift,
    blocks,
    after_ref,
    ids_ref,
    off_ref,
    count_ref,
    model_in,
    damp_in,
    north_ref,
    south_ref,
    east_ref,
    west_ref,
    meta_ref,
    slabs,
    sems,
):
    systems, clat, clon, depth = model_in.shape
    copies = []
    for k, (ref, at) in enumerate(((model_in, 0), (model_in, clon - 8), (damp_in, 0), (damp_in, clon - 8))):
        copies.append(pltpu.make_async_copy(ref.at[:, :, pl.ds(at, 8)], slabs.at[k], sems.at[k]))
    last = clat - 1
    pairs = (
        (model_in.at[:, pl.ds(last - 1, 2)], south_ref.at[:, pl.ds(0, 2)]),
        (damp_in.at[:, pl.ds(last, 1)], south_ref.at[:, pl.ds(2, 1)]),
        (model_in.at[:, pl.ds(0, 2)], north_ref.at[:, pl.ds(0, 2)]),
        (damp_in.at[:, pl.ds(0, 1)], north_ref.at[:, pl.ds(2, 1)]),
    )
    copies += [pltpu.make_async_copy(a, b, sems.at[i + 4]) for i, (a, b) in enumerate(pairs)]
    for copy in copies:
        copy.start()
    tiles = ids_ref.shape[-1]
    lanes = 128
    ids = jnp.concatenate([ids_ref[0], jnp.full((1, lanes - tiles), -1, I32)], axis=1)
    owner = lax.shift_right_arithmetic(ids, shift)
    square = (lanes, lanes)
    down, across = iota(square, 0), iota(square, 1)
    owner_f = jnp.broadcast_to(owner.astype(F32), square)
    owner_col = jnp.sum(jnp.where(down == across, owner_f, 0.0), axis=1, keepdims=True)
    same = jnp.where((owner_f == owner_col) & (down < across), 1.0, 0.0)
    rank = jnp.sum(same, axis=0, keepdims=True).astype(I32)
    lane = iota((1, lanes), 1)
    block = jnp.zeros((1, lanes), I32)
    starts = off_ref[0]
    for b in range(1, blocks + 1):
        block = block + (lane >= jnp.broadcast_to(starts[:, b : b + 1], (1, lanes))).astype(I32)
    count = jnp.broadcast_to(count_ref[...], (1, lanes))
    meta_ref[...] = jnp.concatenate([owner, rank, block, count] + [owner] * 4, axis=0)
    for copy in copies:
        copy.wait()
    rows = slabs.reshape(4, systems, clat * 8, depth)
    for r in range(systems):
        for out, slab, near_at, beyond in ((east_ref, 1, 7, 6), (west_ref, 0, 0, 1)):
            out[r, 0:clat] = rows[slab, r, pl.ds(near_at, clat, stride=8), :]
            out[r, clat : 2 * clat] = rows[slab, r, pl.ds(beyond, clat, stride=8), :]
            out[r, 2 * clat : 3 * clat] = rows[slab + 2, r, pl.ds(near_at, clat, stride=8), :]


def six(x, north, south, west, east):
    lane = iota(x.shape, 1)
    rows, depth = x.shape
    left, right = pltpu.roll(x, 1, 0), pltpu.roll(x, rows - 1, 0)
    ends = (8, depth)
    row = iota(ends, 0)
    left = jnp.concatenate([jnp.where(row == 0, jnp.broadcast_to(west, ends), left[:8]), left[8:]], axis=0)
    right = jnp.concatenate([right[:-8], jnp.where(row == 7, jnp.broadcast_to(east, ends), right[-8:])], axis=0)
    above = jnp.where(lane == 0, 0.0, pltpu.roll(x, 1, 1))
    below = jnp.where(lane == depth - 1, 0.0, pltpu.roll(x, depth - 1, 1))
    beside = north + south + left + right + above + below
    return DAMP_WEIGHT * (6.0 * x - beside)


def fold(x):
    parts = [x[i * 8 : (i + 1) * 8] for i in range(x.shape[0] // 8)]
    return functools.reduce(lambda a, b: a + b, parts)


def place(row, lane, value):
    return row + jnp.where(iota(row.shape, 1) == lane, jnp.broadcast_to(value, row.shape), 0.0)


def line(ref, r, i, clon):
    return ref[r, pl.ds(pl.multiple_of(i * clon, clon), clon), :]


def stencils(ref, r, k, clat, clon, first, last, west, east):
    base = k * STEP
    for j in range(STEP):
        i = base + j
        x = line(ref, r, i, clon)
        if j == 0:
            above = jnp.where(k > 0, line(ref, r, jnp.maximum(i - 1, 0), clon), first)
        else:
            above = line(ref, r, i - 1, clon)
        if j == STEP - 1:
            below = jnp.where(i + 1 < clat, line(ref, r, jnp.minimum(i + 1, clat - 1), clon), last)
        else:
            below = line(ref, r, i + 1, clon)
        yield i, x, six(x, above, below, west[pl.ds(i, 1)], east[pl.ds(i, 1)])


def damp_body(
    clat,
    clon,
    rec_ref,
    diagonal_ref,
    model_in,
    damp_in,
    north_ref,
    south_ref,
    west_ref,
    east_ref,
    bar_sent,
    north_out,
    south_out,
    west_out,
    east_out,
    sums_out,
    model_ref,
    damp_ref,
    bar_out,
    alphas,
    sems,
):
    systems, _, depth = model_ref.shape

    def incoming(r):
        return (
            pltpu.make_async_copy(model_in.at[r], model_ref.at[r], sems.at[r, 0]),
            pltpu.make_async_copy(damp_in.at[r], damp_ref.at[r], sems.at[r, 1]),
        )

    def outgoing(r):
        return pltpu.make_async_copy(bar_out.at[r], bar_sent.at[r], sems.at[r, 2])

    for r in range(systems):
        for copy in incoming(r):
            copy.start()
    for r in range(systems):
        alphas[r] = jnp.sum(rec_ref[0:1, r : r + 1])
    lat_at, lon_at = lax.axis_index("lat"), lax.axis_index("lon")
    has_north = (lat_at > 0).astype(F32)
    has_south = (lat_at < lax.axis_size("lat") - 1).astype(F32)
    has_west = (lon_at > 0).astype(F32)
    has_east = (lon_at < lax.axis_size("lon") - 1).astype(F32)

    def diagonal(k, r):
        return diagonal_ref[pl.ds(k * systems + r, 1), :]

    def system(r, row):
        alpha = alphas[r]
        for copy in incoming(r):
            copy.wait()

        def side(ref, own, flag, east):
            x, beyond, old = ref[r, 0:clat], ref[r, clat : 2 * clat], ref[r, 2 * clat : 3 * clat]
            upper, lower = diagonal(east, r), diagonal(2 + east, r)
            return (six(x, beyond, own, upper, lower) - alpha * old) * flag

        west_out[r] = side(west_ref, model_ref[r, pl.ds(0, clat, stride=clon), :], has_west, 0)
        east_out[r] = side(east_ref, model_ref[r, pl.ds(clon - 1, clat, stride=clon), :], has_east, 1)
        top, bottom = line(model_ref, r, 0, clon), line(model_ref, r, clat - 1, clon)
        edge = six(north_ref[r, 1], north_ref[r, 0], top, diagonal(0, r), diagonal(1, r))
        north_out[r] = has_north * (edge - alpha * north_ref[r, 2])
        edge = six(south_ref[r, 0], bottom, south_ref[r, 1], diagonal(2, r), diagonal(3, r))
        south_out[r] = has_south * (edge - alpha * south_ref[r, 2])

        def damped(k, acc):
            bar_sq, model_sq = acc
            ends = (north_ref[r, 1], south_ref[r, 0], west_ref.at[r], east_ref.at[r])
            for i, x, got in stencils(model_ref, r, k, clat, clon, *ends):
                bar = got - alpha * line(damp_ref, r, i, clon)
                bar_out[r, pl.ds(pl.multiple_of(i * clon, clon), clon), :] = bar
                bar_sq, model_sq = bar_sq + fold(bar * bar), model_sq + fold(x * x)
            return bar_sq, model_sq

        zero = jnp.zeros((8, depth), F32)
        bar_sq, model_sq = lax.fori_loop(0, clat // STEP, damped, (zero, zero))
        outgoing(r).start()
        row = place(row, r, jnp.sum(bar_sq, keepdims=True))
        return place(row, 3 * systems + r, jnp.sum(model_sq, keepdims=True))

    sums_out[...] = lax.fori_loop(0, systems, system, jnp.zeros((1, depth), F32))
    for r in range(systems):
        outgoing(r).wait()


def image_body(
    chunk,
    clat,
    clon,
    corner_ref,
    wanted_ref,
    bar_in,
    north_ref,
    south_ref,
    west_ref,
    east_ref,
    model_in,
    sums_ref,
    image_sent,
    sums_out,
    patch_out,
    model_patch_out,
    chosen_out,
    bar_ref,
    model_ref,
    image_out,
    sems,
):
    systems, _, depth = model_ref.shape

    def incoming(r):
        return (
            pltpu.make_async_copy(bar_in.at[r], bar_ref.at[r], sems.at[r, 0]),
            pltpu.make_async_copy(model_in.at[r], model_ref.at[r], sems.at[r, 1]),
        )

    def outgoing(r):
        return pltpu.make_async_copy(image_out.at[r], image_sent.at[r], sems.at[r, 2])

    for r in range(systems):
        for copy in incoming(r):
            copy.start()
    corner = corner_ref[0]
    wanted = wanted_ref[...]
    devices = wanted.shape[0]
    height, slots = chosen_out.shape
    width = PATCH * clon
    at = iota((1, slots), 1)
    source = jnp.floor((at.astype(F32) + 0.5) * (1.0 / chunk)).astype(I32)
    inner = at - source * chunk
    from_e = (jnp.broadcast_to(source, (devices, slots)) == iota((devices, slots), 0)).astype(F32).astype(BF16)
    turned = jnp.transpose(wanted)[0:8].astype(BF16)
    listed = jnp.dot(turned, from_e, preferred_element_type=F32)
    slot_of = lax.shift_right_logical(inner, systems.bit_length() - 1)
    mine = jnp.broadcast_to(slot_of, listed.shape) == iota(listed.shape, 0)
    flat = jnp.sum(jnp.where(mine, listed, 0.0), axis=0, keepdims=True).astype(I32)
    used = (flat > 0) & (inner < chunk - 1)
    target = jnp.where(used, (inner & (systems - 1)) * width + flat - 1, -1)
    for k in range(height // 64):
        shape = (64, slots)
        hit = jnp.broadcast_to(target, shape) == iota(shape, 0) + k * 64
        chosen_out[k * 64 : (k + 1) * 64] = hit.astype(F32).astype(BF16)

    def system(r, row):
        for copy in incoming(r):
            copy.wait()

        def imaged(k, acc):
            image_sq, cross = acc
            ends = (north_ref[r], south_ref[r], west_ref.at[r], east_ref.at[r])
            for i, x, image in stencils(bar_ref, r, k, clat, clon, *ends):
                image_out[r, pl.ds(pl.multiple_of(i * clon, clon), clon), :] = image
                image_sq = image_sq + fold(image * image)
                cross = cross + fold(image * line(model_ref, r, i, clon))
            return image_sq, cross

        zero = jnp.zeros((8, depth), F32)
        image_sq, cross = lax.fori_loop(0, clat // STEP, imaged, (zero, zero))
        outgoing(r).start()
        here = pl.ds(pl.multiple_of(corner * clon, clon), width)
        there = pl.ds(pl.multiple_of(r * width, width), width)
        patch_out[there, :] = image_out[r, here, :]
        model_patch_out[there, :] = model_ref[r, here, :]
        row = place(row, systems + r, jnp.sum(image_sq, keepdims=True))
        return place(row, 2 * systems + r, jnp.sum(cross, keepdims=True))

    sums_out[...] = lax.fori_loop(0, systems, system, sums_ref[...])
    for r in range(systems):
        outgoing(r).wait()


def rays_body(
    cap, blocks, meta_ref, rec_ref, tiles_in, fetched_ref, old_ref, sums_ref, bar_ref, term_ref, tiles_ref, masks, lows, sems
):
    tiles, width, depth = tiles_in.shape[2:]
    part = -(-tiles // PARTS)
    copies = []
    for k in range(PARTS):
        at = (0, 0, pl.ds(k * part, min(part, tiles - k * part)))
        copies.append(pltpu.make_async_copy(tiles_in.at[at], tiles_ref.at[at], sems.at[k]))
    for copy in copies:
        copy.start()
    systems = old_ref.shape[0]
    group = cap * systems
    chunk = group + 1
    devices = term_ref.shape[0] // chunk
    for c in range(cap + 1):
        here = lax.shift_right_logical(iota((group, depth), 0), systems.bit_length() - 1) == c
        masks[c] = here.astype(F32).astype(BF16)
    term_ref[...] = jnp.zeros(term_ref.shape, F32)
    lows[...] = jnp.zeros(lows.shape, BF16)
    total = jnp.zeros((blocks * group, width), F32)
    for t in range(tiles):
        if t % part == 0:
            copies[t // part].wait()
        owner, rank, block = meta_ref[0, t], meta_ref[1, t], meta_ref[2, t]
        rows = fetched_ref[pl.ds(pl.multiple_of(owner * group, group), group), :]
        left = jnp.concatenate(
            [rows * masks[jnp.where(block == b, rank, cap)] for b in range(blocks)], axis=0
        )
        total = total + lax.dot_general(
            left, tiles_ref[0, 0, t], (((1,), (1,)), ((), ())), preferred_element_type=F32
        )
    square = jnp.zeros((systems, width), F32)
    for b in range(blocks):
        traced = jnp.zeros((systems, width), F32)
        for c in range(cap):
            at = b * group + c * systems
            traced = traced + total[at : at + systems]
        old = jnp.concatenate(
            [old_ref[r, 0, :, b * width : (b + 1) * width] * rec_ref[0:1, r : r + 1] for r in range(systems)], axis=0
        )
        live = iota((systems, width), 1) + b * width < meta_ref[3, 0]
        bar = jnp.where(live, traced - old, 0.0)
        square = square + bar * bar
        for r in range(systems):
            bar_ref[r, 0, :, b * width : (b + 1) * width] = bar[r : r + 1]
        lows[b] = jnp.concatenate([bar, jnp.zeros((16 - systems, width), F32)], axis=0).astype(BF16)
    ray_sq = jnp.sum(square, axis=1, keepdims=True)
    part = sums_ref[...]
    for r in range(systems):
        part = place(part, r, ray_sq[r : r + 1])
    for e in range(devices):
        term_ref[e * chunk + group] = part
    for t in range(tiles):
        row = meta_ref[0, t] * chunk + meta_ref[1, t] * systems
        term = jnp.dot(lows[meta_ref[2, t]], tiles_ref[0, 0, t], preferred_element_type=F32)
        for r in range(systems):
            term_ref[row + r] = term[r : r + 1]


def combine_body(chunk, systems, terms_ref, chosen_ref, patch_ref, model_patch_ref, sums_ref, added_ref, residual_ref, parts_ref, split):
    arrived, depth = terms_ref.shape
    devices = parts_ref.shape[0]
    width = patch_ref.shape[0]
    x = terms_ref[...]
    high = x.astype(BF16)
    rest = x - high.astype(F32)
    middle = rest.astype(BF16)
    low = (rest - middle.astype(F32)).astype(BF16)
    padded = split.shape[0]
    if padded > arrived:
        split[arrived:] = jnp.zeros((padded - arrived, split.shape[1]), BF16)
    split[0:arrived, 0:depth] = high
    split[0:arrived, depth : 2 * depth] = middle
    split[0:arrived, 2 * depth :] = low
    three = jnp.dot(chosen_ref[...], split[...], preferred_element_type=F32)
    added = three[:, 0:depth] + (three[:, depth : 2 * depth] + three[:, 2 * depth :])
    added_ref[...] = added
    every = terms_ref[pl.ds(chunk - 1, devices, stride=chunk), :]
    residual_ref[...] = jnp.sum(every, axis=0, keepdims=True)
    square = added * (2.0 * patch_ref[...] + added)
    cross = added * model_patch_ref[...]
    row = sums_ref[...]
    each = width // systems
    for r in range(systems):
        row = place(row, systems + r, jnp.sum(square[r * each : (r + 1) * each], keepdims=True))
        row = place(row, 2 * systems + r, jnp.sum(cross[r * each : (r + 1) * each], keepdims=True))
    parts_ref[...] = jnp.broadcast_to(row, parts_ref.shape)


def first_norm(residual_ref, systems, rows_all):
    return jnp.sqrt(residual_ref[0:1, 0:systems] / rows_all + EPSILON)


def early_body(
    rows_all,
    residual_ref,
    rec_ref,
    ray_ref,
    bar_in,
    solution_in,
    search_in,
    ray_out,
    damp_out,
    solution_out,
    bar_ref,
    solution_ref,
    search_ref,
    damp_s,
    solution_s,
    coef,
    in_sems,
    sems,
):
    systems, columns, _ = bar_ref.shape
    rows = columns // PIECES
    ins = ((bar_in, bar_ref), (solution_in, solution_ref), (search_in, search_ref))
    outs = ((damp_s, damp_out), (solution_s, solution_out))
    for n in range(AHEAD):
        start_one(ins, in_sems, n, systems, rows)
    rho_bar, phi_bar = rec_ref[1:2], rec_ref[2:3]
    beta = first_norm(residual_ref, systems, rows_all)
    rho = jnp.sqrt(rho_bar * rho_bar + beta * beta)
    scales = (1.0 / beta, (rho_bar / rho) * phi_bar / rho)
    for q, scale in enumerate(scales):
        for s in range(systems):
            coef[q, s] = scale[0, s]
    for s in range(systems):
        ray_out[s] = ray_ref[s] * coef[0, s]

    def piece(n, _):
        r, p = n // PIECES, n % PIECES
        at = pl.ds(pl.multiple_of(p * rows, rows), rows)
        start_one(ins, in_sems, n + AHEAD, systems, rows)
        for copy in pieces(ins, in_sems, r, p, rows):
            copy.wait()
        damp_s[r, at, :] = bar_ref[r, at, :] * coef[0, r]
        solution_s[r, at, :] = solution_ref[r, at, :] + search_ref[r, at, :] * coef[1, r]
        for copy in pieces(outs, sems, r, p, rows):
            copy.start()
        return 0

    lax.fori_loop(0, systems * PIECES, piece, 0)
    wait_all(outs, sems, systems, rows)


def finish_body(
    rows_all,
    cells_all,
    clon,
    corner_ref,
    residual_ref,
    parts_ref,
    rec_ref,
    added_ref,
    image_in,
    model_in,
    search_in,
    model_out,
    search_out,
    rec_out,
    image_ref,
    model_ref,
    search_ref,
    model_s,
    search_s,
    coef,
    in_sems,
    sems,
):
    systems, columns, _ = image_ref.shape
    rows = columns // PIECES
    ins = ((image_in, image_ref), (model_in, model_ref), (search_in, search_ref))
    outs = ((model_s, model_out), (search_s, search_out))
    for n in range(AHEAD):
        start_one(ins, in_sems, n, systems, rows)
    total = jnp.sum(parts_ref[...], axis=0, keepdims=True)
    image_sq, cross, model_sq = (total[:, q * systems : (q + 1) * systems] for q in range(1, 4))
    rho_bar, phi_bar = rec_ref[1:2], rec_ref[2:3]
    beta = first_norm(residual_ref, systems, rows_all)
    update_sq = image_sq / (beta * beta) - 2.0 * cross + beta * beta * model_sq
    alpha = jnp.sqrt(jnp.maximum(update_sq, 0.0) / cells_all + EPSILON)
    rho = jnp.sqrt(rho_bar * rho_bar + beta * beta)
    cosine = rho_bar / rho
    sine = beta / rho
    rec_out[...] = jnp.concatenate([alpha, -cosine * alpha, sine * phi_bar], axis=0)
    scales = (1.0 / (beta * alpha), beta / alpha, sine * alpha / rho)
    for q, scale in enumerate(scales):
        for s in range(systems):
            coef[q, s] = scale[0, s]
    width = PATCH * clon

    def piece(n, _):
        r, p = n // PIECES, n % PIECES
        at = pl.ds(pl.multiple_of(p * rows, rows), rows)
        start_one(ins, in_sems, n + AHEAD, systems, rows)
        for copy in pieces(ins, in_sems, r, p, rows):
            copy.wait()
        new = image_ref[r, at, :] * coef[0, r] - model_ref[r, at, :] * coef[1, r]
        model_s[r, at, :] = new
        search_s[r, at, :] = new - search_ref[r, at, :] * coef[2, r]
        for k in range(PATCH):
            begin = (corner_ref[0] + k) * clon

            @pl.when((begin >= p * rows) & (begin < (p + 1) * rows))
            def _():
                cells = pl.ds(pl.multiple_of(begin, clon), clon)
                source = pl.ds(pl.multiple_of(r * width + k * clon, clon), clon)
                more = added_ref[source, :] * coef[0, r]
                model_s[r, cells, :] = model_s[r, cells, :] + more
                search_s[r, cells, :] = search_s[r, cells, :] + more

        for copy in pieces(outs, sems, r, p, rows):
            copy.start()
        return 0

    lax.fori_loop(0, systems * PIECES, piece, 0)
    wait_all(outs, sems, systems, rows)


PIECES = 2
AHEAD = 4


def pieces(pairs, sems, r, p, rows):
    at = pl.ds(pl.multiple_of(p * rows, rows), rows)
    return [pltpu.make_async_copy(a.at[r, at], b.at[r, at], sems.at[r, p, k]) for k, (a, b) in enumerate(pairs)]


def start_one(pairs, sems, n, systems, rows):
    @pl.when(n < systems * PIECES)
    def _():
        for copy in pieces(pairs, sems, n // PIECES, n % PIECES, rows):
            copy.start()


def wait_all(pairs, sems, systems, rows):
    def one(n, _):
        for copy in pieces(pairs, sems, n // PIECES, n % PIECES, rows):
            copy.wait()
        return 0

    lax.fori_loop(0, systems * PIECES, one, 0)


PARTS = 6


def shifted(x, axis, step):
    count = lax.axis_size(axis)
    if step > 0:
        pairs = [(i, i + 1) for i in range(count - 1)]
    else:
        pairs = [(i + 1, i) for i in range(count - 1)]
    return lax.ppermute(x, axis, pairs)


def exchange(x):
    return lax.all_to_all(x, AXES, split_axis=0, concat_axis=0, tiled=True)


def per_device(
    sensitivity,
    block_ids,
    block_offsets,
    ray_counts,
    ray_vector,
    damping_vector,
    model_vector,
    solution,
    search,
    recurrence,
):
    lat_size, lon_size = lax.axis_size("lat"), lax.axis_size("lon")
    devices = lat_size * lon_size
    tiles, width, depth = sensitivity.shape[2:]
    blocks = block_offsets.shape[-1] - 1
    systems, clat, clon, _ = model_vector.shape
    columns = clat * clon
    cap = max(2 * ((tiles + devices - 1) // devices), 16 // systems)
    slots = devices * cap
    group = cap * systems
    chunk = group + 1
    cells_all = devices * columns * depth
    rows_all = devices * blocks * width + cells_all
    lanes = 128
    full, flat = model_vector.shape, (systems, columns, depth)
    lines = (systems, PATCH * clon, depth)
    here, there, plain = pltpu.VMEM, pltpu.HBM, jax.ShapeDtypeStruct
    dma = pltpu.SemaphoreType.DMA
    model, damping = far(model_vector), far(damping_vector)
    model_flat, damping_flat = far(model_vector.reshape(flat)), far(damping_vector.reshape(flat))

    asked = (devices, 1, (1 + systems) * depth)
    asking = call(
        ask_body,
        "ask",
        there(asked, F32),
        [vmem(), hbm()],
        vmem(),
        scratch=[pltpu.VMEM((4, systems, 1, 8, depth), F32), dma((4,))],
    )(far(block_ids), model)
    lists = exchange(asking)

    side = there((systems, 3 * clat, depth), F32)
    band = there((systems, 3, clon, depth), F32)
    north_msg, south_msg, east_msg, west_msg, meta = call(
        functools.partial(flanks_body, columns.bit_length() - 1, blocks),
        "flanks",
        (band, band, side, side, there((8, lanes), I32)),
        [hbm()] + [vmem()] * 3 + [hbm(), hbm()],
        (vmem(),) * 5,
        scratch=[pltpu.VMEM((4, systems, clat, 8, depth), F32), dma((8,))],
        flops=1,
        moved=128 * systems * clat * depth,
    )(far(asking), far(block_ids), block_offsets, ray_counts, model, damping)

    north = shifted(south_msg, "lat", 1)
    south = shifted(north_msg, "lat", -1)
    west = shifted(east_msg, "lon", 1)
    east = shifted(west_msg, "lon", -1)

    served, wanted, corner, diagonal = call(
        functools.partial(serve_body, cap, clat, clon),
        "serve",
        (
            there((slots * systems, depth), BF16),
            plain((devices, lanes), F32),
            plain((1,), I32),
            plain((4 * systems, depth), F32),
        ),
        [vmem(), hbm()] + [pl.BlockSpec(memory_space=pl.ANY)] * 4,
        (vmem(), vmem(), smem(), vmem()),
        scratch=[pltpu.VMEM(lines, F32), pltpu.VMEM((slots * systems, depth), F32), dma((systems,))],
    )(lists, model_flat, north, south, west, east)
    fetched = exchange(served.reshape(devices, group, depth)).reshape(slots * systems, depth)

    edge, flank = there((systems, clon, depth), F32), there((systems, clat, depth), F32)
    bar, *border, sums = call(
        functools.partial(damp_body, clat, clon),
        "damp",
        (there(flat, F32), edge, edge, flank, flank, there((1, lanes), F32)),
        [vmem()] * 2 + [hbm()] * 2 + [vmem()] * 4,
        (hbm(),) + (vmem(),) * 5,
        scratch=[pltpu.VMEM(flat, F32)] * 3 + [pltpu.SMEM((systems,), F32), dma((systems, 3))],
        flops=20 * systems * columns * depth,
        moved=12 * systems * columns * depth,
    )(far(recurrence), diagonal, model_flat, damping_flat, north, south, west, east)

    ray_bar, terms = call(
        functools.partial(rays_body, cap, blocks),
        "rays",
        (there(ray_vector.shape, F32), there((devices * chunk, 1, depth), F32)),
        [smem(), vmem(), hbm()] + [vmem()] * 3,
        (vmem(), vmem()),
        scratch=[
            pltpu.VMEM(sensitivity.shape, BF16),
            pltpu.VMEM((cap + 1, group, depth), BF16),
            pltpu.VMEM((blocks + 1, 16, width), BF16),
            dma((PARTS,)),
        ],
        flops=4 * tiles * width * depth * 16,
        moved=2 * tiles * width * depth,
    )(meta, far(recurrence), far(sensitivity), fetched, far(ray_vector), far(sums))
    arrived = exchange(terms.reshape(devices, 1, chunk * depth)).reshape(devices * chunk, depth)

    padded = -(-devices * chunk // lanes) * lanes
    height = systems * PATCH * clon
    patch = (height, depth)
    image, sums, patched, model_patch, chosen = call(
        functools.partial(image_body, chunk, clat, clon),
        "image",
        (
            there(flat, F32),
            plain((1, lanes), F32),
            plain(patch, F32),
            plain(patch, F32),
            plain((height, padded), BF16),
        ),
        [smem(), vmem(), hbm()] + [vmem()] * 4 + [hbm(), vmem()],
        (hbm(),) + (vmem(),) * 4,
        scratch=[pltpu.VMEM(flat, F32)] * 3 + [dma((systems, 3))],
        flops=20 * systems * columns * depth,
        moved=12 * systems * columns * depth,
    )(corner, wanted, far(bar), *(far(x) for x in border), model_flat, far(sums))

    added, residual, parts = call(
        functools.partial(combine_body, chunk, systems),
        "combine",
        (plain(patch, F32), plain((1, lanes), F32), there((devices, lanes), F32)),
        [vmem()] * 5,
        (vmem(),) * 3,
        scratch=[pltpu.VMEM((padded, 3 * depth), BF16)],
    )(arrived, chosen, patched, model_patch, sums)
    every = exchange(parts.reshape(devices, 1, lanes)).reshape(devices, lanes)

    search_flat = far(search.reshape(flat))
    ray_out, damp_out, solution_out = call(
        functools.partial(early_body, float(rows_all)),
        "early",
        (there(ray_vector.shape, F32), there(flat, F32), there(flat, F32)),
        [vmem()] * 3 + [hbm()] * 3,
        (vmem(), hbm(), hbm()),
        scratch=[pltpu.VMEM(flat, F32)] * 5
        + [pltpu.SMEM((2, systems), F32), dma((systems, PIECES, 3)), dma((systems, PIECES, 2))],
        mib=32,
        flops=4 * systems * columns * depth,
        moved=20 * systems * columns * depth,
    )(residual, far(recurrence), far(ray_bar), far(bar), far(solution.reshape(flat)), search_flat)
    model_out, search_out, rec_out = call(
        functools.partial(finish_body, float(rows_all), float(cells_all), clon),
        "finish",
        (there(flat, F32), there(flat, F32), there(recurrence.shape, F32)),
        [smem()] + [vmem()] * 4 + [hbm()] * 3,
        (hbm(), hbm(), vmem()),
        scratch=[pltpu.VMEM(flat, F32)] * 5
        + [pltpu.SMEM((3, systems), F32), dma((systems, PIECES, 3)), dma((systems, PIECES, 2))],
        mib=32,
        flops=6 * systems * columns * depth,
        moved=20 * systems * columns * depth,
    )(corner, residual, every, far(recurrence), added, far(image), model_flat, search_flat)
    fields = (x.reshape(full) for x in (damp_out, model_out, solution_out, search_out))
    return (ray_out, *fields, rec_out)


def solution(mesh):
    fields = P(None, "lat", "lon", None)
    return jax.shard_map(
        per_device,
        mesh=mesh,
        in_specs=(
            P("lat", "lon", None, None, None),
            P("lat", "lon", None),
            P("lat", "lon", None),
            P("lat", "lon"),
            fields,
            fields,
            fields,
            fields,
            fields,
            P(),
        ),
        out_specs=(fields, fields, fields, fields, fields, P()),
        check_vma=False,
    )
```

```python
import functools

import jax
import jax.numpy as jnp
from jax import lax
from jax.experimental import pallas as pl
from jax.experimental.pallas import tpu as pltpu
from jax.sharding import PartitionSpec as P

DAMP_WEIGHT = 0.15
EPSILON = 1e-05
AXES = ("lat", "lon")
PATCH = 4
F32, BF16, I32 = jnp.float32, jnp.bfloat16, jnp.int32


def iota(shape, dim):
    return lax.broadcasted_iota(I32, shape, dim)


def vmem():
    return pl.BlockSpec(memory_space=pltpu.VMEM)


def hbm():
    return pl.BlockSpec(memory_space=pltpu.HBM)


def near(x):
    return pltpu.with_memory_space_constraint(x, pltpu.VMEM)


def far(x):
    return pltpu.with_memory_space_constraint(x, pltpu.HBM)


def smem():
    return pl.BlockSpec(memory_space=pltpu.SMEM)


def call(body, name, out_shape, in_specs, out_specs, scratch=(), grid=(), mib=16, flops=0, moved=0):
    return pl.pallas_call(
        body,
        name=name,
        grid=grid,
        out_shape=out_shape,
        in_specs=in_specs,
        out_specs=out_specs,
        scratch_shapes=list(scratch),
        compiler_params=pltpu.CompilerParams(vmem_limit_bytes=mib * 2**20),
        cost_estimate=pl.CostEstimate(flops=flops, bytes_accessed=moved, transcendentals=0),
    )


STEP = 8


def wanted_column(wanted, cap):
    devices, lanes = wanted.shape
    rows = devices * cap
    spread = jnp.broadcast_to(wanted[:, None, :], (devices, cap, lanes)).reshape(rows, lanes)
    pick = iota((rows, lanes), 1) == (iota((rows, lanes), 0) & (cap - 1))
    return jnp.sum(jnp.where(pick, spread, 0.0), axis=1, keepdims=True)


def serve_body(cap, clat, clon, lists_ref, model_in, north, south, west, east, served_ref, wanted_ref, corner_ref, diagonal_ref, patch, mixed, sems):
    systems, width, depth = patch.shape
    devices = lists_ref.shape[0]
    lanes = 128
    shift = (clat * clon).bit_length() - 1
    me = lax.axis_index("lat") * lax.axis_size("lon") + lax.axis_index("lon")
    ids = lists_ref[:, 0, 0:lanes].astype(I32)
    column = ids - lax.shift_left(me, shift)
    mine = (column >= 0) & (column < clat * clon) & (ids >= 0)
    first = jnp.min(jnp.where(mine, column, clat * clon))
    corner = jnp.minimum(lax.shift_right_logical(first, clon.bit_length() - 1), clat - PATCH)
    corner_ref[0] = corner
    at = pl.ds(pl.multiple_of(corner * clon, clon), width)
    copies = [pltpu.make_async_copy(model_in.at[r, at], patch.at[r], sems.at[r]) for r in range(systems)]
    for copy in copies:
        copy.start()
    ahead = (iota((lanes, lanes), 0) < iota((lanes, lanes), 1)).astype(F32).astype(BF16)
    rank = jnp.dot(mine.astype(F32).astype(BF16), ahead, preferred_element_type=F32)
    value = (column - corner * clon + 1).astype(F32)
    at = iota((devices, lanes), 1)
    wanted = jnp.zeros((devices, lanes), F32)
    for c in range(cap):
        picked = jnp.sum(jnp.where(mine & (rank == c), value, 0.0), axis=1, keepdims=True)
        wanted = jnp.where(at == c, picked, wanted)
    wanted_ref[...] = wanted
    target = wanted_column(wanted, cap).astype(I32) - 1
    rows = target.shape[0]
    chosen = (jnp.broadcast_to(target, (rows, width)) == iota((rows, width), 1)).astype(F32).astype(BF16)
    for r in range(systems):
        copies[r].wait()
        table = patch[r].astype(BF16)
        mixed[pl.ds(r, rows, stride=systems), :] = jnp.dot(chosen, table, preferred_element_type=F32)
    served_ref[...] = mixed[...].astype(BF16)
    lat_at, lon_at = lax.axis_index("lat"), lax.axis_index("lon")
    lat_size, lon_size = lax.axis_size("lat"), lax.axis_size("lon")
    for k in range(4):
        lat_to, lon_to = lat_at + 2 * (k // 2) - 1, lon_at + 2 * (k % 2) - 1
        inside = (lat_to >= 0) & (lat_to < lat_size) & (lon_to >= 0) & (lon_to < lon_size)
        source = jnp.where(inside, lat_to * lon_size + lon_to, 0)
        flag = inside.astype(F32)
        for r in range(systems):
            got = lists_ref[source, :, (r + 1) * depth : (r + 2) * depth]
            diagonal_ref[k * systems + r : k * systems + r + 1, :] = got * flag


def flanks_body(
    shift,
    blocks,
    ids_ref,
    off_ref,
    count_ref,
    model_in,
    damp_in,
    asking_ref,
    north_ref,
    south_ref,
    east_ref,
    west_ref,
    meta_ref,
    slabs,
    sems,
):
    systems, clat, clon, depth = model_in.shape
    copies = []
    for k, (ref, at) in enumerate(((model_in, 0), (model_in, clon - 8), (damp_in, 0), (damp_in, clon - 8))):
        copies.append(pltpu.make_async_copy(ref.at[:, :, pl.ds(at, 8)], slabs.at[k], sems.at[k]))
    last = clat - 1
    pairs = (
        (model_in.at[:, pl.ds(last - 1, 2)], south_ref.at[:, pl.ds(0, 2)]),
        (damp_in.at[:, pl.ds(last, 1)], south_ref.at[:, pl.ds(2, 1)]),
        (model_in.at[:, pl.ds(0, 2)], north_ref.at[:, pl.ds(0, 2)]),
        (damp_in.at[:, pl.ds(0, 1)], north_ref.at[:, pl.ds(2, 1)]),
    )
    copies += [pltpu.make_async_copy(a, b, sems.at[i + 4]) for i, (a, b) in enumerate(pairs)]
    for copy in copies:
        copy.start()
    tiles = ids_ref.shape[-1]
    lanes = 128
    ids = jnp.concatenate([ids_ref[0], jnp.full((1, lanes - tiles), -1, I32)], axis=1)
    owner = lax.shift_right_arithmetic(ids, shift)
    square = (lanes, lanes)
    down, across = iota(square, 0), iota(square, 1)
    owner_f = jnp.broadcast_to(owner.astype(F32), square)
    owner_col = jnp.sum(jnp.where(down == across, owner_f, 0.0), axis=1, keepdims=True)
    same = jnp.where((owner_f == owner_col) & (down < across), 1.0, 0.0)
    rank = jnp.sum(same, axis=0, keepdims=True).astype(I32)
    lane = iota((1, lanes), 1)
    block = jnp.zeros((1, lanes), I32)
    starts = off_ref[0]
    for b in range(1, blocks + 1):
        block = block + (lane >= jnp.broadcast_to(starts[:, b : b + 1], (1, lanes))).astype(I32)
    count = jnp.broadcast_to(count_ref[...], (1, lanes))
    meta_ref[...] = jnp.concatenate([owner, rank, block, count] + [owner] * 4, axis=0)
    for copy in copies:
        copy.wait()
    listed = ids.astype(F32)
    corners = [
        [slabs[k % 2, r, (k // 2) * last, (k % 2) * 7 : (k % 2) * 7 + 1] for r in range(systems)]
        for k in range(4)
    ]
    lat_at, lon_at = lax.axis_index("lat"), lax.axis_index("lon")
    width = lax.axis_size("lon")
    for e in range(asking_ref.shape[0]):
        asking_ref[e, :, 0:depth] = listed
        to_south, to_east = e // width > lat_at, e % width > lon_at
        for r in range(systems):
            upper = jnp.where(to_east, corners[1][r], corners[0][r])
            lower = jnp.where(to_east, corners[3][r], corners[2][r])
            asking_ref[e, :, (r + 1) * depth : (r + 2) * depth] = jnp.where(to_south, lower, upper)
    rows = slabs.reshape(4, systems, clat * 8, depth)
    for r in range(systems):
        for out, slab, near_at, beyond in ((east_ref, 1, 7, 6), (west_ref, 0, 0, 1)):
            out[r, 0:clat] = rows[slab, r, pl.ds(near_at, clat, stride=8), :]
            out[r, clat : 2 * clat] = rows[slab, r, pl.ds(beyond, clat, stride=8), :]
            out[r, 2 * clat : 3 * clat] = rows[slab + 2, r, pl.ds(near_at, clat, stride=8), :]


def six(x, north, south, west, east):
    lane = iota(x.shape, 1)
    rows, depth = x.shape
    left, right = pltpu.roll(x, 1, 0), pltpu.roll(x, rows - 1, 0)
    ends = (8, depth)
    row = iota(ends, 0)
    left = jnp.concatenate([jnp.where(row == 0, jnp.broadcast_to(west, ends), left[:8]), left[8:]], axis=0)
    right = jnp.concatenate([right[:-8], jnp.where(row == 7, jnp.broadcast_to(east, ends), right[-8:])], axis=0)
    above = jnp.where(lane == 0, 0.0, pltpu.roll(x, 1, 1))
    below = jnp.where(lane == depth - 1, 0.0, pltpu.roll(x, depth - 1, 1))
    beside = north + south + left + right + above + below
    return DAMP_WEIGHT * (6.0 * x - beside)


def fold(x):
    parts = [x[i * 8 : (i + 1) * 8] for i in range(x.shape[0] // 8)]
    return functools.reduce(lambda a, b: a + b, parts)


def place(row, lane, value):
    return row + jnp.where(iota(row.shape, 1) == lane, jnp.broadcast_to(value, row.shape), 0.0)


def line(ref, r, i, clon):
    return ref[r, pl.ds(pl.multiple_of(i * clon, clon), clon), :]


def stencils(ref, r, k, clat, clon, first, last, west, east):
    base = k * STEP
    for j in range(STEP):
        i = base + j
        x = line(ref, r, i, clon)
        if j == 0:
            above = jnp.where(k > 0, line(ref, r, jnp.maximum(i - 1, 0), clon), first)
        else:
            above = line(ref, r, i - 1, clon)
        if j == STEP - 1:
            below = jnp.where(i + 1 < clat, line(ref, r, jnp.minimum(i + 1, clat - 1), clon), last)
        else:
            below = line(ref, r, i + 1, clon)
        yield i, x, six(x, above, below, west[pl.ds(i, 1)], east[pl.ds(i, 1)])


def damp_body(
    clat,
    clon,
    rec_ref,
    diagonal_ref,
    model_in,
    damp_in,
    north_ref,
    south_ref,
    west_ref,
    east_ref,
    tiles_in,
    bar_sent,
    held_out,
    north_out,
    south_out,
    west_out,
    east_out,
    sums_out,
    model_ref,
    damp_ref,
    bar_out,
    alphas,
    sems,
    hold_sem,
):
    systems, _, depth = model_ref.shape

    def incoming(r):
        return (
            pltpu.make_async_copy(model_in.at[r], model_ref.at[r], sems.at[r, 0]),
            pltpu.make_async_copy(damp_in.at[r], damp_ref.at[r], sems.at[r, 1]),
        )

    def outgoing(r):
        return pltpu.make_async_copy(bar_out.at[r], bar_sent.at[r], sems.at[r, 2])

    holding = pltpu.make_async_copy(tiles_in.at[0, 0, pl.ds(0, HELD)], held_out, hold_sem)
    for r in range(systems):
        for copy in incoming(r):
            copy.start()
    holding.start()
    for r in range(systems):
        alphas[r] = jnp.sum(rec_ref[0:1, r : r + 1])
    lat_at, lon_at = lax.axis_index("lat"), lax.axis_index("lon")
    has_north = (lat_at > 0).astype(F32)
    has_south = (lat_at < lax.axis_size("lat") - 1).astype(F32)
    has_west = (lon_at > 0).astype(F32)
    has_east = (lon_at < lax.axis_size("lon") - 1).astype(F32)

    def diagonal(k, r):
        return diagonal_ref[pl.ds(k * systems + r, 1), :]

    def system(r, row):
        alpha = alphas[r]
        for copy in incoming(r):
            copy.wait()

        def side(ref, own, flag, east):
            x, beyond, old = ref[r, 0:clat], ref[r, clat : 2 * clat], ref[r, 2 * clat : 3 * clat]
            upper, lower = diagonal(east, r), diagonal(2 + east, r)
            return (six(x, beyond, own, upper, lower) - alpha * old) * flag

        west_out[r] = side(west_ref, model_ref[r, pl.ds(0, clat, stride=clon), :], has_west, 0)
        east_out[r] = side(east_ref, model_ref[r, pl.ds(clon - 1, clat, stride=clon), :], has_east, 1)
        top, bottom = line(model_ref, r, 0, clon), line(model_ref, r, clat - 1, clon)
        edge = six(north_ref[r, 1], north_ref[r, 0], top, diagonal(0, r), diagonal(1, r))
        north_out[r] = has_north * (edge - alpha * north_ref[r, 2])
        edge = six(south_ref[r, 0], bottom, south_ref[r, 1], diagonal(2, r), diagonal(3, r))
        south_out[r] = has_south * (edge - alpha * south_ref[r, 2])

        def damped(k, acc):
            bar_sq, model_sq = acc
            ends = (north_ref[r, 1], south_ref[r, 0], west_ref.at[r], east_ref.at[r])
            for i, x, got in stencils(model_ref, r, k, clat, clon, *ends):
                bar = got - alpha * line(damp_ref, r, i, clon)
                bar_out[r, pl.ds(pl.multiple_of(i * clon, clon), clon), :] = bar
                bar_sq, model_sq = bar_sq + fold(bar * bar), model_sq + fold(x * x)
            return bar_sq, model_sq

        zero = jnp.zeros((8, depth), F32)
        bar_sq, model_sq = lax.fori_loop(0, clat // STEP, damped, (zero, zero))
        outgoing(r).start()
        row = place(row, r, jnp.sum(bar_sq, keepdims=True))
        return place(row, 3 * systems + r, jnp.sum(model_sq, keepdims=True))

    sums_out[...] = lax.fori_loop(0, systems, system, jnp.zeros((1, depth), F32))
    holding.wait()
    for r in range(systems):
        outgoing(r).wait()


def image_body(
    chunk,
    clat,
    clon,
    corner_ref,
    wanted_ref,
    bar_in,
    north_ref,
    south_ref,
    west_ref,
    east_ref,
    model_in,
    sums_ref,
    image_sent,
    sums_out,
    patch_out,
    model_patch_out,
    chosen_out,
    bar_ref,
    model_ref,
    image_out,
    sems,
):
    systems, _, depth = model_ref.shape

    def incoming(r):
        return (
            pltpu.make_async_copy(bar_in.at[r], bar_ref.at[r], sems.at[r, 0]),
            pltpu.make_async_copy(model_in.at[r], model_ref.at[r], sems.at[r, 1]),
        )

    def outgoing(r):
        return pltpu.make_async_copy(image_out.at[r], image_sent.at[r], sems.at[r, 2])

    for r in range(systems):
        for copy in incoming(r):
            copy.start()
    corner = corner_ref[0]
    wanted = wanted_ref[...]
    devices = wanted.shape[0]
    height, slots = chosen_out.shape
    width = PATCH * clon
    at = iota((1, slots), 1)
    source = jnp.floor((at.astype(F32) + 0.5) * (1.0 / chunk)).astype(I32)
    inner = at - source * chunk
    from_e = (jnp.broadcast_to(source, (devices, slots)) == iota((devices, slots), 0)).astype(F32).astype(BF16)
    turned = jnp.transpose(wanted)[0:8].astype(BF16)
    listed = jnp.dot(turned, from_e, preferred_element_type=F32)
    slot_of = lax.shift_right_logical(inner, systems.bit_length() - 1)
    mine = jnp.broadcast_to(slot_of, listed.shape) == iota(listed.shape, 0)
    flat = jnp.sum(jnp.where(mine, listed, 0.0), axis=0, keepdims=True).astype(I32)
    used = (flat > 0) & (inner < chunk - 1)
    target = jnp.where(used, (inner & (systems - 1)) * width + flat - 1, -1)
    for k in range(height // 64):
        shape = (64, slots)
        hit = jnp.broadcast_to(target, shape) == iota(shape, 0) + k * 64
        chosen_out[k * 64 : (k + 1) * 64] = hit.astype(F32).astype(BF16)

    def system(r, row):
        for copy in incoming(r):
            copy.wait()

        def imaged(k, acc):
            image_sq, cross = acc
            ends = (north_ref[r], south_ref[r], west_ref.at[r], east_ref.at[r])
            for i, x, image in stencils(bar_ref, r, k, clat, clon, *ends):
                image_out[r, pl.ds(pl.multiple_of(i * clon, clon), clon), :] = image
                image_sq = image_sq + fold(image * image)
                cross = cross + fold(image * line(model_ref, r, i, clon))
            return image_sq, cross

        zero = jnp.zeros((8, depth), F32)
        image_sq, cross = lax.fori_loop(0, clat // STEP, imaged, (zero, zero))
        outgoing(r).start()
        here = pl.ds(pl.multiple_of(corner * clon, clon), width)
        there = pl.ds(pl.multiple_of(r * width, width), width)
        patch_out[there, :] = image_out[r, here, :]
        model_patch_out[there, :] = model_ref[r, here, :]
        row = place(row, systems + r, jnp.sum(image_sq, keepdims=True))
        return place(row, 2 * systems + r, jnp.sum(cross, keepdims=True))

    sums_out[...] = lax.fori_loop(0, systems, system, sums_ref[...])
    for r in range(systems):
        outgoing(r).wait()


def rays_body(
    cap, blocks, meta_ref, rec_ref, tiles_in, held_ref, fetched_ref, old_ref, sums_ref, bar_ref, term_ref, rest_ref, masks, lows, sems
):
    tiles, width, depth = tiles_in.shape[2:]
    part = -(-(tiles - HELD) // PARTS)
    copies = []
    for k in range(PARTS):
        count = min(part, tiles - HELD - k * part)
        source = tiles_in.at[0, 0, pl.ds(HELD + k * part, count)]
        copies.append(pltpu.make_async_copy(source, rest_ref.at[pl.ds(k * part, count)], sems.at[k]))
    for copy in copies:
        copy.start()

    def tile(t):
        return held_ref[t] if t < HELD else rest_ref[t - HELD]

    systems = old_ref.shape[0]
    group = cap * systems
    chunk = group + 1
    devices = term_ref.shape[0] // chunk
    for c in range(cap + 1):
        here = lax.shift_right_logical(iota((group, depth), 0), systems.bit_length() - 1) == c
        masks[c] = here.astype(F32).astype(BF16)
    term_ref[...] = jnp.zeros(term_ref.shape, F32)
    lows[...] = jnp.zeros(lows.shape, BF16)
    total = jnp.zeros((blocks * group, width), F32)
    for t in range(tiles):
        if t >= HELD and (t - HELD) % part == 0:
            copies[(t - HELD) // part].wait()
        owner, rank, block = meta_ref[0, t], meta_ref[1, t], meta_ref[2, t]
        rows = fetched_ref[pl.ds(pl.multiple_of(owner * group, group), group), :]
        left = jnp.concatenate(
            [rows * masks[jnp.where(block == b, rank, cap)] for b in range(blocks)], axis=0
        )
        total = total + lax.dot_general(
            left, tile(t), (((1,), (1,)), ((), ())), preferred_element_type=F32
        )
    square = jnp.zeros((systems, width), F32)
    for b in range(blocks):
        traced = jnp.zeros((systems, width), F32)
        for c in range(cap):
            at = b * group + c * systems
            traced = traced + total[at : at + systems]
        old = jnp.concatenate(
            [old_ref[r, 0, :, b * width : (b + 1) * width] * rec_ref[0:1, r : r + 1] for r in range(systems)], axis=0
        )
        live = iota((systems, width), 1) + b * width < meta_ref[3, 0]
        bar = jnp.where(live, traced - old, 0.0)
        square = square + bar * bar
        for r in range(systems):
            bar_ref[r, 0, :, b * width : (b + 1) * width] = bar[r : r + 1]
        lows[b] = jnp.concatenate([bar, jnp.zeros((16 - systems, width), F32)], axis=0).astype(BF16)
    ray_sq = jnp.sum(square, axis=1, keepdims=True)
    part = sums_ref[...]
    for r in range(systems):
        part = place(part, r, ray_sq[r : r + 1])
    for e in range(devices):
        term_ref[e * chunk + group] = part
    for t in range(tiles):
        row = meta_ref[0, t] * chunk + meta_ref[1, t] * systems
        term = jnp.dot(lows[meta_ref[2, t]], tile(t), preferred_element_type=F32)
        for r in range(systems):
            term_ref[row + r] = term[r : r + 1]


def combine_body(chunk, systems, terms_ref, chosen_ref, patch_ref, model_patch_ref, sums_ref, added_ref, residual_ref, parts_ref, split):
    arrived, depth = terms_ref.shape
    devices = parts_ref.shape[0]
    width = patch_ref.shape[0]
    x = terms_ref[...]
    high = x.astype(BF16)
    rest = x - high.astype(F32)
    middle = rest.astype(BF16)
    low = (rest - middle.astype(F32)).astype(BF16)
    padded = split.shape[0]
    if padded > arrived:
        split[arrived:] = jnp.zeros((padded - arrived, split.shape[1]), BF16)
    split[0:arrived, 0:depth] = high
    split[0:arrived, depth : 2 * depth] = middle
    split[0:arrived, 2 * depth :] = low
    three = jnp.dot(chosen_ref[...], split[...], preferred_element_type=F32)
    added = three[:, 0:depth] + (three[:, depth : 2 * depth] + three[:, 2 * depth :])
    added_ref[...] = added
    every = terms_ref[pl.ds(chunk - 1, devices, stride=chunk), :]
    residual_ref[...] = jnp.sum(every, axis=0, keepdims=True)
    square = added * (2.0 * patch_ref[...] + added)
    cross = added * model_patch_ref[...]
    row = sums_ref[...]
    each = width // systems
    for r in range(systems):
        row = place(row, systems + r, jnp.sum(square[r * each : (r + 1) * each], keepdims=True))
        row = place(row, 2 * systems + r, jnp.sum(cross[r * each : (r + 1) * each], keepdims=True))
    parts_ref[...] = jnp.broadcast_to(row, parts_ref.shape)


def first_norm(residual_ref, systems, rows_all):
    return jnp.sqrt(residual_ref[0:1, 0:systems] / rows_all + EPSILON)


def early_body(
    rows_all,
    residual_ref,
    rec_ref,
    ray_ref,
    bar_in,
    solution_in,
    search_in,
    ray_out,
    damp_out,
    solution_out,
    kept_ref,
    bar_ref,
    solution_ref,
    search_ref,
    damp_s,
    solution_s,
    coef,
    in_sems,
    sems,
):
    systems, columns, _ = bar_ref.shape
    rows = columns // PIECES
    kept = kept_ref.shape[0]
    ins = ((bar_in, bar_ref), (solution_in, solution_ref))
    outs = ((damp_s, damp_out), (solution_s, solution_out))

    def start(n):
        if n < systems * PIECES:
            begin(fetch(n))

    def fetch(n):
        r, p = n // PIECES, n % PIECES
        at = pl.ds(p * rows, rows)
        target = kept_ref.at[r, at] if r < kept else search_ref.at[0, at]
        return pieces(ins, in_sems, r, p, rows) + [
            pltpu.make_async_copy(search_in.at[r, at], target, in_sems.at[r, p, 2])
        ]

    for n in range(AHEAD):
        start(n)
    rho_bar, phi_bar = rec_ref[1:2], rec_ref[2:3]
    beta = first_norm(residual_ref, systems, rows_all)
    rho = jnp.sqrt(rho_bar * rho_bar + beta * beta)
    scales = (1.0 / beta, (rho_bar / rho) * phi_bar / rho)
    for q, scale in enumerate(scales):
        for s in range(systems):
            coef[q, s] = scale[0, s]
    for s in range(systems):
        ray_out[s] = ray_ref[s] * coef[0, s]

    for n in range(systems * PIECES):
        r, p = n // PIECES, n % PIECES
        at = pl.ds(p * rows, rows)
        start(n + AHEAD)
        settle(fetch(n))
        search = kept_ref[r, at, :] if r < kept else search_ref[0, at, :]
        damp_s[r, at, :] = bar_ref[r, at, :] * coef[0, r]
        solution_s[r, at, :] = solution_ref[r, at, :] + search * coef[1, r]
        begin(pieces(outs, sems, r, p, rows))

    wait_all(outs, sems, systems, rows)


def finish_body(
    rows_all,
    cells_all,
    clon,
    corner_ref,
    residual_ref,
    parts_ref,
    rec_ref,
    added_ref,
    kept_ref,
    image_in,
    model_in,
    search_in,
    model_out,
    search_out,
    rec_out,
    image_ref,
    model_ref,
    search_ref,
    model_s,
    search_s,
    coef,
    in_sems,
    sems,
):
    systems, columns, _ = image_ref.shape
    rows = columns // PIECES
    kept = kept_ref.shape[0]
    ins = ((image_in, image_ref), (model_in, model_ref))
    outs = ((model_s, model_out), (search_s, search_out))

    def start(n):
        if n < systems * PIECES:
            begin(fetch(n))

    def fetch(n):
        r, p = n // PIECES, n % PIECES
        copies = pieces(ins, in_sems, r, p, rows)
        if r >= kept:
            at = pl.ds(p * rows, rows)
            copies.append(pltpu.make_async_copy(search_in.at[r, at], search_ref.at[0, at], in_sems.at[r, p, 2]))
        return copies

    for n in range(AHEAD):
        start(n)
    total = jnp.sum(parts_ref[...], axis=0, keepdims=True)
    image_sq, cross, model_sq = (total[:, q * systems : (q + 1) * systems] for q in range(1, 4))
    rho_bar, phi_bar = rec_ref[1:2], rec_ref[2:3]
    beta = first_norm(residual_ref, systems, rows_all)
    update_sq = image_sq / (beta * beta) - 2.0 * cross + beta * beta * model_sq
    alpha = jnp.sqrt(jnp.maximum(update_sq, 0.0) / cells_all + EPSILON)
    rho = jnp.sqrt(rho_bar * rho_bar + beta * beta)
    cosine = rho_bar / rho
    sine = beta / rho
    rec_out[...] = jnp.concatenate([alpha, -cosine * alpha, sine * phi_bar], axis=0)
    scales = (1.0 / (beta * alpha), beta / alpha, sine * alpha / rho)
    for q, scale in enumerate(scales):
        for s in range(systems):
            coef[q, s] = scale[0, s]
    width = PATCH * clon

    for n in range(systems * PIECES):
        r, p = n // PIECES, n % PIECES
        at = pl.ds(p * rows, rows)
        start(n + AHEAD)
        settle(fetch(n))
        search = kept_ref[r, at, :] if r < kept else search_ref[0, at, :]
        new = image_ref[r, at, :] * coef[0, r] - model_ref[r, at, :] * coef[1, r]
        model_s[r, at, :] = new
        search_s[r, at, :] = new - search * coef[2, r]
        for k in range(PATCH):
            first = (corner_ref[0] + k) * clon

            @pl.when((first >= p * rows) & (first < (p + 1) * rows))
            def _():
                cells = pl.ds(pl.multiple_of(first, clon), clon)
                more = added_ref[r * width + k * clon : r * width + (k + 1) * clon, :] * coef[0, r]
                model_s[r, cells, :] = model_s[r, cells, :] + more
                search_s[r, cells, :] = search_s[r, cells, :] + more

        begin(pieces(outs, sems, r, p, rows))

    wait_all(outs, sems, systems, rows)


PIECES = 2
AHEAD = 4


def pieces(pairs, sems, r, p, rows):
    at = pl.ds(pl.multiple_of(p * rows, rows), rows)
    return [pltpu.make_async_copy(a.at[r, at], b.at[r, at], sems.at[r, p, k]) for k, (a, b) in enumerate(pairs)]


def begin(copies):
    for copy in copies:
        copy.start()


def settle(copies):
    for copy in copies:
        copy.wait()


def wait_all(pairs, sems, systems, rows):
    def one(n, _):
        for copy in pieces(pairs, sems, n // PIECES, n % PIECES, rows):
            copy.wait()
        return 0

    lax.fori_loop(0, systems * PIECES, one, 0)


PARTS = 3
HELD = 30


def shifted(x, axis, step):
    count = lax.axis_size(axis)
    if step > 0:
        pairs = [(i, i + 1) for i in range(count - 1)]
    else:
        pairs = [(i + 1, i) for i in range(count - 1)]
    return lax.ppermute(x, axis, pairs)


def exchange(x):
    return lax.all_to_all(x, AXES, split_axis=0, concat_axis=0, tiled=True)


def per_device(
    sensitivity,
    block_ids,
    block_offsets,
    ray_counts,
    ray_vector,
    damping_vector,
    model_vector,
    solution,
    search,
    recurrence,
):
    lat_size, lon_size = lax.axis_size("lat"), lax.axis_size("lon")
    devices = lat_size * lon_size
    tiles, width, depth = sensitivity.shape[2:]
    blocks = block_offsets.shape[-1] - 1
    systems, clat, clon, _ = model_vector.shape
    columns = clat * clon
    cap = max(2 * ((tiles + devices - 1) // devices), 16 // systems)
    slots = devices * cap
    group = cap * systems
    chunk = group + 1
    cells_all = devices * columns * depth
    rows_all = devices * blocks * width + cells_all
    lanes = 128
    full, flat = model_vector.shape, (systems, columns, depth)
    lines = (systems, PATCH * clon, depth)
    here, there, plain = pltpu.VMEM, pltpu.HBM, jax.ShapeDtypeStruct
    dma = pltpu.SemaphoreType.DMA
    model, damping = far(model_vector), far(damping_vector)
    model_flat, damping_flat = far(model_vector.reshape(flat)), far(damping_vector.reshape(flat))

    side = there((systems, 3 * clat, depth), F32)
    band = there((systems, 3, clon, depth), F32)
    asking, north_msg, south_msg, east_msg, west_msg, meta = call(
        functools.partial(flanks_body, columns.bit_length() - 1, blocks),
        "flanks",
        (there((devices, 1, (1 + systems) * depth), F32), band, band, side, side, there((8, lanes), I32)),
        [vmem()] * 3 + [hbm(), hbm()],
        (vmem(),) * 6,
        scratch=[pltpu.VMEM((4, systems, clat, 8, depth), F32), dma((8,))],
        flops=1,
        moved=128 * systems * clat * depth,
    )(far(block_ids), block_offsets, ray_counts, model, damping)
    lists = exchange(asking)
    north = shifted(south_msg, "lat", 1)
    south = shifted(north_msg, "lat", -1)
    west = shifted(east_msg, "lon", 1)
    east = shifted(west_msg, "lon", -1)

    served, wanted, corner, diagonal = call(
        functools.partial(serve_body, cap, clat, clon),
        "serve",
        (
            there((slots * systems, depth), BF16),
            plain((devices, lanes), F32),
            plain((1,), I32),
            plain((4 * systems, depth), F32),
        ),
        [vmem(), hbm()] + [pl.BlockSpec(memory_space=pl.ANY)] * 4,
        (vmem(), vmem(), smem(), vmem()),
        scratch=[pltpu.VMEM(lines, F32), pltpu.VMEM((slots * systems, depth), F32), dma((systems,))],
    )(lists, model_flat, north, south, west, east)
    fetched = exchange(served.reshape(devices, group, depth)).reshape(slots * systems, depth)

    edge, flank = there((systems, clon, depth), F32), there((systems, clat, depth), F32)
    bar, held, *border, sums = call(
        functools.partial(damp_body, clat, clon),
        "damp",
        (
            there(flat, F32),
            here((HELD, width, depth), BF16),
            edge,
            edge,
            flank,
            flank,
            there((1, lanes), F32),
        ),
        [vmem()] * 2 + [hbm()] * 2 + [vmem()] * 4 + [hbm()],
        (hbm(),) + (vmem(),) * 6,
        scratch=[pltpu.VMEM(flat, F32)] * 3 + [pltpu.SMEM((systems,), F32), dma((systems, 3)), dma],
        flops=20 * systems * columns * depth,
        moved=12 * systems * columns * depth,
    )(far(recurrence), diagonal, model_flat, damping_flat, north, south, west, east, far(sensitivity))

    ray_bar, terms = call(
        functools.partial(rays_body, cap, blocks),
        "rays",
        (there(ray_vector.shape, F32), there((devices * chunk, 1, depth), F32)),
        [smem(), vmem(), hbm()] + [vmem()] * 4,
        (vmem(), vmem()),
        scratch=[
            pltpu.VMEM((tiles - HELD, width, depth), BF16),
            pltpu.VMEM((cap + 1, group, depth), BF16),
            pltpu.VMEM((blocks + 1, 16, width), BF16),
            dma((PARTS,)),
        ],
        flops=4 * tiles * width * depth * 16,
        moved=2 * tiles * width * depth,
    )(meta, far(recurrence), far(sensitivity), near(held), fetched, far(ray_vector), far(sums))
    arrived = exchange(terms.reshape(devices, 1, chunk * depth)).reshape(devices * chunk, depth)

    padded = -(-devices * chunk // lanes) * lanes
    height = systems * PATCH * clon
    patch = (height, depth)
    image, sums, patched, model_patch, chosen = call(
        functools.partial(image_body, chunk, clat, clon),
        "image",
        (
            there(flat, F32),
            plain((1, lanes), F32),
            plain(patch, F32),
            plain(patch, F32),
            plain((height, padded), BF16),
        ),
        [smem(), vmem(), hbm()] + [vmem()] * 4 + [hbm(), vmem()],
        (hbm(),) + (vmem(),) * 4,
        scratch=[pltpu.VMEM(flat, F32)] * 3 + [dma((systems, 3))],
        flops=20 * systems * columns * depth,
        moved=12 * systems * columns * depth,
    )(corner, wanted, far(bar), *(far(x) for x in border), model_flat, far(sums))

    added, residual, parts = call(
        functools.partial(combine_body, chunk, systems),
        "combine",
        (plain(patch, F32), plain((1, lanes), F32), there((devices, lanes), F32)),
        [vmem()] * 5,
        (vmem(),) * 3,
        scratch=[pltpu.VMEM((padded, 3 * depth), BF16)],
    )(arrived, chosen, patched, model_patch, sums)
    every = exchange(parts.reshape(devices, 1, lanes)).reshape(devices, lanes)

    search_flat = far(search.reshape(flat))
    ray_out, damp_out, solution_out, kept = call(
        functools.partial(early_body, float(rows_all)),
        "early",
        (there(ray_vector.shape, F32), there(flat, F32), there(flat, F32), here((systems - 1, columns, depth), F32)),
        [vmem()] * 3 + [hbm()] * 3,
        (vmem(), hbm(), hbm(), vmem()),
        scratch=[pltpu.VMEM(flat, F32)] * 2
        + [pltpu.VMEM((1, columns, depth), F32)]
        + [pltpu.VMEM(flat, F32)] * 2
        + [pltpu.SMEM((2, systems), F32), dma((systems, PIECES, 3)), dma((systems, PIECES, 2))],
        mib=32,
        flops=4 * systems * columns * depth,
        moved=20 * systems * columns * depth,
    )(residual, far(recurrence), far(ray_bar), far(bar), far(solution.reshape(flat)), search_flat)
    model_out, search_out, rec_out = call(
        functools.partial(finish_body, float(rows_all), float(cells_all), clon),
        "finish",
        (there(flat, F32), there(flat, F32), there(recurrence.shape, F32)),
        [smem()] + [vmem()] * 5 + [hbm()] * 3,
        (hbm(), hbm(), vmem()),
        scratch=[pltpu.VMEM(flat, F32)] * 2
        + [pltpu.VMEM((1, columns, depth), F32)]
        + [pltpu.VMEM(flat, F32)] * 2
        + [pltpu.SMEM((3, systems), F32), dma((systems, PIECES, 3)), dma((systems, PIECES, 2))],
        mib=32,
        flops=6 * systems * columns * depth,
        moved=20 * systems * columns * depth,
    )(corner, residual, every, far(recurrence), added, near(kept), far(image), model_flat, search_flat)
    fields = (x.reshape(full) for x in (damp_out, model_out, solution_out, search_out))
    return (ray_out, *fields, rec_out)


def solution(mesh):
    fields = P(None, "lat", "lon", None)
    return jax.shard_map(
        per_device,
        mesh=mesh,
        in_specs=(
            P("lat", "lon", None, None, None),
            P("lat", "lon", None),
            P("lat", "lon", None),
            P("lat", "lon"),
            fields,
            fields,
            fields,
            fields,
            fields,
            P(),
        ),
        out_specs=(fields, fields, fields, fields, fields, P()),
        check_vma=False,
    )
```

```python
import functools

import jax
import jax.numpy as jnp
from jax import lax
from jax.experimental import pallas as pl
from jax.experimental.pallas import tpu as pltpu
from jax.sharding import PartitionSpec as P

DAMP_WEIGHT = 0.15
EPSILON = 1e-05
AXES = ("lat", "lon")
PATCH = 4
F32, BF16, I32 = jnp.float32, jnp.bfloat16, jnp.int32


def iota(shape, dim):
    return lax.broadcasted_iota(I32, shape, dim)


def vmem():
    return pl.BlockSpec(memory_space=pltpu.VMEM)


def hbm():
    return pl.BlockSpec(memory_space=pltpu.HBM)


def near(x):
    return pltpu.with_memory_space_constraint(x, pltpu.VMEM)


def far(x):
    return pltpu.with_memory_space_constraint(x, pltpu.HBM)


def smem():
    return pl.BlockSpec(memory_space=pltpu.SMEM)


def call(body, name, out_shape, in_specs, out_specs, scratch=(), grid=(), mib=16, flops=0, moved=0):
    return pl.pallas_call(
        body,
        name=name,
        grid=grid,
        out_shape=out_shape,
        in_specs=in_specs,
        out_specs=out_specs,
        scratch_shapes=list(scratch),
        compiler_params=pltpu.CompilerParams(vmem_limit_bytes=mib * 2**20),
        cost_estimate=pl.CostEstimate(flops=flops, bytes_accessed=moved, transcendentals=0),
    )


STEP = 8


def wanted_column(wanted, cap):
    devices, lanes = wanted.shape
    rows = devices * cap
    spread = jnp.broadcast_to(wanted[:, None, :], (devices, cap, lanes)).reshape(rows, lanes)
    pick = iota((rows, lanes), 1) == (iota((rows, lanes), 0) & (cap - 1))
    return jnp.sum(jnp.where(pick, spread, 0.0), axis=1, keepdims=True)


def rank_body(cap, clat, clon, lists_ref, wanted_ref, corner_ref, diagonal_ref):
    devices = lists_ref.shape[0]
    depth = lists_ref.shape[2] // (diagonal_ref.shape[0] // 4 + 1)
    systems = diagonal_ref.shape[0] // 4
    lanes = 128
    shift = (clat * clon).bit_length() - 1
    lat_at, lon_at = lax.axis_index("lat"), lax.axis_index("lon")
    lat_size, lon_size = lax.axis_size("lat"), lax.axis_size("lon")
    me = lat_at * lon_size + lon_at
    ids = lists_ref[:, 0, 0:lanes].astype(I32)
    column = ids - lax.shift_left(me, shift)
    mine = (column >= 0) & (column < clat * clon) & (ids >= 0)
    first = jnp.min(jnp.where(mine, column, clat * clon))
    corner = jnp.minimum(lax.shift_right_logical(first, clon.bit_length() - 1), clat - PATCH)
    corner_ref[0] = corner
    ahead = (iota((lanes, lanes), 0) < iota((lanes, lanes), 1)).astype(F32).astype(BF16)
    rank = jnp.dot(mine.astype(F32).astype(BF16), ahead, preferred_element_type=F32)
    value = (column - corner * clon + 1).astype(F32)
    at = iota((devices, lanes), 1)
    wanted = jnp.zeros((devices, lanes), F32)
    for c in range(cap):
        picked = jnp.sum(jnp.where(mine & (rank == c), value, 0.0), axis=1, keepdims=True)
        wanted = jnp.where(at == c, picked, wanted)
    wanted_ref[...] = wanted
    for k in range(4):
        lat_to, lon_to = lat_at + 2 * (k // 2) - 1, lon_at + 2 * (k % 2) - 1
        inside = (lat_to >= 0) & (lat_to < lat_size) & (lon_to >= 0) & (lon_to < lon_size)
        source = jnp.where(inside, lat_to * lon_size + lon_to, 0)
        flag = inside.astype(F32)
        for r in range(systems):
            got = lists_ref[source, :, (r + 1) * depth : (r + 2) * depth]
            diagonal_ref[k * systems + r : k * systems + r + 1, :] = got * flag


def serve_body(cap, clon, corner_ref, wanted_ref, model_in, north, south, west, east, served_ref, patch, mixed, sems):
    systems, width, depth = patch.shape
    at = pl.ds(pl.multiple_of(corner_ref[0] * clon, clon), width)
    copies = [pltpu.make_async_copy(model_in.at[r, at], patch.at[r], sems.at[r]) for r in range(systems)]
    for copy in copies:
        copy.start()
    target = wanted_column(wanted_ref[...], cap).astype(I32) - 1
    rows = target.shape[0]
    chosen = (jnp.broadcast_to(target, (rows, width)) == iota((rows, width), 1)).astype(F32).astype(BF16)
    for r in range(systems):
        copies[r].wait()
        table = patch[r].astype(BF16)
        mixed[pl.ds(r, rows, stride=systems), :] = jnp.dot(chosen, table, preferred_element_type=F32)
    served_ref[...] = mixed[...].astype(BF16)


def flanks_body(
    shift,
    blocks,
    ids_ref,
    off_ref,
    count_ref,
    model_in,
    damp_in,
    asking_ref,
    north_ref,
    south_ref,
    east_ref,
    west_ref,
    meta_ref,
    slabs,
    sems,
):
    systems, clat, clon, depth = model_in.shape
    copies = []
    for k, (ref, at) in enumerate(((model_in, 0), (model_in, clon - 8), (damp_in, 0), (damp_in, clon - 8))):
        copies.append(pltpu.make_async_copy(ref.at[:, :, pl.ds(at, 8)], slabs.at[k], sems.at[k]))
    last = clat - 1
    pairs = (
        (model_in.at[:, pl.ds(last - 1, 2)], south_ref.at[:, pl.ds(0, 2)]),
        (damp_in.at[:, pl.ds(last, 1)], south_ref.at[:, pl.ds(2, 1)]),
        (model_in.at[:, pl.ds(0, 2)], north_ref.at[:, pl.ds(0, 2)]),
        (damp_in.at[:, pl.ds(0, 1)], north_ref.at[:, pl.ds(2, 1)]),
    )
    copies += [pltpu.make_async_copy(a, b, sems.at[i + 4]) for i, (a, b) in enumerate(pairs)]
    for copy in copies:
        copy.start()
    tiles = ids_ref.shape[-1]
    lanes = 128
    ids = jnp.concatenate([ids_ref[0], jnp.full((1, lanes - tiles), -1, I32)], axis=1)
    owner = lax.shift_right_arithmetic(ids, shift)
    square = (lanes, lanes)
    down, across = iota(square, 0), iota(square, 1)
    owner_f = jnp.broadcast_to(owner.astype(F32), square)
    owner_col = jnp.sum(jnp.where(down == across, owner_f, 0.0), axis=1, keepdims=True)
    same = jnp.where((owner_f == owner_col) & (down < across), 1.0, 0.0)
    rank = jnp.sum(same, axis=0, keepdims=True).astype(I32)
    lane = iota((1, lanes), 1)
    block = jnp.zeros((1, lanes), I32)
    starts = off_ref[0]
    for b in range(1, blocks + 1):
        block = block + (lane >= jnp.broadcast_to(starts[:, b : b + 1], (1, lanes))).astype(I32)
    count = jnp.broadcast_to(count_ref[...], (1, lanes))
    meta_ref[...] = jnp.concatenate([owner, rank, block, count] + [owner] * 4, axis=0)
    for copy in copies:
        copy.wait()
    listed = ids.astype(F32)
    corners = [
        [slabs[k % 2, r, (k // 2) * last, (k % 2) * 7 : (k % 2) * 7 + 1] for r in range(systems)]
        for k in range(4)
    ]
    lat_at, lon_at = lax.axis_index("lat"), lax.axis_index("lon")
    width = lax.axis_size("lon")
    for e in range(asking_ref.shape[0]):
        asking_ref[e, :, 0:depth] = listed
        to_south, to_east = e // width > lat_at, e % width > lon_at
        for r in range(systems):
            upper = jnp.where(to_east, corners[1][r], corners[0][r])
            lower = jnp.where(to_east, corners[3][r], corners[2][r])
            asking_ref[e, :, (r + 1) * depth : (r + 2) * depth] = jnp.where(to_south, lower, upper)
    rows = slabs.reshape(4, systems, clat * 8, depth)
    for r in range(systems):
        for out, slab, near_at, beyond in ((east_ref, 1, 7, 6), (west_ref, 0, 0, 1)):
            out[r, 0:clat] = rows[slab, r, pl.ds(near_at, clat, stride=8), :]
            out[r, clat : 2 * clat] = rows[slab, r, pl.ds(beyond, clat, stride=8), :]
            out[r, 2 * clat : 3 * clat] = rows[slab + 2, r, pl.ds(near_at, clat, stride=8), :]


def six(x, north, south, west, east):
    lane = iota(x.shape, 1)
    rows, depth = x.shape
    left, right = pltpu.roll(x, 1, 0), pltpu.roll(x, rows - 1, 0)
    ends = (8, depth)
    row = iota(ends, 0)
    left = jnp.concatenate([jnp.where(row == 0, jnp.broadcast_to(west, ends), left[:8]), left[8:]], axis=0)
    right = jnp.concatenate([right[:-8], jnp.where(row == 7, jnp.broadcast_to(east, ends), right[-8:])], axis=0)
    above = jnp.where(lane == 0, 0.0, pltpu.roll(x, 1, 1))
    below = jnp.where(lane == depth - 1, 0.0, pltpu.roll(x, depth - 1, 1))
    beside = north + south + left + right + above + below
    return DAMP_WEIGHT * (6.0 * x - beside)


def fold(x):
    parts = [x[i * 8 : (i + 1) * 8] for i in range(x.shape[0] // 8)]
    return functools.reduce(lambda a, b: a + b, parts)


def place(row, lane, value):
    return row + jnp.where(iota(row.shape, 1) == lane, jnp.broadcast_to(value, row.shape), 0.0)


def line(ref, r, i, clon):
    return ref[r, pl.ds(pl.multiple_of(i * clon, clon), clon), :]


def stencils(ref, r, k, clat, clon, first, last, west, east):
    base = k * STEP
    for j in range(STEP):
        i = base + j
        x = line(ref, r, i, clon)
        if j == 0:
            above = jnp.where(k > 0, line(ref, r, jnp.maximum(i - 1, 0), clon), first)
        else:
            above = line(ref, r, i - 1, clon)
        if j == STEP - 1:
            below = jnp.where(i + 1 < clat, line(ref, r, jnp.minimum(i + 1, clat - 1), clon), last)
        else:
            below = line(ref, r, i + 1, clon)
        yield i, x, six(x, above, below, west[pl.ds(i, 1)], east[pl.ds(i, 1)])


def damp_body(
    clat,
    clon,
    rec_ref,
    diagonal_ref,
    model_in,
    damp_in,
    north_ref,
    south_ref,
    west_ref,
    east_ref,
    tiles_in,
    bar_sent,
    held_out,
    north_out,
    south_out,
    west_out,
    east_out,
    sums_out,
    model_ref,
    damp_ref,
    bar_out,
    alphas,
    sems,
    hold_sem,
):
    systems, _, depth = model_ref.shape

    def incoming(r):
        return (
            pltpu.make_async_copy(model_in.at[r], model_ref.at[r], sems.at[r, 0]),
            pltpu.make_async_copy(damp_in.at[r], damp_ref.at[r], sems.at[r, 1]),
        )

    def outgoing(r):
        return pltpu.make_async_copy(bar_out.at[r], bar_sent.at[r], sems.at[r, 2])

    holding = pltpu.make_async_copy(tiles_in.at[0, 0, pl.ds(0, HELD)], held_out, hold_sem)
    for r in range(systems):
        for copy in incoming(r):
            copy.start()
    holding.start()
    for r in range(systems):
        alphas[r] = jnp.sum(rec_ref[0:1, r : r + 1])
    lat_at, lon_at = lax.axis_index("lat"), lax.axis_index("lon")
    has_north = (lat_at > 0).astype(F32)
    has_south = (lat_at < lax.axis_size("lat") - 1).astype(F32)
    has_west = (lon_at > 0).astype(F32)
    has_east = (lon_at < lax.axis_size("lon") - 1).astype(F32)

    def diagonal(k, r):
        return diagonal_ref[pl.ds(k * systems + r, 1), :]

    def system(r, row):
        alpha = alphas[r]
        for copy in incoming(r):
            copy.wait()

        def side(ref, own, flag, east):
            x, beyond, old = ref[r, 0:clat], ref[r, clat : 2 * clat], ref[r, 2 * clat : 3 * clat]
            upper, lower = diagonal(east, r), diagonal(2 + east, r)
            return (six(x, beyond, own, upper, lower) - alpha * old) * flag

        west_out[r] = side(west_ref, model_ref[r, pl.ds(0, clat, stride=clon), :], has_west, 0)
        east_out[r] = side(east_ref, model_ref[r, pl.ds(clon - 1, clat, stride=clon), :], has_east, 1)
        top, bottom = line(model_ref, r, 0, clon), line(model_ref, r, clat - 1, clon)
        edge = six(north_ref[r, 1], north_ref[r, 0], top, diagonal(0, r), diagonal(1, r))
        north_out[r] = has_north * (edge - alpha * north_ref[r, 2])
        edge = six(south_ref[r, 0], bottom, south_ref[r, 1], diagonal(2, r), diagonal(3, r))
        south_out[r] = has_south * (edge - alpha * south_ref[r, 2])

        def damped(k, acc):
            bar_sq, model_sq = acc
            ends = (north_ref[r, 1], south_ref[r, 0], west_ref.at[r], east_ref.at[r])
            for i, x, got in stencils(model_ref, r, k, clat, clon, *ends):
                bar = got - alpha * line(damp_ref, r, i, clon)
                bar_out[r, pl.ds(pl.multiple_of(i * clon, clon), clon), :] = bar
                bar_sq, model_sq = bar_sq + fold(bar * bar), model_sq + fold(x * x)
            return bar_sq, model_sq

        zero = jnp.zeros((8, depth), F32)
        bar_sq, model_sq = lax.fori_loop(0, clat // STEP, damped, (zero, zero))
        outgoing(r).start()
        row = place(row, r, jnp.sum(bar_sq, keepdims=True))
        return place(row, 3 * systems + r, jnp.sum(model_sq, keepdims=True))

    sums_out[...] = lax.fori_loop(0, systems, system, jnp.zeros((1, depth), F32))
    holding.wait()
    for r in range(systems):
        outgoing(r).wait()


def image_body(
    chunk,
    clat,
    clon,
    corner_ref,
    wanted_ref,
    bar_in,
    north_ref,
    south_ref,
    west_ref,
    east_ref,
    model_in,
    sums_ref,
    image_sent,
    sums_out,
    patch_out,
    model_patch_out,
    chosen_out,
    bar_ref,
    model_ref,
    image_out,
    sems,
):
    systems, _, depth = model_ref.shape

    def incoming(r):
        return (
            pltpu.make_async_copy(bar_in.at[r], bar_ref.at[r], sems.at[r, 0]),
            pltpu.make_async_copy(model_in.at[r], model_ref.at[r], sems.at[r, 1]),
        )

    def outgoing(r):
        return pltpu.make_async_copy(image_out.at[r], image_sent.at[r], sems.at[r, 2])

    for r in range(systems):
        for copy in incoming(r):
            copy.start()
    corner = corner_ref[0]
    wanted = wanted_ref[...]
    devices = wanted.shape[0]
    height, slots = chosen_out.shape
    width = PATCH * clon
    at = iota((1, slots), 1)
    source = jnp.floor((at.astype(F32) + 0.5) * (1.0 / chunk)).astype(I32)
    inner = at - source * chunk
    from_e = (jnp.broadcast_to(source, (devices, slots)) == iota((devices, slots), 0)).astype(F32).astype(BF16)
    turned = jnp.transpose(wanted)[0:8].astype(BF16)
    listed = jnp.dot(turned, from_e, preferred_element_type=F32)
    slot_of = lax.shift_right_logical(inner, systems.bit_length() - 1)
    mine = jnp.broadcast_to(slot_of, listed.shape) == iota(listed.shape, 0)
    flat = jnp.sum(jnp.where(mine, listed, 0.0), axis=0, keepdims=True).astype(I32)
    used = (flat > 0) & (inner < chunk - 1)
    target = jnp.where(used, (inner & (systems - 1)) * width + flat - 1, -1)
    for k in range(height // 64):
        shape = (64, slots)
        hit = jnp.broadcast_to(target, shape) == iota(shape, 0) + k * 64
        chosen_out[k * 64 : (k + 1) * 64] = hit.astype(F32).astype(BF16)

    def system(r, row):
        for copy in incoming(r):
            copy.wait()

        def imaged(k, acc):
            image_sq, cross = acc
            ends = (north_ref[r], south_ref[r], west_ref.at[r], east_ref.at[r])
            for i, x, image in stencils(bar_ref, r, k, clat, clon, *ends):
                image_out[r, pl.ds(pl.multiple_of(i * clon, clon), clon), :] = image
                image_sq = image_sq + fold(image * image)
                cross = cross + fold(image * line(model_ref, r, i, clon))
            return image_sq, cross

        zero = jnp.zeros((8, depth), F32)
        image_sq, cross = lax.fori_loop(0, clat // STEP, imaged, (zero, zero))
        outgoing(r).start()
        here = pl.ds(pl.multiple_of(corner * clon, clon), width)
        there = pl.ds(pl.multiple_of(r * width, width), width)
        patch_out[there, :] = image_out[r, here, :]
        model_patch_out[there, :] = model_ref[r, here, :]
        row = place(row, systems + r, jnp.sum(image_sq, keepdims=True))
        return place(row, 2 * systems + r, jnp.sum(cross, keepdims=True))

    row = lax.fori_loop(0, systems, system, sums_ref[...])
    sums_out[...] = place(row, depth - 1, corner.astype(F32))
    for r in range(systems):
        outgoing(r).wait()


def rays_body(
    cap, blocks, meta_ref, held_ref, fetched_ref, tiles_in, *refs
):
    rec_in, old_in, sums_in, bar_ref, term_ref, rest_ref, masks, lows, rec_ref, old_ref, sums_ref, sems = refs
    tiles, width, depth = tiles_in.shape[2:]
    small = [
        pltpu.make_async_copy(a, b, sems.at[PARTS + k])
        for k, (a, b) in enumerate(((rec_in, rec_ref), (old_in, old_ref), (sums_in, sums_ref)))
    ]
    part = -(-(tiles - HELD) // PARTS)
    copies = []
    for k in range(PARTS):
        count = min(part, tiles - HELD - k * part)
        source = tiles_in.at[0, 0, pl.ds(HELD + k * part, count)]
        copies.append(pltpu.make_async_copy(source, rest_ref.at[pl.ds(k * part, count)], sems.at[k]))
    for copy in copies + small:
        copy.start()

    def tile(t):
        return held_ref[t] if t < HELD else rest_ref[t - HELD]

    systems = old_ref.shape[0]
    group = cap * systems
    chunk = group + 1
    devices = term_ref.shape[0] // chunk
    for c in range(cap + 1):
        here = lax.shift_right_logical(iota((group, depth), 0), systems.bit_length() - 1) == c
        masks[c] = here.astype(F32).astype(BF16)
    term_ref[...] = jnp.zeros(term_ref.shape, F32)
    lows[...] = jnp.zeros(lows.shape, BF16)
    total = jnp.zeros((blocks * group, width), F32)
    for t in range(tiles):
        if t >= HELD and (t - HELD) % part == 0:
            copies[(t - HELD) // part].wait()
        owner, rank, block = meta_ref[0, t], meta_ref[1, t], meta_ref[2, t]
        rows = fetched_ref[pl.ds(pl.multiple_of(owner * group, group), group), :]
        left = jnp.concatenate(
            [rows * masks[jnp.where(block == b, rank, cap)] for b in range(blocks)], axis=0
        )
        total = total + lax.dot_general(
            left, tile(t), (((1,), (1,)), ((), ())), preferred_element_type=F32
        )
    for copy in small:
        copy.wait()
    square = jnp.zeros((systems, width), F32)
    for b in range(blocks):
        traced = jnp.zeros((systems, width), F32)
        for c in range(cap):
            at = b * group + c * systems
            traced = traced + total[at : at + systems]
        old = jnp.concatenate(
            [old_ref[r, 0, :, b * width : (b + 1) * width] * rec_ref[0:1, r : r + 1] for r in range(systems)], axis=0
        )
        live = iota((systems, width), 1) + b * width < meta_ref[3, 0]
        bar = jnp.where(live, traced - old, 0.0)
        square = square + bar * bar
        for r in range(systems):
            bar_ref[r, 0, :, b * width : (b + 1) * width] = bar[r : r + 1]
        lows[b] = jnp.concatenate([bar, jnp.zeros((16 - systems, width), F32)], axis=0).astype(BF16)
    ray_sq = jnp.sum(square, axis=1, keepdims=True)
    part = sums_ref[...]
    for r in range(systems):
        part = place(part, r, ray_sq[r : r + 1])
    for e in range(devices):
        term_ref[e * chunk + group] = part
    for t in range(tiles):
        row = meta_ref[0, t] * chunk + meta_ref[1, t] * systems
        term = jnp.dot(lows[meta_ref[2, t]], tile(t), preferred_element_type=F32)
        for r in range(systems):
            term_ref[row + r] = term[r : r + 1]


def combine_body(chunk, systems, terms_ref, chosen_ref, patch_ref, model_patch_ref, sums_ref, added_ref, residual_ref, parts_ref, split):
    arrived, depth = terms_ref.shape
    devices = parts_ref.shape[0]
    width = patch_ref.shape[0]
    x = terms_ref[...]
    high = x.astype(BF16)
    rest = x - high.astype(F32)
    middle = rest.astype(BF16)
    low = (rest - middle.astype(F32)).astype(BF16)
    padded = split.shape[0]
    if padded > arrived:
        split[arrived:] = jnp.zeros((padded - arrived, split.shape[1]), BF16)
    split[0:arrived, 0:depth] = high
    split[0:arrived, depth : 2 * depth] = middle
    split[0:arrived, 2 * depth :] = low
    three = jnp.dot(chosen_ref[...], split[...], preferred_element_type=F32)
    added = three[:, 0:depth] + (three[:, depth : 2 * depth] + three[:, 2 * depth :])
    added_ref[...] = added
    every = terms_ref[pl.ds(chunk - 1, devices, stride=chunk), :]
    total = jnp.sum(every, axis=0, keepdims=True)
    residual_ref[...] = jnp.where(iota(total.shape, 1) == depth - 1, sums_ref[...], total)
    square = added * (2.0 * patch_ref[...] + added)
    cross = added * model_patch_ref[...]
    row = sums_ref[...]
    each = width // systems
    for r in range(systems):
        row = place(row, systems + r, jnp.sum(square[r * each : (r + 1) * each], keepdims=True))
        row = place(row, 2 * systems + r, jnp.sum(cross[r * each : (r + 1) * each], keepdims=True))
    parts_ref[...] = jnp.broadcast_to(row, parts_ref.shape)


def first_norm(residual_ref, systems, rows_all):
    return jnp.sqrt(residual_ref[0:1, 0:systems] / rows_all + EPSILON)


def early_body(
    rows_all,
    residual_ref,
    rec_ref,
    ray_ref,
    bar_in,
    solution_in,
    search_in,
    ray_out,
    damp_out,
    solution_out,
    kept_ref,
    bar_ref,
    solution_ref,
    search_ref,
    damp_s,
    solution_s,
    coef,
    in_sems,
    sems,
):
    systems, columns, _ = bar_ref.shape
    rows = columns // PIECES
    kept = kept_ref.shape[0]
    ins = ((bar_in, bar_ref), (solution_in, solution_ref))
    outs = ((damp_s, damp_out), (solution_s, solution_out))

    def start(n):
        if n < systems * PIECES:
            begin(fetch(n))

    def fetch(n):
        r, p = n // PIECES, n % PIECES
        at = pl.ds(p * rows, rows)
        target = kept_ref.at[r, at] if r < kept else search_ref.at[0, at]
        return pieces(ins, in_sems, r, p, rows) + [
            pltpu.make_async_copy(search_in.at[r, at], target, in_sems.at[r, p, 2])
        ]

    for n in range(AHEAD):
        start(n)
    rho_bar, phi_bar = rec_ref[1:2], rec_ref[2:3]
    beta = first_norm(residual_ref, systems, rows_all)
    rho = jnp.sqrt(rho_bar * rho_bar + beta * beta)
    scales = (1.0 / beta, (rho_bar / rho) * phi_bar / rho)
    for q, scale in enumerate(scales):
        for s in range(systems):
            coef[q, s] = scale[0, s]
    for s in range(systems):
        ray_out[s] = ray_ref[s] * coef[0, s]

    for n in range(systems * PIECES):
        r, p = n // PIECES, n % PIECES
        at = pl.ds(p * rows, rows)
        start(n + AHEAD)
        settle(fetch(n))
        search = kept_ref[r, at, :] if r < kept else search_ref[0, at, :]
        damp_s[r, at, :] = bar_ref[r, at, :] * coef[0, r]
        solution_s[r, at, :] = solution_ref[r, at, :] + search * coef[1, r]
        begin(pieces(outs, sems, r, p, rows))

    wait_all(outs, sems, systems, rows)


def finish_body(
    rows_all,
    cells_all,
    clon,
    residual_ref,
    parts_ref,
    added_ref,
    kept_ref,
    image_in,
    model_in,
    search_in,
    rec_in,
    model_out,
    search_out,
    rec_sent,
    image_ref,
    model_ref,
    search_ref,
    model_s,
    search_s,
    rec_ref,
    rec_out,
    coef,
    in_sems,
    sems,
    rec_sems,
):
    systems, columns, depth = image_ref.shape
    rec_copy = pltpu.make_async_copy(rec_in, rec_ref, rec_sems.at[0])
    rec_copy.start()
    rows = columns // PIECES
    kept = kept_ref.shape[0]
    ins = ((image_in, image_ref), (model_in, model_ref))
    outs = ((model_s, model_out), (search_s, search_out))

    def start(n):
        if n < systems * PIECES:
            begin(fetch(n))

    def fetch(n):
        r, p = n // PIECES, n % PIECES
        copies = pieces(ins, in_sems, r, p, rows)
        if r >= kept:
            at = pl.ds(p * rows, rows)
            copies.append(pltpu.make_async_copy(search_in.at[r, at], search_ref.at[0, at], in_sems.at[r, p, 2]))
        return copies

    for n in range(AHEAD):
        start(n)
    corner = residual_ref[0, depth - 1].astype(I32)
    total = jnp.sum(parts_ref[...], axis=0, keepdims=True)
    rec_copy.wait()
    image_sq, cross, model_sq = (total[:, q * systems : (q + 1) * systems] for q in range(1, 4))
    rho_bar, phi_bar = rec_ref[1:2], rec_ref[2:3]
    beta = first_norm(residual_ref, systems, rows_all)
    update_sq = image_sq / (beta * beta) - 2.0 * cross + beta * beta * model_sq
    alpha = jnp.sqrt(jnp.maximum(update_sq, 0.0) / cells_all + EPSILON)
    rho = jnp.sqrt(rho_bar * rho_bar + beta * beta)
    cosine = rho_bar / rho
    sine = beta / rho
    rec_out[...] = jnp.concatenate([alpha, -cosine * alpha, sine * phi_bar], axis=0)
    rec_done = pltpu.make_async_copy(rec_out, rec_sent, rec_sems.at[1])
    rec_done.start()
    scales = (1.0 / (beta * alpha), beta / alpha, sine * alpha / rho)
    for q, scale in enumerate(scales):
        for s in range(systems):
            coef[q, s] = scale[0, s]
    width = PATCH * clon

    for n in range(systems * PIECES):
        r, p = n // PIECES, n % PIECES
        at = pl.ds(p * rows, rows)
        start(n + AHEAD)
        settle(fetch(n))
        search = kept_ref[r, at, :] if r < kept else search_ref[0, at, :]
        new = image_ref[r, at, :] * coef[0, r] - model_ref[r, at, :] * coef[1, r]
        model_s[r, at, :] = new
        search_s[r, at, :] = new - search * coef[2, r]
        for k in range(PATCH):
            first = (corner + k) * clon

            @pl.when((first >= p * rows) & (first < (p + 1) * rows))
            def _():
                cells = pl.ds(pl.multiple_of(first, clon), clon)
                more = added_ref[r * width + k * clon : r * width + (k + 1) * clon, :] * coef[0, r]
                model_s[r, cells, :] = model_s[r, cells, :] + more
                search_s[r, cells, :] = search_s[r, cells, :] + more

        begin(pieces(outs, sems, r, p, rows))

    wait_all(outs, sems, systems, rows)
    rec_done.wait()


PIECES = 2
AHEAD = 4


def pieces(pairs, sems, r, p, rows):
    at = pl.ds(pl.multiple_of(p * rows, rows), rows)
    return [pltpu.make_async_copy(a.at[r, at], b.at[r, at], sems.at[r, p, k]) for k, (a, b) in enumerate(pairs)]


def begin(copies):
    for copy in copies:
        copy.start()


def settle(copies):
    for copy in copies:
        copy.wait()


def wait_all(pairs, sems, systems, rows):
    def one(n, _):
        for copy in pieces(pairs, sems, n // PIECES, n % PIECES, rows):
            copy.wait()
        return 0

    lax.fori_loop(0, systems * PIECES, one, 0)


PARTS = 3
HELD = 30


def shifted(x, axis, step):
    count = lax.axis_size(axis)
    if step > 0:
        pairs = [(i, i + 1) for i in range(count - 1)]
    else:
        pairs = [(i + 1, i) for i in range(count - 1)]
    return lax.ppermute(x, axis, pairs)


def exchange(x):
    return lax.all_to_all(x, AXES, split_axis=0, concat_axis=0, tiled=True)


def per_device(
    sensitivity,
    block_ids,
    block_offsets,
    ray_counts,
    ray_vector,
    damping_vector,
    model_vector,
    solution,
    search,
    recurrence,
):
    lat_size, lon_size = lax.axis_size("lat"), lax.axis_size("lon")
    devices = lat_size * lon_size
    tiles, width, depth = sensitivity.shape[2:]
    blocks = block_offsets.shape[-1] - 1
    systems, clat, clon, _ = model_vector.shape
    columns = clat * clon
    cap = max(2 * ((tiles + devices - 1) // devices), 16 // systems)
    slots = devices * cap
    group = cap * systems
    chunk = group + 1
    cells_all = devices * columns * depth
    rows_all = devices * blocks * width + cells_all
    lanes = 128
    full, flat = model_vector.shape, (systems, columns, depth)
    lines = (systems, PATCH * clon, depth)
    here, there, plain = pltpu.VMEM, pltpu.HBM, jax.ShapeDtypeStruct
    dma = pltpu.SemaphoreType.DMA
    model, damping = far(model_vector), far(damping_vector)
    model_flat, damping_flat = far(model_vector.reshape(flat)), far(damping_vector.reshape(flat))

    side = there((systems, 3 * clat, depth), F32)
    band = there((systems, 3, clon, depth), F32)
    asking, north_msg, south_msg, east_msg, west_msg, meta = call(
        functools.partial(flanks_body, columns.bit_length() - 1, blocks),
        "flanks",
        (there((devices, 1, (1 + systems) * depth), F32), band, band, side, side, there((8, lanes), I32)),
        [vmem()] * 3 + [hbm(), hbm()],
        (vmem(),) * 6,
        scratch=[pltpu.VMEM((4, systems, clat, 8, depth), F32), dma((8,))],
        flops=1,
        moved=128 * systems * clat * depth,
    )(far(block_ids), block_offsets, ray_counts, model, damping)
    lists = exchange(asking)
    north = shifted(south_msg, "lat", 1)
    south = shifted(north_msg, "lat", -1)
    west = shifted(east_msg, "lon", 1)
    east = shifted(west_msg, "lon", -1)

    wanted, corner, diagonal = call(
        functools.partial(rank_body, cap, clat, clon),
        "rank",
        (plain((devices, lanes), F32), plain((1,), I32), plain((4 * systems, depth), F32)),
        [vmem()],
        (vmem(), smem(), vmem()),
        flops=2 * devices * lanes * lanes,
        moved=24 * systems * columns * depth,
    )(lists)
    served = call(
        functools.partial(serve_body, cap, clon),
        "serve",
        there((slots * systems, depth), BF16),
        [smem(), vmem(), hbm()] + [pl.BlockSpec(memory_space=pl.ANY)] * 4,
        vmem(),
        scratch=[pltpu.VMEM(lines, F32), pltpu.VMEM((slots * systems, depth), F32), dma((systems,))],
    )(corner, wanted, model_flat, north, south, west, east)
    fetched = exchange(served.reshape(devices, group, depth)).reshape(slots * systems, depth)

    edge, flank = there((systems, clon, depth), F32), there((systems, clat, depth), F32)
    bar, held, *border, sums = call(
        functools.partial(damp_body, clat, clon),
        "damp",
        (
            there(flat, F32),
            here((HELD, width, depth), BF16),
            edge,
            edge,
            flank,
            flank,
            there((1, lanes), F32),
        ),
        [vmem()] * 2 + [hbm()] * 2 + [vmem()] * 4 + [hbm()],
        (hbm(),) + (vmem(),) * 6,
        scratch=[pltpu.VMEM(flat, F32)] * 3 + [pltpu.SMEM((systems,), F32), dma((systems, 3)), dma],
        flops=20 * systems * columns * depth,
        moved=12 * systems * columns * depth,
    )(far(recurrence), diagonal, model_flat, damping_flat, north, south, west, east, far(sensitivity))

    ray_bar, terms = call(
        functools.partial(rays_body, cap, blocks),
        "rays",
        (there(ray_vector.shape, F32), there((devices * chunk, 1, depth), F32)),
        [smem(), vmem(), vmem()] + [hbm()] * 4,
        (vmem(), vmem()),
        scratch=[
            pltpu.VMEM((tiles - HELD, width, depth), BF16),
            pltpu.VMEM((cap + 1, group, depth), BF16),
            pltpu.VMEM((blocks + 1, 16, width), BF16),
            pltpu.VMEM(recurrence.shape, F32),
            pltpu.VMEM(ray_vector.shape, F32),
            pltpu.VMEM((1, lanes), F32),
            dma((PARTS + 3,)),
        ],
        flops=4 * tiles * width * depth * 16,
        moved=2 * tiles * width * depth,
    )(meta, near(held), fetched, far(sensitivity), far(recurrence), far(ray_vector), far(sums))
    arrived = exchange(terms.reshape(devices, 1, chunk * depth)).reshape(devices * chunk, depth)

    padded = -(-devices * chunk // lanes) * lanes
    height = systems * PATCH * clon
    patch = (height, depth)
    image, sums, patched, model_patch, chosen = call(
        functools.partial(image_body, chunk, clat, clon),
        "image",
        (
            there(flat, F32),
            plain((1, lanes), F32),
            plain(patch, F32),
            plain(patch, F32),
            plain((height, padded), BF16),
        ),
        [smem(), vmem(), hbm()] + [vmem()] * 4 + [hbm(), vmem()],
        (hbm(),) + (vmem(),) * 4,
        scratch=[pltpu.VMEM(flat, F32)] * 3 + [dma((systems, 3))],
        flops=20 * systems * columns * depth,
        moved=12 * systems * columns * depth,
    )(corner, wanted, far(bar), *(far(x) for x in border), model_flat, far(sums))

    added, residual, parts = call(
        functools.partial(combine_body, chunk, systems),
        "combine",
        (plain(patch, F32), plain((1, lanes), F32), there((devices, lanes), F32)),
        [vmem()] * 5,
        (vmem(),) * 3,
        scratch=[pltpu.VMEM((padded, 3 * depth), BF16)],
    )(arrived, chosen, patched, model_patch, sums)
    every = exchange(parts.reshape(devices, 1, lanes)).reshape(devices, lanes)

    search_flat = far(search.reshape(flat))
    ray_out, damp_out, solution_out, kept = call(
        functools.partial(early_body, float(rows_all)),
        "early",
        (there(ray_vector.shape, F32), there(flat, F32), there(flat, F32), here((systems - 1, columns, depth), F32)),
        [vmem()] * 3 + [hbm()] * 3,
        (vmem(), hbm(), hbm(), vmem()),
        scratch=[pltpu.VMEM(flat, F32)] * 2
        + [pltpu.VMEM((1, columns, depth), F32)]
        + [pltpu.VMEM(flat, F32)] * 2
        + [pltpu.SMEM((2, systems), F32), dma((systems, PIECES, 3)), dma((systems, PIECES, 2))],
        mib=32,
        flops=4 * systems * columns * depth,
        moved=20 * systems * columns * depth,
    )(residual, far(recurrence), far(ray_bar), far(bar), far(solution.reshape(flat)), search_flat)
    model_out, search_out, rec_out = call(
        functools.partial(finish_body, float(rows_all), float(cells_all), clon),
        "finish",
        (there(flat, F32), there(flat, F32), there(recurrence.shape, F32)),
        [vmem()] * 4 + [hbm()] * 4,
        (hbm(),) * 3,
        scratch=[pltpu.VMEM(flat, F32)] * 2
        + [pltpu.VMEM((1, columns, depth), F32)]
        + [pltpu.VMEM(flat, F32)] * 2
        + [pltpu.VMEM(recurrence.shape, F32)] * 2
        + [pltpu.SMEM((3, systems), F32), dma((systems, PIECES, 3)), dma((systems, PIECES, 2)), dma((2,))],
        mib=32,
        flops=6 * systems * columns * depth,
        moved=20 * systems * columns * depth,
    )(residual, every, added, near(kept), far(image), model_flat, search_flat, far(recurrence))
    fields = (x.reshape(full) for x in (damp_out, model_out, solution_out, search_out))
    return (ray_out, *fields, rec_out)


def solution(mesh):
    fields = P(None, "lat", "lon", None)
    return jax.shard_map(
        per_device,
        mesh=mesh,
        in_specs=(
            P("lat", "lon", None, None, None),
            P("lat", "lon", None),
            P("lat", "lon", None),
            P("lat", "lon"),
            fields,
            fields,
            fields,
            fields,
            fields,
            P(),
        ),
        out_specs=(fields, fields, fields, fields, fields, P()),
        check_vma=False,
    )
```

```python
import functools

import jax
import jax.numpy as jnp
from jax import lax
from jax.experimental import pallas as pl
from jax.experimental.pallas import tpu as pltpu
from jax.sharding import PartitionSpec as P

DAMP_WEIGHT = 0.15
EPSILON = 1e-05
AXES = ("lat", "lon")
PATCH = 4
F32, BF16, I32 = jnp.float32, jnp.bfloat16, jnp.int32


def iota(shape, dim):
    return lax.broadcasted_iota(I32, shape, dim)


def vmem():
    return pl.BlockSpec(memory_space=pltpu.VMEM)


def hbm():
    return pl.BlockSpec(memory_space=pltpu.HBM)


def near(x):
    return pltpu.with_memory_space_constraint(x, pltpu.VMEM)


def far(x):
    return pltpu.with_memory_space_constraint(x, pltpu.HBM)


def smem():
    return pl.BlockSpec(memory_space=pltpu.SMEM)


def call(body, name, out_shape, in_specs, out_specs, scratch=(), grid=(), mib=16, flops=0, moved=0):
    return pl.pallas_call(
        body,
        name=name,
        grid=grid,
        out_shape=out_shape,
        in_specs=in_specs,
        out_specs=out_specs,
        scratch_shapes=list(scratch),
        compiler_params=pltpu.CompilerParams(vmem_limit_bytes=mib * 2**20),
        cost_estimate=pl.CostEstimate(flops=flops, bytes_accessed=moved, transcendentals=0),
    )


STEP = 8


def wanted_column(wanted, cap):
    devices, lanes = wanted.shape
    rows = devices * cap
    spread = jnp.broadcast_to(wanted[:, None, :], (devices, cap, lanes)).reshape(rows, lanes)
    pick = iota((rows, lanes), 1) == (iota((rows, lanes), 0) & (cap - 1))
    return jnp.sum(jnp.where(pick, spread, 0.0), axis=1, keepdims=True)


def serve_body(cap, clat, clon, lists_ref, model_in, north, south, west, east, served_ref, wanted_ref, corner_ref, diagonal_ref, patch, mixed, sems):
    systems, width, depth = patch.shape
    devices = lists_ref.shape[0]
    lanes = 128
    shift = (clat * clon).bit_length() - 1
    me = lax.axis_index("lat") * lax.axis_size("lon") + lax.axis_index("lon")
    ids = lists_ref[:, 0, 0:lanes].astype(I32)
    column = ids - lax.shift_left(me, shift)
    mine = (column >= 0) & (column < clat * clon) & (ids >= 0)
    first = jnp.min(jnp.where(mine, column, clat * clon))
    corner = jnp.minimum(lax.shift_right_logical(first, clon.bit_length() - 1), clat - PATCH)
    corner_ref[0] = corner
    at = pl.ds(pl.multiple_of(corner * clon, clon), width)
    copies = [pltpu.make_async_copy(model_in.at[r, at], patch.at[r], sems.at[r]) for r in range(systems)]
    for copy in copies:
        copy.start()
    ahead = (iota((lanes, lanes), 0) < iota((lanes, lanes), 1)).astype(F32).astype(BF16)
    rank = jnp.dot(mine.astype(F32).astype(BF16), ahead, preferred_element_type=F32)
    value = (column - corner * clon + 1).astype(F32)
    at = iota((devices, lanes), 1)
    wanted = jnp.zeros((devices, lanes), F32)
    for c in range(cap):
        picked = jnp.sum(jnp.where(mine & (rank == c), value, 0.0), axis=1, keepdims=True)
        wanted = jnp.where(at == c, picked, wanted)
    wanted_ref[...] = wanted
    target = wanted_column(wanted, cap).astype(I32) - 1
    rows = target.shape[0]
    chosen = (jnp.broadcast_to(target, (rows, width)) == iota((rows, width), 1)).astype(F32).astype(BF16)
    for r in range(systems):
        copies[r].wait()
        table = patch[r].astype(BF16)
        mixed[pl.ds(r, rows, stride=systems), :] = jnp.dot(chosen, table, preferred_element_type=F32)
    served_ref[...] = mixed[...].astype(BF16)
    lat_at, lon_at = lax.axis_index("lat"), lax.axis_index("lon")
    lat_size, lon_size = lax.axis_size("lat"), lax.axis_size("lon")
    for k in range(4):
        lat_to, lon_to = lat_at + 2 * (k // 2) - 1, lon_at + 2 * (k % 2) - 1
        inside = (lat_to >= 0) & (lat_to < lat_size) & (lon_to >= 0) & (lon_to < lon_size)
        source = jnp.where(inside, lat_to * lon_size + lon_to, 0)
        flag = inside.astype(F32)
        for r in range(systems):
            got = lists_ref[source, :, (r + 1) * depth : (r + 2) * depth]
            diagonal_ref[k * systems + r : k * systems + r + 1, :] = got * flag


def flanks_body(
    shift,
    blocks,
    ids_ref,
    off_ref,
    count_ref,
    model_in,
    damp_in,
    asking_ref,
    north_ref,
    south_ref,
    east_ref,
    west_ref,
    meta_ref,
    slabs,
    sems,
):
    systems, clat, clon, depth = model_in.shape
    copies = []
    for k, (ref, at) in enumerate(((model_in, 0), (model_in, clon - 8), (damp_in, 0), (damp_in, clon - 8))):
        copies.append(pltpu.make_async_copy(ref.at[:, :, pl.ds(at, 8)], slabs.at[k], sems.at[k]))
    last = clat - 1
    pairs = (
        (model_in.at[:, pl.ds(last - 1, 2)], south_ref.at[:, pl.ds(0, 2)]),
        (damp_in.at[:, pl.ds(last, 1)], south_ref.at[:, pl.ds(2, 1)]),
        (model_in.at[:, pl.ds(0, 2)], north_ref.at[:, pl.ds(0, 2)]),
        (damp_in.at[:, pl.ds(0, 1)], north_ref.at[:, pl.ds(2, 1)]),
    )
    copies += [pltpu.make_async_copy(a, b, sems.at[i + 4]) for i, (a, b) in enumerate(pairs)]
    for copy in copies:
        copy.start()
    tiles = ids_ref.shape[-1]
    lanes = 128
    ids = jnp.concatenate([ids_ref[0], jnp.full((1, lanes - tiles), -1, I32)], axis=1)
    owner = lax.shift_right_arithmetic(ids, shift)
    square = (lanes, lanes)
    down, across = iota(square, 0), iota(square, 1)
    owner_f = jnp.broadcast_to(owner.astype(F32), square)
    owner_col = jnp.sum(jnp.where(down == across, owner_f, 0.0), axis=1, keepdims=True)
    same = jnp.where((owner_f == owner_col) & (down < across), 1.0, 0.0)
    rank = jnp.sum(same, axis=0, keepdims=True).astype(I32)
    lane = iota((1, lanes), 1)
    block = jnp.zeros((1, lanes), I32)
    starts = off_ref[0]
    for b in range(1, blocks + 1):
        block = block + (lane >= jnp.broadcast_to(starts[:, b : b + 1], (1, lanes))).astype(I32)
    count = jnp.broadcast_to(count_ref[...], (1, lanes))
    meta_ref[...] = jnp.concatenate([owner, rank, block, count] + [owner] * 4, axis=0)
    for copy in copies:
        copy.wait()
    listed = ids.astype(F32)
    asking_ref[...] = jnp.zeros(asking_ref.shape, F32)
    corners = [
        [slabs[k % 2, r, (k // 2) * last, (k % 2) * 7 : (k % 2) * 7 + 1] for r in range(systems)]
        for k in range(4)
    ]
    lat_at, lon_at = lax.axis_index("lat"), lax.axis_index("lon")
    width = lax.axis_size("lon")
    for e in range(asking_ref.shape[0]):
        asking_ref[e, :, 0:depth] = listed
        to_south, to_east = e // width > lat_at, e % width > lon_at
        for r in range(systems):
            upper = jnp.where(to_east, corners[1][r], corners[0][r])
            lower = jnp.where(to_east, corners[3][r], corners[2][r])
            asking_ref[e, :, (r + 1) * depth : (r + 2) * depth] = jnp.where(to_south, lower, upper)
    rows = slabs.reshape(4, systems, clat * 8, depth)
    for r in range(systems):
        for out, slab, near_at, beyond in ((east_ref, 1, 7, 6), (west_ref, 0, 0, 1)):
            out[r, 0:clat] = rows[slab, r, pl.ds(near_at, clat, stride=8), :]
            out[r, clat : 2 * clat] = rows[slab, r, pl.ds(beyond, clat, stride=8), :]
            out[r, 2 * clat : 3 * clat] = rows[slab + 2, r, pl.ds(near_at, clat, stride=8), :]


def six(x, north, south, west, east):
    lane = iota(x.shape, 1)
    rows, depth = x.shape
    left, right = pltpu.roll(x, 1, 0), pltpu.roll(x, rows - 1, 0)
    ends = (8, depth)
    row = iota(ends, 0)
    left = jnp.concatenate([jnp.where(row == 0, jnp.broadcast_to(west, ends), left[:8]), left[8:]], axis=0)
    right = jnp.concatenate([right[:-8], jnp.where(row == 7, jnp.broadcast_to(east, ends), right[-8:])], axis=0)
    above = jnp.where(lane == 0, 0.0, pltpu.roll(x, 1, 1))
    below = jnp.where(lane == depth - 1, 0.0, pltpu.roll(x, depth - 1, 1))
    beside = north + south + left + right + above + below
    return DAMP_WEIGHT * (6.0 * x - beside)


def fold(x):
    parts = [x[i * 8 : (i + 1) * 8] for i in range(x.shape[0] // 8)]
    return functools.reduce(lambda a, b: a + b, parts)


def place(row, lane, value):
    return row + jnp.where(iota(row.shape, 1) == lane, jnp.broadcast_to(value, row.shape), 0.0)


def line(ref, r, i, clon):
    return ref[r, pl.ds(pl.multiple_of(i * clon, clon), clon), :]


def stencils(ref, r, k, clat, clon, first, last, west, east):
    base = k * STEP
    for j in range(STEP):
        i = base + j
        x = line(ref, r, i, clon)
        if j == 0:
            above = jnp.where(k > 0, line(ref, r, jnp.maximum(i - 1, 0), clon), first)
        else:
            above = line(ref, r, i - 1, clon)
        if j == STEP - 1:
            below = jnp.where(i + 1 < clat, line(ref, r, jnp.minimum(i + 1, clat - 1), clon), last)
        else:
            below = line(ref, r, i + 1, clon)
        yield i, x, six(x, above, below, west[pl.ds(i, 1)], east[pl.ds(i, 1)])


def damp_body(
    clat,
    clon,
    rec_ref,
    diagonal_ref,
    model_in,
    damp_in,
    north_ref,
    south_ref,
    west_ref,
    east_ref,
    tiles_in,
    bar_sent,
    held_out,
    north_out,
    south_out,
    west_out,
    east_out,
    sums_out,
    model_ref,
    damp_ref,
    bar_out,
    alphas,
    sems,
    hold_sem,
):
    systems, _, depth = model_ref.shape

    def incoming(r):
        return (
            pltpu.make_async_copy(model_in.at[r], model_ref.at[r], sems.at[r, 0]),
            pltpu.make_async_copy(damp_in.at[r], damp_ref.at[r], sems.at[r, 1]),
        )

    def outgoing(r):
        return pltpu.make_async_copy(bar_out.at[r], bar_sent.at[r], sems.at[r, 2])

    holding = pltpu.make_async_copy(tiles_in.at[0, 0, pl.ds(0, HELD)], held_out, hold_sem)
    for r in range(systems):
        for copy in incoming(r):
            copy.start()
    holding.start()
    for r in range(systems):
        alphas[r] = jnp.sum(rec_ref[0:1, r : r + 1])
    lat_at, lon_at = lax.axis_index("lat"), lax.axis_index("lon")
    has_north = (lat_at > 0).astype(F32)
    has_south = (lat_at < lax.axis_size("lat") - 1).astype(F32)
    has_west = (lon_at > 0).astype(F32)
    has_east = (lon_at < lax.axis_size("lon") - 1).astype(F32)

    def diagonal(k, r):
        return diagonal_ref[pl.ds(k * systems + r, 1), :]

    def system(r, row):
        alpha = alphas[r]
        for copy in incoming(r):
            copy.wait()

        def side(ref, own, flag, east):
            x, beyond, old = ref[r, 0:clat], ref[r, clat : 2 * clat], ref[r, 2 * clat : 3 * clat]
            upper, lower = diagonal(east, r), diagonal(2 + east, r)
            return (six(x, beyond, own, upper, lower) - alpha * old) * flag

        west_out[r] = side(west_ref, model_ref[r, pl.ds(0, clat, stride=clon), :], has_west, 0)
        east_out[r] = side(east_ref, model_ref[r, pl.ds(clon - 1, clat, stride=clon), :], has_east, 1)
        top, bottom = line(model_ref, r, 0, clon), line(model_ref, r, clat - 1, clon)
        edge = six(north_ref[r, 1], north_ref[r, 0], top, diagonal(0, r), diagonal(1, r))
        north_out[r] = has_north * (edge - alpha * north_ref[r, 2])
        edge = six(south_ref[r, 0], bottom, south_ref[r, 1], diagonal(2, r), diagonal(3, r))
        south_out[r] = has_south * (edge - alpha * south_ref[r, 2])

        def damped(k, acc):
            bar_sq, model_sq = acc
            ends = (north_ref[r, 1], south_ref[r, 0], west_ref.at[r], east_ref.at[r])
            for i, x, got in stencils(model_ref, r, k, clat, clon, *ends):
                bar = got - alpha * line(damp_ref, r, i, clon)
                bar_out[r, pl.ds(pl.multiple_of(i * clon, clon), clon), :] = bar
                bar_sq, model_sq = bar_sq + fold(bar * bar), model_sq + fold(x * x)
            return bar_sq, model_sq

        zero = jnp.zeros((8, depth), F32)
        bar_sq, model_sq = lax.fori_loop(0, clat // STEP, damped, (zero, zero))
        outgoing(r).start()
        row = place(row, r, jnp.sum(bar_sq, keepdims=True))
        return place(row, 3 * systems + r, jnp.sum(model_sq, keepdims=True))

    sums_out[...] = lax.fori_loop(0, systems, system, jnp.zeros((1, depth), F32))
    holding.wait()
    for r in range(systems):
        outgoing(r).wait()


def image_body(
    chunk,
    clat,
    clon,
    corner_ref,
    wanted_ref,
    bar_in,
    north_ref,
    south_ref,
    west_ref,
    east_ref,
    model_in,
    sums_ref,
    image_sent,
    sums_out,
    patch_out,
    model_patch_out,
    chosen_out,
    bar_ref,
    model_ref,
    image_out,
    sems,
):
    systems, _, depth = model_ref.shape

    def incoming(r):
        return (
            pltpu.make_async_copy(bar_in.at[r], bar_ref.at[r], sems.at[r, 0]),
            pltpu.make_async_copy(model_in.at[r], model_ref.at[r], sems.at[r, 1]),
        )

    def outgoing(r):
        return pltpu.make_async_copy(image_out.at[r], image_sent.at[r], sems.at[r, 2])

    for r in range(systems):
        for copy in incoming(r):
            copy.start()
    corner = corner_ref[0]
    wanted = wanted_ref[...]
    devices = wanted.shape[0]
    height, slots = chosen_out.shape
    width = PATCH * clon
    at = iota((1, slots), 1)
    source = jnp.floor((at.astype(F32) + 0.5) * (1.0 / chunk)).astype(I32)
    inner = at - source * chunk
    from_e = (jnp.broadcast_to(source, (devices, slots)) == iota((devices, slots), 0)).astype(F32).astype(BF16)
    turned = jnp.transpose(wanted)[0:8].astype(BF16)
    listed = jnp.dot(turned, from_e, preferred_element_type=F32)
    slot_of = lax.shift_right_logical(inner, systems.bit_length() - 1)
    mine = jnp.broadcast_to(slot_of, listed.shape) == iota(listed.shape, 0)
    flat = jnp.sum(jnp.where(mine, listed, 0.0), axis=0, keepdims=True).astype(I32)
    used = (flat > 0) & (inner < chunk - 1)
    target = jnp.where(used, (inner & (systems - 1)) * width + flat - 1, -1)
    for k in range(height // 64):
        shape = (64, slots)
        hit = jnp.broadcast_to(target, shape) == iota(shape, 0) + k * 64
        chosen_out[k * 64 : (k + 1) * 64] = hit.astype(F32).astype(BF16)

    def system(r, row):
        for copy in incoming(r):
            copy.wait()

        def imaged(k, acc):
            image_sq, cross = acc
            ends = (north_ref[r], south_ref[r], west_ref.at[r], east_ref.at[r])
            for i, x, image in stencils(bar_ref, r, k, clat, clon, *ends):
                image_out[r, pl.ds(pl.multiple_of(i * clon, clon), clon), :] = image
                image_sq = image_sq + fold(image * image)
                cross = cross + fold(image * line(model_ref, r, i, clon))
            return image_sq, cross

        zero = jnp.zeros((8, depth), F32)
        image_sq, cross = lax.fori_loop(0, clat // STEP, imaged, (zero, zero))
        outgoing(r).start()
        here = pl.ds(pl.multiple_of(corner * clon, clon), width)
        there = pl.ds(pl.multiple_of(r * width, width), width)
        patch_out[there, :] = image_out[r, here, :]
        model_patch_out[there, :] = model_ref[r, here, :]
        row = place(row, systems + r, jnp.sum(image_sq, keepdims=True))
        return place(row, 2 * systems + r, jnp.sum(cross, keepdims=True))

    row = lax.fori_loop(0, systems, system, sums_ref[...])
    sums_out[...] = place(row, depth - 1, corner.astype(F32))
    for r in range(systems):
        outgoing(r).wait()


def rays_body(
    cap, blocks, meta_ref, held_ref, fetched_ref, tiles_in, *refs
):
    rec_in, old_in, sums_in, bar_ref, term_ref, rest_ref, masks, lows, rec_ref, old_ref, sums_ref, sems = refs
    tiles, width, depth = tiles_in.shape[2:]
    small = [
        pltpu.make_async_copy(a, b, sems.at[PARTS + k])
        for k, (a, b) in enumerate(((rec_in, rec_ref), (old_in, old_ref), (sums_in, sums_ref)))
    ]
    part = -(-(tiles - HELD) // PARTS)
    copies = []
    for k in range(PARTS):
        count = min(part, tiles - HELD - k * part)
        source = tiles_in.at[0, 0, pl.ds(HELD + k * part, count)]
        copies.append(pltpu.make_async_copy(source, rest_ref.at[pl.ds(k * part, count)], sems.at[k]))
    for copy in copies + small:
        copy.start()

    def tile(t):
        return held_ref[t] if t < HELD else rest_ref[t - HELD]

    systems = old_ref.shape[0]
    group = cap * systems
    chunk = group + 1
    devices = term_ref.shape[0] // chunk
    for c in range(cap + 1):
        here = lax.shift_right_logical(iota((group, depth), 0), systems.bit_length() - 1) == c
        masks[c] = here.astype(F32).astype(BF16)
    term_ref[...] = jnp.zeros(term_ref.shape, F32)
    lows[...] = jnp.zeros(lows.shape, BF16)
    total = jnp.zeros((blocks * group, width), F32)
    for t in range(tiles):
        if t >= HELD and (t - HELD) % part == 0:
            copies[(t - HELD) // part].wait()
        owner, rank, block = meta_ref[0, t], meta_ref[1, t], meta_ref[2, t]
        rows = fetched_ref[pl.ds(pl.multiple_of(owner * group, group), group), :]
        left = jnp.concatenate(
            [rows * masks[jnp.where(block == b, rank, cap)] for b in range(blocks)], axis=0
        )
        total = total + lax.dot_general(
            left, tile(t), (((1,), (1,)), ((), ())), preferred_element_type=F32
        )
    for copy in small:
        copy.wait()
    square = jnp.zeros((systems, width), F32)
    for b in range(blocks):
        traced = jnp.zeros((systems, width), F32)
        for c in range(cap):
            at = b * group + c * systems
            traced = traced + total[at : at + systems]
        old = jnp.concatenate(
            [old_ref[r, 0, :, b * width : (b + 1) * width] * rec_ref[0:1, r : r + 1] for r in range(systems)], axis=0
        )
        live = iota((systems, width), 1) + b * width < meta_ref[3, 0]
        bar = jnp.where(live, traced - old, 0.0)
        square = square + bar * bar
        for r in range(systems):
            bar_ref[r, 0, :, b * width : (b + 1) * width] = bar[r : r + 1]
        lows[b] = jnp.concatenate([bar, jnp.zeros((16 - systems, width), F32)], axis=0).astype(BF16)
    ray_sq = jnp.sum(square, axis=1, keepdims=True)
    part = sums_ref[...]
    for r in range(systems):
        part = place(part, r, ray_sq[r : r + 1])
    for e in range(devices):
        term_ref[e * chunk + group] = part
    for t in range(tiles):
        row = meta_ref[0, t] * chunk + meta_ref[1, t] * systems
        term = jnp.dot(lows[meta_ref[2, t]], tile(t), preferred_element_type=F32)
        for r in range(systems):
            term_ref[row + r] = term[r : r + 1]


def combine_body(chunk, systems, terms_ref, chosen_ref, patch_ref, model_patch_ref, sums_ref, added_ref, residual_ref, parts_ref, split):
    arrived, depth = terms_ref.shape
    devices = parts_ref.shape[0]
    width = patch_ref.shape[0]
    x = terms_ref[...]
    high = x.astype(BF16)
    rest = x - high.astype(F32)
    middle = rest.astype(BF16)
    low = (rest - middle.astype(F32)).astype(BF16)
    padded = split.shape[0]
    if padded > arrived:
        split[arrived:] = jnp.zeros((padded - arrived, split.shape[1]), BF16)
    split[0:arrived, 0:depth] = high
    split[0:arrived, depth : 2 * depth] = middle
    split[0:arrived, 2 * depth :] = low
    three = jnp.dot(chosen_ref[...], split[...], preferred_element_type=F32)
    added = three[:, 0:depth] + (three[:, depth : 2 * depth] + three[:, 2 * depth :])
    added_ref[...] = added
    every = terms_ref[pl.ds(chunk - 1, devices, stride=chunk), :]
    total = jnp.sum(every, axis=0, keepdims=True)
    residual_ref[...] = jnp.where(iota(total.shape, 1) == depth - 1, sums_ref[...], total)
    square = added * (2.0 * patch_ref[...] + added)
    cross = added * model_patch_ref[...]
    row = sums_ref[...]
    each = width // systems
    for r in range(systems):
        row = place(row, systems + r, jnp.sum(square[r * each : (r + 1) * each], keepdims=True))
        row = place(row, 2 * systems + r, jnp.sum(cross[r * each : (r + 1) * each], keepdims=True))
    parts_ref[...] = jnp.broadcast_to(row, parts_ref.shape)


def first_norm(residual_ref, systems, rows_all):
    return jnp.sqrt(residual_ref[0:1, 0:systems] / rows_all + EPSILON)


def early_body(
    rows_all,
    residual_ref,
    rec_ref,
    ray_ref,
    bar_in,
    solution_in,
    search_in,
    ray_out,
    damp_out,
    solution_out,
    kept_ref,
    bar_ref,
    solution_ref,
    search_ref,
    damp_s,
    solution_s,
    coef,
    in_sems,
    sems,
):
    systems, columns, _ = bar_ref.shape
    rows = columns // PIECES
    kept = kept_ref.shape[0]
    ins = ((bar_in, bar_ref), (solution_in, solution_ref))
    outs = ((damp_s, damp_out), (solution_s, solution_out))

    def start(n):
        if n < systems * PIECES:
            begin(fetch(n))

    def fetch(n):
        r, p = n // PIECES, n % PIECES
        at = pl.ds(p * rows, rows)
        target = kept_ref.at[r, at] if r < kept else search_ref.at[0, at]
        return pieces(ins, in_sems, r, p, rows) + [
            pltpu.make_async_copy(search_in.at[r, at], target, in_sems.at[r, p, 2])
        ]

    for n in range(AHEAD):
        start(n)
    rho_bar, phi_bar = rec_ref[1:2], rec_ref[2:3]
    beta = first_norm(residual_ref, systems, rows_all)
    rho = jnp.sqrt(rho_bar * rho_bar + beta * beta)
    scales = (1.0 / beta, (rho_bar / rho) * phi_bar / rho)
    for q, scale in enumerate(scales):
        for s in range(systems):
            coef[q, s] = scale[0, s]
    for s in range(systems):
        ray_out[s] = ray_ref[s] * coef[0, s]

    for n in range(systems * PIECES):
        r, p = n // PIECES, n % PIECES
        at = pl.ds(p * rows, rows)
        start(n + AHEAD)
        settle(fetch(n))
        search = kept_ref[r, at, :] if r < kept else search_ref[0, at, :]
        damp_s[r, at, :] = bar_ref[r, at, :] * coef[0, r]
        solution_s[r, at, :] = solution_ref[r, at, :] + search * coef[1, r]
        begin(pieces(outs, sems, r, p, rows))

    wait_all(outs, sems, systems, rows)


def finish_body(
    rows_all,
    cells_all,
    clon,
    residual_ref,
    parts_ref,
    added_ref,
    kept_ref,
    image_in,
    model_in,
    search_in,
    rec_in,
    model_out,
    search_out,
    rec_sent,
    image_ref,
    model_ref,
    search_ref,
    model_s,
    search_s,
    rec_ref,
    rec_out,
    coef,
    in_sems,
    sems,
    rec_sems,
):
    systems, columns, depth = image_ref.shape
    rec_copy = pltpu.make_async_copy(rec_in, rec_ref, rec_sems.at[0])
    rec_copy.start()
    rows = columns // PIECES
    kept = kept_ref.shape[0]
    ins = ((image_in, image_ref), (model_in, model_ref))
    outs = ((model_s, model_out), (search_s, search_out))

    def start(n):
        if n < systems * PIECES:
            begin(fetch(n))

    def fetch(n):
        r, p = n // PIECES, n % PIECES
        copies = pieces(ins, in_sems, r, p, rows)
        if r >= kept:
            at = pl.ds(p * rows, rows)
            copies.append(pltpu.make_async_copy(search_in.at[r, at], search_ref.at[0, at], in_sems.at[r, p, 2]))
        return copies

    for n in range(AHEAD):
        start(n)
    corner = residual_ref[0, depth - 1].astype(I32)
    total = jnp.sum(parts_ref[...], axis=0, keepdims=True)
    rec_copy.wait()
    image_sq, cross, model_sq = (total[:, q * systems : (q + 1) * systems] for q in range(1, 4))
    rho_bar, phi_bar = rec_ref[1:2], rec_ref[2:3]
    beta = first_norm(residual_ref, systems, rows_all)
    update_sq = image_sq / (beta * beta) - 2.0 * cross + beta * beta * model_sq
    alpha = jnp.sqrt(jnp.maximum(update_sq, 0.0) / cells_all + EPSILON)
    rho = jnp.sqrt(rho_bar * rho_bar + beta * beta)
    cosine = rho_bar / rho
    sine = beta / rho
    rec_out[...] = jnp.concatenate([alpha, -cosine * alpha, sine * phi_bar], axis=0)
    rec_done = pltpu.make_async_copy(rec_out, rec_sent, rec_sems.at[1])
    rec_done.start()
    scales = (1.0 / (beta * alpha), beta / alpha, sine * alpha / rho)
    for q, scale in enumerate(scales):
        for s in range(systems):
            coef[q, s] = scale[0, s]
    width = PATCH * clon

    for n in range(systems * PIECES):
        r, p = n // PIECES, n % PIECES
        at = pl.ds(p * rows, rows)
        start(n + AHEAD)
        settle(fetch(n))
        search = kept_ref[r, at, :] if r < kept else search_ref[0, at, :]
        new = image_ref[r, at, :] * coef[0, r] - model_ref[r, at, :] * coef[1, r]
        model_s[r, at, :] = new
        search_s[r, at, :] = new - search * coef[2, r]
        for k in range(PATCH):
            first = (corner + k) * clon

            @pl.when((first >= p * rows) & (first < (p + 1) * rows))
            def _():
                cells = pl.ds(pl.multiple_of(first, clon), clon)
                more = added_ref[r * width + k * clon : r * width + (k + 1) * clon, :] * coef[0, r]
                model_s[r, cells, :] = model_s[r, cells, :] + more
                search_s[r, cells, :] = search_s[r, cells, :] + more

        begin(pieces(outs, sems, r, p, rows))

    wait_all(outs, sems, systems, rows)
    rec_done.wait()


PIECES = 2
AHEAD = 4


def pieces(pairs, sems, r, p, rows):
    at = pl.ds(pl.multiple_of(p * rows, rows), rows)
    return [pltpu.make_async_copy(a.at[r, at], b.at[r, at], sems.at[r, p, k]) for k, (a, b) in enumerate(pairs)]


def begin(copies):
    for copy in copies:
        copy.start()


def settle(copies):
    for copy in copies:
        copy.wait()


def wait_all(pairs, sems, systems, rows):
    def one(n, _):
        for copy in pieces(pairs, sems, n // PIECES, n % PIECES, rows):
            copy.wait()
        return 0

    lax.fori_loop(0, systems * PIECES, one, 0)


PARTS = 3
HELD = 30


def shifted(x, axis, step):
    count = lax.axis_size(axis)
    if step > 0:
        pairs = [(i, i + 1) for i in range(count - 1)]
    else:
        pairs = [(i + 1, i) for i in range(count - 1)]
    return lax.ppermute(x, axis, pairs)


def exchange(x):
    return lax.all_to_all(x, AXES, split_axis=0, concat_axis=0, tiled=True)


def per_device(
    sensitivity,
    block_ids,
    block_offsets,
    ray_counts,
    ray_vector,
    damping_vector,
    model_vector,
    solution,
    search,
    recurrence,
):
    lat_size, lon_size = lax.axis_size("lat"), lax.axis_size("lon")
    devices = lat_size * lon_size
    tiles, width, depth = sensitivity.shape[2:]
    blocks = block_offsets.shape[-1] - 1
    systems, clat, clon, _ = model_vector.shape
    columns = clat * clon
    cap = max(2 * ((tiles + devices - 1) // devices), 16 // systems)
    slots = devices * cap
    group = cap * systems
    chunk = group + 1
    cells_all = devices * columns * depth
    rows_all = devices * blocks * width + cells_all
    lanes = 128
    full, flat = model_vector.shape, (systems, columns, depth)
    lines = (systems, PATCH * clon, depth)
    here, there, plain = pltpu.VMEM, pltpu.HBM, jax.ShapeDtypeStruct
    dma = pltpu.SemaphoreType.DMA
    model, damping = far(model_vector), far(damping_vector)
    model_flat, damping_flat = far(model_vector.reshape(flat)), far(damping_vector.reshape(flat))

    side = there((systems, 3 * clat, depth), F32)
    band = there((systems, 3, clon, depth), F32)
    asking, north_msg, south_msg, east_msg, west_msg, meta = call(
        functools.partial(flanks_body, columns.bit_length() - 1, blocks),
        "flanks",
        (there((devices, 1, 2 * systems * depth), F32), band, band, side, side, there((8, lanes), I32)),
        [vmem()] * 3 + [hbm(), hbm()],
        (vmem(),) * 6,
        scratch=[pltpu.VMEM((4, systems, clat, 8, depth), F32), dma((8,))],
        flops=1,
        moved=128 * systems * clat * depth,
    )(far(block_ids), block_offsets, ray_counts, model, damping)
    lists = exchange(asking)
    north = shifted(south_msg, "lat", 1)
    south = shifted(north_msg, "lat", -1)
    west = shifted(east_msg, "lon", 1)
    east = shifted(west_msg, "lon", -1)

    served, wanted, corner, diagonal = call(
        functools.partial(serve_body, cap, clat, clon),
        "serve",
        (
            there((slots * systems, depth), BF16),
            plain((devices, lanes), F32),
            plain((1,), I32),
            plain((4 * systems, depth), F32),
        ),
        [vmem(), hbm()] + [pl.BlockSpec(memory_space=pl.ANY)] * 4,
        (vmem(), vmem(), smem(), vmem()),
        scratch=[pltpu.VMEM(lines, F32), pltpu.VMEM((slots * systems, depth), F32), dma((systems,))],
    )(lists, model_flat, north, south, west, east)
    fetched = exchange(served.reshape(devices, group, depth)).reshape(slots * systems, depth)

    edge, flank = there((systems, clon, depth), F32), there((systems, clat, depth), F32)
    bar, held, *border, sums = call(
        functools.partial(damp_body, clat, clon),
        "damp",
        (
            there(flat, F32),
            here((HELD, width, depth), BF16),
            edge,
            edge,
            flank,
            flank,
            there((1, lanes), F32),
        ),
        [vmem()] * 2 + [hbm()] * 2 + [vmem()] * 4 + [hbm()],
        (hbm(),) + (vmem(),) * 6,
        scratch=[pltpu.VMEM(flat, F32)] * 3 + [pltpu.SMEM((systems,), F32), dma((systems, 3)), dma],
        flops=20 * systems * columns * depth,
        moved=12 * systems * columns * depth,
    )(far(recurrence), diagonal, model_flat, damping_flat, north, south, west, east, far(sensitivity))

    ray_bar, terms = call(
        functools.partial(rays_body, cap, blocks),
        "rays",
        (there(ray_vector.shape, F32), there((devices * chunk, 1, depth), F32)),
        [smem(), vmem(), vmem()] + [hbm()] * 4,
        (vmem(), vmem()),
        scratch=[
            pltpu.VMEM((tiles - HELD, width, depth), BF16),
            pltpu.VMEM((cap + 1, group, depth), BF16),
            pltpu.VMEM((blocks + 1, 16, width), BF16),
            pltpu.VMEM(recurrence.shape, F32),
            pltpu.VMEM(ray_vector.shape, F32),
            pltpu.VMEM((1, lanes), F32),
            dma((PARTS + 3,)),
        ],
        flops=4 * tiles * width * depth * 16,
        moved=2 * tiles * width * depth,
    )(meta, near(held), fetched, far(sensitivity), far(recurrence), far(ray_vector), far(sums))
    arrived = exchange(terms.reshape(devices, 1, chunk * depth)).reshape(devices * chunk, depth)

    padded = -(-devices * chunk // lanes) * lanes
    height = systems * PATCH * clon
    patch = (height, depth)
    image, sums, patched, model_patch, chosen = call(
        functools.partial(image_body, chunk, clat, clon),
        "image",
        (
            there(flat, F32),
            plain((1, lanes), F32),
            plain(patch, F32),
            plain(patch, F32),
            plain((height, padded), BF16),
        ),
        [smem(), vmem(), hbm()] + [vmem()] * 4 + [hbm(), vmem()],
        (hbm(),) + (vmem(),) * 4,
        scratch=[pltpu.VMEM(flat, F32)] * 3 + [dma((systems, 3))],
        flops=20 * systems * columns * depth,
        moved=12 * systems * columns * depth,
    )(corner, wanted, far(bar), *(far(x) for x in border), model_flat, far(sums))

    added, residual, parts = call(
        functools.partial(combine_body, chunk, systems),
        "combine",
        (plain(patch, F32), plain((1, lanes), F32), there((devices, lanes), F32)),
        [vmem()] * 5,
        (vmem(),) * 3,
        scratch=[pltpu.VMEM((padded, 3 * depth), BF16)],
    )(arrived, chosen, patched, model_patch, sums)
    every = exchange(parts.reshape(devices, 1, lanes)).reshape(devices, lanes)

    search_flat = far(search.reshape(flat))
    ray_out, damp_out, solution_out, kept = call(
        functools.partial(early_body, float(rows_all)),
        "early",
        (there(ray_vector.shape, F32), there(flat, F32), there(flat, F32), here((systems - 1, columns, depth), F32)),
        [vmem()] * 3 + [hbm()] * 3,
        (vmem(), hbm(), hbm(), vmem()),
        scratch=[pltpu.VMEM(flat, F32)] * 2
        + [pltpu.VMEM((1, columns, depth), F32)]
        + [pltpu.VMEM(flat, F32)] * 2
        + [pltpu.SMEM((2, systems), F32), dma((systems, PIECES, 3)), dma((systems, PIECES, 2))],
        mib=32,
        flops=4 * systems * columns * depth,
        moved=20 * systems * columns * depth,
    )(residual, far(recurrence), far(ray_bar), far(bar), far(solution.reshape(flat)), search_flat)
    model_out, search_out, rec_out = call(
        functools.partial(finish_body, float(rows_all), float(cells_all), clon),
        "finish",
        (there(flat, F32), there(flat, F32), there(recurrence.shape, F32)),
        [vmem()] * 4 + [hbm()] * 4,
        (hbm(),) * 3,
        scratch=[pltpu.VMEM(flat, F32)] * 2
        + [pltpu.VMEM((1, columns, depth), F32)]
        + [pltpu.VMEM(flat, F32)] * 2
        + [pltpu.VMEM(recurrence.shape, F32)] * 2
        + [pltpu.SMEM((3, systems), F32), dma((systems, PIECES, 3)), dma((systems, PIECES, 2)), dma((2,))],
        mib=32,
        flops=6 * systems * columns * depth,
        moved=20 * systems * columns * depth,
    )(residual, every, added, near(kept), far(image), model_flat, search_flat, far(recurrence))
    fields = (x.reshape(full) for x in (damp_out, model_out, solution_out, search_out))
    return (ray_out, *fields, rec_out)


def solution(mesh):
    fields = P(None, "lat", "lon", None)
    return jax.shard_map(
        per_device,
        mesh=mesh,
        in_specs=(
            P("lat", "lon", None, None, None),
            P("lat", "lon", None),
            P("lat", "lon", None),
            P("lat", "lon"),
            fields,
            fields,
            fields,
            fields,
            fields,
            P(),
        ),
        out_specs=(fields, fields, fields, fields, fields, P()),
        check_vma=False,
    )
```

```python
import functools

import jax
import jax.numpy as jnp
from jax import lax
from jax.experimental import pallas as pl
from jax.experimental.pallas import tpu as pltpu
from jax.sharding import PartitionSpec as P

DAMP_WEIGHT = 0.15
EPSILON = 1e-05
AXES = ("lat", "lon")
PATCH = 4
F32, BF16, I32 = jnp.float32, jnp.bfloat16, jnp.int32


def iota(shape, dim):
    return lax.broadcasted_iota(I32, shape, dim)


def vmem():
    return pl.BlockSpec(memory_space=pltpu.VMEM)


def hbm():
    return pl.BlockSpec(memory_space=pltpu.HBM)


def near(x):
    return pltpu.with_memory_space_constraint(x, pltpu.VMEM)


def far(x):
    return pltpu.with_memory_space_constraint(x, pltpu.HBM)


def smem():
    return pl.BlockSpec(memory_space=pltpu.SMEM)


def call(body, name, out_shape, in_specs, out_specs, scratch=(), grid=(), mib=16, flops=0, moved=0):
    return pl.pallas_call(
        body,
        name=name,
        grid=grid,
        out_shape=out_shape,
        in_specs=in_specs,
        out_specs=out_specs,
        scratch_shapes=list(scratch),
        compiler_params=pltpu.CompilerParams(vmem_limit_bytes=mib * 2**20),
        cost_estimate=pl.CostEstimate(flops=flops, bytes_accessed=moved, transcendentals=0),
    )


STEP = 8


def wanted_column(wanted, cap):
    devices, lanes = wanted.shape
    rows = devices * cap
    spread = jnp.broadcast_to(wanted[:, None, :], (devices, cap, lanes)).reshape(rows, lanes)
    pick = iota((rows, lanes), 1) == (iota((rows, lanes), 0) & (cap - 1))
    return jnp.sum(jnp.where(pick, spread, 0.0), axis=1, keepdims=True)


def serve_body(cap, clat, clon, lists_ref, model_in, served_ref, wanted_ref, corner_ref, diagonal_ref, patch, mixed, sems):
    systems, width, depth = patch.shape
    devices = lists_ref.shape[0]
    lanes = 128
    shift = (clat * clon).bit_length() - 1
    me = lax.axis_index("lat") * lax.axis_size("lon") + lax.axis_index("lon")
    ids = lists_ref[:, 0, 0:lanes].astype(I32)
    column = ids - lax.shift_left(me, shift)
    mine = (column >= 0) & (column < clat * clon) & (ids >= 0)
    first = jnp.min(jnp.where(mine, column, clat * clon))
    corner = jnp.minimum(lax.shift_right_logical(first, clon.bit_length() - 1), clat - PATCH)
    corner_ref[0] = corner
    at = pl.ds(pl.multiple_of(corner * clon, clon), width)
    copies = [pltpu.make_async_copy(model_in.at[r, at], patch.at[r], sems.at[r]) for r in range(systems)]
    for copy in copies:
        copy.start()
    ahead = (iota((lanes, lanes), 0) < iota((lanes, lanes), 1)).astype(F32).astype(BF16)
    rank = jnp.dot(mine.astype(F32).astype(BF16), ahead, preferred_element_type=F32)
    value = (column - corner * clon + 1).astype(F32)
    at = iota((devices, lanes), 1)
    wanted = jnp.zeros((devices, lanes), F32)
    for c in range(cap):
        picked = jnp.sum(jnp.where(mine & (rank == c), value, 0.0), axis=1, keepdims=True)
        wanted = jnp.where(at == c, picked, wanted)
    wanted_ref[...] = wanted
    target = wanted_column(wanted, cap).astype(I32) - 1
    rows = target.shape[0]
    chosen = (jnp.broadcast_to(target, (rows, width)) == iota((rows, width), 1)).astype(F32).astype(BF16)
    for r in range(systems):
        copies[r].wait()
        table = patch[r].astype(BF16)
        mixed[pl.ds(r, rows, stride=systems), :] = jnp.dot(chosen, table, preferred_element_type=F32)
    served_ref[...] = mixed[...].astype(BF16)
    lat_at, lon_at = lax.axis_index("lat"), lax.axis_index("lon")
    lat_size, lon_size = lax.axis_size("lat"), lax.axis_size("lon")
    for k in range(4):
        lat_to, lon_to = lat_at + 2 * (k // 2) - 1, lon_at + 2 * (k % 2) - 1
        inside = (lat_to >= 0) & (lat_to < lat_size) & (lon_to >= 0) & (lon_to < lon_size)
        source = jnp.where(inside, lat_to * lon_size + lon_to, 0)
        flag = inside.astype(F32)
        for r in range(systems):
            got = lists_ref[source, :, (r + 1) * depth : (r + 2) * depth]
            diagonal_ref[k * systems + r : k * systems + r + 1, :] = got * flag


def flanks_body(
    shift,
    blocks,
    ids_ref,
    off_ref,
    count_ref,
    model_in,
    damp_in,
    asking_ref,
    north_ref,
    south_ref,
    east_ref,
    west_ref,
    meta_ref,
    slabs,
    sems,
):
    systems, clat, clon, depth = model_in.shape
    copies = []
    for k, (ref, at) in enumerate(((model_in, 0), (model_in, clon - 8), (damp_in, 0), (damp_in, clon - 8))):
        copies.append(pltpu.make_async_copy(ref.at[:, :, pl.ds(at, 8)], slabs.at[k], sems.at[k]))
    last = clat - 1
    pairs = (
        (model_in.at[:, pl.ds(last - 1, 2)], south_ref.at[:, pl.ds(0, 2)]),
        (damp_in.at[:, pl.ds(last, 1)], south_ref.at[:, pl.ds(2, 1)]),
        (model_in.at[:, pl.ds(0, 2)], north_ref.at[:, pl.ds(0, 2)]),
        (damp_in.at[:, pl.ds(0, 1)], north_ref.at[:, pl.ds(2, 1)]),
    )
    copies += [pltpu.make_async_copy(a, b, sems.at[i + 4]) for i, (a, b) in enumerate(pairs)]
    for copy in copies:
        copy.start()
    tiles = ids_ref.shape[-1]
    lanes = 128
    ids = jnp.concatenate([ids_ref[0], jnp.full((1, lanes - tiles), -1, I32)], axis=1)
    owner = lax.shift_right_arithmetic(ids, shift)
    square = (lanes, lanes)
    down, across = iota(square, 0), iota(square, 1)
    owner_f = jnp.broadcast_to(owner.astype(F32), square)
    owner_col = jnp.sum(jnp.where(down == across, owner_f, 0.0), axis=1, keepdims=True)
    same = jnp.where((owner_f == owner_col) & (down < across), 1.0, 0.0)
    rank = jnp.sum(same, axis=0, keepdims=True).astype(I32)
    lane = iota((1, lanes), 1)
    block = jnp.zeros((1, lanes), I32)
    starts = off_ref[0]
    for b in range(1, blocks + 1):
        block = block + (lane >= jnp.broadcast_to(starts[:, b : b + 1], (1, lanes))).astype(I32)
    count = jnp.broadcast_to(count_ref[...], (1, lanes))
    meta_ref[...] = jnp.concatenate([owner, rank, block, count] + [owner] * 4, axis=0)
    for copy in copies:
        copy.wait()
    listed = ids.astype(F32)
    asking_ref[...] = jnp.zeros(asking_ref.shape, F32)
    corners = [
        [slabs[k % 2, r, (k // 2) * last, (k % 2) * 7 : (k % 2) * 7 + 1] for r in range(systems)]
        for k in range(4)
    ]
    lat_at, lon_at = lax.axis_index("lat"), lax.axis_index("lon")
    width = lax.axis_size("lon")
    for e in range(asking_ref.shape[0]):
        asking_ref[e, :, 0:depth] = listed
        to_south, to_east = e // width > lat_at, e % width > lon_at
        for r in range(systems):
            upper = jnp.where(to_east, corners[1][r], corners[0][r])
            lower = jnp.where(to_east, corners[3][r], corners[2][r])
            asking_ref[e, :, (r + 1) * depth : (r + 2) * depth] = jnp.where(to_south, lower, upper)
    rows = slabs.reshape(4, systems, clat * 8, depth)
    for r in range(systems):
        for out, slab, near_at, beyond in ((east_ref, 1, 7, 6), (west_ref, 0, 0, 1)):
            out[r, 0:clat] = rows[slab, r, pl.ds(near_at, clat, stride=8), :]
            out[r, clat : 2 * clat] = rows[slab, r, pl.ds(beyond, clat, stride=8), :]
            out[r, 2 * clat : 3 * clat] = rows[slab + 2, r, pl.ds(near_at, clat, stride=8), :]


def six(x, north, south, west, east):
    lane = iota(x.shape, 1)
    rows, depth = x.shape
    left, right = pltpu.roll(x, 1, 0), pltpu.roll(x, rows - 1, 0)
    ends = (8, depth)
    row = iota(ends, 0)
    left = jnp.concatenate([jnp.where(row == 0, jnp.broadcast_to(west, ends), left[:8]), left[8:]], axis=0)
    right = jnp.concatenate([right[:-8], jnp.where(row == 7, jnp.broadcast_to(east, ends), right[-8:])], axis=0)
    above = jnp.where(lane == 0, 0.0, pltpu.roll(x, 1, 1))
    below = jnp.where(lane == depth - 1, 0.0, pltpu.roll(x, depth - 1, 1))
    beside = north + south + left + right + above + below
    return DAMP_WEIGHT * (6.0 * x - beside)


def fold(x):
    parts = [x[i * 8 : (i + 1) * 8] for i in range(x.shape[0] // 8)]
    return functools.reduce(lambda a, b: a + b, parts)


def place(row, lane, value):
    return row + jnp.where(iota(row.shape, 1) == lane, jnp.broadcast_to(value, row.shape), 0.0)


def line(ref, r, i, clon):
    return ref[r, pl.ds(pl.multiple_of(i * clon, clon), clon), :]


def stencils(ref, r, k, clat, clon, first, last, west, east):
    base = k * STEP
    for j in range(STEP):
        i = base + j
        x = line(ref, r, i, clon)
        if j == 0:
            above = jnp.where(k > 0, line(ref, r, jnp.maximum(i - 1, 0), clon), first)
        else:
            above = line(ref, r, i - 1, clon)
        if j == STEP - 1:
            below = jnp.where(i + 1 < clat, line(ref, r, jnp.minimum(i + 1, clat - 1), clon), last)
        else:
            below = line(ref, r, i + 1, clon)
        yield i, x, six(x, above, below, west[pl.ds(i, 1)], east[pl.ds(i, 1)])


def damp_body(
    clat,
    clon,
    rec_ref,
    diagonal_ref,
    model_in,
    damp_in,
    north_ref,
    south_ref,
    west_ref,
    east_ref,
    tiles_in,
    bar_sent,
    held_out,
    north_out,
    south_out,
    west_out,
    east_out,
    sums_out,
    model_ref,
    damp_ref,
    bar_out,
    alphas,
    sems,
    hold_sem,
):
    systems, _, depth = model_ref.shape

    def incoming(r):
        return (
            pltpu.make_async_copy(model_in.at[r], model_ref.at[r], sems.at[r, 0]),
            pltpu.make_async_copy(damp_in.at[r], damp_ref.at[r], sems.at[r, 1]),
        )

    def outgoing(r):
        return pltpu.make_async_copy(bar_out.at[r], bar_sent.at[r], sems.at[r, 2])

    holding = pltpu.make_async_copy(tiles_in.at[0, 0, pl.ds(0, HELD)], held_out, hold_sem)
    for r in range(systems):
        for copy in incoming(r):
            copy.start()
    holding.start()
    for r in range(systems):
        alphas[r] = jnp.sum(rec_ref[0:1, r : r + 1])
    lat_at, lon_at = lax.axis_index("lat"), lax.axis_index("lon")
    has_north = (lat_at > 0).astype(F32)
    has_south = (lat_at < lax.axis_size("lat") - 1).astype(F32)
    has_west = (lon_at > 0).astype(F32)
    has_east = (lon_at < lax.axis_size("lon") - 1).astype(F32)

    def diagonal(k, r):
        return diagonal_ref[pl.ds(k * systems + r, 1), :]

    def system(r, row):
        alpha = alphas[r]
        for copy in incoming(r):
            copy.wait()

        def side(ref, own, flag, east):
            x, beyond, old = ref[r, 0:clat], ref[r, clat : 2 * clat], ref[r, 2 * clat : 3 * clat]
            upper, lower = diagonal(east, r), diagonal(2 + east, r)
            return (six(x, beyond, own, upper, lower) - alpha * old) * flag

        west_out[r] = side(west_ref, model_ref[r, pl.ds(0, clat, stride=clon), :], has_west, 0)
        east_out[r] = side(east_ref, model_ref[r, pl.ds(clon - 1, clat, stride=clon), :], has_east, 1)
        top, bottom = line(model_ref, r, 0, clon), line(model_ref, r, clat - 1, clon)
        edge = six(north_ref[r, 1], north_ref[r, 0], top, diagonal(0, r), diagonal(1, r))
        north_out[r] = has_north * (edge - alpha * north_ref[r, 2])
        edge = six(south_ref[r, 0], bottom, south_ref[r, 1], diagonal(2, r), diagonal(3, r))
        south_out[r] = has_south * (edge - alpha * south_ref[r, 2])

        def damped(k, acc):
            bar_sq, model_sq = acc
            ends = (north_ref[r, 1], south_ref[r, 0], west_ref.at[r], east_ref.at[r])
            for i, x, got in stencils(model_ref, r, k, clat, clon, *ends):
                bar = got - alpha * line(damp_ref, r, i, clon)
                bar_out[r, pl.ds(pl.multiple_of(i * clon, clon), clon), :] = bar
                bar_sq, model_sq = bar_sq + fold(bar * bar), model_sq + fold(x * x)
            return bar_sq, model_sq

        zero = jnp.zeros((8, depth), F32)
        bar_sq, model_sq = lax.fori_loop(0, clat // STEP, damped, (zero, zero))
        outgoing(r).start()
        row = place(row, r, jnp.sum(bar_sq, keepdims=True))
        return place(row, 3 * systems + r, jnp.sum(model_sq, keepdims=True))

    sums_out[...] = lax.fori_loop(0, systems, system, jnp.zeros((1, depth), F32))
    holding.wait()
    for r in range(systems):
        outgoing(r).wait()


def image_body(
    chunk,
    clat,
    clon,
    corner_ref,
    wanted_ref,
    bar_in,
    north_ref,
    south_ref,
    west_ref,
    east_ref,
    model_in,
    sums_ref,
    image_sent,
    sums_out,
    patch_out,
    model_patch_out,
    chosen_out,
    bar_ref,
    model_ref,
    image_out,
    sems,
):
    systems, _, depth = model_ref.shape

    def incoming(r):
        return (
            pltpu.make_async_copy(bar_in.at[r], bar_ref.at[r], sems.at[r, 0]),
            pltpu.make_async_copy(model_in.at[r], model_ref.at[r], sems.at[r, 1]),
        )

    def outgoing(r):
        return pltpu.make_async_copy(image_out.at[r], image_sent.at[r], sems.at[r, 2])

    for r in range(systems):
        for copy in incoming(r):
            copy.start()
    corner = corner_ref[0]
    wanted = wanted_ref[...]
    devices = wanted.shape[0]
    height, slots = chosen_out.shape
    width = PATCH * clon
    at = iota((1, slots), 1)
    source = jnp.floor((at.astype(F32) + 0.5) * (1.0 / chunk)).astype(I32)
    inner = at - source * chunk
    from_e = (jnp.broadcast_to(source, (devices, slots)) == iota((devices, slots), 0)).astype(F32).astype(BF16)
    turned = jnp.transpose(wanted)[0:8].astype(BF16)
    listed = jnp.dot(turned, from_e, preferred_element_type=F32)
    slot_of = lax.shift_right_logical(inner, systems.bit_length() - 1)
    mine = jnp.broadcast_to(slot_of, listed.shape) == iota(listed.shape, 0)
    flat = jnp.sum(jnp.where(mine, listed, 0.0), axis=0, keepdims=True).astype(I32)
    used = (flat > 0) & (inner < chunk - 1)
    target = jnp.where(used, (inner & (systems - 1)) * width + flat - 1, -1)
    for k in range(height // 64):
        shape = (64, slots)
        hit = jnp.broadcast_to(target, shape) == iota(shape, 0) + k * 64
        chosen_out[k * 64 : (k + 1) * 64] = hit.astype(F32).astype(BF16)

    def system(r, row):
        for copy in incoming(r):
            copy.wait()

        def imaged(k, acc):
            image_sq, cross = acc
            ends = (north_ref[r], south_ref[r], west_ref.at[r], east_ref.at[r])
            for i, x, image in stencils(bar_ref, r, k, clat, clon, *ends):
                image_out[r, pl.ds(pl.multiple_of(i * clon, clon), clon), :] = image
                image_sq = image_sq + fold(image * image)
                cross = cross + fold(image * line(model_ref, r, i, clon))
            return image_sq, cross

        zero = jnp.zeros((8, depth), F32)
        image_sq, cross = lax.fori_loop(0, clat // STEP, imaged, (zero, zero))
        outgoing(r).start()
        here = pl.ds(pl.multiple_of(corner * clon, clon), width)
        there = pl.ds(pl.multiple_of(r * width, width), width)
        patch_out[there, :] = image_out[r, here, :]
        model_patch_out[there, :] = model_ref[r, here, :]
        row = place(row, systems + r, jnp.sum(image_sq, keepdims=True))
        return place(row, 2 * systems + r, jnp.sum(cross, keepdims=True))

    row = lax.fori_loop(0, systems, system, sums_ref[...])
    sums_out[...] = place(row, depth - 1, corner.astype(F32))
    for r in range(systems):
        outgoing(r).wait()


def rays_body(
    cap, blocks, meta_ref, held_ref, fetched_ref, tiles_in, *refs
):
    rec_in, old_in, sums_in, bar_ref, term_ref, rest_ref, masks, lows, rec_ref, old_ref, sums_ref, sems = refs
    tiles, width, depth = tiles_in.shape[2:]
    small = [
        pltpu.make_async_copy(a, b, sems.at[PARTS + k])
        for k, (a, b) in enumerate(((rec_in, rec_ref), (old_in, old_ref), (sums_in, sums_ref)))
    ]
    part = -(-(tiles - HELD) // PARTS)
    copies = []
    for k in range(PARTS):
        count = min(part, tiles - HELD - k * part)
        source = tiles_in.at[0, 0, pl.ds(HELD + k * part, count)]
        copies.append(pltpu.make_async_copy(source, rest_ref.at[pl.ds(k * part, count)], sems.at[k]))
    for copy in copies + small:
        copy.start()

    def tile(t):
        return held_ref[t] if t < HELD else rest_ref[t - HELD]

    systems = old_ref.shape[0]
    group = cap * systems
    chunk = group + 1
    devices = term_ref.shape[0] // chunk
    for c in range(cap + 1):
        here = lax.shift_right_logical(iota((group, depth), 0), systems.bit_length() - 1) == c
        masks[c] = here.astype(F32).astype(BF16)
    term_ref[...] = jnp.zeros(term_ref.shape, F32)
    lows[...] = jnp.zeros(lows.shape, BF16)
    total = jnp.zeros((blocks * group, width), F32)
    for t in range(tiles):
        if t >= HELD and (t - HELD) % part == 0:
            copies[(t - HELD) // part].wait()
        owner, rank, block = meta_ref[0, t], meta_ref[1, t], meta_ref[2, t]
        rows = fetched_ref[pl.ds(pl.multiple_of(owner * group, group), group), :]
        left = jnp.concatenate(
            [rows * masks[jnp.where(block == b, rank, cap)] for b in range(blocks)], axis=0
        )
        total = total + lax.dot_general(
            left, tile(t), (((1,), (1,)), ((), ())), preferred_element_type=F32
        )
    for copy in small:
        copy.wait()
    square = jnp.zeros((systems, width), F32)
    for b in range(blocks):
        traced = jnp.zeros((systems, width), F32)
        for c in range(cap):
            at = b * group + c * systems
            traced = traced + total[at : at + systems]
        old = jnp.concatenate(
            [old_ref[r, 0, :, b * width : (b + 1) * width] * rec_ref[0:1, r : r + 1] for r in range(systems)], axis=0
        )
        live = iota((systems, width), 1) + b * width < meta_ref[3, 0]
        bar = jnp.where(live, traced - old, 0.0)
        square = square + bar * bar
        for r in range(systems):
            bar_ref[r, 0, :, b * width : (b + 1) * width] = bar[r : r + 1]
        lows[b] = jnp.concatenate([bar, jnp.zeros((16 - systems, width), F32)], axis=0).astype(BF16)
    ray_sq = jnp.sum(square, axis=1, keepdims=True)
    part = sums_ref[...]
    for r in range(systems):
        part = place(part, r, ray_sq[r : r + 1])
    for e in range(devices):
        term_ref[e * chunk + group] = part
    for t in range(tiles):
        row = meta_ref[0, t] * chunk + meta_ref[1, t] * systems
        term = jnp.dot(lows[meta_ref[2, t]], tile(t), preferred_element_type=F32)
        for r in range(systems):
            term_ref[row + r] = term[r : r + 1]


def combine_body(chunk, systems, terms_ref, chosen_ref, patch_ref, model_patch_ref, sums_ref, added_ref, residual_ref, parts_ref, split):
    arrived, depth = terms_ref.shape
    devices = parts_ref.shape[0]
    width = patch_ref.shape[0]
    x = terms_ref[...]
    high = x.astype(BF16)
    rest = x - high.astype(F32)
    middle = rest.astype(BF16)
    low = (rest - middle.astype(F32)).astype(BF16)
    padded = split.shape[0]
    if padded > arrived:
        split[arrived:] = jnp.zeros((padded - arrived, split.shape[1]), BF16)
    split[0:arrived, 0:depth] = high
    split[0:arrived, depth : 2 * depth] = middle
    split[0:arrived, 2 * depth :] = low
    three = jnp.dot(chosen_ref[...], split[...], preferred_element_type=F32)
    added = three[:, 0:depth] + (three[:, depth : 2 * depth] + three[:, 2 * depth :])
    added_ref[...] = added
    every = terms_ref[pl.ds(chunk - 1, devices, stride=chunk), :]
    total = jnp.sum(every, axis=0, keepdims=True)
    residual_ref[...] = jnp.where(iota(total.shape, 1) == depth - 1, sums_ref[...], total)
    square = added * (2.0 * patch_ref[...] + added)
    cross = added * model_patch_ref[...]
    row = sums_ref[...]
    each = width // systems
    for r in range(systems):
        row = place(row, systems + r, jnp.sum(square[r * each : (r + 1) * each], keepdims=True))
        row = place(row, 2 * systems + r, jnp.sum(cross[r * each : (r + 1) * each], keepdims=True))
    parts_ref[...] = jnp.broadcast_to(row, parts_ref.shape)


def first_norm(residual_ref, systems, rows_all):
    return jnp.sqrt(residual_ref[0:1, 0:systems] / rows_all + EPSILON)


def early_body(
    rows_all,
    residual_ref,
    rec_ref,
    ray_ref,
    bar_in,
    solution_in,
    search_in,
    ray_out,
    damp_out,
    solution_out,
    kept_ref,
    bar_ref,
    solution_ref,
    search_ref,
    damp_s,
    solution_s,
    coef,
    in_sems,
    sems,
):
    systems, columns, _ = bar_ref.shape
    rows = columns // PIECES
    kept = kept_ref.shape[0]
    ins = ((bar_in, bar_ref), (solution_in, solution_ref))
    outs = ((damp_s, damp_out), (solution_s, solution_out))

    def start(n):
        if n < systems * PIECES:
            begin(fetch(n))

    def fetch(n):
        r, p = n // PIECES, n % PIECES
        at = pl.ds(p * rows, rows)
        target = kept_ref.at[r, at] if r < kept else search_ref.at[0, at]
        return pieces(ins, in_sems, r, p, rows) + [
            pltpu.make_async_copy(search_in.at[r, at], target, in_sems.at[r, p, 2])
        ]

    for n in range(AHEAD):
        start(n)
    rho_bar, phi_bar = rec_ref[1:2], rec_ref[2:3]
    beta = first_norm(residual_ref, systems, rows_all)
    rho = jnp.sqrt(rho_bar * rho_bar + beta * beta)
    scales = (1.0 / beta, (rho_bar / rho) * phi_bar / rho)
    for q, scale in enumerate(scales):
        for s in range(systems):
            coef[q, s] = scale[0, s]
    for s in range(systems):
        ray_out[s] = ray_ref[s] * coef[0, s]

    for n in range(systems * PIECES):
        r, p = n // PIECES, n % PIECES
        at = pl.ds(p * rows, rows)
        start(n + AHEAD)
        settle(fetch(n))
        search = kept_ref[r, at, :] if r < kept else search_ref[0, at, :]
        damp_s[r, at, :] = bar_ref[r, at, :] * coef[0, r]
        solution_s[r, at, :] = solution_ref[r, at, :] + search * coef[1, r]
        begin(pieces(outs, sems, r, p, rows))

    wait_all(outs, sems, systems, rows)


def finish_body(
    rows_all,
    cells_all,
    clon,
    residual_ref,
    parts_ref,
    added_ref,
    kept_ref,
    image_in,
    model_in,
    search_in,
    rec_in,
    model_out,
    search_out,
    rec_sent,
    image_ref,
    model_ref,
    search_ref,
    model_s,
    search_s,
    rec_ref,
    rec_out,
    coef,
    in_sems,
    sems,
    rec_sems,
):
    systems, columns, depth = image_ref.shape
    rec_copy = pltpu.make_async_copy(rec_in, rec_ref, rec_sems.at[0])
    rec_copy.start()
    rows = columns // PIECES
    kept = kept_ref.shape[0]
    ins = ((image_in, image_ref), (model_in, model_ref))
    outs = ((model_s, model_out), (search_s, search_out))

    def start(n):
        if n < systems * PIECES:
            begin(fetch(n))

    def fetch(n):
        r, p = n // PIECES, n % PIECES
        copies = pieces(ins, in_sems, r, p, rows)
        if r >= kept:
            at = pl.ds(p * rows, rows)
            copies.append(pltpu.make_async_copy(search_in.at[r, at], search_ref.at[0, at], in_sems.at[r, p, 2]))
        return copies

    for n in range(AHEAD):
        start(n)
    corner = residual_ref[0, depth - 1].astype(I32)
    total = jnp.sum(parts_ref[...], axis=0, keepdims=True)
    rec_copy.wait()
    image_sq, cross, model_sq = (total[:, q * systems : (q + 1) * systems] for q in range(1, 4))
    rho_bar, phi_bar = rec_ref[1:2], rec_ref[2:3]
    beta = first_norm(residual_ref, systems, rows_all)
    update_sq = image_sq / (beta * beta) - 2.0 * cross + beta * beta * model_sq
    alpha = jnp.sqrt(jnp.maximum(update_sq, 0.0) / cells_all + EPSILON)
    rho = jnp.sqrt(rho_bar * rho_bar + beta * beta)
    cosine = rho_bar / rho
    sine = beta / rho
    rec_out[...] = jnp.concatenate([alpha, -cosine * alpha, sine * phi_bar], axis=0)
    rec_done = pltpu.make_async_copy(rec_out, rec_sent, rec_sems.at[1])
    rec_done.start()
    scales = (1.0 / (beta * alpha), beta / alpha, sine * alpha / rho)
    for q, scale in enumerate(scales):
        for s in range(systems):
            coef[q, s] = scale[0, s]
    width = PATCH * clon

    for n in range(systems * PIECES):
        r, p = n // PIECES, n % PIECES
        at = pl.ds(p * rows, rows)
        start(n + AHEAD)
        settle(fetch(n))
        search = kept_ref[r, at, :] if r < kept else search_ref[0, at, :]
        new = image_ref[r, at, :] * coef[0, r] - model_ref[r, at, :] * coef[1, r]
        model_s[r, at, :] = new
        search_s[r, at, :] = new - search * coef[2, r]
        for k in range(PATCH):
            first = (corner + k) * clon

            @pl.when((first >= p * rows) & (first < (p + 1) * rows))
            def _():
                cells = pl.ds(pl.multiple_of(first, clon), clon)
                more = added_ref[r * width + k * clon : r * width + (k + 1) * clon, :] * coef[0, r]
                model_s[r, cells, :] = model_s[r, cells, :] + more
                search_s[r, cells, :] = search_s[r, cells, :] + more

        begin(pieces(outs, sems, r, p, rows))

    wait_all(outs, sems, systems, rows)
    rec_done.wait()


PIECES = 2
AHEAD = 4


def pieces(pairs, sems, r, p, rows):
    at = pl.ds(pl.multiple_of(p * rows, rows), rows)
    return [pltpu.make_async_copy(a.at[r, at], b.at[r, at], sems.at[r, p, k]) for k, (a, b) in enumerate(pairs)]


def begin(copies):
    for copy in copies:
        copy.start()


def settle(copies):
    for copy in copies:
        copy.wait()


def wait_all(pairs, sems, systems, rows):
    def one(n, _):
        for copy in pieces(pairs, sems, n // PIECES, n % PIECES, rows):
            copy.wait()
        return 0

    lax.fori_loop(0, systems * PIECES, one, 0)


PARTS = 3
HELD = 30


def shifted(x, axis, step):
    count = lax.axis_size(axis)
    if step > 0:
        pairs = [(i, i + 1) for i in range(count - 1)]
    else:
        pairs = [(i + 1, i) for i in range(count - 1)]
    return lax.ppermute(x, axis, pairs)


def exchange(x):
    return lax.all_to_all(x, AXES, split_axis=0, concat_axis=0, tiled=True)


def per_device(
    sensitivity,
    block_ids,
    block_offsets,
    ray_counts,
    ray_vector,
    damping_vector,
    model_vector,
    solution,
    search,
    recurrence,
):
    lat_size, lon_size = lax.axis_size("lat"), lax.axis_size("lon")
    devices = lat_size * lon_size
    tiles, width, depth = sensitivity.shape[2:]
    blocks = block_offsets.shape[-1] - 1
    systems, clat, clon, _ = model_vector.shape
    columns = clat * clon
    cap = max(2 * ((tiles + devices - 1) // devices), 16 // systems)
    slots = devices * cap
    group = cap * systems
    chunk = group + 1
    cells_all = devices * columns * depth
    rows_all = devices * blocks * width + cells_all
    lanes = 128
    full, flat = model_vector.shape, (systems, columns, depth)
    lines = (systems, PATCH * clon, depth)
    here, there, plain = pltpu.VMEM, pltpu.HBM, jax.ShapeDtypeStruct
    dma = pltpu.SemaphoreType.DMA
    model, damping = far(model_vector), far(damping_vector)
    model_flat, damping_flat = far(model_vector.reshape(flat)), far(damping_vector.reshape(flat))

    side = there((systems, 3 * clat, depth), F32)
    band = there((systems, 3, clon, depth), F32)
    asking, north_msg, south_msg, east_msg, west_msg, meta = call(
        functools.partial(flanks_body, columns.bit_length() - 1, blocks),
        "flanks",
        (there((devices, 1, 2 * systems * depth), F32), band, band, side, side, there((8, lanes), I32)),
        [vmem()] * 3 + [hbm(), hbm()],
        (vmem(),) * 6,
        scratch=[pltpu.VMEM((4, systems, clat, 8, depth), F32), dma((8,))],
        flops=1,
        moved=128 * systems * clat * depth,
    )(far(block_ids), block_offsets, ray_counts, model, damping)
    lists = exchange(asking)
    north = shifted(south_msg, "lat", 1)
    south = shifted(north_msg, "lat", -1)
    west = shifted(east_msg, "lon", 1)
    east = shifted(west_msg, "lon", -1)

    served, wanted, corner, diagonal = call(
        functools.partial(serve_body, cap, clat, clon),
        "serve",
        (
            there((slots * systems, depth), BF16),
            plain((devices, lanes), F32),
            plain((1,), I32),
            plain((4 * systems, depth), F32),
        ),
        [vmem(), hbm()],
        (vmem(), vmem(), smem(), vmem()),
        scratch=[pltpu.VMEM(lines, F32), pltpu.VMEM((slots * systems, depth), F32), dma((systems,))],
    )(lists, model_flat)
    fetched = exchange(served.reshape(devices, group, depth)).reshape(slots * systems, depth)

    edge, flank = there((systems, clon, depth), F32), there((systems, clat, depth), F32)
    bar, held, *border, sums = call(
        functools.partial(damp_body, clat, clon),
        "damp",
        (
            there(flat, F32),
            here((HELD, width, depth), BF16),
            edge,
            edge,
            flank,
            flank,
            there((1, lanes), F32),
        ),
        [vmem()] * 2 + [hbm()] * 2 + [vmem()] * 4 + [hbm()],
        (hbm(),) + (vmem(),) * 6,
        scratch=[pltpu.VMEM(flat, F32)] * 3 + [pltpu.SMEM((systems,), F32), dma((systems, 3)), dma],
        flops=20 * systems * columns * depth,
        moved=128 * systems * columns * depth,
    )(far(recurrence), diagonal, model_flat, damping_flat, north, south, west, east, far(sensitivity))

    ray_bar, terms = call(
        functools.partial(rays_body, cap, blocks),
        "rays",
        (there(ray_vector.shape, F32), there((devices * chunk, 1, depth), F32)),
        [smem(), vmem(), vmem()] + [hbm()] * 4,
        (vmem(), vmem()),
        scratch=[
            pltpu.VMEM((tiles - HELD, width, depth), BF16),
            pltpu.VMEM((cap + 1, group, depth), BF16),
            pltpu.VMEM((blocks + 1, 16, width), BF16),
            pltpu.VMEM(recurrence.shape, F32),
            pltpu.VMEM(ray_vector.shape, F32),
            pltpu.VMEM((1, lanes), F32),
            dma((PARTS + 3,)),
        ],
        flops=4 * tiles * width * depth * 16,
        moved=2 * tiles * width * depth,
    )(meta, near(held), fetched, far(sensitivity), far(recurrence), far(ray_vector), far(sums))
    arrived = exchange(terms.reshape(devices, 1, chunk * depth)).reshape(devices * chunk, depth)

    padded = -(-devices * chunk // lanes) * lanes
    height = systems * PATCH * clon
    patch = (height, depth)
    image, sums, patched, model_patch, chosen = call(
        functools.partial(image_body, chunk, clat, clon),
        "image",
        (
            there(flat, F32),
            plain((1, lanes), F32),
            plain(patch, F32),
            plain(patch, F32),
            plain((height, padded), BF16),
        ),
        [smem(), vmem(), hbm()] + [vmem()] * 4 + [hbm(), vmem()],
        (hbm(),) + (vmem(),) * 4,
        scratch=[pltpu.VMEM(flat, F32)] * 3 + [dma((systems, 3))],
        flops=20 * systems * columns * depth,
        moved=12 * systems * columns * depth,
    )(corner, wanted, far(bar), *(far(x) for x in border), model_flat, far(sums))

    added, residual, parts = call(
        functools.partial(combine_body, chunk, systems),
        "combine",
        (plain(patch, F32), plain((1, lanes), F32), there((devices, lanes), F32)),
        [vmem()] * 5,
        (vmem(),) * 3,
        scratch=[pltpu.VMEM((padded, 3 * depth), BF16)],
    )(arrived, chosen, patched, model_patch, sums)
    every = exchange(parts.reshape(devices, 1, lanes)).reshape(devices, lanes)

    search_flat = far(search.reshape(flat))
    ray_out, damp_out, solution_out, kept = call(
        functools.partial(early_body, float(rows_all)),
        "early",
        (there(ray_vector.shape, F32), there(flat, F32), there(flat, F32), here((systems - 1, columns, depth), F32)),
        [vmem()] * 3 + [hbm()] * 3,
        (vmem(), hbm(), hbm(), vmem()),
        scratch=[pltpu.VMEM(flat, F32)] * 2
        + [pltpu.VMEM((1, columns, depth), F32)]
        + [pltpu.VMEM(flat, F32)] * 2
        + [pltpu.SMEM((2, systems), F32), dma((systems, PIECES, 3)), dma((systems, PIECES, 2))],
        mib=32,
        flops=4 * systems * columns * depth,
        moved=20 * systems * columns * depth,
    )(residual, far(recurrence), far(ray_bar), far(bar), far(solution.reshape(flat)), search_flat)
    model_out, search_out, rec_out = call(
        functools.partial(finish_body, float(rows_all), float(cells_all), clon),
        "finish",
        (there(flat, F32), there(flat, F32), there(recurrence.shape, F32)),
        [vmem()] * 4 + [hbm()] * 4,
        (hbm(),) * 3,
        scratch=[pltpu.VMEM(flat, F32)] * 2
        + [pltpu.VMEM((1, columns, depth), F32)]
        + [pltpu.VMEM(flat, F32)] * 2
        + [pltpu.VMEM(recurrence.shape, F32)] * 2
        + [pltpu.SMEM((3, systems), F32), dma((systems, PIECES, 3)), dma((systems, PIECES, 2)), dma((2,))],
        mib=32,
        flops=6 * systems * columns * depth,
        moved=20 * systems * columns * depth,
    )(residual, every, added, near(kept), far(image), model_flat, search_flat, far(recurrence))
    fields = (x.reshape(full) for x in (damp_out, model_out, solution_out, search_out))
    return (ray_out, *fields, rec_out)


def solution(mesh):
    fields = P(None, "lat", "lon", None)
    return jax.shard_map(
        per_device,
        mesh=mesh,
        in_specs=(
            P("lat", "lon", None, None, None),
            P("lat", "lon", None),
            P("lat", "lon", None),
            P("lat", "lon"),
            fields,
            fields,
            fields,
            fields,
            fields,
            P(),
        ),
        out_specs=(fields, fields, fields, fields, fields, P()),
        check_vma=False,
    )
```

```python
import functools

import jax
import jax.numpy as jnp
from jax import lax
from jax.experimental import pallas as pl
from jax.experimental.pallas import tpu as pltpu
from jax.sharding import PartitionSpec as P

DAMP_WEIGHT = 0.15
EPSILON = 1e-05
AXES = ("lat", "lon")
PATCH = 4
F32, BF16, I32 = jnp.float32, jnp.bfloat16, jnp.int32


def iota(shape, dim):
    return lax.broadcasted_iota(I32, shape, dim)


def vmem():
    return pl.BlockSpec(memory_space=pltpu.VMEM)


def hbm():
    return pl.BlockSpec(memory_space=pltpu.HBM)


def near(x):
    return pltpu.with_memory_space_constraint(x, pltpu.VMEM)


def far(x):
    return pltpu.with_memory_space_constraint(x, pltpu.HBM)


def smem():
    return pl.BlockSpec(memory_space=pltpu.SMEM)


def call(body, name, out_shape, in_specs, out_specs, scratch=(), grid=(), mib=16, flops=0, moved=0):
    return pl.pallas_call(
        body,
        name=name,
        grid=grid,
        out_shape=out_shape,
        in_specs=in_specs,
        out_specs=out_specs,
        scratch_shapes=list(scratch),
        compiler_params=pltpu.CompilerParams(vmem_limit_bytes=mib * 2**20),
        cost_estimate=pl.CostEstimate(flops=flops, bytes_accessed=moved, transcendentals=0),
    )


STEP = 8


def wanted_column(wanted, cap):
    devices, lanes = wanted.shape
    rows = devices * cap
    spread = jnp.broadcast_to(wanted[:, None, :], (devices, cap, lanes)).reshape(rows, lanes)
    pick = iota((rows, lanes), 1) == (iota((rows, lanes), 0) & (cap - 1))
    return jnp.sum(jnp.where(pick, spread, 0.0), axis=1, keepdims=True)


def serve_body(cap, clat, clon, lists_ref, model_in, north, south, west, east, served_ref, wanted_ref, corner_ref, diagonal_ref, patch, mixed, sems):
    systems, width, depth = patch.shape
    devices = lists_ref.shape[0]
    lanes = 128
    shift = (clat * clon).bit_length() - 1
    me = lax.axis_index("lat") * lax.axis_size("lon") + lax.axis_index("lon")
    ids = lists_ref[:, 0, 0:lanes].astype(I32)
    column = ids - lax.shift_left(me, shift)
    mine = (column >= 0) & (column < clat * clon) & (ids >= 0)
    first = jnp.min(jnp.where(mine, column, clat * clon))
    corner = jnp.minimum(lax.shift_right_logical(first, clon.bit_length() - 1), clat - PATCH)
    corner_ref[0] = corner
    at = pl.ds(pl.multiple_of(corner * clon, clon), width)
    copies = [pltpu.make_async_copy(model_in.at[r, at], patch.at[r], sems.at[r]) for r in range(systems)]
    for copy in copies:
        copy.start()
    ahead = (iota((lanes, lanes), 0) < iota((lanes, lanes), 1)).astype(F32).astype(BF16)
    rank = jnp.dot(mine.astype(F32).astype(BF16), ahead, preferred_element_type=F32)
    value = (column - corner * clon + 1).astype(F32)
    at = iota((devices, lanes), 1)
    wanted = jnp.zeros((devices, lanes), F32)
    for c in range(cap):
        picked = jnp.sum(jnp.where(mine & (rank == c), value, 0.0), axis=1, keepdims=True)
        wanted = jnp.where(at == c, picked, wanted)
    wanted_ref[...] = wanted
    target = wanted_column(wanted, cap).astype(I32) - 1
    rows = target.shape[0]
    chosen = (jnp.broadcast_to(target, (rows, width)) == iota((rows, width), 1)).astype(F32).astype(BF16)
    for r in range(systems):
        copies[r].wait()
        table = patch[r].astype(BF16)
        mixed[pl.ds(r, rows, stride=systems), :] = jnp.dot(chosen, table, preferred_element_type=F32)
    served_ref[...] = mixed[...].astype(BF16)
    lat_at, lon_at = lax.axis_index("lat"), lax.axis_index("lon")
    lat_size, lon_size = lax.axis_size("lat"), lax.axis_size("lon")
    for k in range(4):
        lat_to, lon_to = lat_at + 2 * (k // 2) - 1, lon_at + 2 * (k % 2) - 1
        inside = (lat_to >= 0) & (lat_to < lat_size) & (lon_to >= 0) & (lon_to < lon_size)
        source = jnp.where(inside, lat_to * lon_size + lon_to, 0)
        flag = inside.astype(F32)
        for r in range(systems):
            got = lists_ref[source, :, (r + 1) * depth : (r + 2) * depth]
            diagonal_ref[k * systems + r : k * systems + r + 1, :] = got * flag


def flanks_body(
    shift,
    blocks,
    ids_in,
    off_in,
    count_ref,
    model_in,
    damp_in,
    asking_ref,
    north_ref,
    south_ref,
    east_ref,
    west_ref,
    meta_ref,
    slabs,
    ids_ref,
    off_ref,
    sems,
):
    systems, clat, clon, depth = model_in.shape
    copies = []
    for k, (ref, at) in enumerate(((model_in, 0), (model_in, clon - 8), (damp_in, 0), (damp_in, clon - 8))):
        copies.append(pltpu.make_async_copy(ref.at[:, :, pl.ds(at, 8)], slabs.at[k], sems.at[k]))
    last = clat - 1
    pairs = (
        (model_in.at[:, pl.ds(last - 1, 2)], south_ref.at[:, pl.ds(0, 2)]),
        (damp_in.at[:, pl.ds(last, 1)], south_ref.at[:, pl.ds(2, 1)]),
        (model_in.at[:, pl.ds(0, 2)], north_ref.at[:, pl.ds(0, 2)]),
        (damp_in.at[:, pl.ds(0, 1)], north_ref.at[:, pl.ds(2, 1)]),
    )
    copies += [pltpu.make_async_copy(a, b, sems.at[i + 4]) for i, (a, b) in enumerate(pairs)]
    small = [
        pltpu.make_async_copy(a, b, sems.at[i + 8]) for i, (a, b) in enumerate(((ids_in, ids_ref), (off_in, off_ref)))
    ]
    begin(small + copies)
    settle(small)
    tiles = ids_ref.shape[-1]
    lanes = 128
    ids = jnp.concatenate([ids_ref[0], jnp.full((1, lanes - tiles), -1, I32)], axis=1)
    owner = lax.shift_right_arithmetic(ids, shift)
    square = (lanes, lanes)
    down, across = iota(square, 0), iota(square, 1)
    owner_f = jnp.broadcast_to(owner.astype(F32), square)
    owner_col = jnp.sum(jnp.where(down == across, owner_f, 0.0), axis=1, keepdims=True)
    same = jnp.where((owner_f == owner_col) & (down < across), 1.0, 0.0)
    rank = jnp.sum(same, axis=0, keepdims=True).astype(I32)
    lane = iota((1, lanes), 1)
    block = jnp.zeros((1, lanes), I32)
    starts = off_ref[0]
    for b in range(1, blocks + 1):
        block = block + (lane >= jnp.broadcast_to(starts[:, b : b + 1], (1, lanes))).astype(I32)
    count = jnp.full((1, lanes), count_ref[0, 0], I32)
    meta_ref[...] = jnp.concatenate([owner, rank, block, count] + [owner] * 4, axis=0)
    for copy in copies:
        copy.wait()
    listed = ids.astype(F32)
    asking_ref[...] = jnp.zeros(asking_ref.shape, F32)
    corners = [
        [slabs[k % 2, r, (k // 2) * last, (k % 2) * 7 : (k % 2) * 7 + 1] for r in range(systems)]
        for k in range(4)
    ]
    lat_at, lon_at = lax.axis_index("lat"), lax.axis_index("lon")
    width = lax.axis_size("lon")
    for e in range(asking_ref.shape[0]):
        asking_ref[e, :, 0:depth] = listed
        to_south, to_east = e // width > lat_at, e % width > lon_at
        for r in range(systems):
            upper = jnp.where(to_east, corners[1][r], corners[0][r])
            lower = jnp.where(to_east, corners[3][r], corners[2][r])
            asking_ref[e, :, (r + 1) * depth : (r + 2) * depth] = jnp.where(to_south, lower, upper)
    rows = slabs.reshape(4, systems, clat * 8, depth)
    for r in range(systems):
        for out, slab, near_at, beyond in ((east_ref, 1, 7, 6), (west_ref, 0, 0, 1)):
            out[r, 0:clat] = rows[slab, r, pl.ds(near_at, clat, stride=8), :]
            out[r, clat : 2 * clat] = rows[slab, r, pl.ds(beyond, clat, stride=8), :]
            out[r, 2 * clat : 3 * clat] = rows[slab + 2, r, pl.ds(near_at, clat, stride=8), :]


def six(x, north, south, west, east):
    lane = iota(x.shape, 1)
    rows, depth = x.shape
    left, right = pltpu.roll(x, 1, 0), pltpu.roll(x, rows - 1, 0)
    ends = (8, depth)
    row = iota(ends, 0)
    left = jnp.concatenate([jnp.where(row == 0, jnp.broadcast_to(west, ends), left[:8]), left[8:]], axis=0)
    right = jnp.concatenate([right[:-8], jnp.where(row == 7, jnp.broadcast_to(east, ends), right[-8:])], axis=0)
    above = jnp.where(lane == 0, 0.0, pltpu.roll(x, 1, 1))
    below = jnp.where(lane == depth - 1, 0.0, pltpu.roll(x, depth - 1, 1))
    beside = north + south + left + right + above + below
    return DAMP_WEIGHT * (6.0 * x - beside)


def fold(x):
    parts = [x[i * 8 : (i + 1) * 8] for i in range(x.shape[0] // 8)]
    return functools.reduce(lambda a, b: a + b, parts)


def place(row, lane, value):
    return row + jnp.where(iota(row.shape, 1) == lane, jnp.broadcast_to(value, row.shape), 0.0)


def line(ref, r, i, clon):
    return ref[r, pl.ds(pl.multiple_of(i * clon, clon), clon), :]


def stencils(ref, r, k, clat, clon, first, last, west, east):
    base = k * STEP
    for j in range(STEP):
        i = base + j
        x = line(ref, r, i, clon)
        if j == 0:
            above = jnp.where(k > 0, line(ref, r, jnp.maximum(i - 1, 0), clon), first)
        else:
            above = line(ref, r, i - 1, clon)
        if j == STEP - 1:
            below = jnp.where(i + 1 < clat, line(ref, r, jnp.minimum(i + 1, clat - 1), clon), last)
        else:
            below = line(ref, r, i + 1, clon)
        yield i, x, six(x, above, below, west[pl.ds(i, 1)], east[pl.ds(i, 1)])


def damp_body(
    clat,
    clon,
    diagonal_ref,
    model_in,
    damp_in,
    rec_in,
    north_in,
    south_in,
    west_in,
    east_in,
    tiles_in,
    bar_sent,
    held_out,
    north_out,
    south_out,
    west_out,
    east_out,
    sums_out,
    model_ref,
    damp_ref,
    bar_out,
    rec_ref,
    north_ref,
    south_ref,
    west_ref,
    east_ref,
    alphas,
    sems,
    hold_sem,
    halo_sems,
):
    systems, _, depth = model_ref.shape

    def incoming(r):
        return (
            pltpu.make_async_copy(model_in.at[r], model_ref.at[r], sems.at[r, 0]),
            pltpu.make_async_copy(damp_in.at[r], damp_ref.at[r], sems.at[r, 1]),
        )

    def outgoing(r):
        return pltpu.make_async_copy(bar_out.at[r], bar_sent.at[r], sems.at[r, 2])

    holding = pltpu.make_async_copy(tiles_in.at[0, 0, pl.ds(0, HELD)], held_out, hold_sem)
    halos = [
        pltpu.make_async_copy(a, b, halo_sems.at[k])
        for k, (a, b) in enumerate(
            (
                (rec_in, rec_ref),
                (north_in, north_ref),
                (south_in, south_ref),
                (west_in, west_ref),
                (east_in, east_ref),
            )
        )
    ]
    begin(halos)
    for r in range(systems):
        begin(incoming(r))
    holding.start()
    settle(halos)
    for r in range(systems):
        alphas[r] = jnp.sum(rec_ref[0:1, r : r + 1])
    lat_at, lon_at = lax.axis_index("lat"), lax.axis_index("lon")
    has_north = (lat_at > 0).astype(F32)
    has_south = (lat_at < lax.axis_size("lat") - 1).astype(F32)
    has_west = (lon_at > 0).astype(F32)
    has_east = (lon_at < lax.axis_size("lon") - 1).astype(F32)

    def diagonal(k, r):
        return diagonal_ref[pl.ds(k * systems + r, 1), :]

    def system(r, row):
        alpha = alphas[r]
        for copy in incoming(r):
            copy.wait()

        def side(ref, own, flag, east):
            x, beyond, old = ref[r, 0:clat], ref[r, clat : 2 * clat], ref[r, 2 * clat : 3 * clat]
            upper, lower = diagonal(east, r), diagonal(2 + east, r)
            return (six(x, beyond, own, upper, lower) - alpha * old) * flag

        west_out[r] = side(west_ref, model_ref[r, pl.ds(0, clat, stride=clon), :], has_west, 0)
        east_out[r] = side(east_ref, model_ref[r, pl.ds(clon - 1, clat, stride=clon), :], has_east, 1)
        top, bottom = line(model_ref, r, 0, clon), line(model_ref, r, clat - 1, clon)
        edge = six(north_ref[r, 1], north_ref[r, 0], top, diagonal(0, r), diagonal(1, r))
        north_out[r] = has_north * (edge - alpha * north_ref[r, 2])
        edge = six(south_ref[r, 0], bottom, south_ref[r, 1], diagonal(2, r), diagonal(3, r))
        south_out[r] = has_south * (edge - alpha * south_ref[r, 2])

        def damped(k, acc):
            bar_sq, model_sq = acc
            ends = (north_ref[r, 1], south_ref[r, 0], west_ref.at[r], east_ref.at[r])
            for i, x, got in stencils(model_ref, r, k, clat, clon, *ends):
                bar = got - alpha * line(damp_ref, r, i, clon)
                bar_out[r, pl.ds(pl.multiple_of(i * clon, clon), clon), :] = bar
                bar_sq, model_sq = bar_sq + fold(bar * bar), model_sq + fold(x * x)
            return bar_sq, model_sq

        zero = jnp.zeros((8, depth), F32)
        bar_sq, model_sq = lax.fori_loop(0, clat // STEP, damped, (zero, zero))
        outgoing(r).start()
        row = place(row, r, jnp.sum(bar_sq, keepdims=True))
        return place(row, 3 * systems + r, jnp.sum(model_sq, keepdims=True))

    sums_out[...] = lax.fori_loop(0, systems, system, jnp.zeros((1, depth), F32))
    holding.wait()
    for r in range(systems):
        outgoing(r).wait()


def image_body(
    chunk,
    clat,
    clon,
    corner_ref,
    wanted_ref,
    bar_in,
    north_ref,
    south_ref,
    west_ref,
    east_ref,
    model_in,
    sums_ref,
    image_sent,
    sums_out,
    patch_out,
    model_patch_out,
    chosen_out,
    bar_ref,
    model_ref,
    image_out,
    sems,
):
    systems, _, depth = model_ref.shape

    def incoming(r):
        return (
            pltpu.make_async_copy(bar_in.at[r], bar_ref.at[r], sems.at[r, 0]),
            pltpu.make_async_copy(model_in.at[r], model_ref.at[r], sems.at[r, 1]),
        )

    def outgoing(r):
        return pltpu.make_async_copy(image_out.at[r], image_sent.at[r], sems.at[r, 2])

    for r in range(systems):
        for copy in incoming(r):
            copy.start()
    corner = corner_ref[0]
    wanted = wanted_ref[...]
    devices = wanted.shape[0]
    height, slots = chosen_out.shape
    width = PATCH * clon
    at = iota((1, slots), 1)
    source = jnp.floor((at.astype(F32) + 0.5) * (1.0 / chunk)).astype(I32)
    inner = at - source * chunk
    from_e = (jnp.broadcast_to(source, (devices, slots)) == iota((devices, slots), 0)).astype(F32).astype(BF16)
    turned = jnp.transpose(wanted)[0:8].astype(BF16)
    listed = jnp.dot(turned, from_e, preferred_element_type=F32)
    slot_of = lax.shift_right_logical(inner, systems.bit_length() - 1)
    mine = jnp.broadcast_to(slot_of, listed.shape) == iota(listed.shape, 0)
    flat = jnp.sum(jnp.where(mine, listed, 0.0), axis=0, keepdims=True).astype(I32)
    used = (flat > 0) & (inner < chunk - 1)
    target = jnp.where(used, (inner & (systems - 1)) * width + flat - 1, -1)
    for k in range(height // 64):
        shape = (64, slots)
        hit = jnp.broadcast_to(target, shape) == iota(shape, 0) + k * 64
        chosen_out[k * 64 : (k + 1) * 64] = hit.astype(F32).astype(BF16)

    def system(r, row):
        for copy in incoming(r):
            copy.wait()

        def imaged(k, acc):
            image_sq, cross = acc
            ends = (north_ref[r], south_ref[r], west_ref.at[r], east_ref.at[r])
            for i, x, image in stencils(bar_ref, r, k, clat, clon, *ends):
                image_out[r, pl.ds(pl.multiple_of(i * clon, clon), clon), :] = image
                image_sq = image_sq + fold(image * image)
                cross = cross + fold(image * line(model_ref, r, i, clon))
            return image_sq, cross

        zero = jnp.zeros((8, depth), F32)
        image_sq, cross = lax.fori_loop(0, clat // STEP, imaged, (zero, zero))
        outgoing(r).start()
        here = pl.ds(pl.multiple_of(corner * clon, clon), width)
        there = pl.ds(pl.multiple_of(r * width, width), width)
        patch_out[there, :] = image_out[r, here, :]
        model_patch_out[there, :] = model_ref[r, here, :]
        row = place(row, systems + r, jnp.sum(image_sq, keepdims=True))
        return place(row, 2 * systems + r, jnp.sum(cross, keepdims=True))

    row = lax.fori_loop(0, systems, system, sums_ref[...])
    sums_out[...] = place(row, depth - 1, corner.astype(F32))
    for r in range(systems):
        outgoing(r).wait()


def rays_body(
    cap, blocks, meta_ref, held_ref, fetched_ref, tiles_in, *refs
):
    rec_in, old_in, sums_in, bar_ref, term_ref, rest_ref, masks, lows, rec_ref, old_ref, sums_ref, sems = refs
    tiles, width, depth = tiles_in.shape[2:]
    small = [
        pltpu.make_async_copy(a, b, sems.at[PARTS + k])
        for k, (a, b) in enumerate(((rec_in, rec_ref), (old_in, old_ref), (sums_in, sums_ref)))
    ]
    part = -(-(tiles - HELD) // PARTS)
    copies = []
    for k in range(PARTS):
        count = min(part, tiles - HELD - k * part)
        source = tiles_in.at[0, 0, pl.ds(HELD + k * part, count)]
        copies.append(pltpu.make_async_copy(source, rest_ref.at[pl.ds(k * part, count)], sems.at[k]))
    for copy in copies + small:
        copy.start()

    def tile(t):
        return held_ref[t] if t < HELD else rest_ref[t - HELD]

    systems = old_ref.shape[0]
    group = cap * systems
    chunk = group + 1
    devices = term_ref.shape[0] // chunk
    for c in range(cap + 1):
        here = lax.shift_right_logical(iota((group, depth), 0), systems.bit_length() - 1) == c
        masks[c] = here.astype(F32).astype(BF16)
    term_ref[...] = jnp.zeros(term_ref.shape, F32)
    lows[...] = jnp.zeros(lows.shape, BF16)
    total = jnp.zeros((blocks * group, width), F32)
    for t in range(tiles):
        if t >= HELD and (t - HELD) % part == 0:
            copies[(t - HELD) // part].wait()
        owner, rank, block = meta_ref[0, t], meta_ref[1, t], meta_ref[2, t]
        rows = fetched_ref[pl.ds(pl.multiple_of(owner * group, group), group), :]
        left = jnp.concatenate(
            [rows * masks[jnp.where(block == b, rank, cap)] for b in range(blocks)], axis=0
        )
        total = total + lax.dot_general(
            left, tile(t), (((1,), (1,)), ((), ())), preferred_element_type=F32
        )
    for copy in small:
        copy.wait()
    square = jnp.zeros((systems, width), F32)
    for b in range(blocks):
        traced = jnp.zeros((systems, width), F32)
        for c in range(cap):
            at = b * group + c * systems
            traced = traced + total[at : at + systems]
        old = jnp.concatenate(
            [old_ref[r, 0, :, b * width : (b + 1) * width] * rec_ref[0:1, r : r + 1] for r in range(systems)], axis=0
        )
        live = iota((systems, width), 1) + b * width < meta_ref[3, 0]
        bar = jnp.where(live, traced - old, 0.0)
        square = square + bar * bar
        for r in range(systems):
            bar_ref[r, 0, :, b * width : (b + 1) * width] = bar[r : r + 1]
        lows[b] = jnp.concatenate([bar, jnp.zeros((16 - systems, width), F32)], axis=0).astype(BF16)
    ray_sq = jnp.sum(square, axis=1, keepdims=True)
    part = sums_ref[...]
    for r in range(systems):
        part = place(part, r, ray_sq[r : r + 1])
    for e in range(devices):
        term_ref[e * chunk + group] = part
    for t in range(tiles):
        row = meta_ref[0, t] * chunk + meta_ref[1, t] * systems
        term = jnp.dot(lows[meta_ref[2, t]], tile(t), preferred_element_type=F32)
        for r in range(systems):
            term_ref[row + r] = term[r : r + 1]


def combine_body(chunk, systems, terms_ref, chosen_ref, patch_ref, model_patch_ref, sums_ref, added_ref, residual_ref, parts_ref, split):
    arrived, depth = terms_ref.shape
    devices = parts_ref.shape[0]
    width = patch_ref.shape[0]
    x = terms_ref[...]
    high = x.astype(BF16)
    rest = x - high.astype(F32)
    middle = rest.astype(BF16)
    low = (rest - middle.astype(F32)).astype(BF16)
    padded = split.shape[0]
    if padded > arrived:
        split[arrived:] = jnp.zeros((padded - arrived, split.shape[1]), BF16)
    split[0:arrived, 0:depth] = high
    split[0:arrived, depth : 2 * depth] = middle
    split[0:arrived, 2 * depth :] = low
    three = jnp.dot(chosen_ref[...], split[...], preferred_element_type=F32)
    added = three[:, 0:depth] + (three[:, depth : 2 * depth] + three[:, 2 * depth :])
    added_ref[...] = added
    every = terms_ref[pl.ds(chunk - 1, devices, stride=chunk), :]
    total = jnp.sum(every, axis=0, keepdims=True)
    residual_ref[...] = jnp.where(iota(total.shape, 1) == depth - 1, sums_ref[...], total)
    square = added * (2.0 * patch_ref[...] + added)
    cross = added * model_patch_ref[...]
    row = sums_ref[...]
    each = width // systems
    for r in range(systems):
        row = place(row, systems + r, jnp.sum(square[r * each : (r + 1) * each], keepdims=True))
        row = place(row, 2 * systems + r, jnp.sum(cross[r * each : (r + 1) * each], keepdims=True))
    parts_ref[...] = jnp.broadcast_to(row, parts_ref.shape)


def first_norm(residual_ref, systems, rows_all):
    return jnp.sqrt(residual_ref[0:1, 0:systems] / rows_all + EPSILON)


def early_body(
    rows_all,
    residual_ref,
    rec_ref,
    ray_ref,
    bar_in,
    solution_in,
    search_in,
    ray_out,
    damp_out,
    solution_out,
    kept_ref,
    bar_ref,
    solution_ref,
    search_ref,
    damp_s,
    solution_s,
    coef,
    in_sems,
    sems,
):
    systems, columns, _ = bar_ref.shape
    rows = columns // PIECES
    kept = kept_ref.shape[0]
    ins = ((bar_in, bar_ref), (solution_in, solution_ref))
    outs = ((damp_s, damp_out), (solution_s, solution_out))

    def start(n):
        if n < systems * PIECES:
            begin(fetch(n))

    def fetch(n):
        r, p = n // PIECES, n % PIECES
        at = pl.ds(p * rows, rows)
        target = kept_ref.at[r, at] if r < kept else search_ref.at[0, at]
        return pieces(ins, in_sems, r, p, rows) + [
            pltpu.make_async_copy(search_in.at[r, at], target, in_sems.at[r, p, 2])
        ]

    for n in range(AHEAD):
        start(n)
    rho_bar, phi_bar = rec_ref[1:2], rec_ref[2:3]
    beta = first_norm(residual_ref, systems, rows_all)
    rho = jnp.sqrt(rho_bar * rho_bar + beta * beta)
    scales = (1.0 / beta, (rho_bar / rho) * phi_bar / rho)
    for q, scale in enumerate(scales):
        for s in range(systems):
            coef[q, s] = scale[0, s]
    for s in range(systems):
        ray_out[s] = ray_ref[s] * coef[0, s]

    for n in range(systems * PIECES):
        r, p = n // PIECES, n % PIECES
        at = pl.ds(p * rows, rows)
        start(n + AHEAD)
        settle(fetch(n))
        search = kept_ref[r, at, :] if r < kept else search_ref[0, at, :]
        damp_s[r, at, :] = bar_ref[r, at, :] * coef[0, r]
        solution_s[r, at, :] = solution_ref[r, at, :] + search * coef[1, r]
        begin(pieces(outs, sems, r, p, rows))

    wait_all(outs, sems, systems, rows)


def finish_body(
    rows_all,
    cells_all,
    clon,
    residual_ref,
    parts_ref,
    added_ref,
    kept_ref,
    image_in,
    model_in,
    search_in,
    rec_in,
    model_out,
    search_out,
    rec_sent,
    image_ref,
    model_ref,
    search_ref,
    model_s,
    search_s,
    rec_ref,
    rec_out,
    coef,
    in_sems,
    sems,
    rec_sems,
):
    systems, columns, depth = image_ref.shape
    rec_copy = pltpu.make_async_copy(rec_in, rec_ref, rec_sems.at[0])
    rec_copy.start()
    rows = columns // PIECES
    kept = kept_ref.shape[0]
    ins = ((image_in, image_ref), (model_in, model_ref))
    outs = ((model_s, model_out), (search_s, search_out))

    def start(n):
        if n < systems * PIECES:
            begin(fetch(n))

    def fetch(n):
        r, p = n // PIECES, n % PIECES
        copies = pieces(ins, in_sems, r, p, rows)
        if r >= kept:
            at = pl.ds(p * rows, rows)
            copies.append(pltpu.make_async_copy(search_in.at[r, at], search_ref.at[0, at], in_sems.at[r, p, 2]))
        return copies

    for n in range(AHEAD):
        start(n)
    corner = residual_ref[0, depth - 1].astype(I32)
    total = jnp.sum(parts_ref[...], axis=0, keepdims=True)
    rec_copy.wait()
    image_sq, cross, model_sq = (total[:, q * systems : (q + 1) * systems] for q in range(1, 4))
    rho_bar, phi_bar = rec_ref[1:2], rec_ref[2:3]
    beta = first_norm(residual_ref, systems, rows_all)
    update_sq = image_sq / (beta * beta) - 2.0 * cross + beta * beta * model_sq
    alpha = jnp.sqrt(jnp.maximum(update_sq, 0.0) / cells_all + EPSILON)
    rho = jnp.sqrt(rho_bar * rho_bar + beta * beta)
    cosine = rho_bar / rho
    sine = beta / rho
    rec_out[...] = jnp.concatenate([alpha, -cosine * alpha, sine * phi_bar], axis=0)
    rec_done = pltpu.make_async_copy(rec_out, rec_sent, rec_sems.at[1])
    rec_done.start()
    scales = (1.0 / (beta * alpha), beta / alpha, sine * alpha / rho)
    for q, scale in enumerate(scales):
        for s in range(systems):
            coef[q, s] = scale[0, s]
    width = PATCH * clon

    for n in range(systems * PIECES):
        r, p = n // PIECES, n % PIECES
        at = pl.ds(p * rows, rows)
        start(n + AHEAD)
        settle(fetch(n))
        search = kept_ref[r, at, :] if r < kept else search_ref[0, at, :]
        new = image_ref[r, at, :] * coef[0, r] - model_ref[r, at, :] * coef[1, r]
        model_s[r, at, :] = new
        search_s[r, at, :] = new - search * coef[2, r]
        for k in range(PATCH):
            first = (corner + k) * clon

            @pl.when((first >= p * rows) & (first < (p + 1) * rows))
            def _():
                cells = pl.ds(pl.multiple_of(first, clon), clon)
                more = added_ref[r * width + k * clon : r * width + (k + 1) * clon, :] * coef[0, r]
                model_s[r, cells, :] = model_s[r, cells, :] + more
                search_s[r, cells, :] = search_s[r, cells, :] + more

        begin(pieces(outs, sems, r, p, rows))

    wait_all(outs, sems, systems, rows)
    rec_done.wait()


PIECES = 2
AHEAD = 4


def pieces(pairs, sems, r, p, rows):
    at = pl.ds(pl.multiple_of(p * rows, rows), rows)
    return [pltpu.make_async_copy(a.at[r, at], b.at[r, at], sems.at[r, p, k]) for k, (a, b) in enumerate(pairs)]


def begin(copies):
    for copy in copies:
        copy.start()


def settle(copies):
    for copy in copies:
        copy.wait()


def wait_all(pairs, sems, systems, rows):
    def one(n, _):
        for copy in pieces(pairs, sems, n // PIECES, n % PIECES, rows):
            copy.wait()
        return 0

    lax.fori_loop(0, systems * PIECES, one, 0)


PARTS = 3
HELD = 30


def shifted(x, axis, step):
    count = lax.axis_size(axis)
    if step > 0:
        pairs = [(i, i + 1) for i in range(count - 1)]
    else:
        pairs = [(i + 1, i) for i in range(count - 1)]
    return lax.ppermute(x, axis, pairs)


def exchange(x):
    return lax.all_to_all(x, AXES, split_axis=0, concat_axis=0, tiled=True)


def per_device(
    sensitivity,
    block_ids,
    block_offsets,
    ray_counts,
    ray_vector,
    damping_vector,
    model_vector,
    solution,
    search,
    recurrence,
):
    lat_size, lon_size = lax.axis_size("lat"), lax.axis_size("lon")
    devices = lat_size * lon_size
    tiles, width, depth = sensitivity.shape[2:]
    blocks = block_offsets.shape[-1] - 1
    systems, clat, clon, _ = model_vector.shape
    columns = clat * clon
    cap = max(2 * ((tiles + devices - 1) // devices), 16 // systems)
    slots = devices * cap
    group = cap * systems
    chunk = group + 1
    cells_all = devices * columns * depth
    rows_all = devices * blocks * width + cells_all
    lanes = 128
    full, flat = model_vector.shape, (systems, columns, depth)
    lines = (systems, PATCH * clon, depth)
    here, there, plain = pltpu.VMEM, pltpu.HBM, jax.ShapeDtypeStruct
    dma = pltpu.SemaphoreType.DMA
    model, damping = far(model_vector), far(damping_vector)
    model_flat, damping_flat = far(model_vector.reshape(flat)), far(damping_vector.reshape(flat))

    side = there((systems, 3 * clat, depth), F32)
    band = there((systems, 3, clon, depth), F32)
    asking, north_msg, south_msg, east_msg, west_msg, meta = call(
        functools.partial(flanks_body, columns.bit_length() - 1, blocks),
        "flanks",
        (there((devices, 1, 2 * systems * depth), F32), band, band, side, side, there((8, lanes), I32)),
        [hbm(), hbm(), smem(), hbm(), hbm()],
        (vmem(),) * 6,
        scratch=[pltpu.VMEM((4, systems, clat, 8, depth), F32), pltpu.VMEM(block_ids.shape, I32), pltpu.VMEM(block_offsets.shape, I32), dma((10,))],
        flops=1,
        moved=128 * systems * clat * depth,
    )(far(block_ids), far(block_offsets), ray_counts, model, damping)
    lists = exchange(asking)
    north = shifted(south_msg, "lat", 1)
    south = shifted(north_msg, "lat", -1)
    west = shifted(east_msg, "lon", 1)
    east = shifted(west_msg, "lon", -1)

    served, wanted, corner, diagonal = call(
        functools.partial(serve_body, cap, clat, clon),
        "serve",
        (
            there((slots * systems, depth), BF16),
            plain((devices, lanes), F32),
            plain((1,), I32),
            plain((4 * systems, depth), F32),
        ),
        [vmem(), hbm()] + [pl.BlockSpec(memory_space=pl.ANY)] * 4,
        (vmem(), vmem(), smem(), vmem()),
        scratch=[pltpu.VMEM(lines, F32), pltpu.VMEM((slots * systems, depth), F32), dma((systems,))],
    )(lists, model_flat, north, south, west, east)
    fetched = exchange(served.reshape(devices, group, depth)).reshape(slots * systems, depth)

    edge, flank = there((systems, clon, depth), F32), there((systems, clat, depth), F32)
    bar, held, *border, sums = call(
        functools.partial(damp_body, clat, clon),
        "damp",
        (
            there(flat, F32),
            here((HELD, width, depth), BF16),
            edge,
            edge,
            flank,
            flank,
            there((1, lanes), F32),
        ),
        [vmem()] + [hbm()] * 3 + [pl.BlockSpec(memory_space=pl.ANY)] * 4 + [hbm()],
        (hbm(),) + (vmem(),) * 6,
        scratch=[pltpu.VMEM(flat, F32)] * 3
        + [pltpu.VMEM(x.shape, F32) for x in (recurrence, north, south, west, east)]
        + [pltpu.SMEM((systems,), F32), dma((systems, 3)), dma, dma((5,))],
        flops=20 * systems * columns * depth,
        moved=12 * systems * columns * depth,
    )(diagonal, model_flat, damping_flat, far(recurrence), north, south, west, east, far(sensitivity))

    ray_bar, terms = call(
        functools.partial(rays_body, cap, blocks),
        "rays",
        (there(ray_vector.shape, F32), there((devices * chunk, 1, depth), F32)),
        [smem(), vmem(), vmem()] + [hbm()] * 4,
        (vmem(), vmem()),
        scratch=[
            pltpu.VMEM((tiles - HELD, width, depth), BF16),
            pltpu.VMEM((cap + 1, group, depth), BF16),
            pltpu.VMEM((blocks + 1, 16, width), BF16),
            pltpu.VMEM(recurrence.shape, F32),
            pltpu.VMEM(ray_vector.shape, F32),
            pltpu.VMEM((1, lanes), F32),
            dma((PARTS + 3,)),
        ],
        flops=4 * tiles * width * depth * 16,
        moved=2 * tiles * width * depth,
    )(meta, near(held), fetched, far(sensitivity), far(recurrence), far(ray_vector), far(sums))
    arrived = exchange(terms.reshape(devices, 1, chunk * depth)).reshape(devices * chunk, depth)

    padded = -(-devices * chunk // lanes) * lanes
    height = systems * PATCH * clon
    patch = (height, depth)
    image, sums, patched, model_patch, chosen = call(
        functools.partial(image_body, chunk, clat, clon),
        "image",
        (
            there(flat, F32),
            plain((1, lanes), F32),
            plain(patch, F32),
            plain(patch, F32),
            plain((height, padded), BF16),
        ),
        [smem(), vmem(), hbm()] + [vmem()] * 4 + [hbm(), vmem()],
        (hbm(),) + (vmem(),) * 4,
        scratch=[pltpu.VMEM(flat, F32)] * 3 + [dma((systems, 3))],
        flops=20 * systems * columns * depth,
        moved=12 * systems * columns * depth,
    )(corner, wanted, far(bar), *(far(x) for x in border), model_flat, far(sums))

    added, residual, parts = call(
        functools.partial(combine_body, chunk, systems),
        "combine",
        (plain(patch, F32), plain((1, lanes), F32), there((devices, lanes), F32)),
        [vmem()] * 5,
        (vmem(),) * 3,
        scratch=[pltpu.VMEM((padded, 3 * depth), BF16)],
    )(arrived, chosen, patched, model_patch, sums)
    every = exchange(parts.reshape(devices, 1, lanes)).reshape(devices, lanes)

    search_flat = far(search.reshape(flat))
    ray_out, damp_out, solution_out, kept = call(
        functools.partial(early_body, float(rows_all)),
        "early",
        (there(ray_vector.shape, F32), there(flat, F32), there(flat, F32), here((systems - 1, columns, depth), F32)),
        [vmem()] * 3 + [hbm()] * 3,
        (vmem(), hbm(), hbm(), vmem()),
        scratch=[pltpu.VMEM(flat, F32)] * 2
        + [pltpu.VMEM((1, columns, depth), F32)]
        + [pltpu.VMEM(flat, F32)] * 2
        + [pltpu.SMEM((2, systems), F32), dma((systems, PIECES, 3)), dma((systems, PIECES, 2))],
        mib=32,
        flops=4 * systems * columns * depth,
        moved=20 * systems * columns * depth,
    )(residual, far(recurrence), far(ray_bar), far(bar), far(solution.reshape(flat)), search_flat)
    model_out, search_out, rec_out = call(
        functools.partial(finish_body, float(rows_all), float(cells_all), clon),
        "finish",
        (there(flat, F32), there(flat, F32), there(recurrence.shape, F32)),
        [vmem()] * 4 + [hbm()] * 4,
        (hbm(),) * 3,
        scratch=[pltpu.VMEM(flat, F32)] * 2
        + [pltpu.VMEM((1, columns, depth), F32)]
        + [pltpu.VMEM(flat, F32)] * 2
        + [pltpu.VMEM(recurrence.shape, F32)] * 2
        + [pltpu.SMEM((3, systems), F32), dma((systems, PIECES, 3)), dma((systems, PIECES, 2)), dma((2,))],
        mib=32,
        flops=6 * systems * columns * depth,
        moved=20 * systems * columns * depth,
    )(residual, every, added, near(kept), far(image), model_flat, search_flat, far(recurrence))
    fields = (x.reshape(full) for x in (damp_out, model_out, solution_out, search_out))
    return (ray_out, *fields, rec_out)


def solution(mesh):
    fields = P(None, "lat", "lon", None)
    return jax.shard_map(
        per_device,
        mesh=mesh,
        in_specs=(
            P("lat", "lon", None, None, None),
            P("lat", "lon", None),
            P("lat", "lon", None),
            P("lat", "lon"),
            fields,
            fields,
            fields,
            fields,
            fields,
            P(),
        ),
        out_specs=(fields, fields, fields, fields, fields, P()),
        check_vma=False,
    )
```

```python
import functools

import jax
import jax.numpy as jnp
from jax import lax
from jax.experimental import pallas as pl
from jax.experimental.pallas import tpu as pltpu
from jax.sharding import PartitionSpec as P

DAMP_WEIGHT = 0.15
EPSILON = 1e-05
AXES = ("lat", "lon")
PATCH = 4
F32, BF16, I32 = jnp.float32, jnp.bfloat16, jnp.int32


def iota(shape, dim):
    return lax.broadcasted_iota(I32, shape, dim)


def vmem():
    return pl.BlockSpec(memory_space=pltpu.VMEM)


def hbm():
    return pl.BlockSpec(memory_space=pltpu.HBM)


def near(x):
    return pltpu.with_memory_space_constraint(x, pltpu.VMEM)


def far(x):
    return pltpu.with_memory_space_constraint(x, pltpu.HBM)


def smem():
    return pl.BlockSpec(memory_space=pltpu.SMEM)


def call(body, name, out_shape, in_specs, out_specs, scratch=(), grid=(), mib=16, flops=0, moved=0):
    return pl.pallas_call(
        body,
        name=name,
        grid=grid,
        out_shape=out_shape,
        in_specs=in_specs,
        out_specs=out_specs,
        scratch_shapes=list(scratch),
        compiler_params=pltpu.CompilerParams(vmem_limit_bytes=mib * 2**20),
        cost_estimate=pl.CostEstimate(flops=flops, bytes_accessed=moved, transcendentals=0),
    )


STEP = 8


def wanted_column(wanted, cap):
    devices, lanes = wanted.shape
    rows = devices * cap
    spread = jnp.broadcast_to(wanted[:, None, :], (devices, cap, lanes)).reshape(rows, lanes)
    pick = iota((rows, lanes), 1) == (iota((rows, lanes), 0) & (cap - 1))
    return jnp.sum(jnp.where(pick, spread, 0.0), axis=1, keepdims=True)


def serve_body(cap, clat, clon, lists_ref, model_in, north, south, west, east, served_ref, wanted_ref, corner_ref, diagonal_ref, patch, mixed, sems):
    systems, width, depth = patch.shape
    devices = lists_ref.shape[0]
    lanes = 128
    shift = (clat * clon).bit_length() - 1
    me = lax.axis_index("lat") * lax.axis_size("lon") + lax.axis_index("lon")
    ids = lists_ref[:, 0, 0:lanes].astype(I32)
    column = ids - lax.shift_left(me, shift)
    mine = (column >= 0) & (column < clat * clon) & (ids >= 0)
    first = jnp.min(jnp.where(mine, column, clat * clon))
    corner = jnp.minimum(lax.shift_right_logical(first, clon.bit_length() - 1), clat - PATCH)
    corner_ref[0] = corner
    at = pl.ds(pl.multiple_of(corner * clon, clon), width)
    copies = [pltpu.make_async_copy(model_in.at[r, at], patch.at[r], sems.at[r]) for r in range(systems)]
    for copy in copies:
        copy.start()
    ahead = (iota((lanes, lanes), 0) < iota((lanes, lanes), 1)).astype(F32).astype(BF16)
    rank = jnp.dot(mine.astype(F32).astype(BF16), ahead, preferred_element_type=F32)
    value = (column - corner * clon + 1).astype(F32)
    at = iota((devices, lanes), 1)
    wanted = jnp.zeros((devices, lanes), F32)
    for c in range(cap):
        picked = jnp.sum(jnp.where(mine & (rank == c), value, 0.0), axis=1, keepdims=True)
        wanted = jnp.where(at == c, picked, wanted)
    wanted_ref[...] = wanted
    target = wanted_column(wanted, cap).astype(I32) - 1
    rows = target.shape[0]
    chosen = (jnp.broadcast_to(target, (rows, width)) == iota((rows, width), 1)).astype(F32).astype(BF16)
    for r in range(systems):
        copies[r].wait()
        table = patch[r].astype(BF16)
        mixed[pl.ds(r, rows, stride=systems), :] = jnp.dot(chosen, table, preferred_element_type=F32)
    served_ref[...] = mixed[...].astype(BF16)
    lat_at, lon_at = lax.axis_index("lat"), lax.axis_index("lon")
    lat_size, lon_size = lax.axis_size("lat"), lax.axis_size("lon")
    for k in range(4):
        lat_to, lon_to = lat_at + 2 * (k // 2) - 1, lon_at + 2 * (k % 2) - 1
        inside = (lat_to >= 0) & (lat_to < lat_size) & (lon_to >= 0) & (lon_to < lon_size)
        source = jnp.where(inside, lat_to * lon_size + lon_to, 0)
        flag = inside.astype(F32)
        for r in range(systems):
            got = lists_ref[source, :, (r + 1) * depth : (r + 2) * depth]
            diagonal_ref[k * systems + r : k * systems + r + 1, :] = got * flag


def flanks_body(
    shift,
    blocks,
    ids_in,
    off_in,
    count_ref,
    model_in,
    damp_in,
    asking_ref,
    north_ref,
    south_ref,
    east_ref,
    west_ref,
    meta_ref,
    slabs,
    ids_ref,
    off_ref,
    sems,
):
    systems, clat, clon, depth = model_in.shape
    copies = []
    for k, (ref, at) in enumerate(((model_in, 0), (model_in, clon - 8), (damp_in, 0), (damp_in, clon - 8))):
        copies.append(pltpu.make_async_copy(ref.at[:, :, pl.ds(at, 8)], slabs.at[k], sems.at[k]))
    last = clat - 1
    pairs = (
        (model_in.at[:, pl.ds(last - 1, 2)], south_ref.at[:, pl.ds(0, 2)]),
        (damp_in.at[:, pl.ds(last, 1)], south_ref.at[:, pl.ds(2, 1)]),
        (model_in.at[:, pl.ds(0, 2)], north_ref.at[:, pl.ds(0, 2)]),
        (damp_in.at[:, pl.ds(0, 1)], north_ref.at[:, pl.ds(2, 1)]),
    )
    copies += [pltpu.make_async_copy(a, b, sems.at[i + 4]) for i, (a, b) in enumerate(pairs)]
    small = [
        pltpu.make_async_copy(a, b, sems.at[i + 8]) for i, (a, b) in enumerate(((ids_in, ids_ref), (off_in, off_ref)))
    ]
    begin(small + copies)
    settle(small)
    tiles = ids_ref.shape[-1]
    lanes = 128
    ids = jnp.concatenate([ids_ref[0], jnp.full((1, lanes - tiles), -1, I32)], axis=1)
    owner = lax.shift_right_arithmetic(ids, shift)
    square = (lanes, lanes)
    down, across = iota(square, 0), iota(square, 1)
    owner_f = jnp.broadcast_to(owner.astype(F32), square)
    owner_col = jnp.sum(jnp.where(down == across, owner_f, 0.0), axis=1, keepdims=True)
    same = jnp.where((owner_f == owner_col) & (down < across), 1.0, 0.0)
    rank = jnp.sum(same, axis=0, keepdims=True).astype(I32)
    lane = iota((1, lanes), 1)
    block = jnp.zeros((1, lanes), I32)
    starts = off_ref[0]
    for b in range(1, blocks + 1):
        block = block + (lane >= jnp.broadcast_to(starts[:, b : b + 1], (1, lanes))).astype(I32)
    count = jnp.full((1, lanes), count_ref[0, 0], I32)
    meta_ref[...] = jnp.concatenate([owner, rank, block, count] + [owner] * 4, axis=0)
    for copy in copies:
        copy.wait()
    listed = ids.astype(F32)
    asking_ref[...] = jnp.zeros(asking_ref.shape, F32)
    corners = [
        [slabs[k % 2, r, (k // 2) * last, (k % 2) * 7 : (k % 2) * 7 + 1] for r in range(systems)]
        for k in range(4)
    ]
    lat_at, lon_at = lax.axis_index("lat"), lax.axis_index("lon")
    width = lax.axis_size("lon")
    for e in range(asking_ref.shape[0]):
        asking_ref[e, :, 0:depth] = listed
        to_south, to_east = e // width > lat_at, e % width > lon_at
        for r in range(systems):
            upper = jnp.where(to_east, corners[1][r], corners[0][r])
            lower = jnp.where(to_east, corners[3][r], corners[2][r])
            asking_ref[e, :, (r + 1) * depth : (r + 2) * depth] = jnp.where(to_south, lower, upper)
    rows = slabs.reshape(4, systems, clat * 8, depth)
    for r in range(systems):
        for out, slab, near_at, beyond in ((east_ref, 1, 7, 6), (west_ref, 0, 0, 1)):
            out[r, 0:clat] = rows[slab, r, pl.ds(near_at, clat, stride=8), :]
            out[r, clat : 2 * clat] = rows[slab, r, pl.ds(beyond, clat, stride=8), :]
            out[r, 2 * clat : 3 * clat] = rows[slab + 2, r, pl.ds(near_at, clat, stride=8), :]


def six(x, north, south, west, east):
    lane = iota(x.shape, 1)
    rows, depth = x.shape
    left, right = pltpu.roll(x, 1, 0), pltpu.roll(x, rows - 1, 0)
    ends = (8, depth)
    row = iota(ends, 0)
    left = jnp.concatenate([jnp.where(row == 0, jnp.broadcast_to(west, ends), left[:8]), left[8:]], axis=0)
    right = jnp.concatenate([right[:-8], jnp.where(row == 7, jnp.broadcast_to(east, ends), right[-8:])], axis=0)
    above = jnp.where(lane == 0, 0.0, pltpu.roll(x, 1, 1))
    below = jnp.where(lane == depth - 1, 0.0, pltpu.roll(x, depth - 1, 1))
    beside = north + south + left + right + above + below
    return DAMP_WEIGHT * (6.0 * x - beside)


def fold(x):
    parts = [x[i * 8 : (i + 1) * 8] for i in range(x.shape[0] // 8)]
    return functools.reduce(lambda a, b: a + b, parts)


def place(row, lane, value):
    return row + jnp.where(iota(row.shape, 1) == lane, jnp.broadcast_to(value, row.shape), 0.0)


def line(ref, r, i, clon):
    return ref[r, pl.ds(pl.multiple_of(i * clon, clon), clon), :]


def stencils(ref, r, k, clat, clon, first, last, west, east):
    base = k * STEP
    for j in range(STEP):
        i = base + j
        x = line(ref, r, i, clon)
        if j == 0:
            above = jnp.where(k > 0, line(ref, r, jnp.maximum(i - 1, 0), clon), first)
        else:
            above = line(ref, r, i - 1, clon)
        if j == STEP - 1:
            below = jnp.where(i + 1 < clat, line(ref, r, jnp.minimum(i + 1, clat - 1), clon), last)
        else:
            below = line(ref, r, i + 1, clon)
        yield i, x, six(x, above, below, west[pl.ds(i, 1)], east[pl.ds(i, 1)])


def damp_body(
    clat,
    clon,
    rec_ref,
    diagonal_ref,
    model_in,
    damp_in,
    north_ref,
    south_ref,
    west_ref,
    east_ref,
    tiles_in,
    bar_sent,
    held_out,
    north_out,
    south_out,
    west_out,
    east_out,
    sums_out,
    model_ref,
    damp_ref,
    bar_out,
    alphas,
    sems,
    hold_sem,
):
    systems, _, depth = model_ref.shape

    def incoming(r):
        return (
            pltpu.make_async_copy(model_in.at[r], model_ref.at[r], sems.at[r, 0]),
            pltpu.make_async_copy(damp_in.at[r], damp_ref.at[r], sems.at[r, 1]),
        )

    def outgoing(r):
        return pltpu.make_async_copy(bar_out.at[r], bar_sent.at[r], sems.at[r, 2])

    holding = pltpu.make_async_copy(tiles_in.at[0, 0, pl.ds(0, HELD)], held_out, hold_sem)
    for r in range(systems):
        for copy in incoming(r):
            copy.start()
    holding.start()
    for r in range(systems):
        alphas[r] = jnp.sum(rec_ref[0:1, r : r + 1])
    lat_at, lon_at = lax.axis_index("lat"), lax.axis_index("lon")
    has_north = (lat_at > 0).astype(F32)
    has_south = (lat_at < lax.axis_size("lat") - 1).astype(F32)
    has_west = (lon_at > 0).astype(F32)
    has_east = (lon_at < lax.axis_size("lon") - 1).astype(F32)

    def diagonal(k, r):
        return diagonal_ref[pl.ds(k * systems + r, 1), :]

    def system(r, row):
        alpha = alphas[r]
        for copy in incoming(r):
            copy.wait()

        def side(ref, own, flag, east):
            x, beyond, old = ref[r, 0:clat], ref[r, clat : 2 * clat], ref[r, 2 * clat : 3 * clat]
            upper, lower = diagonal(east, r), diagonal(2 + east, r)
            return (six(x, beyond, own, upper, lower) - alpha * old) * flag

        west_out[r] = side(west_ref, model_ref[r, pl.ds(0, clat, stride=clon), :], has_west, 0)
        east_out[r] = side(east_ref, model_ref[r, pl.ds(clon - 1, clat, stride=clon), :], has_east, 1)
        top, bottom = line(model_ref, r, 0, clon), line(model_ref, r, clat - 1, clon)
        edge = six(north_ref[r, 1], north_ref[r, 0], top, diagonal(0, r), diagonal(1, r))
        north_out[r] = has_north * (edge - alpha * north_ref[r, 2])
        edge = six(south_ref[r, 0], bottom, south_ref[r, 1], diagonal(2, r), diagonal(3, r))
        south_out[r] = has_south * (edge - alpha * south_ref[r, 2])

        def damped(k, acc):
            bar_sq, model_sq = acc
            ends = (north_ref[r, 1], south_ref[r, 0], west_ref.at[r], east_ref.at[r])
            for i, x, got in stencils(model_ref, r, k, clat, clon, *ends):
                bar = got - alpha * line(damp_ref, r, i, clon)
                bar_out[r, pl.ds(pl.multiple_of(i * clon, clon), clon), :] = bar
                bar_sq, model_sq = bar_sq + fold(bar * bar), model_sq + fold(x * x)
            return bar_sq, model_sq

        zero = jnp.zeros((8, depth), F32)
        bar_sq, model_sq = lax.fori_loop(0, clat // STEP, damped, (zero, zero))
        outgoing(r).start()
        row = place(row, r, jnp.sum(bar_sq, keepdims=True))
        return place(row, 3 * systems + r, jnp.sum(model_sq, keepdims=True))

    sums_out[...] = lax.fori_loop(0, systems, system, jnp.zeros((1, depth), F32))
    holding.wait()
    for r in range(systems):
        outgoing(r).wait()


def image_body(
    chunk,
    clat,
    clon,
    corner_ref,
    wanted_ref,
    bar_in,
    north_ref,
    south_ref,
    west_ref,
    east_ref,
    model_in,
    sums_ref,
    image_sent,
    sums_out,
    patch_out,
    model_patch_out,
    chosen_out,
    bar_ref,
    model_ref,
    image_out,
    sems,
):
    systems, _, depth = model_ref.shape

    def incoming(r):
        return (
            pltpu.make_async_copy(bar_in.at[r], bar_ref.at[r], sems.at[r, 0]),
            pltpu.make_async_copy(model_in.at[r], model_ref.at[r], sems.at[r, 1]),
        )

    def outgoing(r):
        return pltpu.make_async_copy(image_out.at[r], image_sent.at[r], sems.at[r, 2])

    for r in range(systems):
        for copy in incoming(r):
            copy.start()
    corner = corner_ref[0]
    wanted = wanted_ref[...]
    devices = wanted.shape[0]
    height, slots = chosen_out.shape
    width = PATCH * clon
    at = iota((1, slots), 1)
    source = jnp.floor((at.astype(F32) + 0.5) * (1.0 / chunk)).astype(I32)
    inner = at - source * chunk
    from_e = (jnp.broadcast_to(source, (devices, slots)) == iota((devices, slots), 0)).astype(F32).astype(BF16)
    turned = jnp.transpose(wanted)[0:8].astype(BF16)
    listed = jnp.dot(turned, from_e, preferred_element_type=F32)
    slot_of = lax.shift_right_logical(inner, systems.bit_length() - 1)
    mine = jnp.broadcast_to(slot_of, listed.shape) == iota(listed.shape, 0)
    flat = jnp.sum(jnp.where(mine, listed, 0.0), axis=0, keepdims=True).astype(I32)
    used = (flat > 0) & (inner < chunk - 1)
    target = jnp.where(used, (inner & (systems - 1)) * width + flat - 1, -1)
    for k in range(height // 64):
        shape = (64, slots)
        hit = jnp.broadcast_to(target, shape) == iota(shape, 0) + k * 64
        chosen_out[k * 64 : (k + 1) * 64] = hit.astype(F32).astype(BF16)

    def system(r, row):
        for copy in incoming(r):
            copy.wait()

        def imaged(k, acc):
            image_sq, cross = acc
            ends = (north_ref[r], south_ref[r], west_ref.at[r], east_ref.at[r])
            for i, x, image in stencils(bar_ref, r, k, clat, clon, *ends):
                image_out[r, pl.ds(pl.multiple_of(i * clon, clon), clon), :] = image
                image_sq = image_sq + fold(image * image)
                cross = cross + fold(image * line(model_ref, r, i, clon))
            return image_sq, cross

        zero = jnp.zeros((8, depth), F32)
        image_sq, cross = lax.fori_loop(0, clat // STEP, imaged, (zero, zero))
        outgoing(r).start()
        here = pl.ds(pl.multiple_of(corner * clon, clon), width)
        there = pl.ds(pl.multiple_of(r * width, width), width)
        patch_out[there, :] = image_out[r, here, :]
        model_patch_out[there, :] = model_ref[r, here, :]
        row = place(row, systems + r, jnp.sum(image_sq, keepdims=True))
        return place(row, 2 * systems + r, jnp.sum(cross, keepdims=True))

    row = lax.fori_loop(0, systems, system, sums_ref[...])
    sums_out[...] = place(row, depth - 1, corner.astype(F32))
    for r in range(systems):
        outgoing(r).wait()


def rays_body(
    cap, blocks, meta_ref, held_ref, fetched_ref, tiles_in, *refs
):
    rec_in, old_in, sums_in, bar_ref, term_ref, rest_ref, masks, lows, rec_ref, old_ref, sums_ref, sems = refs
    tiles, width, depth = tiles_in.shape[2:]
    small = [
        pltpu.make_async_copy(a, b, sems.at[PARTS + k])
        for k, (a, b) in enumerate(((rec_in, rec_ref), (old_in, old_ref), (sums_in, sums_ref)))
    ]
    part = -(-(tiles - HELD) // PARTS)
    copies = []
    for k in range(PARTS):
        count = min(part, tiles - HELD - k * part)
        source = tiles_in.at[0, 0, pl.ds(HELD + k * part, count)]
        copies.append(pltpu.make_async_copy(source, rest_ref.at[pl.ds(k * part, count)], sems.at[k]))
    for copy in copies + small:
        copy.start()

    def tile(t):
        return held_ref[t] if t < HELD else rest_ref[t - HELD]

    systems = old_ref.shape[0]
    group = cap * systems
    chunk = group + 1
    devices = term_ref.shape[0] // chunk
    for c in range(cap + 1):
        here = lax.shift_right_logical(iota((group, depth), 0), systems.bit_length() - 1) == c
        masks[c] = here.astype(F32).astype(BF16)
    term_ref[...] = jnp.zeros(term_ref.shape, F32)
    lows[...] = jnp.zeros(lows.shape, BF16)
    total = jnp.zeros((blocks * group, width), F32)
    for t in range(tiles):
        if t >= HELD and (t - HELD) % part == 0:
            copies[(t - HELD) // part].wait()
        owner, rank, block = meta_ref[0, t], meta_ref[1, t], meta_ref[2, t]
        rows = fetched_ref[pl.ds(pl.multiple_of(owner * group, group), group), :]
        left = jnp.concatenate(
            [rows * masks[jnp.where(block == b, rank, cap)] for b in range(blocks)], axis=0
        )
        total = total + lax.dot_general(
            left, tile(t), (((1,), (1,)), ((), ())), preferred_element_type=F32
        )
    for copy in small:
        copy.wait()
    square = jnp.zeros((systems, width), F32)
    for b in range(blocks):
        traced = jnp.zeros((systems, width), F32)
        for c in range(cap):
            at = b * group + c * systems
            traced = traced + total[at : at + systems]
        old = jnp.concatenate(
            [old_ref[r, 0, :, b * width : (b + 1) * width] * rec_ref[0:1, r : r + 1] for r in range(systems)], axis=0
        )
        live = iota((systems, width), 1) + b * width < meta_ref[3, 0]
        bar = jnp.where(live, traced - old, 0.0)
        square = square + bar * bar
        for r in range(systems):
            bar_ref[r, 0, :, b * width : (b + 1) * width] = bar[r : r + 1]
        lows[b] = jnp.concatenate([bar, jnp.zeros((16 - systems, width), F32)], axis=0).astype(BF16)
    ray_sq = jnp.sum(square, axis=1, keepdims=True)
    part = sums_ref[...]
    for r in range(systems):
        part = place(part, r, ray_sq[r : r + 1])
    for e in range(devices):
        term_ref[e * chunk + group] = part
    for t in range(tiles):
        row = meta_ref[0, t] * chunk + meta_ref[1, t] * systems
        term = jnp.dot(lows[meta_ref[2, t]], tile(t), preferred_element_type=F32)
        for r in range(systems):
            term_ref[row + r] = term[r : r + 1]


def combine_body(chunk, systems, terms_ref, chosen_ref, patch_ref, model_patch_ref, sums_ref, added_ref, residual_ref, parts_ref, split):
    arrived, depth = terms_ref.shape
    devices = parts_ref.shape[0]
    width = patch_ref.shape[0]
    x = terms_ref[...]
    high = x.astype(BF16)
    rest = x - high.astype(F32)
    middle = rest.astype(BF16)
    low = (rest - middle.astype(F32)).astype(BF16)
    padded = split.shape[0]
    if padded > arrived:
        split[arrived:] = jnp.zeros((padded - arrived, split.shape[1]), BF16)
    split[0:arrived, 0:depth] = high
    split[0:arrived, depth : 2 * depth] = middle
    split[0:arrived, 2 * depth :] = low
    three = jnp.dot(chosen_ref[...], split[...], preferred_element_type=F32)
    added = three[:, 0:depth] + (three[:, depth : 2 * depth] + three[:, 2 * depth :])
    added_ref[...] = added
    every = terms_ref[pl.ds(chunk - 1, devices, stride=chunk), :]
    total = jnp.sum(every, axis=0, keepdims=True)
    residual_ref[...] = jnp.where(iota(total.shape, 1) == depth - 1, sums_ref[...], total)
    square = added * (2.0 * patch_ref[...] + added)
    cross = added * model_patch_ref[...]
    row = sums_ref[...]
    each = width // systems
    for r in range(systems):
        row = place(row, systems + r, jnp.sum(square[r * each : (r + 1) * each], keepdims=True))
        row = place(row, 2 * systems + r, jnp.sum(cross[r * each : (r + 1) * each], keepdims=True))
    parts_ref[...] = jnp.broadcast_to(row, parts_ref.shape)


def first_norm(residual_ref, systems, rows_all):
    return jnp.sqrt(residual_ref[0:1, 0:systems] / rows_all + EPSILON)


def early_body(
    rows_all,
    residual_ref,
    rec_ref,
    ray_ref,
    bar_in,
    solution_in,
    search_in,
    ray_out,
    damp_out,
    solution_out,
    kept_ref,
    bar_ref,
    solution_ref,
    search_ref,
    damp_s,
    solution_s,
    coef,
    in_sems,
    sems,
):
    systems, columns, _ = bar_ref.shape
    rows = columns // PIECES
    kept = kept_ref.shape[0]
    ins = ((bar_in, bar_ref), (solution_in, solution_ref))
    outs = ((damp_s, damp_out), (solution_s, solution_out))

    def start(n):
        if n < systems * PIECES:
            begin(fetch(n))

    def fetch(n):
        r, p = n // PIECES, n % PIECES
        at = pl.ds(p * rows, rows)
        target = kept_ref.at[r, at] if r < kept else search_ref.at[0, at]
        return pieces(ins, in_sems, r, p, rows) + [
            pltpu.make_async_copy(search_in.at[r, at], target, in_sems.at[r, p, 2])
        ]

    for n in range(AHEAD):
        start(n)
    rho_bar, phi_bar = rec_ref[1:2], rec_ref[2:3]
    beta = first_norm(residual_ref, systems, rows_all)
    rho = jnp.sqrt(rho_bar * rho_bar + beta * beta)
    scales = (1.0 / beta, (rho_bar / rho) * phi_bar / rho)
    for q, scale in enumerate(scales):
        for s in range(systems):
            coef[q, s] = scale[0, s]
    for s in range(systems):
        ray_out[s] = ray_ref[s] * coef[0, s]

    for n in range(systems * PIECES):
        r, p = n // PIECES, n % PIECES
        at = pl.ds(p * rows, rows)
        start(n + AHEAD)
        settle(fetch(n))
        search = kept_ref[r, at, :] if r < kept else search_ref[0, at, :]
        damp_s[r, at, :] = bar_ref[r, at, :] * coef[0, r]
        solution_s[r, at, :] = solution_ref[r, at, :] + search * coef[1, r]
        begin(pieces(outs, sems, r, p, rows))

    wait_all(outs, sems, systems, rows)


def finish_body(
    rows_all,
    cells_all,
    clon,
    residual_ref,
    parts_ref,
    added_ref,
    kept_ref,
    image_in,
    model_in,
    search_in,
    rec_in,
    model_out,
    search_out,
    rec_sent,
    image_ref,
    model_ref,
    search_ref,
    model_s,
    search_s,
    rec_ref,
    rec_out,
    coef,
    in_sems,
    sems,
    rec_sems,
):
    systems, columns, depth = image_ref.shape
    rec_copy = pltpu.make_async_copy(rec_in, rec_ref, rec_sems.at[0])
    rec_copy.start()
    rows = columns // PIECES
    kept = kept_ref.shape[0]
    ins = ((image_in, image_ref), (model_in, model_ref))
    outs = ((model_s, model_out), (search_s, search_out))

    def start(n):
        if n < systems * PIECES:
            begin(fetch(n))

    def fetch(n):
        r, p = n // PIECES, n % PIECES
        copies = pieces(ins, in_sems, r, p, rows)
        if r >= kept:
            at = pl.ds(p * rows, rows)
            copies.append(pltpu.make_async_copy(search_in.at[r, at], search_ref.at[0, at], in_sems.at[r, p, 2]))
        return copies

    for n in range(AHEAD):
        start(n)
    corner = residual_ref[0, depth - 1].astype(I32)
    total = jnp.sum(parts_ref[...], axis=0, keepdims=True)
    rec_copy.wait()
    image_sq, cross, model_sq = (total[:, q * systems : (q + 1) * systems] for q in range(1, 4))
    rho_bar, phi_bar = rec_ref[1:2], rec_ref[2:3]
    beta = first_norm(residual_ref, systems, rows_all)
    update_sq = image_sq / (beta * beta) - 2.0 * cross + beta * beta * model_sq
    alpha = jnp.sqrt(jnp.maximum(update_sq, 0.0) / cells_all + EPSILON)
    rho = jnp.sqrt(rho_bar * rho_bar + beta * beta)
    cosine = rho_bar / rho
    sine = beta / rho
    rec_out[...] = jnp.concatenate([alpha, -cosine * alpha, sine * phi_bar], axis=0)
    rec_done = pltpu.make_async_copy(rec_out, rec_sent, rec_sems.at[1])
    rec_done.start()
    scales = (1.0 / (beta * alpha), beta / alpha, sine * alpha / rho)
    for q, scale in enumerate(scales):
        for s in range(systems):
            coef[q, s] = scale[0, s]
    width = PATCH * clon

    for n in range(systems * PIECES):
        r, p = n // PIECES, n % PIECES
        at = pl.ds(p * rows, rows)
        start(n + AHEAD)
        settle(fetch(n))
        search = kept_ref[r, at, :] if r < kept else search_ref[0, at, :]
        new = image_ref[r, at, :] * coef[0, r] - model_ref[r, at, :] * coef[1, r]
        model_s[r, at, :] = new
        search_s[r, at, :] = new - search * coef[2, r]
        for k in range(PATCH):
            first = (corner + k) * clon

            @pl.when((first >= p * rows) & (first < (p + 1) * rows))
            def _():
                cells = pl.ds(pl.multiple_of(first, clon), clon)
                more = added_ref[r * width + k * clon : r * width + (k + 1) * clon, :] * coef[0, r]
                model_s[r, cells, :] = model_s[r, cells, :] + more
                search_s[r, cells, :] = search_s[r, cells, :] + more

        begin(pieces(outs, sems, r, p, rows))

    wait_all(outs, sems, systems, rows)
    rec_done.wait()


PIECES = 4
AHEAD = 8


def pieces(pairs, sems, r, p, rows):
    at = pl.ds(pl.multiple_of(p * rows, rows), rows)
    return [pltpu.make_async_copy(a.at[r, at], b.at[r, at], sems.at[r, p, k]) for k, (a, b) in enumerate(pairs)]


def begin(copies):
    for copy in copies:
        copy.start()


def settle(copies):
    for copy in copies:
        copy.wait()


def wait_all(pairs, sems, systems, rows):
    def one(n, _):
        for copy in pieces(pairs, sems, n // PIECES, n % PIECES, rows):
            copy.wait()
        return 0

    lax.fori_loop(0, systems * PIECES, one, 0)


PARTS = 3
HELD = 30


def shifted(x, axis, step):
    count = lax.axis_size(axis)
    if step > 0:
        pairs = [(i, i + 1) for i in range(count - 1)]
    else:
        pairs = [(i + 1, i) for i in range(count - 1)]
    return lax.ppermute(x, axis, pairs)


def exchange(x):
    return lax.all_to_all(x, AXES, split_axis=0, concat_axis=0, tiled=True)


def per_device(
    sensitivity,
    block_ids,
    block_offsets,
    ray_counts,
    ray_vector,
    damping_vector,
    model_vector,
    solution,
    search,
    recurrence,
):
    lat_size, lon_size = lax.axis_size("lat"), lax.axis_size("lon")
    devices = lat_size * lon_size
    tiles, width, depth = sensitivity.shape[2:]
    blocks = block_offsets.shape[-1] - 1
    systems, clat, clon, _ = model_vector.shape
    columns = clat * clon
    cap = max(2 * ((tiles + devices - 1) // devices), 16 // systems)
    slots = devices * cap
    group = cap * systems
    chunk = group + 1
    cells_all = devices * columns * depth
    rows_all = devices * blocks * width + cells_all
    lanes = 128
    full, flat = model_vector.shape, (systems, columns, depth)
    lines = (systems, PATCH * clon, depth)
    here, there, plain = pltpu.VMEM, pltpu.HBM, jax.ShapeDtypeStruct
    dma = pltpu.SemaphoreType.DMA
    model, damping = far(model_vector), far(damping_vector)
    model_flat, damping_flat = far(model_vector.reshape(flat)), far(damping_vector.reshape(flat))

    side = there((systems, 3 * clat, depth), F32)
    band = there((systems, 3, clon, depth), F32)
    asking, north_msg, south_msg, east_msg, west_msg, meta = call(
        functools.partial(flanks_body, columns.bit_length() - 1, blocks),
        "flanks",
        (there((devices, 1, 2 * systems * depth), F32), band, band, side, side, there((8, lanes), I32)),
        [hbm(), hbm(), smem(), hbm(), hbm()],
        (vmem(),) * 6,
        scratch=[pltpu.VMEM((4, systems, clat, 8, depth), F32), pltpu.VMEM(block_ids.shape, I32), pltpu.VMEM(block_offsets.shape, I32), dma((10,))],
        flops=1,
        moved=128 * systems * clat * depth,
    )(far(block_ids), far(block_offsets), ray_counts, model, damping)
    lists = exchange(asking)
    north = shifted(south_msg, "lat", 1)
    south = shifted(north_msg, "lat", -1)
    west = shifted(east_msg, "lon", 1)
    east = shifted(west_msg, "lon", -1)

    served, wanted, corner, diagonal = call(
        functools.partial(serve_body, cap, clat, clon),
        "serve",
        (
            there((slots * systems, depth), BF16),
            plain((devices, lanes), F32),
            plain((1,), I32),
            plain((4 * systems, depth), F32),
        ),
        [vmem(), hbm()] + [pl.BlockSpec(memory_space=pl.ANY)] * 4,
        (vmem(), vmem(), smem(), vmem()),
        scratch=[pltpu.VMEM(lines, F32), pltpu.VMEM((slots * systems, depth), F32), dma((systems,))],
    )(lists, model_flat, north, south, west, east)
    fetched = exchange(served.reshape(devices, group, depth)).reshape(slots * systems, depth)

    edge, flank = there((systems, clon, depth), F32), there((systems, clat, depth), F32)
    bar, held, *border, sums = call(
        functools.partial(damp_body, clat, clon),
        "damp",
        (
            there(flat, F32),
            here((HELD, width, depth), BF16),
            edge,
            edge,
            flank,
            flank,
            there((1, lanes), F32),
        ),
        [vmem()] * 2 + [hbm()] * 2 + [vmem()] * 4 + [hbm()],
        (hbm(),) + (vmem(),) * 6,
        scratch=[pltpu.VMEM(flat, F32)] * 3 + [pltpu.SMEM((systems,), F32), dma((systems, 3)), dma],
        flops=20 * systems * columns * depth,
        moved=12 * systems * columns * depth,
    )(far(recurrence), diagonal, model_flat, damping_flat, north, south, west, east, far(sensitivity))

    ray_bar, terms = call(
        functools.partial(rays_body, cap, blocks),
        "rays",
        (there(ray_vector.shape, F32), there((devices * chunk, 1, depth), F32)),
        [smem(), vmem(), vmem()] + [hbm()] * 4,
        (vmem(), vmem()),
        scratch=[
            pltpu.VMEM((tiles - HELD, width, depth), BF16),
            pltpu.VMEM((cap + 1, group, depth), BF16),
            pltpu.VMEM((blocks + 1, 16, width), BF16),
            pltpu.VMEM(recurrence.shape, F32),
            pltpu.VMEM(ray_vector.shape, F32),
            pltpu.VMEM((1, lanes), F32),
            dma((PARTS + 3,)),
        ],
        flops=4 * tiles * width * depth * 16,
        moved=2 * tiles * width * depth,
    )(meta, near(held), fetched, far(sensitivity), far(recurrence), far(ray_vector), far(sums))
    arrived = exchange(terms.reshape(devices, 1, chunk * depth)).reshape(devices * chunk, depth)

    padded = -(-devices * chunk // lanes) * lanes
    height = systems * PATCH * clon
    patch = (height, depth)
    image, sums, patched, model_patch, chosen = call(
        functools.partial(image_body, chunk, clat, clon),
        "image",
        (
            there(flat, F32),
            plain((1, lanes), F32),
            plain(patch, F32),
            plain(patch, F32),
            plain((height, padded), BF16),
        ),
        [smem(), vmem(), hbm()] + [vmem()] * 4 + [hbm(), vmem()],
        (hbm(),) + (vmem(),) * 4,
        scratch=[pltpu.VMEM(flat, F32)] * 3 + [dma((systems, 3))],
        flops=20 * systems * columns * depth,
        moved=12 * systems * columns * depth,
    )(corner, wanted, far(bar), *(far(x) for x in border), model_flat, far(sums))

    added, residual, parts = call(
        functools.partial(combine_body, chunk, systems),
        "combine",
        (plain(patch, F32), plain((1, lanes), F32), there((devices, lanes), F32)),
        [vmem()] * 5,
        (vmem(),) * 3,
        scratch=[pltpu.VMEM((padded, 3 * depth), BF16)],
    )(arrived, chosen, patched, model_patch, sums)
    every = exchange(parts.reshape(devices, 1, lanes)).reshape(devices, lanes)

    search_flat = far(search.reshape(flat))
    ray_out, damp_out, solution_out, kept = call(
        functools.partial(early_body, float(rows_all)),
        "early",
        (there(ray_vector.shape, F32), there(flat, F32), there(flat, F32), here((systems - 1, columns, depth), F32)),
        [vmem()] * 3 + [hbm()] * 3,
        (vmem(), hbm(), hbm(), vmem()),
        scratch=[pltpu.VMEM(flat, F32)] * 2
        + [pltpu.VMEM((1, columns, depth), F32)]
        + [pltpu.VMEM(flat, F32)] * 2
        + [pltpu.SMEM((2, systems), F32), dma((systems, PIECES, 3)), dma((systems, PIECES, 2))],
        mib=32,
        flops=4 * systems * columns * depth,
        moved=20 * systems * columns * depth,
    )(residual, far(recurrence), far(ray_bar), far(bar), far(solution.reshape(flat)), search_flat)
    model_out, search_out, rec_out = call(
        functools.partial(finish_body, float(rows_all), float(cells_all), clon),
        "finish",
        (there(flat, F32), there(flat, F32), there(recurrence.shape, F32)),
        [vmem()] * 4 + [hbm()] * 4,
        (hbm(),) * 3,
        scratch=[pltpu.VMEM(flat, F32)] * 2
        + [pltpu.VMEM((1, columns, depth), F32)]
        + [pltpu.VMEM(flat, F32)] * 2
        + [pltpu.VMEM(recurrence.shape, F32)] * 2
        + [pltpu.SMEM((3, systems), F32), dma((systems, PIECES, 3)), dma((systems, PIECES, 2)), dma((2,))],
        mib=32,
        flops=6 * systems * columns * depth,
        moved=20 * systems * columns * depth,
    )(residual, every, added, near(kept), far(image), model_flat, search_flat, far(recurrence))
    fields = (x.reshape(full) for x in (damp_out, model_out, solution_out, search_out))
    return (ray_out, *fields, rec_out)


def solution(mesh):
    fields = P(None, "lat", "lon", None)
    return jax.shard_map(
        per_device,
        mesh=mesh,
        in_specs=(
            P("lat", "lon", None, None, None),
            P("lat", "lon", None),
            P("lat", "lon", None),
            P("lat", "lon"),
            fields,
            fields,
            fields,
            fields,
            fields,
            P(),
        ),
        out_specs=(fields, fields, fields, fields, fields, P()),
        check_vma=False,
    )
```
